32 devices in a mesh: batch: 8 (over z, y), gate: 4 (over x, core).
Axes of the slice: x: 2, y: 2, z: 4, core: 2. Of those that a mesh axis runs over, the one named last changes fastest.
Arguments:
- inputs: bfloat16 [2, 384, 20, 512], P(None, 'batch'), may hold values from -6 to 6
- w_in: bfloat16 [2, 512, 4, 4096], P(None, None, None, 'gate'), may hold values from -0.1875 to 0.1875
- w_rec: bfloat16 [2, 512, 4, 4096], P(None, None, None, 'gate'), may hold values from -0.1875 to 0.1875
- bias: bfloat16 [2, 4, 4096], P(None, None, 'gate'), may hold values from -3 to 3
- proj: bfloat16 [2, 4096, 512], P(None, 'gate'), may hold values from -0.375 to 0.375
- state_h: float32 [384, 2, 512], P('batch'), may hold values from -2.9 to 2.9
- state_c: float32 [384, 2, 4096], P('batch', None, 'gate'), may hold values from -2.9 to 2.9
- resets: int32 [384, 20], P('batch'), may hold values from 0 to 1, as said below
- stream_doc: int32 [384], P('batch'), may hold values from 0 to 47, as said below
- cotangent: bfloat16 [2, 384, 20, 512], P(None, 'batch'), may hold values from -6 to 6
Outputs:
- outputs: bfloat16 [2, 384, 20, 512], P(None, 'batch')
- input_grad: bfloat16 [2, 384, 20, 512], P(None, 'batch', None, 'gate')
- grad_w_in: float32 [2, 512, 4, 4096], P(None, 'batch', None, 'gate')
- grad_w_rec: float32 [2, 512, 4, 4096], P(None, 'batch', None, 'gate')
- grad_bias: float32 [2, 4, 4096], P(None, None, ('gate', 'batch'))
- grad_proj: float32 [2, 4096, 512], P(None, 'gate', 'batch')
- final_h: float32 [384, 2, 512], P('batch')
- final_c: float32 [384, 2, 4096], P('batch', None, 'gate')
The draws below stay inside these ranges and needn't reach their ends.
Inputs may be any that keep to these rules, and one draw needn't show every extreme that they name: `resets`: each stream has at most one reset in the window. `stream_doc`: each aligned block of 48 streams holds a permutation of 0 to 47.
All inputs are finite; a program needn't handle non-finite values.
Results may differ from the reference program's by a relative error of at most 0.025.
Values may be sent and summed in bfloat16 or wider, within the bound.
No kernel may reach another device: no remote copies, remote signals or barrier semaphores. Data moves between devices by JAX's collectives and lax.ppermute only.
A program may use at most 256 MiB of HBM per device.

```python
import jax
import jax.numpy as jnp
from jax import lax

D = 512
CELL = 4096
STREAM_DEV = 48
STEPS = 20
STREAMS = 384
N_BATCH = 8


def draw_resets(key, part):
    key = jax.random.fold_in(key, 11)
    first_key, second_key = jax.random.split(key)
    chosen = jax.random.randint(first_key, (STREAMS, 1), 0, 4) == 0
    where_at = jax.random.randint(second_key, (STREAMS, 1), 0, STEPS)
    step_ids = jnp.arange(STEPS, dtype=jnp.int32)[None, :]
    return jnp.where(chosen & (step_ids == where_at), 1, 0).astype(jnp.int32)


def block_order(block_key):
    return jax.random.permutation(block_key, STREAM_DEV)


def draw_stream_doc(key, part):
    key = jax.random.fold_in(key, 23)
    block_keys = jax.random.split(key, STREAMS // STREAM_DEV)
    return jax.vmap(block_order)(block_keys).reshape(STREAMS).astype(jnp.int32)


def raised(entries, own_key, source, target, parts, factor):
    def block_of(axis_at):
        return (jnp.arange(entries.shape[axis_at]) // (entries.shape[axis_at] // parts)).reshape((-1,) + (1,) * (entries.ndim - 1 - axis_at))

    near = jax.random.permutation(own_key, parts)[block_of(target)]
    other_side = (block_of(target) + parts // 2) % parts
    return jnp.where((block_of(source) == near) | (block_of(source) == other_side), factor * entries, entries)


def block_levels(own_key, shape, cuts, smallest, largest):
    gain, own = 1.0, jax.random.fold_in(own_key, 6)
    for position, blocks in cuts:
        draws = jnp.exp(jax.random.uniform(jax.random.fold_in(own, position), (blocks,), jnp.float32, smallest / len(cuts), largest / len(cuts)))
        gain = gain * jnp.repeat(draws, shape[position] // blocks).reshape([-1 if axis == position else 1 for axis in range(len(shape))])
    return gain


def bell_draw(key, dims, scale, bound, shards=(), kind=jnp.bfloat16):
    level = block_levels(key, dims, shards, -0.22, 0.18) if shards else 1.0
    drawn = jax.random.normal(key, dims, jnp.float32) * scale * level
    return jnp.minimum(jnp.maximum(drawn, -bound), bound).astype(kind)


def bell_draw_with(key, extent, deviation, most, cuts, heavy, held_as=jnp.bfloat16):
    drawn = deviation * jax.random.normal(key, extent, jnp.float32)
    if cuts:
        drawn = drawn * block_levels(key, extent, cuts, -0.22, 0.18)
    return jnp.clip(raised(drawn, jax.random.fold_in(key, 3), *heavy), -most, most).astype(held_as)


def setup_inputs(seed: int = 0) -> dict:
    splits = jax.random.split(jax.random.key(seed), 11)
    inputs = bell_draw_with(splits[0], (2, STREAMS, STEPS, D), 1.0, 6.0, ((1, 8),), (1, 3, 8, 2.0))
    w_in = bell_draw(splits[1], (2, D, 4, CELL), (2 * D) ** -0.5, 0.1875, ((3, 4),))
    w_rec = bell_draw(splits[2], (2, D, 4, CELL), (2 * D) ** -0.5, 0.1875, ((3, 4),))
    bias = bell_draw(splits[3], (2, 4, CELL), 0.5, 3.0, ((2, 4),))
    proj = bell_draw(splits[4], (2, CELL, D), (CELL // 16) ** -0.5, 0.375, ((1, 4),))
    state_h = bell_draw(splits[5], (STREAMS, 2, D), 1.0, 2.9, ((0, 8),), jnp.float32)
    state_c = bell_draw(splits[6], (STREAMS, 2, CELL), 1.0, 2.9, ((0, 8), (2, 4)), jnp.float32)
    resets = draw_resets(jax.random.fold_in(splits[10], 71), 0)
    stream_doc = draw_stream_doc(jax.random.fold_in(splits[10], 71), 0)
    cotangent = bell_draw(splits[9], (2, STREAMS, STEPS, D), 1.0, 6.0, ((1, 8),))
    return dict(inputs=inputs, w_in=w_in, w_rec=w_rec, bias=bias, proj=proj, state_h=state_h, state_c=state_c, resets=resets, stream_doc=stream_doc, cotangent=cotangent)


CLIP_LEVEL = 3.0

@jax.custom_vjp
def low(v):
    return lax.optimization_barrier(v.astype(jnp.bfloat16)).astype(jnp.float32)

@jax.custom_vjp
def low_back(v):
    return v

def low_keep(v):
    return (low(v), None)

def low_pass(kept, grad):
    return (grad,)

def back_keep(v):
    return (v, None)

def back_low(kept, grad):
    return (low(grad),)
low.defvjp(low_keep, low_pass)
low_back.defvjp(back_keep, back_low)

def soft_clip(values):
    return CLIP_LEVEL * jnp.tanh(values / CLIP_LEVEL)

def by_direction(stacked):
    return jnp.stack([stacked[0], jnp.flip(stacked[1], axis=1)])

def keep_masks(resets):
    flags = resets.astype(jnp.float32)
    later = jnp.concatenate([flags[:, 1:], jnp.zeros_like(flags[:, :1])], axis=1)
    return jnp.stack([1.0 - flags, 1.0 - jnp.flip(later, axis=1)])

def gate_acts(pre_act):
    return (jax.nn.sigmoid(pre_act[:, :, 0]), jax.nn.sigmoid(pre_act[:, :, 1]), jnp.tanh(pre_act[:, :, 2]), jax.nn.sigmoid(pre_act[:, :, 3]))

def lstm_window(features, w_in, w_rec, bias, proj, keep_mask, start_h, start_c):
    exact_prec = lax.Precision.HIGHEST
    inflow = jnp.einsum('dstk,dkgc->tdsgc', features, w_in, precision=exact_prec)

    def time_step(state_pair, pieces):
        hidden, cell_state = state_pair
        inflow_t, keep_t = pieces
        hidden = hidden * keep_t[:, :, None]
        cell_state = cell_state * keep_t[:, :, None]
        pre_act = low_back(inflow_t + jnp.einsum('dsk,dkgc->dsgc', hidden, w_rec, precision=exact_prec) + bias[:, None])
        ingate, forget, candidate, outgate = gate_acts(pre_act)
        new_cell = soft_clip(forget * cell_state + ingate * candidate)
        cell_out = low(outgate * jnp.tanh(new_cell))
        raw_sum = low_back(jnp.einsum('dsc,dck->dsk', cell_out, proj, precision=exact_prec))
        next_hidden = low(soft_clip(raw_sum))
        return ((next_hidden, new_cell), next_hidden)
    (last_h, last_c), hidden_all = lax.scan(jax.checkpoint(time_step), (low(start_h), start_c), (inflow, jnp.moveaxis(keep_mask, 2, 0)))
    return (features + jnp.moveaxis(hidden_all, 0, 2), (last_h, last_c))

def group_view(stacked):
    shaped = stacked.reshape((2, N_BATCH, STREAM_DEV) + stacked.shape[2:])
    return jnp.moveaxis(shaped, 1, 0)

def ungroup(stacked):
    moved = jnp.moveaxis(stacked, 0, 1)
    return moved.reshape((2, STREAMS) + moved.shape[3:])

def reference(inputs, w_in, w_rec, bias, proj, state_h, state_c, resets, stream_doc, cotangent):
    features = by_direction(inputs.astype(jnp.float32))
    upstream = by_direction(cotangent.astype(jnp.float32))
    keep_mask = keep_masks(resets)
    documents = jnp.arange(STREAMS, dtype=jnp.int32) // STREAM_DEV * STREAM_DEV + stream_doc
    start_h = jnp.transpose(state_h[documents], (1, 0, 2))
    start_c = jnp.transpose(state_c[documents], (1, 0, 2))
    w_in32 = w_in.astype(jnp.float32)
    w_rec32 = w_rec.astype(jnp.float32)
    bias32 = bias.astype(jnp.float32)
    proj32 = proj.astype(jnp.float32)

    def one_group(totals, pieces):
        feat_group, keep_group, h_group, c_group, up_group = pieces

        def forward(feat_in, wi_in, wr_in, wb_in, wp_in):
            return lstm_window(feat_in, wi_in, wr_in, wb_in, wp_in, keep_group, h_group, c_group)
        out_group, pull_back, finals = jax.vjp(forward, feat_group, w_in32, w_rec32, bias32, proj32, has_aux=True)
        grads = pull_back(up_group)
        totals = (totals[0] + grads[1], totals[1] + grads[2], totals[2] + grads[3], totals[3] + grads[4])
        return (totals, (out_group, grads[0], finals[0], finals[1]))
    zeros_init = (jnp.zeros(w_in.shape, jnp.float32), jnp.zeros(w_rec.shape, jnp.float32), jnp.zeros(bias.shape, jnp.float32), jnp.zeros(proj.shape, jnp.float32))
    totals, (out_all, dx_all, last_h, last_c) = lax.scan(one_group, zeros_init, (group_view(features), group_view(keep_mask), group_view(start_h), group_view(start_c), group_view(upstream)))
    outputs = by_direction(ungroup(out_all)).astype(jnp.bfloat16)
    input_grad = by_direction(ungroup(dx_all)).astype(jnp.bfloat16)
    final_h = jnp.zeros((STREAMS, 2, D), jnp.float32).at[documents].set(jnp.transpose(ungroup(last_h), (1, 0, 2)))
    final_c = jnp.zeros((STREAMS, 2, CELL), jnp.float32).at[documents].set(jnp.transpose(ungroup(last_c), (1, 0, 2)))
    return (outputs, input_grad, totals[0], totals[1], totals[2], totals[3], final_h, final_c)
```

```python
import functools

import jax
import jax.numpy as jnp
from jax import lax
from jax.experimental import pallas as pl
from jax.experimental.pallas import tpu as pltpu
from jax.sharding import PartitionSpec as P

CLIP = 3.0
F32, BF16 = jnp.float32, jnp.bfloat16
QUARTERS, HALVES = 2, 2
PIECES = QUARTERS * HALVES
MIB = 2**20

VMEM = pl.BlockSpec(memory_space=pltpu.VMEM)
SMEM = pl.BlockSpec(memory_space=pltpu.SMEM)
ANY = pl.BlockSpec(memory_space=pl.ANY)


def pinned(array):
    return pltpu.with_memory_space_constraint(array, pltpu.VMEM)


def in_hbm(array):
    return pltpu.with_memory_space_constraint(array, pltpu.HBM)


def dot(left, right):
    return jnp.dot(left, right, preferred_element_type=F32)


def place_kernel(count, *refs):
    sources, targets, sems = refs[:count], refs[count : 2 * count], refs[2 * count]
    copies = [pltpu.make_async_copy(a, b, sems.at[i]) for i, (a, b) in enumerate(zip(sources, targets))]
    for copy in copies:
        copy.start()
    for copy in copies:
        copy.wait()


def place(*arrays):
    count = len(arrays)
    return pl.pallas_call(
        functools.partial(place_kernel, count),
        out_shape=tuple(pltpu.VMEM(x.shape, x.dtype) for x in arrays),
        in_specs=[ANY] * count,
        out_specs=[VMEM] * count,
        scratch_shapes=[pltpu.SemaphoreType.DMA((count,))],
        compiler_params=params(1),
        name="place",
    )(*arrays)


def pieces(refs, axis):
    for piece in range(PIECES):
        quarter, half = divmod(piece, HALVES)
        width = refs[0].shape[axis] // HALVES
        yield piece, quarter, width, slice(half * width, (half + 1) * width)


def forward_kernel(
    first, step_ref, p_ref, q_ref, start_ref, keep_ref, cell_ref, inflow_ref, wa_ref, wb_ref, pa_ref, pb_ref,
    part_ref, next_ref, gates_ref, mixed_ref, prev_ref, hidden_ref, slope_ref,
):
    keep = keep_ref[step_ref[1]][:, :1]
    if first:
        hidden = start_ref[...]
    else:
        hidden = clipped(p_ref, q_ref, hidden_ref, slope_ref)
    hidden = hidden * keep.astype(BF16)
    prev_ref[...] = hidden
    part = jnp.zeros(part_ref.shape, F32)
    for piece, quarter, width, cols in pieces((wa_ref, wb_ref), 2):
        w_ref, proj_ref = ((wa_ref, pa_ref), (wb_ref, pb_ref))[quarter]
        acts = []
        for gate in range(4):
            place = slice(gate * width, (gate + 1) * width)
            pre = dot(hidden, w_ref[gate, :, cols]) + inflow_ref[piece, :, place]
            act = jnp.tanh(pre if gate == 2 else 0.5 * pre)
            gates_ref[piece, :, place] = act.astype(BF16)
            acts.append(act if gate == 2 else 0.5 + 0.5 * act)
        ingate, forget, candidate, outgate = acts
        cell = CLIP * jnp.tanh((forget * (keep * cell_ref[piece]) + ingate * candidate) * (1.0 / CLIP))
        next_ref[piece] = cell
        mixed = (outgate * jnp.tanh(cell)).astype(BF16)
        mixed_ref[piece] = mixed
        part = part + dot(mixed, proj_ref[cols, :])
    part_ref[...] = part.astype(BF16)


def clipped(p_ref, q_ref, hidden_ref, slope_ref):
    squash = jnp.tanh((p_ref[...].astype(F32) + q_ref[...].astype(F32)) * (1.0 / CLIP))
    hidden = (CLIP * squash).astype(BF16)
    hidden_ref[...] = hidden
    slope_ref[...] = 1.0 - squash * squash
    return hidden


def between_kernel(
    first, step_ref, feat_ref, bias_ref, wa_ref, wb_ref, cell_ref, gates_ref, mixed_ref, prev_ref, hidden_ref, slope_ref,
    *refs,
):
    out_ref, gates_all, cells_all, mixed_all, prev_all, hidden_all, slope_all, sems = refs if first else refs[6:]
    step, time, time_before, time_after = (step_ref[i] for i in range(4))
    copies = [pltpu.make_async_copy(gates_ref.at[i], gates_all.at[i, step], sems.at[i]) for i in range(PIECES)]
    copies += [
        pltpu.make_async_copy(mixed_ref.at[i], mixed_all.at[i, time], sems.at[PIECES + i]) for i in range(PIECES)
    ]
    copies.append(pltpu.make_async_copy(cell_ref, cells_all.at[step], sems.at[2 * PIECES]))
    copies.append(pltpu.make_async_copy(prev_ref, prev_all.at[time], sems.at[2 * PIECES + 1]))
    if not first:
        copies.append(pltpu.make_async_copy(hidden_ref, hidden_all.at[time_before], sems.at[2 * PIECES + 2]))
        copies.append(pltpu.make_async_copy(slope_ref, slope_all.at[step - 1], sems.at[2 * PIECES + 3]))
    for copy in copies:
        copy.start()
    inflow_into(feat_ref[time_after], bias_ref, wa_ref, wb_ref, out_ref)
    for copy in copies:
        copy.wait()


def inflow_into(feat, bias_ref, wa_ref, wb_ref, out_ref):
    for piece, quarter, width, cols in pieces((wa_ref, wb_ref), 2):
        w_ref = (wa_ref, wb_ref)[quarter]
        for gate in range(4):
            place = slice(gate * width, (gate + 1) * width)
            out_ref[piece, :, place] = dot(feat, w_ref[gate, :, cols]) + bias_ref[piece, :, place]


def inflow_kernel(step_ref, feat_ref, bias_ref, wa_ref, wb_ref, out_ref):
    inflow_into(feat_ref[step_ref[1]], bias_ref, wa_ref, wb_ref, out_ref)


def backward_kernel(
    step_ref, p_ref, q_ref, keep_ref, grad_ref, wa_ref, wb_ref, pa_ref, pb_ref,
    gates_ref, cell_ref, prev_ref, slope_ref, up_ref, start_ref,
    part_ref, next_ref, raw_ref, dz_ref,
):
    step = step_ref[0]
    keep = keep_ref[step_ref[1]][:, :1]
    raw = (up_ref[...].astype(F32) + (p_ref[...].astype(F32) + q_ref[...].astype(F32))) * slope_ref[...]
    raw = raw.astype(BF16)
    raw_ref[...] = raw
    part = jnp.zeros(part_ref.shape, F32)
    for piece, quarter, width, cols in pieces((wa_ref, wb_ref), 1):
        w_ref, proj_ref = ((wa_ref, pa_ref), (wb_ref, pb_ref))[quarter]
        mixed = dot(raw, proj_ref[:, cols])
        acts = [gates_ref[piece, :, gate * width : (gate + 1) * width].astype(F32) for gate in range(4)]
        ingate, forget, outgate = (0.5 + 0.5 * acts[gate] for gate in (0, 1, 3))
        slopes = [1.0 - act * act for act in acts]
        cell = cell_ref[piece]
        prev = keep * jnp.where(step == 0, start_ref[piece], prev_ref[piece])
        squash = jnp.tanh(cell)
        total = grad_ref[piece] + mixed * outgate * (1.0 - squash * squash)
        inner = total * (1.0 - (cell * (1.0 / CLIP)) * (cell * (1.0 / CLIP)))
        next_ref[piece] = keep * inner * forget
        quart = 0.25 * inner
        pre_grads = (
            quart * acts[2] * slopes[0],
            quart * prev * slopes[1],
            inner * ingate * slopes[2],
            0.25 * mixed * squash * slopes[3],
        )
        for gate in range(4):
            low = pre_grads[gate].astype(BF16)
            dz_ref[piece, :, gate * width : (gate + 1) * width] = low
            part = part + dot(low, w_ref[gate, cols, :])
    part_ref[...] = (part * keep).astype(BF16)


def finish_kernel(
    step_ref, p_ref, q_ref, gates_all, cells_all, ups_all, hidden_in, slope_in,
    gates_ref, cell_ref, prev_ref, slope_ref, up_ref, hidden_all, slope_all,
    hidden_buf, sems, hidden_sem,
):
    copies = fetches(
        step_ref[0], step_ref[1], (gates_all, cells_all, ups_all), (gates_ref, cell_ref, prev_ref, up_ref), sems
    )
    for copy in copies:
        copy.start()
    clipped(p_ref, q_ref, hidden_buf, slope_ref)
    hidden_copy = pltpu.make_async_copy(hidden_buf, hidden_all.at[step_ref[1]], hidden_sem)
    hidden_copy.start()
    for copy in copies:
        copy.wait()
    hidden_copy.wait()


def fetches(step, time, sources, targets, sems):
    gates_all, cells_all, ups_all = sources
    gates_ref, cell_ref, prev_ref, up_ref = targets
    before = jnp.maximum(step - 1, 0)
    return [
        pltpu.make_async_copy(gates_all.at[i, step], gates_ref.at[i], sems.at[i]) for i in range(PIECES)
    ] + [
        pltpu.make_async_copy(cells_all.at[step], cell_ref, sems.at[PIECES]),
        pltpu.make_async_copy(cells_all.at[before], prev_ref, sems.at[PIECES + 1]),
        pltpu.make_async_copy(ups_all.at[time], up_ref, sems.at[PIECES + 2]),
    ]


def aside_kernel(
    first, step_ref, dz_ref, raw_ref, wa_ref, wb_ref, gates_all, cells_all, ups_all, slope_all, *refs
):
    gates_ref, cell_ref, prev_ref, slope_ref, up_ref, dz_all, raw_all, dx_all, dx_buf, sems, fetch_sems = (
        refs if first else refs[3:]
    )
    step, time, time_before = (step_ref[i] for i in range(3))
    before = jnp.maximum(step - 1, 0)
    copies = fetches(
        before, time_before, (gates_all, cells_all, ups_all), (gates_ref, cell_ref, prev_ref, up_ref), fetch_sems
    )
    copies.append(pltpu.make_async_copy(slope_all.at[before], slope_ref, fetch_sems.at[PIECES + 3]))
    copies += [pltpu.make_async_copy(dz_ref.at[i], dz_all.at[i, time], sems.at[i]) for i in range(PIECES)]
    copies.append(pltpu.make_async_copy(raw_ref, raw_all.at[time], sems.at[PIECES]))
    for copy in copies:
        copy.start()
    part = jnp.zeros(dx_buf.shape, F32)
    for piece, quarter, width, cols in pieces((wa_ref, wb_ref), 2):
        w_ref = (wa_ref, wb_ref)[quarter]
        for gate in range(4):
            part = part + lax.dot_general(
                dz_ref[piece, :, gate * width : (gate + 1) * width],
                w_ref[gate, :, cols],
                (((1,), (1,)), ((), ())),
                preferred_element_type=F32,
            )
    dx_buf[...] = part
    last = pltpu.make_async_copy(dx_buf, dx_all.at[time], sems.at[PIECES + 1])
    last.start()
    for copy in copies:
        copy.wait()
    last.wait()


def params(mib):
    return pltpu.CompilerParams(vmem_limit_bytes=mib * MIB)


def cost(flops, size):
    return pl.CostEstimate(flops=flops, bytes_accessed=size, transcendentals=0)


def body(inputs, w_in, w_rec, bias, proj, state_h, state_c, resets, stream_doc, cotangent):
    streams, steps, depth = inputs.shape[1:]
    cells = w_in.shape[3]
    width = cells // HALVES
    rank = lax.axis_index("gate")
    own = rank % 2
    gates_size = lax.axis_size("gate")
    swap = [(i, i ^ 1) for i in range(gates_size)]
    across = [(i, i ^ 2) for i in range(gates_size)]

    def pick(stacked, index):
        return lax.dynamic_index_in_dim(stacked, index, 0, keepdims=False)

    def trade(mine, theirs):
        return (mine, lax.ppermute(theirs, "gate", swap))

    def by_gate(stacked, index):
        return jnp.transpose(pick(stacked, index), (1, 0, 2))

    win_a, win_b = trade(by_gate(w_in, own), by_gate(w_in, 1 - own))
    rec_a, rec_b = trade(by_gate(w_rec, own), by_gate(w_rec, 1 - own))
    proj_a, proj_b = trade(pick(proj, own), pick(proj, 1 - own))
    bias_a, bias_b = trade(pick(bias, own), pick(bias, 1 - own))

    def pieces_of(pair):
        split = [x.reshape(4, HALVES, width) for x in pair]
        return jnp.transpose(jnp.stack(split), (0, 2, 1, 3)).reshape(PIECES, 1, 4 * width)

    bias_p = pieces_of((bias_a, bias_b)).astype(F32)

    def cells_to_pieces(pair):
        both = jnp.stack(pair).reshape(QUARTERS, streams, HALVES, width)
        return jnp.transpose(both, (0, 2, 1, 3)).reshape(PIECES, streams, width)

    def by_time(stacked):
        return jnp.transpose(pick(stacked, own), (1, 0, 2))

    feats = by_time(inputs)
    ups = by_time(cotangent)
    flags = resets.astype(F32)
    later = jnp.concatenate([flags[:, 1:], jnp.zeros_like(flags[:, :1])], axis=1)
    keep = 1.0 - jnp.where(own == 0, flags, later)
    keep = jnp.broadcast_to(jnp.transpose(keep)[:, :, None], (steps, streams, 128))

    docs_h = state_h[stream_doc]
    docs_c = state_c[stream_doc]
    start_h = pick(jnp.transpose(docs_h, (1, 0, 2)), own).astype(BF16)
    by_dir_c = jnp.transpose(docs_c, (1, 0, 2))
    start_c = cells_to_pieces(trade(pick(by_dir_c, own), pick(by_dir_c, 1 - own)))

    def at_step(step):
        near = jnp.array([step, step, max(step - 1, 0), min(step + 1, steps - 1)], jnp.int32)
        turned = jnp.array([step] + [steps - 1 - x for x in (step, max(step - 1, 0), min(step + 1, steps - 1))], jnp.int32)
        return jnp.where(own == 0, near, turned)

    def vmem(shape, dtype):
        return pltpu.VMEM(shape, dtype)

    def hbm(shape, dtype):
        return pltpu.HBM(shape, dtype)

    feats_v, keep_v, bias_v, win_av, win_bv = place(feats, keep, bias_p, win_a, win_b)
    rec_av, rec_bv, proj_av, proj_bv, start_hv, start_cv = place(rec_a, rec_b, proj_a, proj_b, start_h, start_c)

    gates_shape, cell_shape = (PIECES, streams, 4 * width), (PIECES, streams, width)
    inflow = pl.pallas_call(
        inflow_kernel,
        out_shape=vmem(gates_shape, F32),
        in_specs=[SMEM] + [VMEM] * 4,
        out_specs=VMEM,
        compiler_params=params(8),
        name="inflow",
    )(at_step(0), pinned(feats_v), pinned(bias_v), pinned(win_av), pinned(win_bv))

    def forward_call(first, step, part, peer, cell, inflow):
        return pl.pallas_call(
            functools.partial(forward_kernel, first),
            out_shape=(
                vmem((streams, depth), BF16),
                vmem(cell_shape, F32),
                vmem(gates_shape, BF16),
                vmem(cell_shape, BF16),
                vmem((streams, depth), BF16),
                vmem((streams, depth), BF16),
                vmem((streams, depth), F32),
            ),
            in_specs=[SMEM] + [VMEM] * 10,
            out_specs=[VMEM] * 7,
            compiler_params=params(8),
            name="forward_step",
        )(
            at_step(step), pinned(part), pinned(peer), pinned(start_hv), pinned(keep_v), pinned(cell), pinned(inflow),
            pinned(rec_av), pinned(rec_bv), pinned(proj_av), pinned(proj_bv),
        )

    def between_call(step, fresh, stacks):
        shapes = (
            hbm((PIECES, steps, streams, 4 * width), BF16),
            hbm((steps,) + cell_shape, F32),
            hbm((PIECES, steps, streams, width), BF16),
            hbm((steps, streams, depth), BF16),
            hbm((steps, streams, depth), BF16),
            hbm((steps, streams, depth), F32),
        )
        inflow, *stacks = pl.pallas_call(
            functools.partial(between_kernel, not stacks),
            out_shape=(vmem(gates_shape, F32),) + shapes,
            in_specs=[SMEM] + [VMEM] * 10 + [ANY] * len(stacks),
            out_specs=[VMEM] + [ANY] * 6,
            scratch_shapes=[pltpu.SemaphoreType.DMA((2 * PIECES + 4,))],
            input_output_aliases={11 + i: 1 + i for i in range(len(stacks))},
            compiler_params=params(8),
            cost_estimate=cost(2 * streams * depth * 8 * cells, 8 * depth * cells * 2),
            name="between",
        )(
            at_step(step), pinned(feats_v), pinned(bias_v), pinned(win_av), pinned(win_bv),
            *(pinned(x) for x in fresh), *(in_hbm(x) for x in stacks),
        )
        return inflow, tuple(stacks)

    def forward_step(step, carry, first=False):
        part, peer, cell, inflow, stacks = carry
        part, cell, *fresh = forward_call(first, step, part, peer, cell, inflow)
        peer = lax.ppermute(part, "gate", across)
        inflow, stacks = between_call(step, (cell, *fresh), stacks)
        return (part, peer, cell, inflow, stacks)

    none = jnp.zeros((streams, depth), BF16)
    carry = forward_step(0, (none, none, start_cv, inflow, ()), True)
    for step in range(1, steps):
        carry = forward_step(step, carry)
    part, peer, cell, _, stacks = carry
    gates_all, cells_all, mixed_all, prev_all, hidden_all, slope_all = stacks

    saved_shapes = (
        vmem(gates_shape, BF16),
        vmem(cell_shape, F32),
        vmem(cell_shape, F32),
        vmem((streams, depth), F32),
        vmem((streams, depth), BF16),
    )
    *saved, hidden_all, slope_all = pl.pallas_call(
        finish_kernel,
        out_shape=saved_shapes + (hbm((steps, streams, depth), BF16), hbm((steps, streams, depth), F32)),
        in_specs=[SMEM, VMEM, VMEM] + [ANY] * 5,
        out_specs=[VMEM] * 5 + [ANY] * 2,
        scratch_shapes=[
            pltpu.VMEM((streams, depth), BF16),
            pltpu.SemaphoreType.DMA((PIECES + 4,)),
            pltpu.SemaphoreType.DMA,
        ],
        input_output_aliases={6: 5, 7: 6},
        compiler_params=params(8),
        name="finish",
    )(
        at_step(steps - 1), pinned(part), pinned(peer), in_hbm(gates_all), in_hbm(cells_all), in_hbm(ups),
        in_hbm(hidden_all), in_hbm(slope_all),
    )

    both_hidden = trade(hidden_all, hidden_all)

    def by_direction(mine, theirs):
        return jnp.stack([jnp.where(own == 0, mine, theirs), jnp.where(own == 0, theirs, mine)])

    hidden_dirs = by_direction(*both_hidden)
    outputs = (inputs.astype(F32) + jnp.transpose(hidden_dirs, (0, 2, 1, 3)).astype(F32)).astype(BF16)
    last_h = jnp.stack([hidden_dirs[0, steps - 1], hidden_dirs[1, 0]], axis=1).astype(F32)
    final_h = jnp.zeros_like(state_h).at[stream_doc].set(last_h)
    last_c = jnp.transpose(cell.reshape(QUARTERS, HALVES, streams, width), (0, 2, 1, 3)).reshape(
        QUARTERS, streams, cells
    )
    last_dirs = by_direction(*trade(last_c[0], last_c[1]))
    final_c = jnp.zeros_like(state_c).at[stream_doc].set(jnp.transpose(last_dirs, (1, 0, 2)))

    rec_at, rec_bt = (jnp.transpose(x, (0, 2, 1)) for x in (rec_a, rec_b))
    proj_at, proj_bt = jnp.transpose(proj_a), jnp.transpose(proj_b)
    rec_atv, rec_btv, proj_atv, proj_btv = place(rec_at, rec_bt, proj_at, proj_bt)

    def backward_call(step, part, peer, grad, saved):
        return pl.pallas_call(
            backward_kernel,
            out_shape=(
                vmem((streams, depth), BF16),
                vmem(cell_shape, F32),
                vmem((streams, depth), BF16),
                vmem(gates_shape, BF16),
            ),
            in_specs=[SMEM] + [VMEM] * 14,
            out_specs=[VMEM] * 4,
            compiler_params=params(8),
            name="backward_step",
        )(
            at_step(step), pinned(part), pinned(peer), pinned(keep_v), pinned(grad),
            pinned(rec_atv), pinned(rec_btv), pinned(proj_atv), pinned(proj_btv),
            *(pinned(x) for x in saved), pinned(start_cv),
        )

    def aside_call(step, dz, raw, stacks):
        shapes = (
            hbm((PIECES, steps, streams, 4 * width), BF16),
            hbm((steps, streams, depth), BF16),
            hbm((steps, streams, depth), F32),
        )
        *outs, dz_all, raw_all, dx_all = pl.pallas_call(
            functools.partial(aside_kernel, not stacks),
            out_shape=saved_shapes + shapes,
            in_specs=[SMEM] + [VMEM] * 4 + [ANY] * (4 + len(stacks)),
            out_specs=[VMEM] * 5 + [ANY] * 3,
            scratch_shapes=[
                pltpu.VMEM((streams, depth), F32),
                pltpu.SemaphoreType.DMA((PIECES + 2,)),
                pltpu.SemaphoreType.DMA((PIECES + 4,)),
            ],
            input_output_aliases={9 + i: 5 + i for i in range(len(stacks))},
            compiler_params=params(8),
            cost_estimate=cost(2 * streams * depth * 8 * cells, 8 * depth * cells * 2),
            name="aside",
        )(
            at_step(step), pinned(dz), pinned(raw), pinned(win_av), pinned(win_bv),
            in_hbm(gates_all), in_hbm(cells_all), in_hbm(ups), in_hbm(slope_all), *(in_hbm(x) for x in stacks),
        )
        return outs, (dz_all, raw_all, dx_all)

    def backward_step(index, carry):
        step = steps - 1 - index
        part, peer, grad, saved, stacks = carry
        part, grad, raw, dz = backward_call(step, part, peer, grad, saved)
        peer = lax.ppermute(part, "gate", across)
        saved, stacks = aside_call(step, dz, raw, stacks)
        return (part, peer, grad, saved, stacks)

    carry = backward_step(0, (none, none, jnp.zeros(cell_shape, F32), saved, ()))
    for index in range(1, steps):
        carry = backward_step(index, carry)
    dz_all, raw_all, dx_all = carry[-1]
    rows = steps * streams
    dz = dz_all.reshape(PIECES, rows, 4 * width)

    def weight_grad(left):
        return jnp.einsum("rk,prn->kpn", left.reshape(rows, depth), dz, preferred_element_type=F32).astype(BF16)

    grad_in = lax.psum_scatter(weight_grad(feats), "batch", scatter_dimension=0, tiled=True)
    grad_rec = lax.psum_scatter(weight_grad(prev_all), "batch", scatter_dimension=0, tiled=True)
    grad_bias = jnp.sum(dz, axis=1, dtype=F32)
    grad_proj = jnp.einsum(
        "ptnc,tnk->kpc", mixed_all, raw_all, preferred_element_type=F32
    ).astype(BF16)
    grad_proj = lax.psum_scatter(grad_proj, "batch", scatter_dimension=0, tiled=True)

    def whole_gates(pieces):
        shaped = pieces.reshape(-1, QUARTERS, HALVES, 4, width)
        return jnp.transpose(shaped, (1, 0, 3, 2, 4)).reshape(QUARTERS, -1, 4, cells)

    def home(quarters):
        return by_direction(*trade(quarters[0], quarters[1])).astype(F32)

    grad_w_in = home(whole_gates(grad_in))
    grad_w_rec = home(whole_gates(grad_rec))
    grad_bias = home(whole_gates(grad_bias[None])[:, 0])
    grad_bias = lax.psum_scatter(grad_bias, "batch", scatter_dimension=2, tiled=True)
    grad_proj = home(jnp.transpose(grad_proj.reshape(-1, QUARTERS, cells), (1, 2, 0)))

    half_cols = depth // 2
    upper = rank // 2
    keep_cols = lax.dynamic_slice_in_dim(dx_all, upper * half_cols, half_cols, 2)
    send_cols = lax.dynamic_slice_in_dim(dx_all, (1 - upper) * half_cols, half_cols, 2).astype(BF16)
    dx_half = keep_cols + lax.ppermute(send_cols, "gate", across).astype(F32)
    up_half = lax.dynamic_slice_in_dim(ups, upper * half_cols, half_cols, 2).astype(F32)
    dx_half = (dx_half + up_half).astype(BF16)
    quarter_cols = half_cols // 2
    mine = lax.dynamic_slice_in_dim(dx_half, own * quarter_cols, quarter_cols, 2)
    theirs = lax.dynamic_slice_in_dim(dx_half, (1 - own) * quarter_cols, quarter_cols, 2)
    dx_dirs = by_direction(*trade(mine, theirs))
    input_grad = jnp.transpose(dx_dirs, (0, 2, 1, 3))
    return (outputs, input_grad, grad_w_in, grad_w_rec, grad_bias, grad_proj, final_h, final_c)


def solution(mesh):
    placed = (
        P(None, "batch", None, None),
        P(None, None, None, "gate"),
        P(None, None, None, "gate"),
        P(None, None, "gate"),
        P(None, "gate", None),
        P("batch", None, None),
        P("batch", None, "gate"),
        P("batch", None),
        P("batch"),
        P(None, "batch", None, None),
    )
    return jax.shard_map(
        body,
        mesh=mesh,
        in_specs=placed,
        out_specs=(
            P(None, "batch", None, None),
            P(None, "batch", None, "gate"),
            P(None, "batch", None, "gate"),
            P(None, "batch", None, "gate"),
            P(None, None, ("gate", "batch")),
            P(None, "gate", "batch"),
            P("batch", None, None),
            P("batch", None, "gate"),
        ),
        check_vma=False,
    )
```

```python
import functools

import jax
import jax.numpy as jnp
from jax import lax
from jax.experimental import pallas as pl
from jax.experimental.pallas import tpu as pltpu
from jax.sharding import PartitionSpec as P

CLIP = 3.0
F32, BF16 = jnp.float32, jnp.bfloat16
QUARTERS, HALVES = 2, 2
PIECES = QUARTERS * HALVES
MIB = 2**20
SHARES = (0.3, 0.3, 0.2, 0.1, 0.1)

VMEM = pl.BlockSpec(memory_space=pltpu.VMEM)
SMEM = pl.BlockSpec(memory_space=pltpu.SMEM)
ANY = pl.BlockSpec(memory_space=pl.ANY)


def pinned(array):
    return pltpu.with_memory_space_constraint(array, pltpu.VMEM)


def in_hbm(array):
    return pltpu.with_memory_space_constraint(array, pltpu.HBM)


def dot(left, right):
    return jnp.dot(left, right, preferred_element_type=F32)


def place_kernel(count, *refs):
    sources, targets, sems = refs[:count], refs[count : 2 * count], refs[2 * count]
    copies = [pltpu.make_async_copy(a, b, sems.at[i]) for i, (a, b) in enumerate(zip(sources, targets))]
    for copy in copies:
        copy.start()
    for copy in copies:
        copy.wait()


def place(*arrays):
    count = len(arrays)
    return pl.pallas_call(
        functools.partial(place_kernel, count),
        out_shape=tuple(pltpu.VMEM(x.shape, x.dtype) for x in arrays),
        in_specs=[ANY] * count,
        out_specs=[VMEM] * count,
        scratch_shapes=[pltpu.SemaphoreType.DMA((count,))],
        compiler_params=params(1),
        name="place",
    )(*arrays)


def pieces(refs, axis):
    for piece in range(PIECES):
        quarter, half = divmod(piece, HALVES)
        width = refs[0].shape[axis] // HALVES
        yield piece, quarter, width, slice(half * width, (half + 1) * width)


def forward_kernel(
    first, step_ref, p_ref, q_ref, start_ref, keep_ref, cell_ref, inflow_ref, wa_ref, wb_ref, pa_ref, pb_ref,
    part_ref, next_ref, gates_ref, mixed_ref, prev_ref, hidden_ref, slope_ref,
):
    keep = keep_ref[step_ref[1]][:, :1]
    if first:
        hidden = start_ref[...]
    else:
        hidden = clipped(p_ref, q_ref, hidden_ref, slope_ref)
    hidden = hidden * keep.astype(BF16)
    prev_ref[...] = hidden
    part = jnp.zeros(part_ref.shape, F32)
    for piece, quarter, width, cols in pieces((wa_ref, wb_ref), 2):
        w_ref, proj_ref = ((wa_ref, pa_ref), (wb_ref, pb_ref))[quarter]
        acts = []
        for gate in range(4):
            place = slice(gate * width, (gate + 1) * width)
            pre = dot(hidden, w_ref[gate, :, cols]) + inflow_ref[piece, :, place]
            act = jnp.tanh(pre if gate == 2 else 0.5 * pre)
            gates_ref[piece, :, place] = act.astype(BF16)
            acts.append(act if gate == 2 else 0.5 + 0.5 * act)
        ingate, forget, candidate, outgate = acts
        cell = CLIP * jnp.tanh((forget * (keep * cell_ref[piece]) + ingate * candidate) * (1.0 / CLIP))
        next_ref[piece] = cell
        mixed = (outgate * jnp.tanh(cell)).astype(BF16)
        mixed_ref[piece] = mixed
        part = part + dot(mixed, proj_ref[cols, :])
    part_ref[...] = part.astype(BF16)


def clipped(p_ref, q_ref, hidden_ref, slope_ref):
    squash = jnp.tanh((p_ref[...].astype(F32) + q_ref[...].astype(F32)) * (1.0 / CLIP))
    hidden = (CLIP * squash).astype(BF16)
    hidden_ref[...] = hidden
    slope_ref[...] = 1.0 - squash * squash
    return hidden


def between_kernel(
    first, step_ref, feat_ref, bias_ref, wa_ref, wb_ref, cell_ref, gates_ref, mixed_ref, prev_ref, hidden_ref, slope_ref,
    *refs,
):
    out_ref, gates_all, cells_all, mixed_all, prev_all, feat_all, hidden_all, slope_all, sems = refs if first else refs[7:]
    step, time, time_before, time_after = (step_ref[i] for i in range(4))
    copies = [pltpu.make_async_copy(gates_ref.at[i], gates_all.at[i, step], sems.at[i]) for i in range(PIECES)]
    copies += [
        pltpu.make_async_copy(mixed_ref.at[i], mixed_all.at[i, step], sems.at[PIECES + i]) for i in range(PIECES)
    ]
    copies.append(pltpu.make_async_copy(cell_ref, cells_all.at[step], sems.at[2 * PIECES]))
    copies.append(pltpu.make_async_copy(prev_ref, prev_all.at[step], sems.at[2 * PIECES + 1]))
    copies.append(pltpu.make_async_copy(feat_ref.at[time], feat_all.at[step], sems.at[2 * PIECES + 4]))
    if not first:
        copies.append(pltpu.make_async_copy(hidden_ref, hidden_all.at[time_before], sems.at[2 * PIECES + 2]))
        copies.append(pltpu.make_async_copy(slope_ref, slope_all.at[step - 1], sems.at[2 * PIECES + 3]))
    for copy in copies:
        copy.start()
    inflow_into(feat_ref[time_after], bias_ref, wa_ref, wb_ref, out_ref)
    for copy in copies:
        copy.wait()


def inflow_into(feat, bias_ref, wa_ref, wb_ref, out_ref):
    for piece, quarter, width, cols in pieces((wa_ref, wb_ref), 2):
        w_ref = (wa_ref, wb_ref)[quarter]
        for gate in range(4):
            place = slice(gate * width, (gate + 1) * width)
            out_ref[piece, :, place] = dot(feat, w_ref[gate, :, cols]) + bias_ref[piece, :, place]


def inflow_kernel(step_ref, feat_ref, bias_ref, wa_ref, wb_ref, out_ref):
    inflow_into(feat_ref[step_ref[1]], bias_ref, wa_ref, wb_ref, out_ref)


def backward_kernel(
    step_ref, p_ref, q_ref, keep_ref, grad_ref, wa_ref, wb_ref, pa_ref, pb_ref,
    gates_ref, cell_ref, prev_ref, slope_ref, up_ref, start_ref,
    part_ref, next_ref, raw_ref, dz_ref,
):
    step = step_ref[0]
    keep = keep_ref[step_ref[1]][:, :1]
    raw = (up_ref[...].astype(F32) + (p_ref[...].astype(F32) + q_ref[...].astype(F32))) * slope_ref[...]
    raw = raw.astype(BF16)
    raw_ref[...] = raw
    part = jnp.zeros(part_ref.shape, F32)
    for piece, quarter, width, cols in pieces((wa_ref, wb_ref), 1):
        w_ref, proj_ref = ((wa_ref, pa_ref), (wb_ref, pb_ref))[quarter]
        mixed = dot(raw, proj_ref[:, cols])
        acts = [gates_ref[piece, :, gate * width : (gate + 1) * width].astype(F32) for gate in range(4)]
        ingate, forget, outgate = (0.5 + 0.5 * acts[gate] for gate in (0, 1, 3))
        slopes = [1.0 - act * act for act in acts]
        cell = cell_ref[piece]
        prev = keep * jnp.where(step == 0, start_ref[piece], prev_ref[piece])
        squash = jnp.tanh(cell)
        total = grad_ref[piece] + mixed * outgate * (1.0 - squash * squash)
        inner = total * (1.0 - (cell * (1.0 / CLIP)) * (cell * (1.0 / CLIP)))
        next_ref[piece] = keep * inner * forget
        quart = 0.25 * inner
        pre_grads = (
            quart * acts[2] * slopes[0],
            quart * prev * slopes[1],
            inner * ingate * slopes[2],
            0.25 * mixed * squash * slopes[3],
        )
        for gate in range(4):
            low = pre_grads[gate].astype(BF16)
            dz_ref[piece, :, gate * width : (gate + 1) * width] = low
            part = part + dot(low, w_ref[gate, cols, :])
    part_ref[...] = (part * keep).astype(BF16)


def finish_kernel(
    step_ref, p_ref, q_ref, gates_all, cells_all, ups_all, hidden_in, slope_in,
    gates_ref, cell_ref, prev_ref, slope_ref, up_ref, hidden_all, slope_all,
    hidden_buf, sems, hidden_sem,
):
    copies = fetches(
        step_ref[0], step_ref[1], (gates_all, cells_all, ups_all), (gates_ref, cell_ref, prev_ref, up_ref), sems
    )
    for copy in copies:
        copy.start()
    clipped(p_ref, q_ref, hidden_buf, slope_ref)
    hidden_copy = pltpu.make_async_copy(hidden_buf, hidden_all.at[step_ref[1]], hidden_sem)
    hidden_copy.start()
    for copy in copies:
        copy.wait()
    hidden_copy.wait()


def fetches(step, time, sources, targets, sems):
    gates_all, cells_all, ups_all = sources
    gates_ref, cell_ref, prev_ref, up_ref = targets
    before = jnp.maximum(step - 1, 0)
    return [
        pltpu.make_async_copy(gates_all.at[i, step], gates_ref.at[i], sems.at[i]) for i in range(PIECES)
    ] + [
        pltpu.make_async_copy(cells_all.at[step], cell_ref, sems.at[PIECES]),
        pltpu.make_async_copy(cells_all.at[before], prev_ref, sems.at[PIECES + 1]),
        pltpu.make_async_copy(ups_all.at[time], up_ref, sems.at[PIECES + 2]),
    ]


def aside_kernel(
    first, opens, step_ref, dz_ref, raw_ref, gates_all, cells_all, ups_all, slope_all, *refs
):
    refs = refs[(0 if first else 4) + (0 if opens else 2) :]
    gates_ref, cell_ref, prev_ref, slope_ref, up_ref = refs[:5]
    dz_all, raw_all, near_all, far_all, near_out, far_out, sems, fetch_sems = refs[5:]
    step, time_before = step_ref[0], step_ref[2]
    slot, low, high = step_ref[4], step_ref[5], step_ref[6]
    before = jnp.maximum(step - 1, 0)
    copies = fetches(
        before, time_before, (gates_all, cells_all, ups_all), (gates_ref, cell_ref, prev_ref, up_ref), fetch_sems
    )
    copies.append(pltpu.make_async_copy(slope_all.at[before], slope_ref, fetch_sems.at[PIECES + 3]))
    copies += [pltpu.make_async_copy(dz_ref.at[i], dz_all.at[i, step], sems.at[i]) for i in range(PIECES)]
    copies.append(pltpu.make_async_copy(raw_ref, raw_all.at[step], sems.at[PIECES]))
    copies.append(pltpu.make_async_copy(dz_ref.at[low], near_all.at[step], sems.at[PIECES + 1]))
    copies.append(pltpu.make_async_copy(dz_ref.at[HALVES + high], far_all.at[step], sems.at[PIECES + 2]))
    copies.append(pltpu.make_async_copy(dz_ref.at[1 - low], near_out.at[slot], sems.at[PIECES + 3]))
    copies.append(pltpu.make_async_copy(dz_ref.at[HALVES + 1 - high], far_out.at[slot], sems.at[PIECES + 4]))
    for copy in copies:
        copy.start()
    for copy in copies:
        copy.wait()


def input_grad_kernel(step_ref, dz_ref, wa_ref, wb_ref, out_ref, acc_ref):
    piece, gate = pl.program_id(0), pl.program_id(1)
    steps, streams, width = dz_ref.shape[1:]

    @pl.when((piece == 0) & (gate == 0))
    def _():
        acc_ref[...] = jnp.zeros(acc_ref.shape, F32)

    weights = jnp.where(piece < HALVES, wa_ref[0], wb_ref[0])
    acc_ref[...] += lax.dot_general(
        dz_ref[0].reshape(steps * streams, width), weights, (((1,), (1,)), ((), ())), preferred_element_type=F32
    )

    @pl.when((piece == PIECES - 1) & (gate == 3))
    def _():
        for step in range(steps):
            time = step_ref[0] + step_ref[1] * step
            out_ref[time] = acc_ref[step * streams : (step + 1) * streams, :]


def params(mib):
    return pltpu.CompilerParams(vmem_limit_bytes=mib * MIB)


def cost(flops, size):
    return pl.CostEstimate(flops=flops, bytes_accessed=size, transcendentals=0)


def body(inputs, w_in, w_rec, bias, proj, state_h, state_c, resets, stream_doc, cotangent):
    streams, steps, depth = inputs.shape[1:]
    cells = w_in.shape[3]
    width = cells // HALVES
    rank = lax.axis_index("gate")
    own = rank % 2
    gates_size = lax.axis_size("gate")
    swap = [(i, i ^ 1) for i in range(gates_size)]
    across = [(i, i ^ 2) for i in range(gates_size)]

    def pick(stacked, index):
        return lax.dynamic_index_in_dim(stacked, index, 0, keepdims=False)

    def trade(mine, theirs):
        return (mine, lax.ppermute(theirs, "gate", swap))

    def by_gate(stacked, index):
        return jnp.transpose(pick(stacked, index), (1, 0, 2))

    win_a, win_b = trade(by_gate(w_in, own), by_gate(w_in, 1 - own))
    rec_a, rec_b = trade(by_gate(w_rec, own), by_gate(w_rec, 1 - own))
    proj_a, proj_b = trade(pick(proj, own), pick(proj, 1 - own))
    bias_a, bias_b = trade(pick(bias, own), pick(bias, 1 - own))

    def pieces_of(pair):
        split = [x.reshape(4, HALVES, width) for x in pair]
        return jnp.transpose(jnp.stack(split), (0, 2, 1, 3)).reshape(PIECES, 1, 4 * width)

    bias_p = pieces_of((bias_a, bias_b)).astype(F32)

    def cells_to_pieces(pair):
        both = jnp.stack(pair).reshape(QUARTERS, streams, HALVES, width)
        return jnp.transpose(both, (0, 2, 1, 3)).reshape(PIECES, streams, width)

    def by_time(stacked):
        return jnp.transpose(pick(stacked, own), (1, 0, 2))

    feats = by_time(inputs)
    ups = by_time(cotangent)
    flags = resets.astype(F32)
    later = jnp.concatenate([flags[:, 1:], jnp.zeros_like(flags[:, :1])], axis=1)
    keep = 1.0 - jnp.where(own == 0, flags, later)
    keep = jnp.broadcast_to(jnp.transpose(keep)[:, :, None], (steps, streams, 128))

    docs_h = state_h[stream_doc]
    docs_c = state_c[stream_doc]
    start_h = pick(jnp.transpose(docs_h, (1, 0, 2)), own).astype(BF16)
    by_dir_c = jnp.transpose(docs_c, (1, 0, 2))
    start_c = cells_to_pieces(trade(pick(by_dir_c, own), pick(by_dir_c, 1 - own)))

    def at_step(step):
        near = jnp.array([step, step, max(step - 1, 0), min(step + 1, steps - 1)], jnp.int32)
        turned = jnp.array([step] + [steps - 1 - x for x in (step, max(step - 1, 0), min(step + 1, steps - 1))], jnp.int32)
        return jnp.where(own == 0, near, turned)

    def vmem(shape, dtype):
        return pltpu.VMEM(shape, dtype)

    def hbm(shape, dtype):
        return pltpu.HBM(shape, dtype)

    feats_v, keep_v, bias_v, win_av, win_bv = place(feats, keep, bias_p, win_a, win_b)
    rec_av, rec_bv, proj_av, proj_bv, start_hv, start_cv = place(rec_a, rec_b, proj_a, proj_b, start_h, start_c)

    gates_shape, cell_shape = (PIECES, streams, 4 * width), (PIECES, streams, width)
    inflow = pl.pallas_call(
        inflow_kernel,
        out_shape=vmem(gates_shape, F32),
        in_specs=[SMEM] + [VMEM] * 4,
        out_specs=VMEM,
        compiler_params=params(8),
        name="inflow",
    )(at_step(0), pinned(feats_v), pinned(bias_v), pinned(win_av), pinned(win_bv))

    def forward_call(first, step, part, peer, cell, inflow):
        return pl.pallas_call(
            functools.partial(forward_kernel, first),
            out_shape=(
                vmem((streams, depth), BF16),
                vmem(cell_shape, F32),
                vmem(gates_shape, BF16),
                vmem(cell_shape, BF16),
                vmem((streams, depth), BF16),
                vmem((streams, depth), BF16),
                vmem((streams, depth), F32),
            ),
            in_specs=[SMEM] + [VMEM] * 10,
            out_specs=[VMEM] * 7,
            compiler_params=params(8),
            name="forward_step",
        )(
            at_step(step), pinned(part), pinned(peer), pinned(start_hv), pinned(keep_v), pinned(cell), pinned(inflow),
            pinned(rec_av), pinned(rec_bv), pinned(proj_av), pinned(proj_bv),
        )

    def between_call(step, fresh, stacks):
        shapes = (
            hbm((PIECES, steps, streams, 4 * width), BF16),
            hbm((steps,) + cell_shape, F32),
            hbm((PIECES, steps, streams, width), BF16),
            hbm((steps, streams, depth), BF16),
            hbm((steps, streams, depth), BF16),
            hbm((steps, streams, depth), BF16),
            hbm((steps, streams, depth), F32),
        )
        inflow, *stacks = pl.pallas_call(
            functools.partial(between_kernel, not stacks),
            out_shape=(vmem(gates_shape, F32),) + shapes,
            in_specs=[SMEM] + [VMEM] * 10 + [ANY] * len(stacks),
            out_specs=[VMEM] + [ANY] * 7,
            scratch_shapes=[pltpu.SemaphoreType.DMA((2 * PIECES + 5,))],
            input_output_aliases={11 + i: 1 + i for i in range(len(stacks))},
            compiler_params=params(8),
            cost_estimate=cost(2 * streams * depth * 8 * cells, 8 * depth * cells * 2),
            name="between",
        )(
            at_step(step), pinned(feats_v), pinned(bias_v), pinned(win_av), pinned(win_bv),
            *(pinned(x) for x in fresh), *(in_hbm(x) for x in stacks),
        )
        return inflow, tuple(stacks)

    def forward_step(step, carry, first=False):
        part, peer, cell, inflow, stacks = carry
        part, cell, *fresh = forward_call(first, step, part, peer, cell, inflow)
        peer = lax.ppermute(part, "gate", across)
        inflow, stacks = between_call(step, (cell, *fresh), stacks)
        return (part, peer, cell, inflow, stacks)

    none = jnp.zeros((streams, depth), BF16)
    carry = forward_step(0, (none, none, start_cv, inflow, ()), True)
    for step in range(1, steps):
        carry = forward_step(step, carry)
    part, peer, cell, _, stacks = carry
    gates_all, cells_all, mixed_all, prev_all, feat_all, hidden_all, slope_all = stacks

    saved_shapes = (
        vmem(gates_shape, BF16),
        vmem(cell_shape, F32),
        vmem(cell_shape, F32),
        vmem((streams, depth), F32),
        vmem((streams, depth), BF16),
    )
    *saved, hidden_all, slope_all = pl.pallas_call(
        finish_kernel,
        out_shape=saved_shapes + (hbm((steps, streams, depth), BF16), hbm((steps, streams, depth), F32)),
        in_specs=[SMEM, VMEM, VMEM] + [ANY] * 5,
        out_specs=[VMEM] * 5 + [ANY] * 2,
        scratch_shapes=[
            pltpu.VMEM((streams, depth), BF16),
            pltpu.SemaphoreType.DMA((PIECES + 4,)),
            pltpu.SemaphoreType.DMA,
        ],
        input_output_aliases={6: 5, 7: 6},
        compiler_params=params(8),
        name="finish",
    )(
        at_step(steps - 1), pinned(part), pinned(peer), in_hbm(gates_all), in_hbm(cells_all), in_hbm(ups),
        in_hbm(hidden_all), in_hbm(slope_all),
    )

    both_hidden = trade(hidden_all, hidden_all)

    def by_direction(mine, theirs):
        return jnp.stack([jnp.where(own == 0, mine, theirs), jnp.where(own == 0, theirs, mine)])

    hidden_dirs = by_direction(*both_hidden)
    outputs = (inputs.astype(F32) + jnp.transpose(hidden_dirs, (0, 2, 1, 3)).astype(F32)).astype(BF16)
    last_h = jnp.stack([hidden_dirs[0, steps - 1], hidden_dirs[1, 0]], axis=1).astype(F32)
    final_h = jnp.zeros_like(state_h).at[stream_doc].set(last_h)
    last_c = jnp.transpose(cell.reshape(QUARTERS, HALVES, streams, width), (0, 2, 1, 3)).reshape(
        QUARTERS, streams, cells
    )
    last_dirs = by_direction(*trade(last_c[0], last_c[1]))
    final_c = jnp.zeros_like(state_c).at[stream_doc].set(jnp.transpose(last_dirs, (1, 0, 2)))

    rec_at, rec_bt = (jnp.transpose(x, (0, 2, 1)) for x in (rec_a, rec_b))
    proj_at, proj_bt = jnp.transpose(proj_a), jnp.transpose(proj_b)
    rec_atv, rec_btv, proj_atv, proj_btv = place(rec_at, rec_bt, proj_at, proj_bt)

    def backward_call(step, part, peer, grad, saved):
        return pl.pallas_call(
            backward_kernel,
            out_shape=(
                vmem((streams, depth), BF16),
                vmem(cell_shape, F32),
                vmem((streams, depth), BF16),
                vmem(gates_shape, BF16),
            ),
            in_specs=[SMEM] + [VMEM] * 14,
            out_specs=[VMEM] * 4,
            compiler_params=params(8),
            name="backward_step",
        )(
            at_step(step), pinned(part), pinned(peer), pinned(keep_v), pinned(grad),
            pinned(rec_atv), pinned(rec_btv), pinned(proj_atv), pinned(proj_btv),
            *(pinned(x) for x in saved), pinned(start_cv),
        )

    n_batch = lax.axis_size("batch")
    spot = lax.axis_index("batch")
    low, high = spot % 2, (spot // 2) % 2
    near_swap = [(i, i ^ 1) for i in range(n_batch)]
    far_swap = [(i, i ^ 2) for i in range(n_batch)]

    def aside_call(step, slot, slots, dz, raw, stacks, sends):
        piece_shape = (streams, 4 * width)
        shapes = (
            hbm((PIECES, steps) + piece_shape, BF16),
            hbm((steps, streams, depth), BF16),
            hbm((steps,) + piece_shape, BF16),
            hbm((steps,) + piece_shape, BF16),
            hbm((slots,) + piece_shape, BF16),
            hbm((slots,) + piece_shape, BF16),
        )
        kept = len(stacks)
        aliases = {7 + i: 5 + i for i in range(kept)}
        aliases.update({7 + kept + i: 9 + i for i in range(len(sends))})
        out = pl.pallas_call(
            functools.partial(aside_kernel, not stacks, not sends),
            out_shape=saved_shapes + shapes,
            in_specs=[SMEM] + [VMEM] * 2 + [ANY] * (4 + kept + len(sends)),
            out_specs=[VMEM] * 5 + [ANY] * 6,
            scratch_shapes=[
                pltpu.SemaphoreType.DMA((PIECES + 5,)),
                pltpu.SemaphoreType.DMA((PIECES + 4,)),
            ],
            input_output_aliases=aliases,
            compiler_params=params(8),
            cost_estimate=cost(0, 8 * MIB),
            name="aside",
        )(
            jnp.concatenate([at_step(step), jnp.stack([jnp.int32(slot), low, high])]), pinned(dz), pinned(raw),
            in_hbm(gates_all), in_hbm(cells_all), in_hbm(ups), in_hbm(slope_all), *(in_hbm(x) for x in (*stacks, *sends)),
        )
        return out[:5], tuple(out[5:9]), tuple(out[9:])

    def swapped(array, pairs):
        return lax.ppermute(array, "batch", pairs)

    carry = (none, none, jnp.zeros(cell_shape, F32), saved, ())
    top, near_in, far_in = steps, [], []
    for index, share in enumerate(SHARES):
        slots = top if index == len(SHARES) - 1 else round(share * steps)
        sends = ()
        for step in range(top - 1, top - slots - 1, -1):
            part, peer, grad, saved, stacks = carry
            part, grad, raw, dz = backward_call(step, part, peer, grad, saved)
            peer = lax.ppermute(part, "gate", across)
            saved, stacks, sends = aside_call(step, step - (top - slots), slots, dz, raw, stacks, sends)
            carry = (part, peer, grad, saved, stacks)
        top -= slots
        near_in.insert(0, swapped(sends[0], near_swap))
        far_in.insert(0, swapped(sends[1], far_swap))
    dz_all, raw_all, near_all, far_all = carry[-1]
    rows = steps * streams

    turn = jnp.where(own == 0, jnp.array([0, 1], jnp.int32), jnp.array([steps - 1, -1], jnp.int32))
    dx_all = pl.pallas_call(
        input_grad_kernel,
        out_shape=jax.ShapeDtypeStruct((steps, streams, depth), F32),
        grid_spec=pltpu.PrefetchScalarGridSpec(
            num_scalar_prefetch=1,
            grid=(PIECES, 4),
            in_specs=[
                pl.BlockSpec((1, steps, streams, width), lambda p, g, turn: (p, 0, 0, g)),
                pl.BlockSpec(
                    (1, depth, width), lambda p, g, turn: (jnp.where(p < 2, g, 3), 0, jnp.where(p < 2, p, 1))
                ),
                pl.BlockSpec(
                    (1, depth, width), lambda p, g, turn: (jnp.where(p < 2, 0, g), 0, jnp.where(p < 2, 0, p - 2))
                ),
            ],
            out_specs=pl.BlockSpec((steps, streams, depth), lambda p, g, turn: (0, 0, 0)),
            scratch_shapes=[pltpu.VMEM((rows, depth), F32)],
        ),
        compiler_params=params(24),
        cost_estimate=cost(2 * rows * depth * 8 * cells, 8 * depth * cells * 4),
        name="input_grad",
    )(turn, dz_all, win_a, win_b)

    def line_sum(chunks, stride, count):
        here = (spot // stride) % count

        def chunk(index):
            return lax.dynamic_index_in_dim(chunks, jnp.clip(index, 0, count - 1), 0, keepdims=False)

        def at(device):
            return (device // stride) % count

        if count == 2:
            pairs = [(i, i + stride if at(i) == 0 else i - stride) for i in range(n_batch)]
            return chunk(here).astype(F32) + swapped(chunk(1 - here), pairs).astype(F32)
        up, down = None, None
        for slot in range(1, count):
            rise, fall = chunk(here + count - slot), chunk(here - count + slot)
            if slot > 1:
                rise = (rise.astype(F32) + up.astype(F32)).astype(BF16)
                fall = (fall.astype(F32) + down.astype(F32)).astype(BF16)
            up = swapped(rise, [(i, i + stride) for i in range(n_batch) if at(i) < min(slot, count - 1)])
            down = swapped(fall, [(i, i - stride) for i in range(n_batch) if at(i) > max(count - 1 - slot, 0)])
        return chunk(here).astype(F32) + up.astype(F32) + down.astype(F32)

    line = n_batch // 2
    share_rows = depth // n_batch

    def own_half(mine, theirs, index):
        return jnp.stack([jnp.where(index == 0, mine, theirs), jnp.where(index == 0, theirs, mine)])

    def finish_halves(halves, index, pairs):
        mine = lax.dynamic_index_in_dim(halves, index, 0, keepdims=False)
        theirs = lax.dynamic_index_in_dim(halves, 1 - index, 0, keepdims=False)
        return own_half(mine, swapped(theirs, pairs), index)

    def near_sum(grad):
        return line_sum(grad.reshape(line, 2, share_rows, -1), 2, line).astype(BF16)

    def far_sum(grad):
        chunks = jnp.moveaxis(grad.reshape(line, 2, share_rows, -1), 1, 0)
        mine = line_sum(chunks, 1, 2).astype(BF16)
        return line_sum(mine.reshape(line // 2, 2, share_rows, -1), 4, line // 2).astype(BF16)

    def rows_of(stacked):
        return stacked.reshape(rows, -1)

    def product(left, right):
        return lax.dot_general(rows_of(left), rows_of(right), (((0,), (0,)), ((), ())), preferred_element_type=F32)

    near_in, far_in = jnp.concatenate(near_in, axis=0), jnp.concatenate(far_in, axis=0)
    near_left = [(x, swapped(x, near_swap)) for x in (feat_all, prev_all)]
    far_left = [(x, swapped(x, far_swap)) for x in (feat_all, prev_all)]
    near_sums = [
        near_sum((product(mine, near_all) + product(theirs, near_in)).astype(BF16)) for mine, theirs in near_left
    ]
    far_sums = [far_sum((product(mine, far_all) + product(theirs, far_in)).astype(BF16)) for mine, theirs in far_left]
    near_sums = [finish_halves(x, low, near_swap) for x in near_sums]
    far_sums = [finish_halves(x, high, far_swap) for x in far_sums]

    grad_bias = jnp.sum(dz_all, axis=(1, 2), dtype=F32)
    grad_proj = jnp.einsum("ptnc,tnk->kpc", mixed_all, raw_all, preferred_element_type=F32).astype(BF16)
    grad_proj = line_sum(jnp.moveaxis(grad_proj.reshape(line, 2, share_rows, -1), 1, 0), 1, 2).astype(BF16)
    grad_proj = line_sum(grad_proj, 2, line).astype(BF16)

    def gate_rows(halves):
        shaped = halves.reshape(HALVES, -1, 4, width)
        return jnp.transpose(shaped, (1, 2, 0, 3)).reshape(-1, 4, cells)

    def home(mine, theirs):
        return by_direction(*trade(mine, theirs)).astype(F32)

    grad_w_in, grad_w_rec = (home(gate_rows(near), gate_rows(far)) for near, far in zip(near_sums, far_sums))
    grad_bias = grad_bias.reshape(QUARTERS, HALVES, 1, 4 * width)
    grad_bias = home(gate_rows(grad_bias[0])[0], gate_rows(grad_bias[1])[0])
    grad_bias = lax.psum_scatter(grad_bias, "batch", scatter_dimension=2, tiled=True)
    grad_proj = grad_proj.reshape(share_rows, QUARTERS, cells)
    grad_proj = home(jnp.transpose(grad_proj[:, 0]), jnp.transpose(grad_proj[:, 1]))

    half_cols = depth // 2
    upper = rank // 2
    keep_cols = lax.dynamic_slice_in_dim(dx_all, upper * half_cols, half_cols, 2)
    send_cols = lax.dynamic_slice_in_dim(dx_all, (1 - upper) * half_cols, half_cols, 2).astype(BF16)
    dx_half = keep_cols + lax.ppermute(send_cols, "gate", across).astype(F32)
    up_half = lax.dynamic_slice_in_dim(ups, upper * half_cols, half_cols, 2).astype(F32)
    dx_half = (dx_half + up_half).astype(BF16)
    quarter_cols = half_cols // 2
    mine = lax.dynamic_slice_in_dim(dx_half, own * quarter_cols, quarter_cols, 2)
    theirs = lax.dynamic_slice_in_dim(dx_half, (1 - own) * quarter_cols, quarter_cols, 2)
    dx_dirs = by_direction(*trade(mine, theirs))
    input_grad = jnp.transpose(dx_dirs, (0, 2, 1, 3))
    return (outputs, input_grad, grad_w_in, grad_w_rec, grad_bias, grad_proj, final_h, final_c)


def solution(mesh):
    placed = (
        P(None, "batch", None, None),
        P(None, None, None, "gate"),
        P(None, None, None, "gate"),
        P(None, None, "gate"),
        P(None, "gate", None),
        P("batch", None, None),
        P("batch", None, "gate"),
        P("batch", None),
        P("batch"),
        P(None, "batch", None, None),
    )
    return jax.shard_map(
        body,
        mesh=mesh,
        in_specs=placed,
        out_specs=(
            P(None, "batch", None, None),
            P(None, "batch", None, "gate"),
            P(None, "batch", None, "gate"),
            P(None, "batch", None, "gate"),
            P(None, None, ("gate", "batch")),
            P(None, "gate", "batch"),
            P("batch", None, None),
            P("batch", None, "gate"),
        ),
        check_vma=False,
    )
```

```python
import functools

import jax
import jax.numpy as jnp
from jax import lax
from jax.experimental import pallas as pl
from jax.experimental.pallas import tpu as pltpu
from jax.sharding import PartitionSpec as P

CLIP = 3.0
F32, BF16 = jnp.float32, jnp.bfloat16
QUARTERS, HALVES = 2, 2
PIECES = QUARTERS * HALVES
MIB = 2**20
SHARES = (0.3, 0.3, 0.2, 0.1, 0.1)

VMEM = pl.BlockSpec(memory_space=pltpu.VMEM)
SMEM = pl.BlockSpec(memory_space=pltpu.SMEM)
ANY = pl.BlockSpec(memory_space=pl.ANY)


def pinned(array):
    return pltpu.with_memory_space_constraint(array, pltpu.VMEM)


def in_hbm(array):
    return pltpu.with_memory_space_constraint(array, pltpu.HBM)


def dot(left, right):
    return jnp.dot(left, right, preferred_element_type=F32)


def place_kernel(count, *refs):
    sources, targets, sems = refs[:count], refs[count : 2 * count], refs[2 * count]
    copies = [pltpu.make_async_copy(a, b, sems.at[i]) for i, (a, b) in enumerate(zip(sources, targets))]
    for copy in copies:
        copy.start()
    for copy in copies:
        copy.wait()


def place(*arrays):
    count = len(arrays)
    return pl.pallas_call(
        functools.partial(place_kernel, count),
        out_shape=tuple(pltpu.VMEM(x.shape, x.dtype) for x in arrays),
        in_specs=[ANY] * count,
        out_specs=[VMEM] * count,
        scratch_shapes=[pltpu.SemaphoreType.DMA((count,))],
        compiler_params=params(1),
        name="place",
    )(*arrays)


def order_kernel(step_ref, feat_ref, out_ref, all_ref, sems, all_sem):
    steps = feat_ref.shape[0]
    copies = [
        pltpu.make_async_copy(feat_ref.at[step_ref[0] + step_ref[1] * i], out_ref.at[i], sems.at[i]) for i in range(steps)
    ]
    for copy in copies:
        copy.start()
    for copy in copies:
        copy.wait()
    whole = pltpu.make_async_copy(out_ref, all_ref, all_sem)
    whole.start()
    whole.wait()


def pieces(refs, axis):
    for piece in range(PIECES):
        quarter, half = divmod(piece, HALVES)
        width = refs[0].shape[axis] // HALVES
        yield piece, quarter, width, slice(half * width, (half + 1) * width)


def forward_kernel(
    first, step_ref, p_ref, q_ref, start_ref, keep_ref, cell_ref, inflow_ref, wa_ref, wb_ref, pa_ref, pb_ref,
    part_ref, next_ref, gates_ref, mixed_ref, prev_ref, hidden_ref, slope_ref,
):
    keep = keep_ref[step_ref[1]][:, :1]
    if first:
        hidden = start_ref[...]
    else:
        hidden = clipped(p_ref, q_ref, hidden_ref, slope_ref)
    hidden = hidden * keep.astype(BF16)
    prev_ref[...] = hidden
    part = jnp.zeros(part_ref.shape, F32)
    for piece, quarter, width, cols in pieces((wa_ref, wb_ref), 2):
        w_ref, proj_ref = ((wa_ref, pa_ref), (wb_ref, pb_ref))[quarter]
        acts = []
        for gate in range(4):
            place = slice(gate * width, (gate + 1) * width)
            pre = dot(hidden, w_ref[gate, :, cols]) + inflow_ref[piece, :, place]
            act = jnp.tanh(pre if gate == 2 else 0.5 * pre)
            gates_ref[piece, :, place] = act.astype(BF16)
            acts.append(act if gate == 2 else 0.5 + 0.5 * act)
        ingate, forget, candidate, outgate = acts
        cell = CLIP * jnp.tanh((forget * (keep * cell_ref[piece]) + ingate * candidate) * (1.0 / CLIP))
        next_ref[piece] = cell
        mixed = (outgate * jnp.tanh(cell)).astype(BF16)
        mixed_ref[piece] = mixed
        part = part + dot(mixed, proj_ref[cols, :])
    part_ref[...] = part.astype(BF16)


def clipped(p_ref, q_ref, hidden_ref, slope_ref):
    squash = jnp.tanh((p_ref[...].astype(F32) + q_ref[...].astype(F32)) * (1.0 / CLIP))
    hidden = (CLIP * squash).astype(BF16)
    hidden_ref[...] = hidden
    slope_ref[...] = 1.0 - squash * squash
    return hidden


def between_kernel(
    first, passed, step_ref, feat_ref, bias_ref, wa_ref, wb_ref, cell_ref, gates_ref, mixed_ref, prev_ref, hidden_ref,
    slope_ref, *refs,
):
    refs = refs[(0 if first else 6) + passed :]
    out_ref, gates_all, cells_all, mixed_all, prev_all, hidden_all, slope_all = refs[:7]
    sems = refs[-1]
    step, time_before = step_ref[0], step_ref[2]
    after = jnp.minimum(step + 1, feat_ref.shape[0] - 1)
    copies = [pltpu.make_async_copy(gates_ref.at[i], gates_all.at[i, step], sems.at[i]) for i in range(PIECES)]
    copies += [
        pltpu.make_async_copy(mixed_ref.at[i], mixed_all.at[i, step], sems.at[PIECES + i]) for i in range(PIECES)
    ]
    copies.append(pltpu.make_async_copy(cell_ref, cells_all.at[step], sems.at[2 * PIECES]))
    copies.append(pltpu.make_async_copy(prev_ref, prev_all.at[step], sems.at[2 * PIECES + 1]))
    if not first:
        copies.append(pltpu.make_async_copy(hidden_ref, hidden_all.at[time_before], sems.at[2 * PIECES + 2]))
        copies.append(pltpu.make_async_copy(slope_ref, slope_all.at[step - 1], sems.at[2 * PIECES + 3]))
    for copy in copies:
        copy.start()
    inflow_into(feat_ref[after], bias_ref, wa_ref, wb_ref, out_ref)
    for copy in copies:
        copy.wait()


def inflow_into(feat, bias_ref, wa_ref, wb_ref, out_ref):
    for piece, quarter, width, cols in pieces((wa_ref, wb_ref), 2):
        w_ref = (wa_ref, wb_ref)[quarter]
        for gate in range(4):
            place = slice(gate * width, (gate + 1) * width)
            out_ref[piece, :, place] = dot(feat, w_ref[gate, :, cols]) + bias_ref[piece, :, place]


def inflow_kernel(step_ref, feat_ref, bias_ref, wa_ref, wb_ref, out_ref):
    inflow_into(feat_ref[0], bias_ref, wa_ref, wb_ref, out_ref)


def backward_kernel(
    step_ref, p_ref, q_ref, keep_ref, grad_ref, wa_ref, wb_ref, pa_ref, pb_ref,
    gates_ref, cell_ref, prev_ref, slope_ref, up_ref, start_ref,
    part_ref, next_ref, raw_ref, dz_ref,
):
    step = step_ref[0]
    keep = keep_ref[step_ref[1]][:, :1]
    raw = (up_ref[...].astype(F32) + (p_ref[...].astype(F32) + q_ref[...].astype(F32))) * slope_ref[...]
    raw = raw.astype(BF16)
    raw_ref[...] = raw
    part = jnp.zeros(part_ref.shape, F32)
    for piece, quarter, width, cols in pieces((wa_ref, wb_ref), 1):
        w_ref, proj_ref = ((wa_ref, pa_ref), (wb_ref, pb_ref))[quarter]
        mixed = dot(raw, proj_ref[:, cols])
        acts = [gates_ref[piece, :, gate * width : (gate + 1) * width].astype(F32) for gate in range(4)]
        ingate, forget, outgate = (0.5 + 0.5 * acts[gate] for gate in (0, 1, 3))
        slopes = [1.0 - act * act for act in acts]
        cell = cell_ref[piece]
        prev = keep * jnp.where(step == 0, start_ref[piece], prev_ref[piece])
        squash = jnp.tanh(cell)
        total = grad_ref[piece] + mixed * outgate * (1.0 - squash * squash)
        inner = total * (1.0 - (cell * (1.0 / CLIP)) * (cell * (1.0 / CLIP)))
        next_ref[piece] = keep * inner * forget
        quart = 0.25 * inner
        pre_grads = (
            quart * acts[2] * slopes[0],
            quart * prev * slopes[1],
            inner * ingate * slopes[2],
            0.25 * mixed * squash * slopes[3],
        )
        for gate in range(4):
            low = pre_grads[gate].astype(BF16)
            dz_ref[piece, :, gate * width : (gate + 1) * width] = low
            part = part + dot(low, w_ref[gate, cols, :])
    part_ref[...] = (part * keep).astype(BF16)


def finish_kernel(
    step_ref, p_ref, q_ref, gates_all, cells_all, ups_all, hidden_in, slope_in,
    gates_ref, cell_ref, prev_ref, slope_ref, up_ref, hidden_all, slope_all,
    hidden_buf, sems, hidden_sem,
):
    copies = fetches(
        step_ref[0], step_ref[1], (gates_all, cells_all, ups_all), (gates_ref, cell_ref, prev_ref, up_ref), sems
    )
    for copy in copies:
        copy.start()
    clipped(p_ref, q_ref, hidden_buf, slope_ref)
    hidden_copy = pltpu.make_async_copy(hidden_buf, hidden_all.at[step_ref[1]], hidden_sem)
    hidden_copy.start()
    for copy in copies:
        copy.wait()
    hidden_copy.wait()


def fetches(step, time, sources, targets, sems):
    gates_all, cells_all, ups_all = sources
    gates_ref, cell_ref, prev_ref, up_ref = targets
    before = jnp.maximum(step - 1, 0)
    return [
        pltpu.make_async_copy(gates_all.at[i, step], gates_ref.at[i], sems.at[i]) for i in range(PIECES)
    ] + [
        pltpu.make_async_copy(cells_all.at[step], cell_ref, sems.at[PIECES]),
        pltpu.make_async_copy(cells_all.at[before], prev_ref, sems.at[PIECES + 1]),
        pltpu.make_async_copy(ups_all.at[time], up_ref, sems.at[PIECES + 2]),
    ]


def aside_kernel(
    first, opens, passed, step_ref, dz_ref, raw_ref, gates_all, cells_all, ups_all, slope_all, *refs
):
    refs = refs[(0 if first else 4) + (0 if opens else 2) + passed :]
    gates_ref, cell_ref, prev_ref, slope_ref, up_ref = refs[:5]
    dz_all, raw_all, near_all, far_all, near_out, far_out = refs[5:11]
    sems, fetch_sems = refs[-2:]
    step, time_before = step_ref[0], step_ref[2]
    slot, low, high = step_ref[4], step_ref[5], step_ref[6]
    before = jnp.maximum(step - 1, 0)
    copies = fetches(
        before, time_before, (gates_all, cells_all, ups_all), (gates_ref, cell_ref, prev_ref, up_ref), fetch_sems
    )
    copies.append(pltpu.make_async_copy(slope_all.at[before], slope_ref, fetch_sems.at[PIECES + 3]))
    copies += [pltpu.make_async_copy(dz_ref.at[i], dz_all.at[i, step], sems.at[i]) for i in range(PIECES)]
    copies.append(pltpu.make_async_copy(raw_ref, raw_all.at[step], sems.at[PIECES]))
    copies.append(pltpu.make_async_copy(dz_ref.at[low], near_all.at[step], sems.at[PIECES + 1]))
    copies.append(pltpu.make_async_copy(dz_ref.at[HALVES + high], far_all.at[step], sems.at[PIECES + 2]))
    copies.append(pltpu.make_async_copy(dz_ref.at[1 - low], near_out.at[slot], sems.at[PIECES + 3]))
    copies.append(pltpu.make_async_copy(dz_ref.at[HALVES + 1 - high], far_out.at[slot], sems.at[PIECES + 4]))
    for copy in copies:
        copy.start()
    for copy in copies:
        copy.wait()


def input_grad_kernel(step_ref, dz_ref, wa_ref, wb_ref, out_ref, acc_ref):
    piece, gate = pl.program_id(0), pl.program_id(1)
    steps, streams, width = dz_ref.shape[1:]

    @pl.when((piece == 0) & (gate == 0))
    def _():
        acc_ref[...] = jnp.zeros(acc_ref.shape, F32)

    weights = jnp.where(piece < HALVES, wa_ref[0], wb_ref[0])
    acc_ref[...] += lax.dot_general(
        dz_ref[0].reshape(steps * streams, width), weights, (((1,), (1,)), ((), ())), preferred_element_type=F32
    )

    @pl.when((piece == PIECES - 1) & (gate == 3))
    def _():
        for step in range(steps):
            time = step_ref[0] + step_ref[1] * step
            out_ref[time] = acc_ref[step * streams : (step + 1) * streams, :]


def params(mib):
    return pltpu.CompilerParams(vmem_limit_bytes=mib * MIB)


def cost(flops, size):
    return pl.CostEstimate(flops=flops, bytes_accessed=size, transcendentals=0)


def body(inputs, w_in, w_rec, bias, proj, state_h, state_c, resets, stream_doc, cotangent):
    streams, steps, depth = inputs.shape[1:]
    cells = w_in.shape[3]
    width = cells // HALVES
    rank = lax.axis_index("gate")
    own = rank % 2
    gates_size = lax.axis_size("gate")
    swap = [(i, i ^ 1) for i in range(gates_size)]
    across = [(i, i ^ 2) for i in range(gates_size)]

    def pick(stacked, index):
        return lax.dynamic_index_in_dim(stacked, index, 0, keepdims=False)

    def trade(mine, theirs):
        return (mine, lax.ppermute(theirs, "gate", swap))

    def by_gate(stacked, index):
        return jnp.transpose(pick(stacked, index), (1, 0, 2))

    win_a, win_b = trade(by_gate(w_in, own), by_gate(w_in, 1 - own))
    rec_a, rec_b = trade(by_gate(w_rec, own), by_gate(w_rec, 1 - own))
    proj_a, proj_b = trade(pick(proj, own), pick(proj, 1 - own))
    bias_a, bias_b = trade(pick(bias, own), pick(bias, 1 - own))

    def pieces_of(pair):
        split = [x.reshape(4, HALVES, width) for x in pair]
        return jnp.transpose(jnp.stack(split), (0, 2, 1, 3)).reshape(PIECES, 1, 4 * width)

    bias_p = pieces_of((bias_a, bias_b)).astype(F32)

    def cells_to_pieces(pair):
        both = jnp.stack(pair).reshape(QUARTERS, streams, HALVES, width)
        return jnp.transpose(both, (0, 2, 1, 3)).reshape(PIECES, streams, width)

    def by_time(stacked):
        return jnp.transpose(pick(stacked, own), (1, 0, 2))

    feats = by_time(inputs)
    ups = by_time(cotangent)
    flags = resets.astype(F32)
    later = jnp.concatenate([flags[:, 1:], jnp.zeros_like(flags[:, :1])], axis=1)
    keep = 1.0 - jnp.where(own == 0, flags, later)
    keep = jnp.broadcast_to(jnp.transpose(keep)[:, :, None], (steps, streams, 128))

    docs_h = state_h[stream_doc]
    docs_c = state_c[stream_doc]
    start_h = pick(jnp.transpose(docs_h, (1, 0, 2)), own).astype(BF16)
    by_dir_c = jnp.transpose(docs_c, (1, 0, 2))
    start_c = cells_to_pieces(trade(pick(by_dir_c, own), pick(by_dir_c, 1 - own)))

    def at_step(step):
        near = jnp.array([step, step, max(step - 1, 0), min(step + 1, steps - 1)], jnp.int32)
        turned = jnp.array([step] + [steps - 1 - x for x in (step, max(step - 1, 0), min(step + 1, steps - 1))], jnp.int32)
        return jnp.where(own == 0, near, turned)

    def vmem(shape, dtype):
        return pltpu.VMEM(shape, dtype)

    def hbm(shape, dtype):
        return pltpu.HBM(shape, dtype)

    n_batch = lax.axis_size("batch")
    spot = lax.axis_index("batch")
    low, high = spot % 2, (spot // 2) % 2
    near_swap = [(i, i ^ 1) for i in range(n_batch)]
    far_swap = [(i, i ^ 2) for i in range(n_batch)]

    def swapped(array, pairs):
        return lax.ppermute(array, "batch", pairs)

    turn = jnp.where(own == 0, jnp.array([0, 1], jnp.int32), jnp.array([steps - 1, -1], jnp.int32))
    feats_v, feat_all = pl.pallas_call(
        order_kernel,
        out_shape=(vmem(feats.shape, BF16), hbm(feats.shape, BF16)),
        in_specs=[SMEM, ANY],
        out_specs=[VMEM, ANY],
        scratch_shapes=[pltpu.SemaphoreType.DMA((steps,)), pltpu.SemaphoreType.DMA],
        compiler_params=params(1),
        name="order",
    )(turn, feats)
    feat_in = (swapped(feat_all, near_swap), swapped(feat_all, far_swap))
    keep_v, bias_v, win_av, win_bv = place(keep, bias_p, win_a, win_b)
    rec_av, rec_bv, proj_av, proj_bv, start_hv, start_cv = place(rec_a, rec_b, proj_a, proj_b, start_h, start_c)

    gates_shape, cell_shape = (PIECES, streams, 4 * width), (PIECES, streams, width)
    inflow = pl.pallas_call(
        inflow_kernel,
        out_shape=vmem(gates_shape, F32),
        in_specs=[SMEM] + [VMEM] * 4,
        out_specs=VMEM,
        compiler_params=params(8),
        name="inflow",
    )(turn, pinned(feats_v), pinned(bias_v), pinned(win_av), pinned(win_bv))

    def forward_call(first, step, part, peer, cell, inflow):
        return pl.pallas_call(
            functools.partial(forward_kernel, first),
            out_shape=(
                vmem((streams, depth), BF16),
                vmem(cell_shape, F32),
                vmem(gates_shape, BF16),
                vmem(cell_shape, BF16),
                vmem((streams, depth), BF16),
                vmem((streams, depth), BF16),
                vmem((streams, depth), F32),
            ),
            in_specs=[SMEM] + [VMEM] * 10,
            out_specs=[VMEM] * 7,
            compiler_params=params(8),
            name="forward_step",
        )(
            at_step(step), pinned(part), pinned(peer), pinned(start_hv), pinned(keep_v), pinned(cell), pinned(inflow),
            pinned(rec_av), pinned(rec_bv), pinned(proj_av), pinned(proj_bv),
        )

    def between_call(step, fresh, stacks, passing=()):
        shapes = (
            hbm((PIECES, steps, streams, 4 * width), BF16),
            hbm((steps,) + cell_shape, F32),
            hbm((PIECES, steps, streams, width), BF16),
            hbm((steps, streams, depth), BF16),
            hbm((steps, streams, depth), BF16),
            hbm((steps, streams, depth), F32),
        )
        aliases = {11 + i: 1 + i for i in range(len(stacks))}
        aliases.update({11 + len(stacks) + i: 7 + i for i in range(len(passing))})
        inflow, *out = pl.pallas_call(
            functools.partial(between_kernel, not stacks, len(passing)),
            out_shape=(vmem(gates_shape, F32),) + shapes + tuple(hbm(x.shape, x.dtype) for x in passing),
            in_specs=[SMEM] + [VMEM] * 10 + [ANY] * (len(stacks) + len(passing)),
            out_specs=[VMEM] + [ANY] * (6 + len(passing)),
            scratch_shapes=[pltpu.SemaphoreType.DMA((2 * PIECES + 4,))],
            input_output_aliases=aliases,
            compiler_params=params(8),
            cost_estimate=cost(2 * streams * depth * 8 * cells, 8 * depth * cells * 2),
            name="between",
        )(
            at_step(step), pinned(feats_v), pinned(bias_v), pinned(win_av), pinned(win_bv),
            *(pinned(x) for x in fresh), *(in_hbm(x) for x in (*stacks, *passing)),
        )
        return inflow, tuple(out[:6]), tuple(out[6:])

    none = jnp.zeros((streams, depth), BF16)
    part, peer, cell, stacks = none, none, start_cv, ()
    for step in range(steps):
        part, cell, *fresh = forward_call(step == 0, step, part, peer, cell, inflow)
        peer = lax.ppermute(part, "gate", across)
        due = step == (2 * steps) // 3
        inflow, stacks, passed = between_call(step, (cell, *fresh), stacks, feat_in if due else ())
        feat_in = passed if due else feat_in
    gates_all, cells_all, mixed_all, prev_all, hidden_all, slope_all = stacks
    prev_in = (swapped(prev_all, near_swap), swapped(prev_all, far_swap))

    saved_shapes = (
        vmem(gates_shape, BF16),
        vmem(cell_shape, F32),
        vmem(cell_shape, F32),
        vmem((streams, depth), F32),
        vmem((streams, depth), BF16),
    )
    *saved, hidden_all, slope_all = pl.pallas_call(
        finish_kernel,
        out_shape=saved_shapes + (hbm((steps, streams, depth), BF16), hbm((steps, streams, depth), F32)),
        in_specs=[SMEM, VMEM, VMEM] + [ANY] * 5,
        out_specs=[VMEM] * 5 + [ANY] * 2,
        scratch_shapes=[
            pltpu.VMEM((streams, depth), BF16),
            pltpu.SemaphoreType.DMA((PIECES + 4,)),
            pltpu.SemaphoreType.DMA,
        ],
        input_output_aliases={6: 5, 7: 6},
        compiler_params=params(8),
        name="finish",
    )(
        at_step(steps - 1), pinned(part), pinned(peer), in_hbm(gates_all), in_hbm(cells_all), in_hbm(ups),
        in_hbm(hidden_all), in_hbm(slope_all),
    )

    both_hidden = trade(hidden_all, hidden_all)

    def by_direction(mine, theirs):
        return jnp.stack([jnp.where(own == 0, mine, theirs), jnp.where(own == 0, theirs, mine)])

    hidden_dirs = by_direction(*both_hidden)
    outputs = (inputs.astype(F32) + jnp.transpose(hidden_dirs, (0, 2, 1, 3)).astype(F32)).astype(BF16)
    last_h = jnp.stack([hidden_dirs[0, steps - 1], hidden_dirs[1, 0]], axis=1).astype(F32)
    final_h = jnp.zeros_like(state_h).at[stream_doc].set(last_h)
    last_c = jnp.transpose(cell.reshape(QUARTERS, HALVES, streams, width), (0, 2, 1, 3)).reshape(
        QUARTERS, streams, cells
    )
    last_dirs = by_direction(*trade(last_c[0], last_c[1]))
    final_c = jnp.zeros_like(state_c).at[stream_doc].set(jnp.transpose(last_dirs, (1, 0, 2)))

    rec_at, rec_bt = (jnp.transpose(x, (0, 2, 1)) for x in (rec_a, rec_b))
    proj_at, proj_bt = jnp.transpose(proj_a), jnp.transpose(proj_b)
    rec_atv, rec_btv, proj_atv, proj_btv = place(rec_at, rec_bt, proj_at, proj_bt)

    def backward_call(step, part, peer, grad, saved):
        return pl.pallas_call(
            backward_kernel,
            out_shape=(
                vmem((streams, depth), BF16),
                vmem(cell_shape, F32),
                vmem((streams, depth), BF16),
                vmem(gates_shape, BF16),
            ),
            in_specs=[SMEM] + [VMEM] * 14,
            out_specs=[VMEM] * 4,
            compiler_params=params(8),
            name="backward_step",
        )(
            at_step(step), pinned(part), pinned(peer), pinned(keep_v), pinned(grad),
            pinned(rec_atv), pinned(rec_btv), pinned(proj_atv), pinned(proj_btv),
            *(pinned(x) for x in saved), pinned(start_cv),
        )

    def aside_call(step, slot, slots, dz, raw, stacks, sends, passing):
        piece_shape = (streams, 4 * width)
        shapes = (
            hbm((PIECES, steps) + piece_shape, BF16),
            hbm((steps, streams, depth), BF16),
            hbm((steps,) + piece_shape, BF16),
            hbm((steps,) + piece_shape, BF16),
            hbm((slots,) + piece_shape, BF16),
            hbm((slots,) + piece_shape, BF16),
        )
        kept = len(stacks)
        aliases = {7 + i: 5 + i for i in range(kept)}
        aliases.update({7 + kept + i: 9 + i for i in range(len(sends))})
        aliases.update({7 + kept + len(sends) + i: 11 + i for i in range(len(passing))})
        out = pl.pallas_call(
            functools.partial(aside_kernel, not stacks, not sends, len(passing)),
            out_shape=saved_shapes + shapes + tuple(hbm(x.shape, x.dtype) for x in passing),
            in_specs=[SMEM] + [VMEM] * 2 + [ANY] * (4 + kept + len(sends) + len(passing)),
            out_specs=[VMEM] * 5 + [ANY] * (6 + len(passing)),
            scratch_shapes=[
                pltpu.SemaphoreType.DMA((PIECES + 5,)),
                pltpu.SemaphoreType.DMA((PIECES + 4,)),
            ],
            input_output_aliases=aliases,
            compiler_params=params(8),
            cost_estimate=cost(0, 8 * MIB),
            name="aside",
        )(
            jnp.concatenate([at_step(step), jnp.stack([jnp.int32(slot), low, high])]), pinned(dz), pinned(raw),
            in_hbm(gates_all), in_hbm(cells_all), in_hbm(ups), in_hbm(slope_all),
            *(in_hbm(x) for x in (*stacks, *sends, *passing)),
        )
        return out[:5], tuple(out[5:9]), tuple(out[9:11]), tuple(out[11:])

    carry = (none, none, jnp.zeros(cell_shape, F32), saved, ())
    pending, arrived, top = [(steps - 1 - steps // 3, prev_in)], [], steps
    for index, share in enumerate(SHARES):
        slots = top if index == len(SHARES) - 1 else round(share * steps)
        sends = ()
        for step in range(top - 1, top - slots - 1, -1):
            part, peer, grad, saved, stacks = carry
            part, grad, raw, dz = backward_call(step, part, peer, grad, saved)
            peer = lax.ppermute(part, "gate", across)
            passing = pending.pop(0)[1] if pending and pending[0][0] >= step else ()
            saved, stacks, sends, passed = aside_call(
                step, step - (top - slots), slots, dz, raw, stacks, sends, passing
            )
            arrived += [passed] if passed else []
            carry = (part, peer, grad, saved, stacks)
        top -= slots
        pending.append((top - 2 - (2 * slots + 2) // 3, (swapped(sends[0], near_swap), swapped(sends[1], far_swap))))
    arrived += [arrays for _, arrays in pending]
    dz_all, raw_all, near_all, far_all = carry[-1]
    prev_in, exchanged = arrived[0], arrived[:0:-1]
    rows = steps * streams

    dx_all = pl.pallas_call(
        input_grad_kernel,
        out_shape=jax.ShapeDtypeStruct((steps, streams, depth), F32),
        grid_spec=pltpu.PrefetchScalarGridSpec(
            num_scalar_prefetch=1,
            grid=(PIECES, 4),
            in_specs=[
                pl.BlockSpec((1, steps, streams, width), lambda p, g, turn: (p, 0, 0, g)),
                pl.BlockSpec(
                    (1, depth, width), lambda p, g, turn: (jnp.where(p < 2, g, 3), 0, jnp.where(p < 2, p, 1))
                ),
                pl.BlockSpec(
                    (1, depth, width), lambda p, g, turn: (jnp.where(p < 2, 0, g), 0, jnp.where(p < 2, 0, p - 2))
                ),
            ],
            out_specs=pl.BlockSpec((steps, streams, depth), lambda p, g, turn: (0, 0, 0)),
            scratch_shapes=[pltpu.VMEM((rows, depth), F32)],
        ),
        compiler_params=params(24),
        cost_estimate=cost(2 * rows * depth * 8 * cells, 8 * depth * cells * 4),
        name="input_grad",
    )(turn, dz_all, win_a, win_b)

    def line_sum(chunks, axis, stride, count):
        here = (spot // stride) % count

        def chunk(index):
            return lax.dynamic_index_in_dim(chunks, jnp.clip(index, 0, count - 1), axis, keepdims=False)

        def at(device):
            return (device // stride) % count

        if count == 2:
            pairs = [(i, i + stride if at(i) == 0 else i - stride) for i in range(n_batch)]
            return (chunk(here).astype(F32) + swapped(chunk(1 - here), pairs).astype(F32)).astype(BF16)
        up, down = None, None
        for slot in range(1, count):
            rise, fall = chunk(here + count - slot), chunk(here - count + slot)
            if slot > 1:
                rise = (rise.astype(F32) + up.astype(F32)).astype(BF16)
                fall = (fall.astype(F32) + down.astype(F32)).astype(BF16)
            up = swapped(rise, [(i, i + stride) for i in range(n_batch) if at(i) < min(slot, count - 1)])
            down = swapped(fall, [(i, i - stride) for i in range(n_batch) if at(i) > max(count - 1 - slot, 0)])
        return (chunk(here).astype(F32) + up.astype(F32) + down.astype(F32)).astype(BF16)

    line = n_batch // 2
    share_rows = depth // n_batch

    def finish_halves(halves, index, pairs):
        mine = lax.dynamic_index_in_dim(halves, index, 1, keepdims=False)
        theirs = swapped(lax.dynamic_index_in_dim(halves, 1 - index, 1, keepdims=False), pairs)
        return jnp.stack([jnp.where(index == 0, mine, theirs), jnp.where(index == 0, theirs, mine)], axis=1)

    def product(left, right):
        return lax.dot_general(
            left.reshape(rows, -1), right.reshape(rows, -1), (((0,), (0,)), ((), ())), preferred_element_type=F32
        )

    def both(feat, prev):
        return jnp.concatenate([feat, prev], axis=2)

    left = both(feat_all, prev_all)
    sums = [
        (product(left, kept) + product(both(feat, prev), jnp.concatenate(taken, axis=0)))
        .astype(BF16)
        .reshape(2, line, 2, share_rows, 4 * width)
        for kept, feat, prev, taken in zip((near_all, far_all), feat_in, prev_in, zip(*exchanged))
    ]
    near = finish_halves(line_sum(sums[0], 1, 2, line), low, near_swap)
    far = line_sum(sums[1], 2, 1, 2).reshape(2, line // 2, 2, share_rows, 4 * width)
    far = finish_halves(line_sum(far, 1, 4, line // 2), high, far_swap)

    grad_proj = jnp.einsum("ptnc,tnk->kpc", mixed_all, raw_all, preferred_element_type=F32).astype(BF16)
    grad_proj = line_sum(grad_proj.reshape(line, 2, share_rows, QUARTERS * cells), 1, 1, 2)
    grad_proj = line_sum(grad_proj, 0, 2, line)

    grad_bias = jnp.sum(dz_all, axis=(1, 2), dtype=F32)
    stride = 1
    while stride < n_batch:
        grad_bias = grad_bias + swapped(grad_bias, [(i, i ^ stride) for i in range(n_batch)])
        stride *= 2

    def gate_rows(halves):
        shaped = halves.reshape(2, HALVES, -1, 4, width)
        return jnp.transpose(shaped, (0, 2, 3, 1, 4)).reshape(2, -1, 4, cells)

    def home(mine, theirs):
        return by_direction(*trade(mine, theirs)).astype(F32)

    grad_w_in, grad_w_rec = jnp.moveaxis(home(gate_rows(near), gate_rows(far)), 1, 0)
    shaped = jnp.transpose(grad_bias.reshape(QUARTERS, HALVES, 4, width), (0, 2, 1, 3)).reshape(QUARTERS, 4, cells)
    own_cells = cells // n_batch
    shaped = lax.dynamic_slice_in_dim(shaped, spot * own_cells, own_cells, 2)
    grad_bias = home(shaped[0], shaped[1])
    grad_proj = grad_proj.reshape(share_rows, QUARTERS, cells)
    grad_proj = home(jnp.transpose(grad_proj[:, 0]), jnp.transpose(grad_proj[:, 1]))

    half_cols = depth // 2
    upper = rank // 2
    keep_cols = lax.dynamic_slice_in_dim(dx_all, upper * half_cols, half_cols, 2)
    send_cols = lax.dynamic_slice_in_dim(dx_all, (1 - upper) * half_cols, half_cols, 2).astype(BF16)
    dx_half = keep_cols + lax.ppermute(send_cols, "gate", across).astype(F32)
    up_half = lax.dynamic_slice_in_dim(ups, upper * half_cols, half_cols, 2).astype(F32)
    dx_half = (dx_half + up_half).astype(BF16)
    quarter_cols = half_cols // 2
    mine = lax.dynamic_slice_in_dim(dx_half, own * quarter_cols, quarter_cols, 2)
    theirs = lax.dynamic_slice_in_dim(dx_half, (1 - own) * quarter_cols, quarter_cols, 2)
    dx_dirs = by_direction(*trade(mine, theirs))
    input_grad = jnp.transpose(dx_dirs, (0, 2, 1, 3))
    return (outputs, input_grad, grad_w_in, grad_w_rec, grad_bias, grad_proj, final_h, final_c)


def solution(mesh):
    placed = (
        P(None, "batch", None, None),
        P(None, None, None, "gate"),
        P(None, None, None, "gate"),
        P(None, None, "gate"),
        P(None, "gate", None),
        P("batch", None, None),
        P("batch", None, "gate"),
        P("batch", None),
        P("batch"),
        P(None, "batch", None, None),
    )
    return jax.shard_map(
        body,
        mesh=mesh,
        in_specs=placed,
        out_specs=(
            P(None, "batch", None, None),
            P(None, "batch", None, "gate"),
            P(None, "batch", None, "gate"),
            P(None, "batch", None, "gate"),
            P(None, None, ("gate", "batch")),
            P(None, "gate", "batch"),
            P("batch", None, None),
            P("batch", None, "gate"),
        ),
        check_vma=False,
    )
```

```python
import functools

import jax
import jax.numpy as jnp
from jax import lax
from jax.experimental import pallas as pl
from jax.experimental.pallas import tpu as pltpu
from jax.sharding import PartitionSpec as P

CLIP = 3.0
F32, BF16 = jnp.float32, jnp.bfloat16
QUARTERS, HALVES = 2, 2
PIECES = QUARTERS * HALVES
MIB = 2**20
SHARES = (0.35, 0.3, 0.2, 0.1, 0.05)

VMEM = pl.BlockSpec(memory_space=pltpu.VMEM)
SMEM = pl.BlockSpec(memory_space=pltpu.SMEM)
ANY = pl.BlockSpec(memory_space=pl.ANY)


def pinned(array):
    return pltpu.with_memory_space_constraint(array, pltpu.VMEM)


def in_hbm(array):
    return pltpu.with_memory_space_constraint(array, pltpu.HBM)


def dot(left, right):
    return jnp.dot(left, right, preferred_element_type=F32)


def place_kernel(count, *refs):
    sources, targets, sems = refs[:count], refs[count : 2 * count], refs[2 * count]
    copies = [pltpu.make_async_copy(a, b, sems.at[i]) for i, (a, b) in enumerate(zip(sources, targets))]
    for copy in copies:
        copy.start()
    for copy in copies:
        copy.wait()


def place(*arrays):
    count = len(arrays)
    return pl.pallas_call(
        functools.partial(place_kernel, count),
        out_shape=tuple(pltpu.VMEM(x.shape, x.dtype) for x in arrays),
        in_specs=[ANY] * count,
        out_specs=[VMEM] * count,
        scratch_shapes=[pltpu.SemaphoreType.DMA((count,))],
        compiler_params=params(1),
        name="place",
    )(*(in_hbm(x) for x in arrays))


def layout_kernel(which_ref, w_ref, out_ref, buf, sems):
    depth, part = w_ref.shape[1], buf.shape[1]

    def fetch(i):
        return pltpu.make_async_copy(w_ref.at[which_ref[0], pl.ds(i * part, part)], buf.at[i % 3], sems.at[i % 3])

    count = depth // part
    for i in range(min(2, count)):
        fetch(i).start()
    for i in range(count):
        if i + 2 < count:
            fetch(i + 2).start()
        fetch(i).wait()
        out_ref[:, i * part : (i + 1) * part, :] = jnp.swapaxes(buf[i % 3], 0, 1)


def turned_kernel(wa_ref, wb_ref, pa_ref, pb_ref, wat_ref, wbt_ref, pat_ref, pbt_ref):
    for w_ref, out_ref in ((wa_ref, wat_ref), (wb_ref, wbt_ref)):
        for gate in range(4):
            for half in range(HALVES):
                width = w_ref.shape[2] // HALVES
                cols = slice(half * width, (half + 1) * width)
                out_ref[gate, cols, :] = w_ref[gate, :, cols].T
    pat_ref[...] = pa_ref[...].T
    pbt_ref[...] = pb_ref[...].T


def pass_kernel(*refs):
    pass


def after(token, *arrays):
    return pl.pallas_call(
        pass_kernel,
        out_shape=tuple(pltpu.HBM(x.shape, x.dtype) for x in arrays),
        in_specs=[ANY] * (1 + len(arrays)),
        out_specs=[ANY] * len(arrays),
        input_output_aliases={1 + i: i for i in range(len(arrays))},
        compiler_params=params(1),
        name="after",
    )(token, *(in_hbm(x) for x in arrays))


def assemble_kernel(place_ref, near_a, near_b, far_a, far_b, in_ref, rec_ref):
    own, low, high = place_ref[0], place_ref[1], place_ref[2]
    width = in_ref.shape[3] // HALVES
    for direction, mine_ref, theirs_ref, index in ((own, near_a, near_b, low), (1 - own, far_a, far_b, high)):
        for which, out_ref in ((0, in_ref), (1, rec_ref)):
            mine, theirs = mine_ref[which].astype(F32), theirs_ref[which].astype(F32)
            for half in range(HALVES):
                whole = jnp.where(index == half, mine, theirs)
                gates = jnp.stack([whole[:, gate * width : (gate + 1) * width] for gate in range(4)])
                out_ref[direction, :, :, half * width : (half + 1) * width] = jnp.swapaxes(gates, 0, 1)


def order_kernel(step_ref, feat_ref, out_ref, all_ref, sems, all_sem):
    steps = feat_ref.shape[0]
    copies = [
        pltpu.make_async_copy(feat_ref.at[step_ref[0] + step_ref[1] * i], out_ref.at[i], sems.at[i]) for i in range(steps)
    ]
    for copy in copies:
        copy.start()
    for copy in copies:
        copy.wait()
    whole = pltpu.make_async_copy(out_ref, all_ref, all_sem)
    whole.start()
    whole.wait()


def pieces(refs, axis):
    for piece in range(PIECES):
        quarter, half = divmod(piece, HALVES)
        width = refs[0].shape[axis] // HALVES
        yield piece, quarter, width, slice(half * width, (half + 1) * width)


def forward_kernel(
    first, step_ref, p_ref, q_ref, start_ref, keep_ref, cell_ref, inflow_ref, wa_ref, wb_ref, pa_ref, pb_ref,
    part_ref, next_ref, gates_ref, mixed_ref, prev_ref, hidden_ref, slope_ref,
):
    keep = keep_ref[step_ref[1]][:, :1]
    if first:
        hidden = start_ref[...]
    else:
        hidden = clipped(p_ref, q_ref, hidden_ref, slope_ref)
    hidden = hidden * keep.astype(BF16)
    prev_ref[...] = hidden
    part = jnp.zeros(part_ref.shape, F32)
    for piece, quarter, width, cols in pieces((wa_ref, wb_ref), 2):
        w_ref, proj_ref = ((wa_ref, pa_ref), (wb_ref, pb_ref))[quarter]
        acts = []
        for gate in range(4):
            place = slice(gate * width, (gate + 1) * width)
            pre = dot(hidden, w_ref[gate, :, cols]) + inflow_ref[piece, :, place]
            act = jnp.tanh(pre if gate == 2 else 0.5 * pre)
            gates_ref[piece, :, place] = act.astype(BF16)
            acts.append(act if gate == 2 else 0.5 + 0.5 * act)
        ingate, forget, candidate, outgate = acts
        cell = CLIP * jnp.tanh((forget * (keep * cell_ref[piece]) + ingate * candidate) * (1.0 / CLIP))
        next_ref[piece] = cell
        mixed = (outgate * jnp.tanh(cell)).astype(BF16)
        mixed_ref[piece] = mixed
        part = part + dot(mixed, proj_ref[cols, :])
    part_ref[...] = part.astype(BF16)


def clipped(p_ref, q_ref, hidden_ref, slope_ref):
    squash = jnp.tanh((p_ref[...].astype(F32) + q_ref[...].astype(F32)) * (1.0 / CLIP))
    hidden = (CLIP * squash).astype(BF16)
    hidden_ref[...] = hidden
    slope_ref[...] = 1.0 - squash * squash
    return hidden


def between_kernel(
    first, last, passed, step_ref, feat_ref, bias_ref, wa_ref, wb_ref, cell_ref, gates_ref, mixed_ref, prev_ref, hidden_ref,
    slope_ref, *refs,
):
    refs = refs[(0 if first else 6) + passed :]
    out_ref, gates_all, cells_all, mixed_all, prev_all, hidden_all, slope_all = refs[:7]
    sems = refs[-1]
    step, time_before = step_ref[0], step_ref[2]
    copies = [pltpu.make_async_copy(gates_ref.at[i], gates_all.at[i, step], sems.at[i]) for i in range(PIECES)]
    copies += [
        pltpu.make_async_copy(mixed_ref.at[i], mixed_all.at[i, step], sems.at[PIECES + i]) for i in range(PIECES)
    ]
    copies.append(pltpu.make_async_copy(cell_ref, cells_all.at[step], sems.at[2 * PIECES]))
    copies.append(pltpu.make_async_copy(prev_ref, prev_all.at[step], sems.at[2 * PIECES + 1]))
    if not first:
        copies.append(pltpu.make_async_copy(hidden_ref, hidden_all.at[time_before], sems.at[2 * PIECES + 2]))
        copies.append(pltpu.make_async_copy(slope_ref, slope_all.at[step - 1], sems.at[2 * PIECES + 3]))
    for copy in copies:
        copy.start()
    if not last:
        inflow_into(feat_ref[step + 1], bias_ref, wa_ref, wb_ref, out_ref)
    for copy in copies:
        copy.wait()


def inflow_into(feat, bias_ref, wa_ref, wb_ref, out_ref):
    for piece, quarter, width, cols in pieces((wa_ref, wb_ref), 2):
        w_ref = (wa_ref, wb_ref)[quarter]
        for gate in range(4):
            place = slice(gate * width, (gate + 1) * width)
            out_ref[piece, :, place] = dot(feat, w_ref[gate, :, cols]) + bias_ref[piece, :, place]


def inflow_kernel(step_ref, feat_ref, bias_ref, wa_ref, wb_ref, out_ref):
    inflow_into(feat_ref[0], bias_ref, wa_ref, wb_ref, out_ref)


def backward_kernel(
    step_ref, p_ref, q_ref, keep_ref, grad_ref, wa_ref, wb_ref, pa_ref, pb_ref,
    gates_ref, cell_ref, prev_ref, slope_ref, up_ref, start_ref,
    part_ref, next_ref, raw_ref, dz_ref,
):
    step = step_ref[0]
    keep = keep_ref[step_ref[1]][:, :1]
    raw = (up_ref[...].astype(F32) + (p_ref[...].astype(F32) + q_ref[...].astype(F32))) * slope_ref[...]
    raw = raw.astype(BF16)
    raw_ref[...] = raw
    part = jnp.zeros(part_ref.shape, F32)
    for piece, quarter, width, cols in pieces((wa_ref, wb_ref), 1):
        w_ref, proj_ref = ((wa_ref, pa_ref), (wb_ref, pb_ref))[quarter]
        mixed = dot(raw, proj_ref[:, cols])
        acts = [gates_ref[piece, :, gate * width : (gate + 1) * width].astype(F32) for gate in range(4)]
        ingate, forget, outgate = (0.5 + 0.5 * acts[gate] for gate in (0, 1, 3))
        slopes = [1.0 - act * act for act in acts]
        cell = cell_ref[piece]
        prev = keep * jnp.where(step == 0, start_ref[piece], prev_ref[piece])
        squash = jnp.tanh(cell)
        total = grad_ref[piece] + mixed * outgate * (1.0 - squash * squash)
        inner = total * (1.0 - (cell * (1.0 / CLIP)) * (cell * (1.0 / CLIP)))
        next_ref[piece] = keep * inner * forget
        quart = 0.25 * inner
        pre_grads = (
            quart * acts[2] * slopes[0],
            quart * prev * slopes[1],
            inner * ingate * slopes[2],
            0.25 * mixed * squash * slopes[3],
        )
        for gate in range(4):
            low = pre_grads[gate].astype(BF16)
            dz_ref[piece, :, gate * width : (gate + 1) * width] = low
            part = part + dot(low, w_ref[gate, cols, :])
    part_ref[...] = (part * keep).astype(BF16)


def finish_kernel(
    step_ref, p_ref, q_ref, gates_all, cells_all, ups_all, hidden_in, slope_in,
    gates_ref, cell_ref, prev_ref, slope_ref, up_ref, hidden_all, slope_all,
    hidden_buf, sems, hidden_sem,
):
    copies = fetches(
        step_ref[0], step_ref[1], (gates_all, cells_all, ups_all), (gates_ref, cell_ref, prev_ref, up_ref), sems
    )
    for copy in copies:
        copy.start()
    clipped(p_ref, q_ref, hidden_buf, slope_ref)
    hidden_copy = pltpu.make_async_copy(hidden_buf, hidden_all.at[step_ref[1]], hidden_sem)
    hidden_copy.start()
    for copy in copies:
        copy.wait()
    hidden_copy.wait()


def fetches(step, time, sources, targets, sems):
    gates_all, cells_all, ups_all = sources
    gates_ref, cell_ref, prev_ref, up_ref = targets
    before = jnp.maximum(step - 1, 0)
    return [
        pltpu.make_async_copy(gates_all.at[i, step], gates_ref.at[i], sems.at[i]) for i in range(PIECES)
    ] + [
        pltpu.make_async_copy(cells_all.at[step], cell_ref, sems.at[PIECES]),
        pltpu.make_async_copy(cells_all.at[before], prev_ref, sems.at[PIECES + 1]),
        pltpu.make_async_copy(ups_all.at[time], up_ref, sems.at[PIECES + 2]),
    ]


def aside_kernel(
    first, opens, passed, step_ref, dz_ref, raw_ref, gates_all, cells_all, ups_all, slope_all, *refs
):
    refs = refs[(0 if first else 4) + (0 if opens else 2) + passed :]
    gates_ref, cell_ref, prev_ref, slope_ref, up_ref = refs[:5]
    dz_all, raw_all, near_all, far_all, near_out, far_out = refs[5:11]
    sems, fetch_sems = refs[-2:]
    step, time_before = step_ref[0], step_ref[2]
    slot, low, high = step_ref[4], step_ref[5], step_ref[6]
    before = jnp.maximum(step - 1, 0)
    copies = fetches(
        before, time_before, (gates_all, cells_all, ups_all), (gates_ref, cell_ref, prev_ref, up_ref), fetch_sems
    )
    copies.append(pltpu.make_async_copy(slope_all.at[before], slope_ref, fetch_sems.at[PIECES + 3]))
    copies += [pltpu.make_async_copy(dz_ref.at[i], dz_all.at[i, step], sems.at[i]) for i in range(PIECES)]
    copies.append(pltpu.make_async_copy(raw_ref, raw_all.at[step], sems.at[PIECES]))
    copies.append(pltpu.make_async_copy(dz_ref.at[low], near_all.at[step], sems.at[PIECES + 1]))
    copies.append(pltpu.make_async_copy(dz_ref.at[HALVES + high], far_all.at[step], sems.at[PIECES + 2]))
    copies.append(pltpu.make_async_copy(dz_ref.at[1 - low], near_out.at[slot], sems.at[PIECES + 3]))
    copies.append(pltpu.make_async_copy(dz_ref.at[HALVES + 1 - high], far_out.at[slot], sems.at[PIECES + 4]))
    for copy in copies:
        copy.start()
    for copy in copies:
        copy.wait()


def input_grad_kernel(step_ref, dz_ref, wa_ref, wb_ref, out_ref, acc_ref):
    piece, gate = pl.program_id(0), pl.program_id(1)
    steps, streams, width = dz_ref.shape[1:]

    @pl.when((piece == 0) & (gate == 0))
    def _():
        acc_ref[...] = jnp.zeros(acc_ref.shape, F32)

    weights = jnp.where(piece < HALVES, wa_ref[0], wb_ref[0])
    acc_ref[...] += lax.dot_general(
        dz_ref[0].reshape(steps * streams, width), weights, (((1,), (1,)), ((), ())), preferred_element_type=F32
    )

    @pl.when((piece == PIECES - 1) & (gate == 3))
    def _():
        for step in range(steps):
            time = step_ref[0] + step_ref[1] * step
            out_ref[time] = acc_ref[step * streams : (step + 1) * streams, :]


def params(mib):
    return pltpu.CompilerParams(vmem_limit_bytes=mib * MIB)


def cost(flops, size):
    return pl.CostEstimate(flops=flops, bytes_accessed=size, transcendentals=0)


def body(inputs, w_in, w_rec, bias, proj, state_h, state_c, resets, stream_doc, cotangent):
    streams, steps, depth = inputs.shape[1:]
    cells = w_in.shape[3]
    width = cells // HALVES
    rank = lax.axis_index("gate")
    own = rank % 2
    gates_size = lax.axis_size("gate")
    swap = [(i, i ^ 1) for i in range(gates_size)]
    across = [(i, i ^ 2) for i in range(gates_size)]

    def pick(stacked, index):
        return lax.dynamic_index_in_dim(stacked, index, 0, keepdims=False)

    def trade(mine, theirs):
        return (mine, lax.ppermute(theirs, "gate", swap))

    def vmem(shape, dtype):
        return pltpu.VMEM(shape, dtype)

    def hbm(shape, dtype):
        return pltpu.HBM(shape, dtype)

    def by_gate(weights, index):
        shape = (4,) + weights.shape[1:2] + weights.shape[3:]
        part = weights.shape[1] // 8
        return pl.pallas_call(
            layout_kernel,
            out_shape=vmem(shape, BF16),
            in_specs=[SMEM, ANY],
            out_specs=VMEM,
            scratch_shapes=[pltpu.VMEM((3, part) + weights.shape[2:], BF16), pltpu.SemaphoreType.DMA((3,))],
            compiler_params=params(8),
            name="layout",
        )(jnp.full((1,), index, jnp.int32), in_hbm(weights))

    sent = [by_gate(w, 1 - own) for w in (w_in, w_rec)]
    win_b, rec_b = (lax.ppermute(x, "gate", swap) for x in sent)
    win_av, rec_av = by_gate(w_in, own), by_gate(w_rec, own)
    proj_a, proj_b = trade(pick(proj, own), pick(proj, 1 - own))
    bias_a, bias_b = trade(pick(bias, own), pick(bias, 1 - own))

    def pieces_of(pair):
        split = [x.reshape(4, HALVES, width) for x in pair]
        return jnp.transpose(jnp.stack(split), (0, 2, 1, 3)).reshape(PIECES, 1, 4 * width)

    bias_p = pieces_of((bias_a, bias_b)).astype(F32)

    def cells_to_pieces(pair):
        both = jnp.stack(pair).reshape(QUARTERS, streams, HALVES, width)
        return jnp.transpose(both, (0, 2, 1, 3)).reshape(PIECES, streams, width)

    def by_time(stacked):
        return jnp.transpose(pick(stacked, own), (1, 0, 2))

    feats = by_time(inputs)
    ups = by_time(cotangent)
    flags = resets.astype(F32)
    later = jnp.concatenate([flags[:, 1:], jnp.zeros_like(flags[:, :1])], axis=1)
    keep = 1.0 - jnp.where(own == 0, flags, later)
    keep = jnp.broadcast_to(jnp.transpose(keep)[:, :, None], (steps, streams, 128))

    docs_h = state_h[stream_doc]
    docs_c = state_c[stream_doc]
    start_h = pick(jnp.transpose(docs_h, (1, 0, 2)), own).astype(BF16)
    by_dir_c = jnp.transpose(docs_c, (1, 0, 2))
    start_c = cells_to_pieces(trade(pick(by_dir_c, own), pick(by_dir_c, 1 - own)))

    def at_step(step):
        near = jnp.array([step, step, max(step - 1, 0), min(step + 1, steps - 1)], jnp.int32)
        turned = jnp.array([step] + [steps - 1 - x for x in (step, max(step - 1, 0), min(step + 1, steps - 1))], jnp.int32)
        return jnp.where(own == 0, near, turned)

    n_batch = lax.axis_size("batch")
    spot = lax.axis_index("batch")
    low, high = spot % 2, (spot // 2) % 2
    near_swap = [(i, i ^ 1) for i in range(n_batch)]
    far_swap = [(i, i ^ 2) for i in range(n_batch)]

    def swapped(array, pairs):
        return lax.ppermute(array, "batch", pairs)

    turn = jnp.where(own == 0, jnp.array([0, 1], jnp.int32), jnp.array([steps - 1, -1], jnp.int32))
    feats_v, feat_all = pl.pallas_call(
        order_kernel,
        out_shape=(vmem(feats.shape, BF16), hbm(feats.shape, BF16)),
        in_specs=[SMEM, ANY],
        out_specs=[VMEM, ANY],
        scratch_shapes=[pltpu.SemaphoreType.DMA((steps,)), pltpu.SemaphoreType.DMA],
        compiler_params=params(1),
        name="order",
    )(turn, feats)
    feat_in = (swapped(feat_all, near_swap), swapped(feat_all, far_swap))
    keep_v, bias_v, win_bv = place(keep, bias_p, win_b)
    rec_bv, proj_av, proj_bv, start_hv, start_cv = place(rec_b, proj_a, proj_b, start_h, start_c)

    gates_shape, cell_shape = (PIECES, streams, 4 * width), (PIECES, streams, width)
    inflow = pl.pallas_call(
        inflow_kernel,
        out_shape=vmem(gates_shape, F32),
        in_specs=[SMEM] + [VMEM] * 4,
        out_specs=VMEM,
        compiler_params=params(8),
        name="inflow",
    )(turn, pinned(feats_v), pinned(bias_v), pinned(win_av), pinned(win_bv))

    def forward_call(first, step, part, peer, cell, inflow):
        return pl.pallas_call(
            functools.partial(forward_kernel, first),
            out_shape=(
                vmem((streams, depth), BF16),
                vmem(cell_shape, F32),
                vmem(gates_shape, BF16),
                vmem(cell_shape, BF16),
                vmem((streams, depth), BF16),
                vmem((streams, depth), BF16),
                vmem((streams, depth), F32),
            ),
            in_specs=[SMEM] + [VMEM] * 10,
            out_specs=[VMEM] * 7,
            compiler_params=params(8),
            name="forward_step",
        )(
            at_step(step), pinned(part), pinned(peer), pinned(start_hv), pinned(keep_v), pinned(cell), pinned(inflow),
            pinned(rec_av), pinned(rec_bv), pinned(proj_av), pinned(proj_bv),
        )

    def between_call(step, fresh, stacks, passing=()):
        shapes = (
            hbm((PIECES, steps, streams, 4 * width), BF16),
            hbm((steps,) + cell_shape, F32),
            hbm((PIECES, steps, streams, width), BF16),
            hbm((steps, streams, depth), BF16),
            hbm((steps, streams, depth), BF16),
            hbm((steps, streams, depth), F32),
        )
        aliases = {11 + i: 1 + i for i in range(len(stacks))}
        aliases.update({11 + len(stacks) + i: 7 + i for i in range(len(passing))})
        inflow, *out = pl.pallas_call(
            functools.partial(between_kernel, not stacks, step == steps - 1, len(passing)),
            out_shape=(vmem(gates_shape, F32),) + shapes + tuple(hbm(x.shape, x.dtype) for x in passing),
            in_specs=[SMEM] + [VMEM] * 10 + [ANY] * (len(stacks) + len(passing)),
            out_specs=[VMEM] + [ANY] * (6 + len(passing)),
            scratch_shapes=[pltpu.SemaphoreType.DMA((2 * PIECES + 4,))],
            input_output_aliases=aliases,
            compiler_params=params(8),
            cost_estimate=cost(2 * streams * depth * 8 * cells, 8 * depth * cells * 2),
            name="between",
        )(
            at_step(step), pinned(feats_v), pinned(bias_v), pinned(win_av), pinned(win_bv),
            *(pinned(x) for x in fresh), *(in_hbm(x) for x in (*stacks, *passing)),
        )
        return inflow, tuple(out[:6]), tuple(out[6:])

    none = jnp.zeros((streams, depth), BF16)
    part, peer, cell, stacks = none, none, start_cv, ()
    for step in range(steps):
        part, cell, *fresh = forward_call(step == 0, step, part, peer, cell, inflow)
        peer = lax.ppermute(part, "gate", across)
        due = step == (2 * steps) // 3
        inflow, stacks, passed = between_call(step, (cell, *fresh), stacks, feat_in if due else ())
        feat_in = passed if due else feat_in
    gates_all, cells_all, mixed_all, prev_all, hidden_all, slope_all = stacks
    prev_in = (swapped(prev_all, near_swap), swapped(prev_all, far_swap))

    saved_shapes = (
        vmem(gates_shape, BF16),
        vmem(cell_shape, F32),
        vmem(cell_shape, F32),
        vmem((streams, depth), F32),
        vmem((streams, depth), BF16),
    )
    *saved, hidden_all, slope_all = pl.pallas_call(
        finish_kernel,
        out_shape=saved_shapes + (hbm((steps, streams, depth), BF16), hbm((steps, streams, depth), F32)),
        in_specs=[SMEM, VMEM, VMEM] + [ANY] * 5,
        out_specs=[VMEM] * 5 + [ANY] * 2,
        scratch_shapes=[
            pltpu.VMEM((streams, depth), BF16),
            pltpu.SemaphoreType.DMA((PIECES + 4,)),
            pltpu.SemaphoreType.DMA,
        ],
        input_output_aliases={6: 5, 7: 6},
        compiler_params=params(8),
        name="finish",
    )(
        at_step(steps - 1), pinned(part), pinned(peer), in_hbm(gates_all), in_hbm(cells_all), in_hbm(ups),
        in_hbm(hidden_all), in_hbm(slope_all),
    )

    rec_atv, rec_btv, proj_atv, proj_btv = pl.pallas_call(
        turned_kernel,
        out_shape=(vmem((4, cells, depth), BF16),) * 2 + (vmem((depth, cells), BF16),) * 2,
        in_specs=[VMEM] * 4,
        out_specs=[VMEM] * 4,
        compiler_params=params(8),
        name="turned",
    )(pinned(rec_av), pinned(rec_bv), pinned(proj_av), pinned(proj_bv))

    def backward_call(step, part, peer, grad, saved):
        return pl.pallas_call(
            backward_kernel,
            out_shape=(
                vmem((streams, depth), BF16),
                vmem(cell_shape, F32),
                vmem((streams, depth), BF16),
                vmem(gates_shape, BF16),
            ),
            in_specs=[SMEM] + [VMEM] * 14,
            out_specs=[VMEM] * 4,
            compiler_params=params(8),
            name="backward_step",
        )(
            at_step(step), pinned(part), pinned(peer), pinned(keep_v), pinned(grad),
            pinned(rec_atv), pinned(rec_btv), pinned(proj_atv), pinned(proj_btv),
            *(pinned(x) for x in saved), pinned(start_cv),
        )

    def aside_call(step, slot, slots, dz, raw, stacks, sends, passing):
        piece_shape = (streams, 4 * width)
        shapes = (
            hbm((PIECES, steps) + piece_shape, BF16),
            hbm((steps, streams, depth), BF16),
            hbm((steps,) + piece_shape, BF16),
            hbm((steps,) + piece_shape, BF16),
            hbm((slots,) + piece_shape, BF16),
            hbm((slots,) + piece_shape, BF16),
        )
        kept = len(stacks)
        aliases = {7 + i: 5 + i for i in range(kept)}
        aliases.update({7 + kept + i: 9 + i for i in range(len(sends))})
        aliases.update({7 + kept + len(sends) + i: 11 + i for i in range(len(passing))})
        out = pl.pallas_call(
            functools.partial(aside_kernel, not stacks, not sends, len(passing)),
            out_shape=saved_shapes + shapes + tuple(hbm(x.shape, x.dtype) for x in passing),
            in_specs=[SMEM] + [VMEM] * 2 + [ANY] * (4 + kept + len(sends) + len(passing)),
            out_specs=[VMEM] * 5 + [ANY] * (6 + len(passing)),
            scratch_shapes=[
                pltpu.SemaphoreType.DMA((PIECES + 5,)),
                pltpu.SemaphoreType.DMA((PIECES + 4,)),
            ],
            input_output_aliases=aliases,
            compiler_params=params(8),
            cost_estimate=cost(0, 8 * MIB),
            name="aside",
        )(
            jnp.concatenate([at_step(step), jnp.stack([jnp.int32(slot), low, high])]), pinned(dz), pinned(raw),
            in_hbm(gates_all), in_hbm(cells_all), in_hbm(ups), in_hbm(slope_all),
            *(in_hbm(x) for x in (*stacks, *sends, *passing)),
        )
        return out[:5], tuple(out[5:9]), tuple(out[9:11]), tuple(out[11:])

    carry = (none, none, jnp.zeros(cell_shape, F32), saved, ())
    pending, arrived, top = [(steps - 1 - steps // 3, prev_in)], [], steps
    for index, share in enumerate(SHARES):
        slots = top if index == len(SHARES) - 1 else round(share * steps)
        sends = ()
        for step in range(top - 1, top - slots - 1, -1):
            part, peer, grad, saved, stacks = carry
            part, grad, raw, dz = backward_call(step, part, peer, grad, saved)
            peer = lax.ppermute(part, "gate", across)
            passing = pending.pop(0)[1] if pending and pending[0][0] >= step else ()
            saved, stacks, sends, passed = aside_call(
                step, step - (top - slots), slots, dz, raw, stacks, sends, passing
            )
            arrived += [passed] if passed else []
            carry = (part, peer, grad, saved, stacks)
        top -= slots
        due = max(top - 1 - (3 * slots + 3) // 4, 0 if slots > 2 else -1)
        pending.append((due, (swapped(sends[0], near_swap), swapped(sends[1], far_swap))))
    arrived += [arrays for _, arrays in pending]
    dz_all, raw_all, near_all, far_all = carry[-1]
    prev_in, exchanged = arrived[0], arrived[1:]
    rows = steps * streams

    def by_direction(mine, theirs):
        return jnp.stack([jnp.where(own == 0, mine, theirs), jnp.where(own == 0, theirs, mine)])

    def line_sum(chunks, axis, stride, count):
        here = (spot // stride) % count

        def chunk(index):
            return lax.dynamic_index_in_dim(chunks, jnp.clip(index, 0, count - 1), axis, keepdims=False)

        def at(device):
            return (device // stride) % count

        if count == 2:
            pairs = [(i, i + stride if at(i) == 0 else i - stride) for i in range(n_batch)]
            return (chunk(here).astype(F32) + swapped(chunk(1 - here), pairs).astype(F32)).astype(BF16)
        up, down = None, None
        for slot in range(1, count):
            rise, fall = chunk(here + count - slot), chunk(here - count + slot)
            if slot > 1:
                rise = (rise.astype(F32) + up.astype(F32)).astype(BF16)
                fall = (fall.astype(F32) + down.astype(F32)).astype(BF16)
            up = swapped(rise, [(i, i + stride) for i in range(n_batch) if at(i) < min(slot, count - 1)])
            down = swapped(fall, [(i, i - stride) for i in range(n_batch) if at(i) > max(count - 1 - slot, 0)])
        return (chunk(here).astype(F32) + up.astype(F32) + down.astype(F32)).astype(BF16)

    line = n_batch // 2
    share_rows = depth // n_batch

    def product(left, right):
        return lax.dot_general(
            left.reshape(rows, -1), right.reshape(rows, -1), (((0,), (0,)), ((), ())), preferred_element_type=F32
        )

    def both(feat, prev):
        return jnp.concatenate([feat, prev], axis=2)

    left = both(feat_all, prev_all)
    halves = []
    for kept, feat, prev, taken in zip((near_all, far_all), feat_in, prev_in, zip(*exchanged)):
        mine = product(left, kept)
        *taken, late, latest = taken
        late, latest = after(mine, late, latest)
        theirs = product(both(feat, prev), jnp.concatenate([latest, late, *taken[::-1]], axis=0))
        halves.append((mine + theirs).astype(BF16).reshape(2, line, 2, share_rows, 4 * width))
    near = line_sum(halves[0], 1, 2, line)
    far = line_sum(halves[1], 2, 1, 2).reshape(2, line // 2, 2, share_rows, 4 * width)
    far = line_sum(far, 1, 4, line // 2)

    def halves_of(summed, index, pairs):
        mine = lax.dynamic_index_in_dim(summed, index, 1, keepdims=False)
        return mine, swapped(lax.dynamic_index_in_dim(summed, 1 - index, 1, keepdims=False), pairs)

    near_pair = halves_of(near, low, near_swap)
    far_pair = [lax.ppermute(x, "gate", swap) for x in halves_of(far, high, far_swap)]
    grad_shape = (2, share_rows, 4, cells)
    grad_w_in, grad_w_rec = pl.pallas_call(
        assemble_kernel,
        out_shape=(jax.ShapeDtypeStruct(grad_shape, F32),) * 2,
        in_specs=[SMEM] + [VMEM] * 4,
        out_specs=[VMEM] * 2,
        compiler_params=params(32),
        name="assemble",
    )(jnp.stack([own, low, high]), *near_pair, *far_pair)

    dz_all, mixed_all, hidden_all, cell = after(halves[1], dz_all, mixed_all, hidden_all, cell)

    grad_proj = jnp.einsum("ptnc,tnk->kpc", mixed_all, raw_all, preferred_element_type=F32).astype(BF16)
    grad_proj = line_sum(grad_proj.reshape(line, 2, share_rows, QUARTERS * cells), 1, 1, 2)
    grad_proj = line_sum(grad_proj, 0, 2, line)

    grad_bias = jnp.sum(dz_all, axis=(1, 2), dtype=F32)
    stride = 1
    while stride < n_batch:
        grad_bias = grad_bias + swapped(grad_bias, [(i, i ^ stride) for i in range(n_batch)])
        stride *= 2

    def home(mine, theirs):
        return by_direction(*trade(mine, theirs)).astype(F32)

    shaped = jnp.transpose(grad_bias.reshape(QUARTERS, HALVES, 4, width), (0, 2, 1, 3)).reshape(QUARTERS, 4, cells)
    own_cells = cells // n_batch
    shaped = lax.dynamic_slice_in_dim(shaped, spot * own_cells, own_cells, 2)
    grad_bias = home(shaped[0], shaped[1])
    grad_proj = grad_proj.reshape(share_rows, QUARTERS, cells)
    grad_proj = home(jnp.transpose(grad_proj[:, 0]), jnp.transpose(grad_proj[:, 1]))

    both_hidden = trade(hidden_all, hidden_all)

    hidden_dirs = by_direction(*both_hidden)
    outputs = (inputs.astype(F32) + jnp.transpose(hidden_dirs, (0, 2, 1, 3)).astype(F32)).astype(BF16)
    last_h = jnp.stack([hidden_dirs[0, steps - 1], hidden_dirs[1, 0]], axis=1).astype(F32)
    final_h = jnp.zeros_like(state_h).at[stream_doc].set(last_h)
    last_c = jnp.transpose(cell.reshape(QUARTERS, HALVES, streams, width), (0, 2, 1, 3)).reshape(
        QUARTERS, streams, cells
    )
    last_dirs = by_direction(*trade(last_c[0], last_c[1]))
    final_c = jnp.zeros_like(state_c).at[stream_doc].set(jnp.transpose(last_dirs, (1, 0, 2)))

    dx_all = pl.pallas_call(
        input_grad_kernel,
        out_shape=jax.ShapeDtypeStruct((steps, streams, depth), F32),
        grid_spec=pltpu.PrefetchScalarGridSpec(
            num_scalar_prefetch=1,
            grid=(PIECES, 4),
            in_specs=[
                pl.BlockSpec((1, steps, streams, width), lambda p, g, turn: (p, 0, 0, g)),
                pl.BlockSpec(
                    (1, depth, width), lambda p, g, turn: (jnp.where(p < 2, g, 3), 0, jnp.where(p < 2, p, 1))
                ),
                pl.BlockSpec(
                    (1, depth, width), lambda p, g, turn: (jnp.where(p < 2, 0, g), 0, jnp.where(p < 2, 0, p - 2))
                ),
            ],
            out_specs=pl.BlockSpec((steps, streams, depth), lambda p, g, turn: (0, 0, 0)),
            scratch_shapes=[pltpu.VMEM((rows, depth), F32)],
        ),
        compiler_params=params(24),
        cost_estimate=cost(2 * rows * depth * 8 * cells, 8 * depth * cells * 4),
        name="input_grad",
    )(turn, dz_all, win_av, win_bv)

    half_cols = depth // 2
    upper = rank // 2
    keep_cols = lax.dynamic_slice_in_dim(dx_all, upper * half_cols, half_cols, 2)
    send_cols = lax.dynamic_slice_in_dim(dx_all, (1 - upper) * half_cols, half_cols, 2).astype(BF16)
    dx_half = keep_cols + lax.ppermute(send_cols, "gate", across).astype(F32)
    up_half = lax.dynamic_slice_in_dim(ups, upper * half_cols, half_cols, 2).astype(F32)
    dx_half = (dx_half + up_half).astype(BF16)
    quarter_cols = half_cols // 2
    mine = lax.dynamic_slice_in_dim(dx_half, own * quarter_cols, quarter_cols, 2)
    theirs = lax.dynamic_slice_in_dim(dx_half, (1 - own) * quarter_cols, quarter_cols, 2)
    dx_dirs = by_direction(*trade(mine, theirs))
    input_grad = jnp.transpose(dx_dirs, (0, 2, 1, 3))
    return (outputs, input_grad, grad_w_in, grad_w_rec, grad_bias, grad_proj, final_h, final_c)


def solution(mesh):
    placed = (
        P(None, "batch", None, None),
        P(None, None, None, "gate"),
        P(None, None, None, "gate"),
        P(None, None, "gate"),
        P(None, "gate", None),
        P("batch", None, None),
        P("batch", None, "gate"),
        P("batch", None),
        P("batch"),
        P(None, "batch", None, None),
    )
    return jax.shard_map(
        body,
        mesh=mesh,
        in_specs=placed,
        out_specs=(
            P(None, "batch", None, None),
            P(None, "batch", None, "gate"),
            P(None, "batch", None, "gate"),
            P(None, "batch", None, "gate"),
            P(None, None, ("gate", "batch")),
            P(None, "gate", "batch"),
            P("batch", None, None),
            P("batch", None, "gate"),
        ),
        check_vma=False,
    )
```

```python
import functools

import jax
import jax.numpy as jnp
from jax import lax
from jax.experimental import pallas as pl
from jax.experimental.pallas import tpu as pltpu
from jax.sharding import PartitionSpec as P

CLIP = 3.0
F32, BF16 = jnp.float32, jnp.bfloat16
QUARTERS, HALVES = 2, 2
PIECES = QUARTERS * HALVES
MIB = 2**20
LATE = 2
SHARES = (0.35, 0.3, 0.15, 0.1, 0.1)

VMEM = pl.BlockSpec(memory_space=pltpu.VMEM)
SMEM = pl.BlockSpec(memory_space=pltpu.SMEM)
ANY = pl.BlockSpec(memory_space=pl.ANY)


def pinned(array):
    return pltpu.with_memory_space_constraint(array, pltpu.VMEM)


def in_hbm(array):
    return pltpu.with_memory_space_constraint(array, pltpu.HBM)


def dot(left, right):
    return jnp.dot(left, right, preferred_element_type=F32)


def place_kernel(count, *refs):
    sources, targets, sems = refs[:count], refs[count : 2 * count], refs[2 * count]
    copies = [pltpu.make_async_copy(a, b, sems.at[i]) for i, (a, b) in enumerate(zip(sources, targets))]
    for copy in copies:
        copy.start()
    for copy in copies:
        copy.wait()


def place(*arrays):
    count = len(arrays)
    return pl.pallas_call(
        functools.partial(place_kernel, count),
        out_shape=tuple(pltpu.VMEM(x.shape, x.dtype) for x in arrays),
        in_specs=[ANY] * count,
        out_specs=[VMEM] * count,
        scratch_shapes=[pltpu.SemaphoreType.DMA((count,))],
        compiler_params=params(1),
        name="place",
    )(*(in_hbm(x) for x in arrays))


def layout_kernel(which_ref, w_ref, out_ref, all_ref, buf, sems, out_sems):
    depth, part = w_ref.shape[1], buf.shape[1]

    def fetch(i):
        return pltpu.make_async_copy(w_ref.at[which_ref[0], pl.ds(i * part, part)], buf.at[i % 3], sems.at[i % 3])

    def store(i):
        rows = pl.ds(i * part, part)
        return pltpu.make_async_copy(out_ref.at[:, rows], all_ref.at[:, rows], out_sems.at[i])

    count = depth // part
    for i in range(min(2, count)):
        fetch(i).start()
    for i in range(count):
        if i + 2 < count:
            fetch(i + 2).start()
        fetch(i).wait()
        out_ref[:, i * part : (i + 1) * part, :] = jnp.swapaxes(buf[i % 3], 0, 1)
        store(i).start()
    for i in range(count):
        store(i).wait()


def turned_kernel(wa_ref, wb_ref, pa_ref, pb_ref, wat_ref, wbt_ref, pat_ref, pbt_ref, buf, sems, proj_buf, proj_sems):
    jobs = [(w_ref, out_ref, gate) for w_ref, out_ref in ((wa_ref, wat_ref), (wb_ref, wbt_ref)) for gate in range(4)]

    def fetch(i):
        return pltpu.make_async_copy(jobs[i][0].at[jobs[i][2]], buf.at[i % 3], sems.at[i % 3])

    proj_fetches = [pltpu.make_async_copy(x, proj_buf.at[i], proj_sems.at[i]) for i, x in enumerate((pa_ref, pb_ref))]
    fetch(0).start()
    fetch(1).start()
    for copy in proj_fetches:
        copy.start()
    for i, (_, out_ref, gate) in enumerate(jobs):
        if i + 2 < len(jobs):
            fetch(i + 2).start()
        fetch(i).wait()
        for half in range(HALVES):
            width = buf.shape[2] // HALVES
            cols = slice(half * width, (half + 1) * width)
            out_ref[gate, cols, :] = buf[i % 3, :, cols].T
    for i, out_ref in enumerate((pat_ref, pbt_ref)):
        proj_fetches[i].wait()
        out_ref[...] = proj_buf[i].T


def pass_kernel(*refs):
    pass


def after(token, *arrays):
    return pl.pallas_call(
        pass_kernel,
        out_shape=tuple(pltpu.HBM(x.shape, x.dtype) for x in arrays),
        in_specs=[ANY] * (1 + len(arrays)),
        out_specs=[ANY] * len(arrays),
        input_output_aliases={1 + i: i for i in range(len(arrays))},
        compiler_params=params(1),
        name="after",
    )(token, *(in_hbm(x) for x in arrays))


def assemble_kernel(place_ref, near_a, near_b, far_a, far_b, in_ref, rec_ref):
    own, low, high = place_ref[0], place_ref[1], place_ref[2]
    width = in_ref.shape[3] // HALVES
    for direction, mine_ref, theirs_ref, index in ((own, near_a, near_b, low), (1 - own, far_a, far_b, high)):
        for which, out_ref in ((0, in_ref), (1, rec_ref)):
            mine, theirs = mine_ref[which].astype(F32), theirs_ref[which].astype(F32)
            for half in range(HALVES):
                whole = jnp.where(index == half, mine, theirs)
                gates = jnp.stack([whole[:, gate * width : (gate + 1) * width] for gate in range(4)])
                out_ref[direction, :, :, half * width : (half + 1) * width] = jnp.swapaxes(gates, 0, 1)


def order_kernel(step_ref, feat_ref, out_ref, all_ref, sems, all_sem):
    steps = feat_ref.shape[0]
    copies = [
        pltpu.make_async_copy(feat_ref.at[step_ref[0] + step_ref[1] * i], out_ref.at[i], sems.at[i]) for i in range(steps)
    ]
    for copy in copies:
        copy.start()
    for copy in copies:
        copy.wait()
    whole = pltpu.make_async_copy(out_ref, all_ref, all_sem)
    whole.start()
    whole.wait()


def pieces(refs, axis):
    for piece in range(PIECES):
        quarter, half = divmod(piece, HALVES)
        width = refs[0].shape[axis] // HALVES
        yield piece, quarter, width, slice(half * width, (half + 1) * width)


def forward_kernel(
    first, step_ref, p_ref, q_ref, start_ref, keep_ref, cell_ref, inflow_ref, wa_ref, wb_ref, pa_ref, pb_ref,
    part_ref, next_ref, gates_ref, mixed_ref, prev_ref, hidden_ref, slope_ref,
):
    keep = keep_ref[step_ref[1]][:, :1]
    if first:
        hidden = start_ref[...]
    else:
        hidden = clipped(p_ref, q_ref, hidden_ref, slope_ref)
    hidden = hidden * keep.astype(BF16)
    prev_ref[...] = hidden
    part = jnp.zeros(part_ref.shape, F32)
    for piece, quarter, width, cols in pieces((wa_ref, wb_ref), 2):
        w_ref, proj_ref = ((wa_ref, pa_ref), (wb_ref, pb_ref))[quarter]
        acts = []
        for gate in range(4):
            place = slice(gate * width, (gate + 1) * width)
            pre = dot(hidden, w_ref[gate, :, cols]) + inflow_ref[piece, :, place]
            act = jnp.tanh(pre if gate == 2 else 0.5 * pre)
            gates_ref[piece, :, place] = act.astype(BF16)
            acts.append(act if gate == 2 else 0.5 + 0.5 * act)
        ingate, forget, candidate, outgate = acts
        cell = CLIP * jnp.tanh((forget * (keep * cell_ref[piece]) + ingate * candidate) * (1.0 / CLIP))
        next_ref[piece] = cell
        mixed = (outgate * jnp.tanh(cell)).astype(BF16)
        mixed_ref[piece] = mixed
        part = part + dot(mixed, proj_ref[cols, :])
    part_ref[...] = part.astype(BF16)


def clipped(p_ref, q_ref, hidden_ref, slope_ref):
    squash = jnp.tanh((p_ref[...].astype(F32) + q_ref[...].astype(F32)) * (1.0 / CLIP))
    hidden = (CLIP * squash).astype(BF16)
    hidden_ref[...] = hidden
    slope_ref[...] = 1.0 - squash * squash
    return hidden


def between_kernel(
    first, last, passed, step_ref, feat_ref, bias_ref, wa_ref, wb_ref, cell_ref, gates_ref, mixed_ref, prev_ref, hidden_ref,
    slope_ref, *refs,
):
    refs = refs[(0 if first else 6) + passed :]
    out_ref, gates_all, cells_all, mixed_all, prev_all, hidden_all, slope_all = refs[:7]
    sems = refs[-1]
    step, time_before = step_ref[0], step_ref[2]
    copies = [pltpu.make_async_copy(gates_ref.at[i], gates_all.at[i, step], sems.at[i]) for i in range(PIECES)]
    copies += [
        pltpu.make_async_copy(mixed_ref.at[i], mixed_all.at[i, step], sems.at[PIECES + i]) for i in range(PIECES)
    ]
    copies.append(pltpu.make_async_copy(cell_ref, cells_all.at[step], sems.at[2 * PIECES]))
    copies.append(pltpu.make_async_copy(prev_ref, prev_all.at[step], sems.at[2 * PIECES + 1]))
    if not first:
        copies.append(pltpu.make_async_copy(hidden_ref, hidden_all.at[time_before], sems.at[2 * PIECES + 2]))
        copies.append(pltpu.make_async_copy(slope_ref, slope_all.at[step - 1], sems.at[2 * PIECES + 3]))
    for copy in copies:
        copy.start()
    if not last:
        inflow_into(feat_ref[step + 1], bias_ref, wa_ref, wb_ref, out_ref)
    for copy in copies:
        copy.wait()


def inflow_into(feat, bias_ref, wa_ref, wb_ref, out_ref):
    for piece, quarter, width, cols in pieces((wa_ref, wb_ref), 2):
        w_ref = (wa_ref, wb_ref)[quarter]
        for gate in range(4):
            place = slice(gate * width, (gate + 1) * width)
            out_ref[piece, :, place] = dot(feat, w_ref[gate, :, cols]) + bias_ref[piece, :, place]


def inflow_kernel(step_ref, feat_ref, bias_ref, wa_ref, wb_ref, out_ref):
    inflow_into(feat_ref[0], bias_ref, wa_ref, wb_ref, out_ref)


def backward_kernel(
    step_ref, p_ref, q_ref, keep_ref, grad_ref, wa_ref, wb_ref, pa_ref, pb_ref,
    gates_ref, cell_ref, prev_ref, slope_ref, up_ref, start_ref,
    part_ref, next_ref, raw_ref, dz_ref,
):
    step = step_ref[0]
    keep = keep_ref[step_ref[1]][:, :1]
    raw = (up_ref[...].astype(F32) + (p_ref[...].astype(F32) + q_ref[...].astype(F32))) * slope_ref[...]
    raw = raw.astype(BF16)
    raw_ref[...] = raw
    part = jnp.zeros(part_ref.shape, F32)
    for piece, quarter, width, cols in pieces((wa_ref, wb_ref), 1):
        w_ref, proj_ref = ((wa_ref, pa_ref), (wb_ref, pb_ref))[quarter]
        mixed = dot(raw, proj_ref[:, cols])
        acts = [gates_ref[piece, :, gate * width : (gate + 1) * width].astype(F32) for gate in range(4)]
        ingate, forget, outgate = (0.5 + 0.5 * acts[gate] for gate in (0, 1, 3))
        slopes = [1.0 - act * act for act in acts]
        cell = cell_ref[piece]
        prev = keep * jnp.where(step == 0, start_ref[piece], prev_ref[piece])
        squash = jnp.tanh(cell)
        total = grad_ref[piece] + mixed * outgate * (1.0 - squash * squash)
        inner = total * (1.0 - (cell * (1.0 / CLIP)) * (cell * (1.0 / CLIP)))
        next_ref[piece] = keep * inner * forget
        quart = 0.25 * inner
        pre_grads = (
            quart * acts[2] * slopes[0],
            quart * prev * slopes[1],
            inner * ingate * slopes[2],
            0.25 * mixed * squash * slopes[3],
        )
        for gate in range(4):
            low = pre_grads[gate].astype(BF16)
            dz_ref[piece, :, gate * width : (gate + 1) * width] = low
            part = part + dot(low, w_ref[gate, cols, :])
    part_ref[...] = (part * keep).astype(BF16)


def finish_kernel(
    step_ref, p_ref, q_ref, gates_all, cells_all, ups_all, hidden_in, slope_in,
    gates_ref, cell_ref, prev_ref, slope_ref, up_ref, hidden_all, slope_all,
    hidden_buf, sems, hidden_sem,
):
    copies = fetches(
        step_ref[0], step_ref[1], (gates_all, cells_all, ups_all), (gates_ref, cell_ref, prev_ref, up_ref), sems
    )
    for copy in copies:
        copy.start()
    clipped(p_ref, q_ref, hidden_buf, slope_ref)
    hidden_copy = pltpu.make_async_copy(hidden_buf, hidden_all.at[step_ref[1]], hidden_sem)
    hidden_copy.start()
    for copy in copies:
        copy.wait()
    hidden_copy.wait()


def fetches(step, time, sources, targets, sems):
    gates_all, cells_all, ups_all = sources
    gates_ref, cell_ref, prev_ref, up_ref = targets
    before = jnp.maximum(step - 1, 0)
    return [
        pltpu.make_async_copy(gates_all.at[i, step], gates_ref.at[i], sems.at[i]) for i in range(PIECES)
    ] + [
        pltpu.make_async_copy(cells_all.at[step], cell_ref, sems.at[PIECES]),
        pltpu.make_async_copy(cells_all.at[before], prev_ref, sems.at[PIECES + 1]),
        pltpu.make_async_copy(ups_all.at[time], up_ref, sems.at[PIECES + 2]),
    ]


def aside_kernel(
    first, last, opens, passed, step_ref, dz_ref, raw_ref, gates_all, cells_all, ups_all, slope_all, *refs
):
    refs = refs[(0 if first else 4) + (0 if opens else 2) + passed :]
    gates_ref, cell_ref, prev_ref, slope_ref, up_ref = refs[:5]
    dz_all, raw_all, near_all, far_all, near_out, far_out = refs[5:11]
    sems, fetch_sems = refs[-2:]
    step, time_before = step_ref[0], step_ref[2]
    slot, low, high = step_ref[4], step_ref[5], step_ref[6]
    before = jnp.maximum(step - 1, 0)
    copies = []
    if not last:
        copies += fetches(
            before, time_before, (gates_all, cells_all, ups_all), (gates_ref, cell_ref, prev_ref, up_ref), fetch_sems
        )
        copies.append(pltpu.make_async_copy(slope_all.at[before], slope_ref, fetch_sems.at[PIECES + 3]))
    copies += [pltpu.make_async_copy(dz_ref.at[i], dz_all.at[i, step], sems.at[i]) for i in range(PIECES)]
    copies.append(pltpu.make_async_copy(raw_ref, raw_all.at[step], sems.at[PIECES]))
    copies.append(pltpu.make_async_copy(dz_ref.at[low], near_all.at[step], sems.at[PIECES + 1]))
    copies.append(pltpu.make_async_copy(dz_ref.at[HALVES + high], far_all.at[step], sems.at[PIECES + 2]))
    copies.append(pltpu.make_async_copy(dz_ref.at[1 - low], near_out.at[slot], sems.at[PIECES + 3]))
    copies.append(pltpu.make_async_copy(dz_ref.at[HALVES + 1 - high], far_out.at[slot], sems.at[PIECES + 4]))
    for copy in copies:
        copy.start()
    for copy in copies:
        copy.wait()


def input_grad_kernel(step_ref, dz_ref, wa_ref, wb_ref, out_ref, acc_ref):
    piece, gate = pl.program_id(0), pl.program_id(1)
    steps, streams, width = dz_ref.shape[1:]

    @pl.when((piece == 0) & (gate == 0))
    def _():
        acc_ref[...] = jnp.zeros(acc_ref.shape, F32)

    weights = jnp.where(piece < HALVES, wa_ref[0], wb_ref[0])
    acc_ref[...] += lax.dot_general(
        dz_ref[0].reshape(steps * streams, width), weights, (((1,), (1,)), ((), ())), preferred_element_type=F32
    )

    @pl.when((piece == PIECES - 1) & (gate == 3))
    def _():
        for step in range(steps):
            time = step_ref[0] + step_ref[1] * step
            out_ref[time] = acc_ref[step * streams : (step + 1) * streams, :]


def params(mib):
    return pltpu.CompilerParams(vmem_limit_bytes=mib * MIB)


def cost(flops, size):
    return pl.CostEstimate(flops=flops, bytes_accessed=size, transcendentals=0)


def body(inputs, w_in, w_rec, bias, proj, state_h, state_c, resets, stream_doc, cotangent):
    streams, steps, depth = inputs.shape[1:]
    cells = w_in.shape[3]
    width = cells // HALVES
    rank = lax.axis_index("gate")
    own = rank % 2
    gates_size = lax.axis_size("gate")
    swap = [(i, i ^ 1) for i in range(gates_size)]
    across = [(i, i ^ 2) for i in range(gates_size)]

    def pick(stacked, index):
        return lax.dynamic_index_in_dim(stacked, index, 0, keepdims=False)

    def trade(mine, theirs):
        return (mine, lax.ppermute(theirs, "gate", swap))

    def vmem(shape, dtype):
        return pltpu.VMEM(shape, dtype)

    def hbm(shape, dtype):
        return pltpu.HBM(shape, dtype)

    def by_gate(weights, index):
        shape = (4,) + weights.shape[1:2] + weights.shape[3:]
        part = weights.shape[1] // 8
        return pl.pallas_call(
            layout_kernel,
            out_shape=(vmem(shape, BF16), hbm(shape, BF16)),
            in_specs=[SMEM, ANY],
            out_specs=[VMEM, ANY],
            scratch_shapes=[
                pltpu.VMEM((3, part) + weights.shape[2:], BF16),
                pltpu.SemaphoreType.DMA((3,)),
                pltpu.SemaphoreType.DMA((8,)),
            ],
            compiler_params=params(8),
            name="layout",
        )(jnp.full((1,), index, jnp.int32), in_hbm(weights))

    win_b, rec_b = (lax.ppermute(by_gate(w, 1 - own)[1], "gate", swap) for w in (w_in, w_rec))
    (win_av, win_a), (rec_av, rec_a) = by_gate(w_in, own), by_gate(w_rec, own)
    proj_a, proj_b = trade(pick(proj, own), pick(proj, 1 - own))
    bias_a, bias_b = trade(pick(bias, own), pick(bias, 1 - own))

    def pieces_of(pair):
        split = [x.reshape(4, HALVES, width) for x in pair]
        return jnp.transpose(jnp.stack(split), (0, 2, 1, 3)).reshape(PIECES, 1, 4 * width)

    bias_p = pieces_of((bias_a, bias_b)).astype(F32)

    def cells_to_pieces(pair):
        both = jnp.stack(pair).reshape(QUARTERS, streams, HALVES, width)
        return jnp.transpose(both, (0, 2, 1, 3)).reshape(PIECES, streams, width)

    def by_time(stacked):
        return jnp.transpose(pick(stacked, own), (1, 0, 2))

    feats = by_time(inputs)
    ups = by_time(cotangent)
    flags = resets.astype(F32)
    later = jnp.concatenate([flags[:, 1:], jnp.zeros_like(flags[:, :1])], axis=1)
    keep = 1.0 - jnp.where(own == 0, flags, later)
    keep = jnp.broadcast_to(jnp.transpose(keep)[:, :, None], (steps, streams, 128))

    docs_h = state_h[stream_doc]
    docs_c = state_c[stream_doc]
    start_h = pick(jnp.transpose(docs_h, (1, 0, 2)), own).astype(BF16)
    by_dir_c = jnp.transpose(docs_c, (1, 0, 2))
    start_c = cells_to_pieces(trade(pick(by_dir_c, own), pick(by_dir_c, 1 - own)))

    def at_step(step):
        near = jnp.array([step, step, max(step - 1, 0), min(step + 1, steps - 1)], jnp.int32)
        turned = jnp.array([step] + [steps - 1 - x for x in (step, max(step - 1, 0), min(step + 1, steps - 1))], jnp.int32)
        return jnp.where(own == 0, near, turned)

    n_batch = lax.axis_size("batch")
    spot = lax.axis_index("batch")
    low, high = spot % 2, (spot // 2) % 2
    near_swap = [(i, i ^ 1) for i in range(n_batch)]
    far_swap = [(i, i ^ 2) for i in range(n_batch)]

    def swapped(array, pairs):
        return lax.ppermute(array, "batch", pairs)

    turn = jnp.where(own == 0, jnp.array([0, 1], jnp.int32), jnp.array([steps - 1, -1], jnp.int32))
    feats_v, feat_all = pl.pallas_call(
        order_kernel,
        out_shape=(vmem(feats.shape, BF16), hbm(feats.shape, BF16)),
        in_specs=[SMEM, ANY],
        out_specs=[VMEM, ANY],
        scratch_shapes=[pltpu.SemaphoreType.DMA((steps,)), pltpu.SemaphoreType.DMA],
        compiler_params=params(1),
        name="order",
    )(turn, feats)
    feat_in = (swapped(feat_all, near_swap), swapped(feat_all, far_swap))
    keep_v, bias_v, win_bv = place(keep, bias_p, win_b)
    rec_bv, proj_av, proj_bv, start_hv, start_cv = place(rec_b, proj_a, proj_b, start_h, start_c)

    gates_shape, cell_shape = (PIECES, streams, 4 * width), (PIECES, streams, width)
    inflow = pl.pallas_call(
        inflow_kernel,
        out_shape=vmem(gates_shape, F32),
        in_specs=[SMEM] + [VMEM] * 4,
        out_specs=VMEM,
        compiler_params=params(8),
        name="inflow",
    )(turn, pinned(feats_v), pinned(bias_v), pinned(win_av), pinned(win_bv))

    def forward_call(first, step, part, peer, cell, inflow):
        return pl.pallas_call(
            functools.partial(forward_kernel, first),
            out_shape=(
                vmem((streams, depth), BF16),
                vmem(cell_shape, F32),
                vmem(gates_shape, BF16),
                vmem(cell_shape, BF16),
                vmem((streams, depth), BF16),
                vmem((streams, depth), BF16),
                vmem((streams, depth), F32),
            ),
            in_specs=[SMEM] + [VMEM] * 10,
            out_specs=[VMEM] * 7,
            compiler_params=params(8),
            name="forward_step",
        )(
            at_step(step), pinned(part), pinned(peer), pinned(start_hv), pinned(keep_v), pinned(cell), pinned(inflow),
            pinned(rec_av), pinned(rec_bv), pinned(proj_av), pinned(proj_bv),
        )

    def between_call(step, fresh, stacks, passing=()):
        shapes = (
            hbm((PIECES, steps, streams, 4 * width), BF16),
            hbm((steps,) + cell_shape, F32),
            hbm((PIECES, steps, streams, width), BF16),
            hbm((steps, streams, depth), BF16),
            hbm((steps, streams, depth), BF16),
            hbm((steps, streams, depth), F32),
        )
        aliases = {11 + i: 1 + i for i in range(len(stacks))}
        aliases.update({11 + len(stacks) + i: 7 + i for i in range(len(passing))})
        inflow, *out = pl.pallas_call(
            functools.partial(between_kernel, not stacks, step == steps - 1, len(passing)),
            out_shape=(vmem(gates_shape, F32),) + shapes + tuple(hbm(x.shape, x.dtype) for x in passing),
            in_specs=[SMEM] + [VMEM] * 10 + [ANY] * (len(stacks) + len(passing)),
            out_specs=[VMEM] + [ANY] * (6 + len(passing)),
            scratch_shapes=[pltpu.SemaphoreType.DMA((2 * PIECES + 4,))],
            input_output_aliases=aliases,
            compiler_params=params(8),
            cost_estimate=cost(2 * streams * depth * 8 * cells, 8 * depth * cells * 2),
            name="between",
        )(
            at_step(step), pinned(feats_v), pinned(bias_v), pinned(win_av), pinned(win_bv),
            *(pinned(x) for x in fresh), *(in_hbm(x) for x in (*stacks, *passing)),
        )
        return inflow, tuple(out[:6]), tuple(out[6:])

    none = jnp.zeros((streams, depth), BF16)
    part, peer, cell, stacks = none, none, start_cv, ()
    for step in range(steps):
        part, cell, *fresh = forward_call(step == 0, step, part, peer, cell, inflow)
        peer = lax.ppermute(part, "gate", across)
        due = step == (2 * steps) // 3
        inflow, stacks, passed = between_call(step, (cell, *fresh), stacks, feat_in if due else ())
        feat_in = passed if due else feat_in
    gates_all, cells_all, mixed_all, prev_all, hidden_all, slope_all = stacks
    prev_in = (swapped(prev_all, near_swap), swapped(prev_all, far_swap))

    saved_shapes = (
        vmem(gates_shape, BF16),
        vmem(cell_shape, F32),
        vmem(cell_shape, F32),
        vmem((streams, depth), F32),
        vmem((streams, depth), BF16),
    )
    *saved, hidden_all, slope_all = pl.pallas_call(
        finish_kernel,
        out_shape=saved_shapes + (hbm((steps, streams, depth), BF16), hbm((steps, streams, depth), F32)),
        in_specs=[SMEM, VMEM, VMEM] + [ANY] * 5,
        out_specs=[VMEM] * 5 + [ANY] * 2,
        scratch_shapes=[
            pltpu.VMEM((streams, depth), BF16),
            pltpu.SemaphoreType.DMA((PIECES + 4,)),
            pltpu.SemaphoreType.DMA,
        ],
        input_output_aliases={6: 5, 7: 6},
        compiler_params=params(8),
        name="finish",
    )(
        at_step(steps - 1), pinned(part), pinned(peer), in_hbm(gates_all), in_hbm(cells_all), in_hbm(ups),
        in_hbm(hidden_all), in_hbm(slope_all),
    )

    rec_atv, rec_btv, proj_atv, proj_btv = pl.pallas_call(
        turned_kernel,
        out_shape=(vmem((4, cells, depth), BF16),) * 2 + (vmem((depth, cells), BF16),) * 2,
        in_specs=[ANY] * 4,
        out_specs=[VMEM] * 4,
        scratch_shapes=[
            pltpu.VMEM((3, depth, cells), BF16),
            pltpu.SemaphoreType.DMA((3,)),
            pltpu.VMEM((2, cells, depth), BF16),
            pltpu.SemaphoreType.DMA((2,)),
        ],
        compiler_params=params(8),
        name="turned",
    )(*(in_hbm(x) for x in (rec_a, rec_b, proj_a, proj_b)))

    def backward_call(step, part, peer, grad, saved):
        return pl.pallas_call(
            backward_kernel,
            out_shape=(
                vmem((streams, depth), BF16),
                vmem(cell_shape, F32),
                vmem((streams, depth), BF16),
                vmem(gates_shape, BF16),
            ),
            in_specs=[SMEM] + [VMEM] * 14,
            out_specs=[VMEM] * 4,
            compiler_params=params(8),
            name="backward_step",
        )(
            at_step(step), pinned(part), pinned(peer), pinned(keep_v), pinned(grad),
            pinned(rec_atv), pinned(rec_btv), pinned(proj_atv), pinned(proj_btv),
            *(pinned(x) for x in saved), pinned(start_cv),
        )

    def aside_call(step, slot, slots, dz, raw, stacks, sends, passing):
        piece_shape = (streams, 4 * width)
        shapes = (
            hbm((PIECES, steps) + piece_shape, BF16),
            hbm((steps, streams, depth), BF16),
            hbm((steps,) + piece_shape, BF16),
            hbm((steps,) + piece_shape, BF16),
            hbm((slots,) + piece_shape, BF16),
            hbm((slots,) + piece_shape, BF16),
        )
        kept = len(stacks)
        aliases = {7 + i: 5 + i for i in range(kept)}
        aliases.update({7 + kept + i: 9 + i for i in range(len(sends))})
        aliases.update({7 + kept + len(sends) + i: 11 + i for i in range(len(passing))})
        out = pl.pallas_call(
            functools.partial(aside_kernel, not stacks, step == 0, not sends, len(passing)),
            out_shape=saved_shapes + shapes + tuple(hbm(x.shape, x.dtype) for x in passing),
            in_specs=[SMEM] + [VMEM] * 2 + [ANY] * (4 + kept + len(sends) + len(passing)),
            out_specs=[VMEM] * 5 + [ANY] * (6 + len(passing)),
            scratch_shapes=[
                pltpu.SemaphoreType.DMA((PIECES + 5,)),
                pltpu.SemaphoreType.DMA((PIECES + 4,)),
            ],
            input_output_aliases=aliases,
            compiler_params=params(8),
            cost_estimate=cost(0, 8 * MIB),
            name="aside",
        )(
            jnp.concatenate([at_step(step), jnp.stack([jnp.int32(slot), low, high])]), pinned(dz), pinned(raw),
            in_hbm(gates_all), in_hbm(cells_all), in_hbm(ups), in_hbm(slope_all),
            *(in_hbm(x) for x in (*stacks, *sends, *passing)),
        )
        return out[:5], tuple(out[5:9]), tuple(out[9:11]), tuple(out[11:])

    carry = (none, none, jnp.zeros(cell_shape, F32), saved, ())
    pending, arrived, ready, top = [(steps - 1 - steps // 3, prev_in)], [], None, steps
    for index, share in enumerate(SHARES):
        slots = top if index == len(SHARES) - 1 else round(share * steps)
        sends = ()
        for step in range(top - 1, top - slots - 1, -1):
            part, peer, grad, saved, stacks = carry
            part, grad, raw, dz = backward_call(step, part, peer, grad, saved)
            peer = lax.ppermute(part, "gate", across)
            if ready is not None:
                due, sides = ready
                sides = after(part, *sides) if step else sides
                pending.append((due, (swapped(sides[0], near_swap), swapped(sides[1], far_swap))))
                ready = None
            passing = pending.pop(0)[1] if pending and pending[0][0] >= step else ()
            saved, stacks, sends, passed = aside_call(
                step, step - (top - slots), slots, dz, raw, stacks, sends, passing
            )
            arrived += [passed] if passed else []
            carry = (part, peer, grad, saved, stacks)
        top -= slots
        ready = (max(top - 1 - (3 * slots + 3) // 4, 0 if slots > 2 else -1), sends)
    pending.append((-1, (swapped(sends[0], near_swap), swapped(sends[1], far_swap))))
    arrived += [arrays for _, arrays in pending]
    dz_all, raw_all, near_all, far_all = carry[-1]
    prev_in, exchanged = arrived[0], arrived[1:]
    rows = steps * streams

    def by_direction(mine, theirs):
        return jnp.stack([jnp.where(own == 0, mine, theirs), jnp.where(own == 0, theirs, mine)])

    def line_sum(chunks, axis, stride, count, first=None):
        here = (spot // stride) % count

        def chunk(index):
            return lax.dynamic_index_in_dim(chunks, jnp.clip(index, 0, count - 1), axis, keepdims=False)

        def at(device):
            return (device // stride) % count

        if count == 2:
            pairs = [(i, i + stride if at(i) == 0 else i - stride) for i in range(n_batch)]
            return (chunk(here).astype(F32) + swapped(chunk(1 - here), pairs).astype(F32)).astype(BF16)
        ends = [(i, i + stride) for i in range(n_batch) if at(i) == 0]
        ends += [(i, i - stride) for i in range(n_batch) if at(i) == count - 1]
        up = down = swapped(chunk(jnp.where(here == 0, count - 1, 0)) if first is None else first, ends)
        for slot in range(2, count):
            rise = (chunk(here + count - slot).astype(F32) + up.astype(F32)).astype(BF16)
            fall = (chunk(here - count + slot).astype(F32) + down.astype(F32)).astype(BF16)
            up = swapped(rise, [(i, i + stride) for i in range(n_batch) if at(i) < min(slot, count - 1)])
            down = swapped(fall, [(i, i - stride) for i in range(n_batch) if at(i) > max(count - 1 - slot, 0)])
        return (chunk(here).astype(F32) + up.astype(F32) + down.astype(F32)).astype(BF16)

    line = n_batch // 2
    share_rows = depth // n_batch

    def product(left, right):
        count = left.shape[0] * left.shape[1]
        return lax.dot_general(
            left.reshape(count, -1), right.reshape(count, -1), (((0,), (0,)), ((), ())), preferred_element_type=F32
        )

    def both(feat, prev):
        return jnp.concatenate([feat, prev], axis=2)

    left = both(feat_all, prev_all)
    early, taken = [], []
    for kept, feat, prev, parts in zip((near_all, far_all), feat_in, prev_in, zip(*exchanged)):
        steps_late = sum(x.shape[0] for x in parts[-LATE:])
        theirs = both(feat, prev)
        total = product(left, kept) + product(theirs[steps_late:], jnp.concatenate(parts[:-LATE][::-1], axis=0))
        early.append(total)
        taken.append((theirs[:steps_late], parts[-LATE:][::-1]))
    near_late, near_parts = taken[0]
    near_parts = jnp.concatenate(after(early[0], *near_parts), axis=0)
    here = spot // 2
    begin = jnp.where(here == 0, line - 1, 0)

    def line_chunk(array, axis):
        shape = array.shape[:axis] + (2, line, 2 * share_rows) + array.shape[axis + 1 :]
        return lax.dynamic_index_in_dim(array.reshape(shape), begin, axis + 1, keepdims=False)

    first = line_chunk(early[0], 0).reshape(4 * share_rows, -1) + product(line_chunk(near_late, 2), near_parts)
    first = first.astype(BF16)
    (near_parts,) = after(first, near_parts)

    def rows_first(total):
        return total.astype(BF16).reshape(2, line, 2, share_rows, 4 * width)

    near = rows_first(early[0] + product(near_late, near_parts))
    far_parts = jnp.concatenate(after(near, *taken[1][1]), axis=0)
    far = rows_first(early[1] + product(taken[1][0], far_parts))
    token = far
    near = line_sum(near, 1, 2, line, first.reshape(2, 2, share_rows, 4 * width))
    far = line_sum(far, 2, 1, 2).reshape(2, line // 2, 2, share_rows, 4 * width)
    far = line_sum(far, 1, 4, line // 2)

    def halves_of(summed, index, pairs):
        mine = lax.dynamic_index_in_dim(summed, index, 1, keepdims=False)
        return mine, swapped(lax.dynamic_index_in_dim(summed, 1 - index, 1, keepdims=False), pairs)

    near_pair = halves_of(near, low, near_swap)
    far_pair = [lax.ppermute(x, "gate", swap) for x in halves_of(far, high, far_swap)]
    grad_shape = (2, share_rows, 4, cells)
    grad_w_in, grad_w_rec = pl.pallas_call(
        assemble_kernel,
        out_shape=(jax.ShapeDtypeStruct(grad_shape, F32),) * 2,
        in_specs=[SMEM] + [VMEM] * 4,
        out_specs=[VMEM] * 2,
        compiler_params=params(32),
        name="assemble",
    )(jnp.stack([own, low, high]), *near_pair, *far_pair)

    dz_all, mixed_all, hidden_all, cell = after(token, dz_all, mixed_all, hidden_all, cell)

    grad_proj = jnp.einsum("ptnc,tnk->kpc", mixed_all, raw_all, preferred_element_type=F32).astype(BF16)
    grad_proj = line_sum(grad_proj.reshape(line, 2, share_rows, QUARTERS * cells), 1, 1, 2)
    grad_proj = line_sum(grad_proj, 0, 2, line)

    grad_bias = jnp.sum(dz_all, axis=(1, 2), dtype=F32)
    stride = 1
    while stride < n_batch:
        grad_bias = grad_bias + swapped(grad_bias, [(i, i ^ stride) for i in range(n_batch)])
        stride *= 2

    def home(mine, theirs):
        return by_direction(*trade(mine, theirs)).astype(F32)

    shaped = jnp.transpose(grad_bias.reshape(QUARTERS, HALVES, 4, width), (0, 2, 1, 3)).reshape(QUARTERS, 4, cells)
    own_cells = cells // n_batch
    shaped = lax.dynamic_slice_in_dim(shaped, spot * own_cells, own_cells, 2)
    grad_bias = home(shaped[0], shaped[1])
    grad_proj = grad_proj.reshape(share_rows, QUARTERS, cells)
    grad_proj = home(jnp.transpose(grad_proj[:, 0]), jnp.transpose(grad_proj[:, 1]))

    both_hidden = trade(hidden_all, hidden_all)

    hidden_dirs = by_direction(*both_hidden)
    outputs = (inputs.astype(F32) + jnp.transpose(hidden_dirs, (0, 2, 1, 3)).astype(F32)).astype(BF16)
    last_h = jnp.stack([hidden_dirs[0, steps - 1], hidden_dirs[1, 0]], axis=1).astype(F32)
    final_h = jnp.zeros_like(state_h).at[stream_doc].set(last_h)
    last_c = jnp.transpose(cell.reshape(QUARTERS, HALVES, streams, width), (0, 2, 1, 3)).reshape(
        QUARTERS, streams, cells
    )
    last_dirs = by_direction(*trade(last_c[0], last_c[1]))
    final_c = jnp.zeros_like(state_c).at[stream_doc].set(jnp.transpose(last_dirs, (1, 0, 2)))

    dx_all = pl.pallas_call(
        input_grad_kernel,
        out_shape=jax.ShapeDtypeStruct((steps, streams, depth), F32),
        grid_spec=pltpu.PrefetchScalarGridSpec(
            num_scalar_prefetch=1,
            grid=(PIECES, 4),
            in_specs=[
                pl.BlockSpec((1, steps, streams, width), lambda p, g, turn: (p, 0, 0, g)),
                pl.BlockSpec(
                    (1, depth, width), lambda p, g, turn: (jnp.where(p < 2, g, 3), 0, jnp.where(p < 2, p, 1))
                ),
                pl.BlockSpec(
                    (1, depth, width), lambda p, g, turn: (jnp.where(p < 2, 0, g), 0, jnp.where(p < 2, 0, p - 2))
                ),
            ],
            out_specs=pl.BlockSpec((steps, streams, depth), lambda p, g, turn: (0, 0, 0)),
            scratch_shapes=[pltpu.VMEM((rows, depth), F32)],
        ),
        compiler_params=params(24),
        cost_estimate=cost(2 * rows * depth * 8 * cells, 8 * depth * cells * 4),
        name="input_grad",
    )(turn, dz_all, in_hbm(win_a), in_hbm(win_b))

    half_cols = depth // 2
    upper = rank // 2
    keep_cols = lax.dynamic_slice_in_dim(dx_all, upper * half_cols, half_cols, 2)
    send_cols = lax.dynamic_slice_in_dim(dx_all, (1 - upper) * half_cols, half_cols, 2).astype(BF16)
    dx_half = keep_cols + lax.ppermute(send_cols, "gate", across).astype(F32)
    up_half = lax.dynamic_slice_in_dim(ups, upper * half_cols, half_cols, 2).astype(F32)
    dx_half = (dx_half + up_half).astype(BF16)
    quarter_cols = half_cols // 2
    mine = lax.dynamic_slice_in_dim(dx_half, own * quarter_cols, quarter_cols, 2)
    theirs = lax.dynamic_slice_in_dim(dx_half, (1 - own) * quarter_cols, quarter_cols, 2)
    dx_dirs = by_direction(*trade(mine, theirs))
    input_grad = jnp.transpose(dx_dirs, (0, 2, 1, 3))
    return (outputs, input_grad, grad_w_in, grad_w_rec, grad_bias, grad_proj, final_h, final_c)


def solution(mesh):
    placed = (
        P(None, "batch", None, None),
        P(None, None, None, "gate"),
        P(None, None, None, "gate"),
        P(None, None, "gate"),
        P(None, "gate", None),
        P("batch", None, None),
        P("batch", None, "gate"),
        P("batch", None),
        P("batch"),
        P(None, "batch", None, None),
    )
    return jax.shard_map(
        body,
        mesh=mesh,
        in_specs=placed,
        out_specs=(
            P(None, "batch", None, None),
            P(None, "batch", None, "gate"),
            P(None, "batch", None, "gate"),
            P(None, "batch", None, "gate"),
            P(None, None, ("gate", "batch")),
            P(None, "gate", "batch"),
            P("batch", None, None),
            P("batch", None, "gate"),
        ),
        check_vma=False,
    )
```

```python
import functools

import jax
import jax.numpy as jnp
from jax import lax
from jax.experimental import pallas as pl
from jax.experimental.pallas import tpu as pltpu
from jax.sharding import PartitionSpec as P

CLIP = 3.0
F32, BF16 = jnp.float32, jnp.bfloat16
QUARTERS, HALVES = 2, 2
PIECES = QUARTERS * HALVES
MIB = 2**20
LATE = 2
SHARES = (0.35, 0.3, 0.15, 0.1, 0.1)

VMEM = pl.BlockSpec(memory_space=pltpu.VMEM)
SMEM = pl.BlockSpec(memory_space=pltpu.SMEM)
ANY = pl.BlockSpec(memory_space=pl.ANY)


def pinned(array):
    return pltpu.with_memory_space_constraint(array, pltpu.VMEM)


def in_hbm(array):
    return pltpu.with_memory_space_constraint(array, pltpu.HBM)


def dot(left, right):
    return jnp.dot(left, right, preferred_element_type=F32)


def place_kernel(count, *refs):
    sources, targets, sems = refs[:count], refs[count : 2 * count], refs[2 * count]
    copies = [pltpu.make_async_copy(a, b, sems.at[i]) for i, (a, b) in enumerate(zip(sources, targets))]
    for copy in copies:
        copy.start()
    for copy in copies:
        copy.wait()


def place(*arrays):
    count = len(arrays)
    return pl.pallas_call(
        functools.partial(place_kernel, count),
        out_shape=tuple(pltpu.VMEM(x.shape, x.dtype) for x in arrays),
        in_specs=[ANY] * count,
        out_specs=[VMEM] * count,
        scratch_shapes=[pltpu.SemaphoreType.DMA((count,))],
        compiler_params=params(1),
        name="place",
    )(*(in_hbm(x) for x in arrays))


def layout_kernel(keep, which_ref, w_ref, first_ref, second_ref, buf, sems, out_sems):
    out_ref, all_ref = (first_ref, second_ref) if keep else (second_ref, first_ref)
    depth, part = w_ref.shape[1], buf.shape[1]

    def fetch(i):
        return pltpu.make_async_copy(w_ref.at[which_ref[0], pl.ds(i * part, part)], buf.at[i % 3], sems.at[i % 3])

    def store(i):
        rows = pl.ds(i * part, part)
        return pltpu.make_async_copy(out_ref.at[:, rows], all_ref.at[:, rows], out_sems.at[i])

    count = depth // part
    for i in range(min(2, count)):
        fetch(i).start()
    for i in range(count):
        if i + 2 < count:
            fetch(i + 2).start()
        fetch(i).wait()
        out_ref[:, i * part : (i + 1) * part, :] = jnp.swapaxes(buf[i % 3], 0, 1)
        store(i).start()
    for i in range(count):
        store(i).wait()


def turned_kernel(wa_ref, wb_ref, pa_ref, pb_ref, wat_ref, wbt_ref, pat_ref, pbt_ref, buf, sems, proj_buf, proj_sems):
    jobs = [(w_ref, out_ref, gate) for w_ref, out_ref in ((wa_ref, wat_ref), (wb_ref, wbt_ref)) for gate in range(4)]

    def fetch(i):
        return pltpu.make_async_copy(jobs[i][0].at[jobs[i][2]], buf.at[i % 3], sems.at[i % 3])

    proj_fetches = [pltpu.make_async_copy(x, proj_buf.at[i], proj_sems.at[i]) for i, x in enumerate((pa_ref, pb_ref))]
    fetch(0).start()
    fetch(1).start()
    for copy in proj_fetches:
        copy.start()
    for i, (_, out_ref, gate) in enumerate(jobs):
        if i + 2 < len(jobs):
            fetch(i + 2).start()
        fetch(i).wait()
        for half in range(HALVES):
            width = buf.shape[2] // HALVES
            cols = slice(half * width, (half + 1) * width)
            out_ref[gate, cols, :] = buf[i % 3, :, cols].T
    for i, out_ref in enumerate((pat_ref, pbt_ref)):
        proj_fetches[i].wait()
        out_ref[...] = proj_buf[i].T


def pass_kernel(*refs):
    pass


def after(tokens, *arrays):
    count = len(tokens)
    return pl.pallas_call(
        pass_kernel,
        out_shape=tuple(jax.ShapeDtypeStruct(x.shape, x.dtype) for x in arrays),
        in_specs=[ANY] * (count + len(arrays)),
        out_specs=[ANY] * len(arrays),
        input_output_aliases={count + i: i for i in range(len(arrays))},
        compiler_params=params(1),
        name="after",
    )(*tokens, *arrays)


def assemble_kernel(place_ref, near_a, near_b, far_a, far_b, in_ref, rec_ref):
    own, low, high = place_ref[0], place_ref[1], place_ref[2]
    width = in_ref.shape[3] // HALVES
    for direction, mine_ref, theirs_ref, index in ((own, near_a, near_b, low), (1 - own, far_a, far_b, high)):
        for which, out_ref in ((0, in_ref), (1, rec_ref)):
            mine, theirs = mine_ref[which].astype(F32), theirs_ref[which].astype(F32)
            for half in range(HALVES):
                whole = jnp.where(index == half, mine, theirs)
                gates = jnp.stack([whole[:, gate * width : (gate + 1) * width] for gate in range(4)])
                out_ref[direction, :, :, half * width : (half + 1) * width] = jnp.swapaxes(gates, 0, 1)


def order_kernel(step_ref, feat_ref, out_ref, all_ref, sems, all_sem):
    steps = feat_ref.shape[0]
    copies = [
        pltpu.make_async_copy(feat_ref.at[step_ref[0] + step_ref[1] * i], out_ref.at[i], sems.at[i]) for i in range(steps)
    ]
    for copy in copies:
        copy.start()
    for copy in copies:
        copy.wait()
    whole = pltpu.make_async_copy(out_ref, all_ref, all_sem)
    whole.start()
    whole.wait()


def pieces(refs, axis):
    for piece in range(PIECES):
        quarter, half = divmod(piece, HALVES)
        width = refs[0].shape[axis] // HALVES
        yield piece, quarter, width, slice(half * width, (half + 1) * width)


def forward_kernel(
    first, step_ref, p_ref, q_ref, start_ref, keep_ref, cell_ref, inflow_ref, wa_ref, wb_ref, pa_ref, pb_ref,
    part_ref, next_ref, gates_ref, mixed_ref, prev_ref, hidden_ref, slope_ref,
):
    keep = keep_ref[step_ref[1]][:, :1]
    if first:
        hidden = start_ref[...]
    else:
        hidden = clipped(p_ref, q_ref, hidden_ref, slope_ref)
    hidden = hidden * keep.astype(BF16)
    prev_ref[...] = hidden
    part = jnp.zeros(part_ref.shape, F32)
    for piece, quarter, width, cols in pieces((wa_ref, wb_ref), 2):
        w_ref, proj_ref = ((wa_ref, pa_ref), (wb_ref, pb_ref))[quarter]
        acts = []
        for gate in range(4):
            place = slice(gate * width, (gate + 1) * width)
            pre = dot(hidden, w_ref[gate, :, cols]) + inflow_ref[piece, :, place]
            act = jnp.tanh(pre if gate == 2 else 0.5 * pre)
            gates_ref[piece, :, place] = act.astype(BF16)
            acts.append(act if gate == 2 else 0.5 + 0.5 * act)
        ingate, forget, candidate, outgate = acts
        cell = CLIP * jnp.tanh((forget * (keep * cell_ref[piece]) + ingate * candidate) * (1.0 / CLIP))
        next_ref[piece] = cell
        mixed = (outgate * jnp.tanh(cell)).astype(BF16)
        mixed_ref[piece] = mixed
        part = part + dot(mixed, proj_ref[cols, :])
    part_ref[...] = part.astype(BF16)


def clipped(p_ref, q_ref, hidden_ref, slope_ref):
    squash = jnp.tanh((p_ref[...].astype(F32) + q_ref[...].astype(F32)) * (1.0 / CLIP))
    hidden = (CLIP * squash).astype(BF16)
    hidden_ref[...] = hidden
    slope_ref[...] = 1.0 - squash * squash
    return hidden


def between_kernel(
    first, last, passed, step_ref, feat_ref, bias_ref, wa_ref, wb_ref, cell_ref, gates_ref, mixed_ref, prev_ref, hidden_ref,
    slope_ref, *refs,
):
    refs = refs[(0 if first else 6) + passed :]
    out_ref, gates_all, cells_all, mixed_all, prev_all, hidden_all, slope_all = refs[:7]
    sems = refs[-1]
    step, time_before = step_ref[0], step_ref[2]
    copies = [pltpu.make_async_copy(gates_ref.at[i], gates_all.at[i, step], sems.at[i]) for i in range(PIECES)]
    copies += [
        pltpu.make_async_copy(mixed_ref.at[i], mixed_all.at[i, step], sems.at[PIECES + i]) for i in range(PIECES)
    ]
    copies.append(pltpu.make_async_copy(cell_ref, cells_all.at[step], sems.at[2 * PIECES]))
    copies.append(pltpu.make_async_copy(prev_ref, prev_all.at[step], sems.at[2 * PIECES + 1]))
    if not first:
        copies.append(pltpu.make_async_copy(hidden_ref, hidden_all.at[time_before], sems.at[2 * PIECES + 2]))
        copies.append(pltpu.make_async_copy(slope_ref, slope_all.at[step - 1], sems.at[2 * PIECES + 3]))
    for copy in copies:
        copy.start()
    if not last:
        inflow_into(feat_ref[step + 1], bias_ref, wa_ref, wb_ref, out_ref)
    for copy in copies:
        copy.wait()


def inflow_into(feat, bias_ref, wa_ref, wb_ref, out_ref):
    for piece, quarter, width, cols in pieces((wa_ref, wb_ref), 2):
        w_ref = (wa_ref, wb_ref)[quarter]
        for gate in range(4):
            place = slice(gate * width, (gate + 1) * width)
            out_ref[piece, :, place] = dot(feat, w_ref[gate, :, cols]) + bias_ref[piece, :, place]


def inflow_kernel(step_ref, feat_ref, bias_ref, wa_ref, wb_ref, out_ref):
    inflow_into(feat_ref[0], bias_ref, wa_ref, wb_ref, out_ref)


def backward_kernel(
    step_ref, p_ref, q_ref, keep_ref, grad_ref, wa_ref, wb_ref, pa_ref, pb_ref,
    gates_ref, cell_ref, prev_ref, slope_ref, up_ref, start_ref,
    part_ref, next_ref, raw_ref, dz_ref,
):
    step = step_ref[0]
    keep = keep_ref[step_ref[1]][:, :1]
    raw = (up_ref[...].astype(F32) + (p_ref[...].astype(F32) + q_ref[...].astype(F32))) * slope_ref[...]
    raw = raw.astype(BF16)
    raw_ref[...] = raw
    part = jnp.zeros(part_ref.shape, F32)
    for piece, quarter, width, cols in pieces((wa_ref, wb_ref), 1):
        w_ref, proj_ref = ((wa_ref, pa_ref), (wb_ref, pb_ref))[quarter]
        mixed = dot(raw, proj_ref[:, cols])
        acts = [gates_ref[piece, :, gate * width : (gate + 1) * width].astype(F32) for gate in range(4)]
        ingate, forget, outgate = (0.5 + 0.5 * acts[gate] for gate in (0, 1, 3))
        slopes = [1.0 - act * act for act in acts]
        cell = cell_ref[piece]
        prev = keep * jnp.where(step == 0, start_ref[piece], prev_ref[piece])
        squash = jnp.tanh(cell)
        total = grad_ref[piece] + mixed * outgate * (1.0 - squash * squash)
        inner = total * (1.0 - (cell * (1.0 / CLIP)) * (cell * (1.0 / CLIP)))
        next_ref[piece] = keep * inner * forget
        quart = 0.25 * inner
        pre_grads = (
            quart * acts[2] * slopes[0],
            quart * prev * slopes[1],
            inner * ingate * slopes[2],
            0.25 * mixed * squash * slopes[3],
        )
        for gate in range(4):
            low = pre_grads[gate].astype(BF16)
            dz_ref[piece, :, gate * width : (gate + 1) * width] = low
            part = part + dot(low, w_ref[gate, cols, :])
    part_ref[...] = (part * keep).astype(BF16)


def finish_kernel(
    step_ref, p_ref, q_ref, gates_all, cells_all, ups_all, hidden_in, slope_in,
    gates_ref, cell_ref, prev_ref, slope_ref, up_ref, hidden_all, slope_all,
    hidden_buf, sems, hidden_sem,
):
    copies = fetches(
        step_ref[0], step_ref[1], (gates_all, cells_all, ups_all), (gates_ref, cell_ref, prev_ref, up_ref), sems
    )
    for copy in copies:
        copy.start()
    clipped(p_ref, q_ref, hidden_buf, slope_ref)
    hidden_copy = pltpu.make_async_copy(hidden_buf, hidden_all.at[step_ref[1]], hidden_sem)
    hidden_copy.start()
    for copy in copies:
        copy.wait()
    hidden_copy.wait()


def fetches(step, time, sources, targets, sems):
    gates_all, cells_all, ups_all = sources
    gates_ref, cell_ref, prev_ref, up_ref = targets
    before = jnp.maximum(step - 1, 0)
    return [
        pltpu.make_async_copy(gates_all.at[i, step], gates_ref.at[i], sems.at[i]) for i in range(PIECES)
    ] + [
        pltpu.make_async_copy(cells_all.at[step], cell_ref, sems.at[PIECES]),
        pltpu.make_async_copy(cells_all.at[before], prev_ref, sems.at[PIECES + 1]),
        pltpu.make_async_copy(ups_all.at[time], up_ref, sems.at[PIECES + 2]),
    ]


def aside_kernel(
    first, last, opens, passed, step_ref, dz_ref, raw_ref, gates_all, cells_all, ups_all, slope_all, *refs
):
    refs = refs[(0 if first else 4) + (0 if opens else 2) + passed :]
    gates_ref, cell_ref, prev_ref, slope_ref, up_ref = refs[:5]
    dz_all, raw_all, near_all, far_all, near_out, far_out = refs[5:11]
    sems, fetch_sems = refs[-2:]
    step, time_before = step_ref[0], step_ref[2]
    slot, low, high = step_ref[4], step_ref[5], step_ref[6]
    before = jnp.maximum(step - 1, 0)
    copies = []
    if not last:
        copies += fetches(
            before, time_before, (gates_all, cells_all, ups_all), (gates_ref, cell_ref, prev_ref, up_ref), fetch_sems
        )
        copies.append(pltpu.make_async_copy(slope_all.at[before], slope_ref, fetch_sems.at[PIECES + 3]))
    copies += [pltpu.make_async_copy(dz_ref.at[i], dz_all.at[i, step], sems.at[i]) for i in range(PIECES)]
    copies.append(pltpu.make_async_copy(raw_ref, raw_all.at[step], sems.at[PIECES]))
    copies.append(pltpu.make_async_copy(dz_ref.at[low], near_all.at[step], sems.at[PIECES + 1]))
    copies.append(pltpu.make_async_copy(dz_ref.at[HALVES + high], far_all.at[step], sems.at[PIECES + 2]))
    copies.append(pltpu.make_async_copy(dz_ref.at[1 - low], near_out.at[slot], sems.at[PIECES + 3]))
    copies.append(pltpu.make_async_copy(dz_ref.at[HALVES + 1 - high], far_out.at[slot], sems.at[PIECES + 4]))
    for copy in copies:
        copy.start()
    for copy in copies:
        copy.wait()


def input_grad_kernel(step_ref, dz_ref, wa_ref, wb_ref, out_ref, acc_ref):
    piece, gate = pl.program_id(0), pl.program_id(1)
    steps, streams, width = dz_ref.shape[1:]

    @pl.when((piece == 0) & (gate == 0))
    def _():
        acc_ref[...] = jnp.zeros(acc_ref.shape, F32)

    weights = jnp.where(piece < HALVES, wa_ref[0], wb_ref[0])
    acc_ref[...] += lax.dot_general(
        dz_ref[0].reshape(steps * streams, width), weights, (((1,), (1,)), ((), ())), preferred_element_type=F32
    )

    @pl.when((piece == PIECES - 1) & (gate == 3))
    def _():
        for step in range(steps):
            time = step_ref[0] + step_ref[1] * step
            out_ref[time] = acc_ref[step * streams : (step + 1) * streams, :]


def params(mib):
    return pltpu.CompilerParams(vmem_limit_bytes=mib * MIB)


def cost(flops, size):
    return pl.CostEstimate(flops=flops, bytes_accessed=size, transcendentals=0)


def body(inputs, w_in, w_rec, bias, proj, state_h, state_c, resets, stream_doc, cotangent):
    streams, steps, depth = inputs.shape[1:]
    cells = w_in.shape[3]
    width = cells // HALVES
    rank = lax.axis_index("gate")
    own = rank % 2
    gates_size = lax.axis_size("gate")
    swap = [(i, i ^ 1) for i in range(gates_size)]
    across = [(i, i ^ 2) for i in range(gates_size)]

    def pick(stacked, index):
        return lax.dynamic_index_in_dim(stacked, index, 0, keepdims=False)

    def trade(mine, theirs):
        return (mine, lax.ppermute(theirs, "gate", swap))

    def vmem(shape, dtype):
        return pltpu.VMEM(shape, dtype)

    def hbm(shape, dtype):
        return pltpu.HBM(shape, dtype)

    def by_gate(weights, index, keep=True):
        shape = (4,) + weights.shape[1:2] + weights.shape[3:]
        kept = (vmem(shape, BF16),) if keep else ()
        part = weights.shape[1] // 8
        return pl.pallas_call(
            functools.partial(layout_kernel, keep),
            out_shape=kept + (hbm(shape, BF16),),
            in_specs=[SMEM, ANY],
            out_specs=[VMEM] * len(kept) + [ANY],
            scratch_shapes=([] if kept else [pltpu.VMEM(shape, BF16)])
            + [
                pltpu.VMEM((3, part) + weights.shape[2:], BF16),
                pltpu.SemaphoreType.DMA((3,)),
                pltpu.SemaphoreType.DMA((8,)),
            ],
            compiler_params=params(8),
            name="layout",
        )(jnp.full((1,), index, jnp.int32), in_hbm(weights))

    win_b, rec_b = (lax.ppermute(by_gate(w, 1 - own, False)[0], "gate", swap) for w in (w_in, w_rec))
    (win_av, win_a), (rec_av, rec_a) = by_gate(w_in, own), by_gate(w_rec, own)
    proj_a, proj_b = trade(pick(proj, own), pick(proj, 1 - own))
    bias_a, bias_b = trade(pick(bias, own), pick(bias, 1 - own))

    def pieces_of(pair):
        split = [x.reshape(4, HALVES, width) for x in pair]
        return jnp.transpose(jnp.stack(split), (0, 2, 1, 3)).reshape(PIECES, 1, 4 * width)

    bias_p = pieces_of((bias_a, bias_b)).astype(F32)

    def cells_to_pieces(pair):
        both = jnp.stack(pair).reshape(QUARTERS, streams, HALVES, width)
        return jnp.transpose(both, (0, 2, 1, 3)).reshape(PIECES, streams, width)

    def by_time(stacked):
        return jnp.transpose(pick(stacked, own), (1, 0, 2))

    feats = by_time(inputs)
    ups = by_time(cotangent)
    flags = resets.astype(F32)
    later = jnp.concatenate([flags[:, 1:], jnp.zeros_like(flags[:, :1])], axis=1)
    keep = 1.0 - jnp.where(own == 0, flags, later)
    keep = jnp.broadcast_to(jnp.transpose(keep)[:, :, None], (steps, streams, 128))

    docs_h = state_h[stream_doc]
    docs_c = state_c[stream_doc]
    start_h = pick(jnp.transpose(docs_h, (1, 0, 2)), own).astype(BF16)
    by_dir_c = jnp.transpose(docs_c, (1, 0, 2))
    start_c = cells_to_pieces(trade(pick(by_dir_c, own), pick(by_dir_c, 1 - own)))

    def at_step(step):
        near = jnp.array([step, step, max(step - 1, 0), min(step + 1, steps - 1)], jnp.int32)
        turned = jnp.array([step] + [steps - 1 - x for x in (step, max(step - 1, 0), min(step + 1, steps - 1))], jnp.int32)
        return jnp.where(own == 0, near, turned)

    n_batch = lax.axis_size("batch")
    spot = lax.axis_index("batch")
    low, high = spot % 2, (spot // 2) % 2
    near_swap = [(i, i ^ 1) for i in range(n_batch)]
    far_swap = [(i, i ^ 2) for i in range(n_batch)]

    def swapped(array, pairs):
        return lax.ppermute(array, "batch", pairs)

    turn = jnp.where(own == 0, jnp.array([0, 1], jnp.int32), jnp.array([steps - 1, -1], jnp.int32))
    feats_v, feat_all = pl.pallas_call(
        order_kernel,
        out_shape=(vmem(feats.shape, BF16), hbm(feats.shape, BF16)),
        in_specs=[SMEM, ANY],
        out_specs=[VMEM, ANY],
        scratch_shapes=[pltpu.SemaphoreType.DMA((steps,)), pltpu.SemaphoreType.DMA],
        compiler_params=params(1),
        name="order",
    )(turn, feats)
    feat_in = (swapped(feat_all, near_swap), swapped(feat_all, far_swap))
    keep_v, bias_v, win_bv = place(keep, bias_p, win_b)
    rec_bv, proj_av, proj_bv, start_hv, start_cv = place(rec_b, proj_a, proj_b, start_h, start_c)

    gates_shape, cell_shape = (PIECES, streams, 4 * width), (PIECES, streams, width)
    inflow = pl.pallas_call(
        inflow_kernel,
        out_shape=vmem(gates_shape, F32),
        in_specs=[SMEM] + [VMEM] * 4,
        out_specs=VMEM,
        compiler_params=params(8),
        name="inflow",
    )(turn, pinned(feats_v), pinned(bias_v), pinned(win_av), pinned(win_bv))

    def forward_call(first, step, part, peer, cell, inflow):
        return pl.pallas_call(
            functools.partial(forward_kernel, first),
            out_shape=(
                vmem((streams, depth), BF16),
                vmem(cell_shape, F32),
                vmem(gates_shape, BF16),
                vmem(cell_shape, BF16),
                vmem((streams, depth), BF16),
                vmem((streams, depth), BF16),
                vmem((streams, depth), F32),
            ),
            in_specs=[SMEM] + [VMEM] * 10,
            out_specs=[VMEM] * 7,
            compiler_params=params(8),
            name="forward_step",
        )(
            at_step(step), pinned(part), pinned(peer), pinned(start_hv), pinned(keep_v), pinned(cell), pinned(inflow),
            pinned(rec_av), pinned(rec_bv), pinned(proj_av), pinned(proj_bv),
        )

    def between_call(step, fresh, stacks, passing=()):
        shapes = (
            hbm((PIECES, steps, streams, 4 * width), BF16),
            hbm((steps,) + cell_shape, F32),
            hbm((PIECES, steps, streams, width), BF16),
            hbm((steps, streams, depth), BF16),
            hbm((steps, streams, depth), BF16),
            hbm((steps, streams, depth), F32),
        )
        aliases = {11 + i: 1 + i for i in range(len(stacks))}
        aliases.update({11 + len(stacks) + i: 7 + i for i in range(len(passing))})
        inflow, *out = pl.pallas_call(
            functools.partial(between_kernel, not stacks, step == steps - 1, len(passing)),
            out_shape=(vmem(gates_shape, F32),) + shapes + tuple(hbm(x.shape, x.dtype) for x in passing),
            in_specs=[SMEM] + [VMEM] * 10 + [ANY] * (len(stacks) + len(passing)),
            out_specs=[VMEM] + [ANY] * (6 + len(passing)),
            scratch_shapes=[pltpu.SemaphoreType.DMA((2 * PIECES + 4,))],
            input_output_aliases=aliases,
            compiler_params=params(8),
            cost_estimate=cost(2 * streams * depth * 8 * cells, 8 * depth * cells * 2),
            name="between",
        )(
            at_step(step), pinned(feats_v), pinned(bias_v), pinned(win_av), pinned(win_bv),
            *(pinned(x) for x in fresh), *(in_hbm(x) for x in (*stacks, *passing)),
        )
        return inflow, tuple(out[:6]), tuple(out[6:])

    none = jnp.zeros((streams, depth), BF16)
    part, peer, cell, stacks = none, none, start_cv, ()
    for step in range(steps):
        part, cell, *fresh = forward_call(step == 0, step, part, peer, cell, inflow)
        peer = lax.ppermute(part, "gate", across)
        due = step == (2 * steps) // 3
        inflow, stacks, passed = between_call(step, (cell, *fresh), stacks, feat_in if due else ())
        feat_in = passed if due else feat_in
    gates_all, cells_all, mixed_all, prev_all, hidden_all, slope_all = stacks
    prev_in = (swapped(prev_all, near_swap), swapped(prev_all, far_swap))

    saved_shapes = (
        vmem(gates_shape, BF16),
        vmem(cell_shape, F32),
        vmem(cell_shape, F32),
        vmem((streams, depth), F32),
        vmem((streams, depth), BF16),
    )
    *saved, hidden_all, slope_all = pl.pallas_call(
        finish_kernel,
        out_shape=saved_shapes + (hbm((steps, streams, depth), BF16), hbm((steps, streams, depth), F32)),
        in_specs=[SMEM, VMEM, VMEM] + [ANY] * 5,
        out_specs=[VMEM] * 5 + [ANY] * 2,
        scratch_shapes=[
            pltpu.VMEM((streams, depth), BF16),
            pltpu.SemaphoreType.DMA((PIECES + 4,)),
            pltpu.SemaphoreType.DMA,
        ],
        input_output_aliases={6: 5, 7: 6},
        compiler_params=params(8),
        name="finish",
    )(
        at_step(steps - 1), pinned(part), pinned(peer), in_hbm(gates_all), in_hbm(cells_all), in_hbm(ups),
        in_hbm(hidden_all), in_hbm(slope_all),
    )

    rec_atv, rec_btv, proj_atv, proj_btv = pl.pallas_call(
        turned_kernel,
        out_shape=(vmem((4, cells, depth), BF16),) * 2 + (vmem((depth, cells), BF16),) * 2,
        in_specs=[ANY] * 4,
        out_specs=[VMEM] * 4,
        scratch_shapes=[
            pltpu.VMEM((3, depth, cells), BF16),
            pltpu.SemaphoreType.DMA((3,)),
            pltpu.VMEM((2, cells, depth), BF16),
            pltpu.SemaphoreType.DMA((2,)),
        ],
        compiler_params=params(8),
        name="turned",
    )(*(in_hbm(x) for x in (rec_a, rec_b, proj_a, proj_b)))

    def backward_call(step, part, peer, grad, saved):
        return pl.pallas_call(
            backward_kernel,
            out_shape=(
                vmem((streams, depth), BF16),
                vmem(cell_shape, F32),
                vmem((streams, depth), BF16),
                vmem(gates_shape, BF16),
            ),
            in_specs=[SMEM] + [VMEM] * 14,
            out_specs=[VMEM] * 4,
            compiler_params=params(8),
            name="backward_step",
        )(
            at_step(step), pinned(part), pinned(peer), pinned(keep_v), pinned(grad),
            pinned(rec_atv), pinned(rec_btv), pinned(proj_atv), pinned(proj_btv),
            *(pinned(x) for x in saved), pinned(start_cv),
        )

    def aside_call(step, slot, slots, dz, raw, stacks, sends, passing):
        piece_shape = (streams, 4 * width)
        shapes = (
            hbm((PIECES, steps) + piece_shape, BF16),
            hbm((steps, streams, depth), BF16),
            hbm((steps,) + piece_shape, BF16),
            hbm((steps,) + piece_shape, BF16),
            hbm((slots,) + piece_shape, BF16),
            hbm((slots,) + piece_shape, BF16),
        )
        kept = len(stacks)
        aliases = {7 + i: 5 + i for i in range(kept)}
        aliases.update({7 + kept + i: 9 + i for i in range(len(sends))})
        aliases.update({7 + kept + len(sends) + i: 11 + i for i in range(len(passing))})
        out = pl.pallas_call(
            functools.partial(aside_kernel, not stacks, step == 0, not sends, len(passing)),
            out_shape=saved_shapes + shapes + tuple(hbm(x.shape, x.dtype) for x in passing),
            in_specs=[SMEM] + [VMEM] * 2 + [ANY] * (4 + kept + len(sends) + len(passing)),
            out_specs=[VMEM] * 5 + [ANY] * (6 + len(passing)),
            scratch_shapes=[
                pltpu.SemaphoreType.DMA((PIECES + 5,)),
                pltpu.SemaphoreType.DMA((PIECES + 4,)),
            ],
            input_output_aliases=aliases,
            compiler_params=params(8),
            cost_estimate=cost(0, 8 * MIB),
            name="aside",
        )(
            jnp.concatenate([at_step(step), jnp.stack([jnp.int32(slot), low, high])]), pinned(dz), pinned(raw),
            in_hbm(gates_all), in_hbm(cells_all), in_hbm(ups), in_hbm(slope_all),
            *(in_hbm(x) for x in (*stacks, *sends, *passing)),
        )
        return out[:5], tuple(out[5:9]), tuple(out[9:11]), tuple(out[11:])

    carry = (none, none, jnp.zeros(cell_shape, F32), saved, ())
    pending, arrived, ready, top = [(steps - 1 - steps // 3, prev_in)], [], None, steps
    for index, share in enumerate(SHARES):
        slots = top if index == len(SHARES) - 1 else round(share * steps)
        sends = ()
        for step in range(top - 1, top - slots - 1, -1):
            part, peer, grad, saved, stacks = carry
            part, grad, raw, dz = backward_call(step, part, peer, grad, saved)
            peer = lax.ppermute(part, "gate", across)
            if ready is not None:
                due, sides = ready
                sides = after((part,), *sides) if step else sides
                pending.append((due, (swapped(sides[0], near_swap), swapped(sides[1], far_swap))))
                ready = None
            passing = pending.pop(0)[1] if pending and pending[0][0] >= step else ()
            saved, stacks, sends, passed = aside_call(
                step, step - (top - slots), slots, dz, raw, stacks, sends, passing
            )
            arrived += [passed] if passed else []
            carry = (part, peer, grad, saved, stacks)
        top -= slots
        ready = (max(top - 1 - (3 * slots + 3) // 4, 0 if slots > 2 else -1), sends)
    pending.append((-1, (swapped(sends[0], near_swap), swapped(sends[1], far_swap))))
    arrived += [arrays for _, arrays in pending]
    dz_all, raw_all, near_all, far_all = carry[-1]
    prev_in, exchanged = arrived[0], arrived[1:]
    rows = steps * streams

    def by_direction(mine, theirs):
        return jnp.stack([jnp.where(own == 0, mine, theirs), jnp.where(own == 0, theirs, mine)])

    def line_sum(chunks, axis, stride, count, first=None, gates={}):
        here = (spot // stride) % count

        def chunk(index):
            return lax.dynamic_index_in_dim(chunks, jnp.clip(index, 0, count - 1), axis, keepdims=False)

        def at(device):
            return (device // stride) % count

        if count == 2:
            pairs = [(i, i + stride if at(i) == 0 else i - stride) for i in range(n_batch)]
            return (chunk(here).astype(F32) + swapped(chunk(1 - here), pairs).astype(F32)).astype(BF16)
        ends = [(i, i + stride) for i in range(n_batch) if at(i) == 0]
        ends += [(i, i - stride) for i in range(n_batch) if at(i) == count - 1]
        up = down = swapped(chunk(jnp.where(here == 0, count - 1, 0)) if first is None else first, ends)
        for slot in range(2, count):
            if slot in gates:
                up, down = gates[slot](up, down)
            rise = (chunk(here + count - slot).astype(F32) + up.astype(F32)).astype(BF16)
            fall = (chunk(here - count + slot).astype(F32) + down.astype(F32)).astype(BF16)
            up = swapped(rise, [(i, i + stride) for i in range(n_batch) if at(i) < min(slot, count - 1)])
            down = swapped(fall, [(i, i - stride) for i in range(n_batch) if at(i) > max(count - 1 - slot, 0)])
        if count in gates:
            up, down = gates[count](up, down)
        return (chunk(here).astype(F32) + up.astype(F32) + down.astype(F32)).astype(BF16)

    line = n_batch // 2
    share_rows = depth // n_batch

    def product(left, right):
        count = left.shape[0] * left.shape[1]
        return lax.dot_general(
            left.reshape(count, -1), right.reshape(count, -1), (((0,), (0,)), ((), ())), preferred_element_type=F32
        )

    def both(feat, prev):
        return jnp.concatenate([feat, prev], axis=2)

    left = both(feat_all, prev_all)
    def input_grad_of(dz):
        return pl.pallas_call(
            input_grad_kernel,
            out_shape=jax.ShapeDtypeStruct((steps, streams, depth), F32),
            grid_spec=pltpu.PrefetchScalarGridSpec(
                num_scalar_prefetch=1,
                grid=(PIECES, 4),
                in_specs=[
                    pl.BlockSpec((1, steps, streams, width), lambda p, g, turn: (p, 0, 0, g)),
                    pl.BlockSpec(
                        (1, depth, width), lambda p, g, turn: (jnp.where(p < 2, g, 3), 0, jnp.where(p < 2, p, 1))
                    ),
                    pl.BlockSpec(
                        (1, depth, width), lambda p, g, turn: (jnp.where(p < 2, 0, g), 0, jnp.where(p < 2, 0, p - 2))
                    ),
                ],
                out_specs=pl.BlockSpec((steps, streams, depth), lambda p, g, turn: (0, 0, 0)),
                scratch_shapes=[pltpu.VMEM((rows, depth), F32)],
            ),
            compiler_params=params(16),
            cost_estimate=cost(2 * rows * depth * 8 * cells, 8 * depth * cells * 4),
            name="input_grad",
        )(turn, dz, in_hbm(win_a), in_hbm(win_b))

    grad_proj = jnp.einsum("ptnc,tnk->pkc", mixed_all, raw_all, preferred_element_type=F32).astype(BF16)
    grad_proj = grad_proj.reshape(PIECES, line, 2, share_rows, width)
    proj_mine = lax.dynamic_index_in_dim(grad_proj, low, 2, keepdims=False)
    proj_send = lax.dynamic_index_in_dim(grad_proj, 1 - low, 2, keepdims=False)
    proj_taken = swapped(proj_send, near_swap)

    def early_sum(kept, theirs, parts):
        taken = jnp.concatenate(parts[:-LATE][::-1], axis=0)
        return product(left, kept) + product(theirs[steps - taken.shape[0] :], taken)

    def rows_first(total):
        return total.astype(BF16).reshape(2, line, 2, share_rows, 4 * width)

    begin = jnp.where(spot // 2 == 0, line - 1, 0)

    def line_chunk(array, axis):
        shape = array.shape[:axis] + (2, line, 2 * share_rows) + array.shape[axis + 1 :]
        return lax.dynamic_index_in_dim(array.reshape(shape), begin, axis + 1, keepdims=False)

    near_parts, far_parts = zip(*exchanged)
    near_left, far_left = (both(feat, prev) for feat, prev in zip(feat_in, prev_in))
    late_steps = sum(x.shape[0] for x in near_parts[-LATE:])
    near_early = early_sum(near_all, near_left, near_parts)
    near_late = jnp.concatenate(after((near_early, proj_send), *near_parts[-LATE:][::-1]), axis=0)
    first = line_chunk(near_early, 0).reshape(4 * share_rows, -1)
    first = (first + product(line_chunk(near_left[:late_steps], 2), near_late)).astype(BF16)
    (near_late,) = after((first,), near_late)
    near = rows_first(near_early + product(near_left[:late_steps], near_late))

    far_all, *far_parts = after((first,), far_all, *far_parts)
    far_early = early_sum(far_all, far_left, far_parts)
    far_late = jnp.concatenate(after((near, proj_taken), *far_parts[-LATE:][::-1]), axis=0)
    far = rows_first(far_early + product(far_left[:late_steps], far_late))

    def with_partner(grad):
        mine = lax.dynamic_index_in_dim(grad, low, 1, keepdims=False)
        taken = swapped(lax.dynamic_index_in_dim(grad, 1 - low, 1, keepdims=False), near_swap)
        return taken, (mine.astype(F32) + taken.astype(F32)).astype(BF16)

    (in_taken, far_in), (rec_taken, far_rec) = (with_partner(far[i]) for i in range(2))

    tokens = {}

    def second(up, down):
        up, down = after((far,), up, down)
        tokens["dz"], tokens["proj"] = after((up,), dz_all, proj_taken)
        return up, down

    def third(up, down):
        tokens["dx"] = input_grad_of(tokens["dz"])
        tokens["hidden"], tokens["cell"], dz = after((up, tokens["dx"]), hidden_all, cell, tokens["dz"])
        tokens["bias"] = jnp.sum(dz, axis=(1, 2), dtype=F32)
        return after((in_taken, tokens["dx"]), up, down)

    def final(up, down):
        return after((rec_taken, tokens["bias"]), up, down)

    gates = {2: second, 3: third, line: final} if line > 3 else {}
    near = line_sum(near, 1, 2, line, first.reshape(2, 2, share_rows, 4 * width), gates)
    far = jnp.stack([far_in, far_rec]).reshape(2, line // 2, 2, share_rows, 4 * width)
    far = line_sum(far, 1, 4, line // 2)
    dx_all, hidden_all, cell, grad_bias = (tokens[x] for x in ("dx", "hidden", "cell", "bias"))

    def halves_of(summed, index, pairs):
        mine = lax.dynamic_index_in_dim(summed, index, 1, keepdims=False)
        return mine, swapped(lax.dynamic_index_in_dim(summed, 1 - index, 1, keepdims=False), pairs)

    near_pair = halves_of(near, low, near_swap)
    far_pair = [lax.ppermute(x, "gate", swap) for x in halves_of(far, high, far_swap)]
    grad_shape = (2, share_rows, 4, cells)
    grad_w_in, grad_w_rec = pl.pallas_call(
        assemble_kernel,
        out_shape=(jax.ShapeDtypeStruct(grad_shape, F32),) * 2,
        in_specs=[SMEM] + [VMEM] * 4,
        out_specs=[VMEM] * 2,
        compiler_params=params(14),
        name="assemble",
    )(jnp.stack([own, low, high]), *near_pair, *far_pair)

    grad_proj = line_sum((proj_mine.astype(F32) + tokens["proj"].astype(F32)).astype(BF16), 1, 2, line)
    stride = 1
    while stride < n_batch:
        grad_bias = grad_bias + swapped(grad_bias, [(i, i ^ stride) for i in range(n_batch)])
        stride *= 2

    def home(mine, theirs):
        return by_direction(*trade(mine, theirs)).astype(F32)

    shaped = jnp.transpose(grad_bias.reshape(QUARTERS, HALVES, 4, width), (0, 2, 1, 3)).reshape(QUARTERS, 4, cells)
    own_cells = cells // n_batch
    shaped = lax.dynamic_slice_in_dim(shaped, spot * own_cells, own_cells, 2)
    grad_bias = home(shaped[0], shaped[1])
    grad_proj = jnp.transpose(grad_proj.reshape(QUARTERS, HALVES, share_rows, width), (0, 1, 3, 2))
    grad_proj = grad_proj.reshape(QUARTERS, cells, share_rows)
    grad_proj = home(grad_proj[0], grad_proj[1])

    both_hidden = trade(hidden_all, hidden_all)

    hidden_dirs = by_direction(*both_hidden)
    outputs = (inputs.astype(F32) + jnp.transpose(hidden_dirs, (0, 2, 1, 3)).astype(F32)).astype(BF16)
    last_h = jnp.stack([hidden_dirs[0, steps - 1], hidden_dirs[1, 0]], axis=1).astype(F32)
    final_h = jnp.zeros_like(state_h).at[stream_doc].set(last_h)
    last_c = jnp.transpose(cell.reshape(QUARTERS, HALVES, streams, width), (0, 2, 1, 3)).reshape(
        QUARTERS, streams, cells
    )
    last_dirs = by_direction(*trade(last_c[0], last_c[1]))
    final_c = jnp.zeros_like(state_c).at[stream_doc].set(jnp.transpose(last_dirs, (1, 0, 2)))

    half_cols = depth // 2
    upper = rank // 2
    keep_cols = lax.dynamic_slice_in_dim(dx_all, upper * half_cols, half_cols, 2)
    send_cols = lax.dynamic_slice_in_dim(dx_all, (1 - upper) * half_cols, half_cols, 2).astype(BF16)
    dx_half = keep_cols + lax.ppermute(send_cols, "gate", across).astype(F32)
    up_half = lax.dynamic_slice_in_dim(ups, upper * half_cols, half_cols, 2).astype(F32)
    dx_half = (dx_half + up_half).astype(BF16)
    quarter_cols = half_cols // 2
    mine = lax.dynamic_slice_in_dim(dx_half, own * quarter_cols, quarter_cols, 2)
    theirs = lax.dynamic_slice_in_dim(dx_half, (1 - own) * quarter_cols, quarter_cols, 2)
    dx_dirs = by_direction(*trade(mine, theirs))
    input_grad = jnp.transpose(dx_dirs, (0, 2, 1, 3))
    return (outputs, input_grad, grad_w_in, grad_w_rec, grad_bias, grad_proj, final_h, final_c)


def solution(mesh):
    placed = (
        P(None, "batch", None, None),
        P(None, None, None, "gate"),
        P(None, None, None, "gate"),
        P(None, None, "gate"),
        P(None, "gate", None),
        P("batch", None, None),
        P("batch", None, "gate"),
        P("batch", None),
        P("batch"),
        P(None, "batch", None, None),
    )
    return jax.shard_map(
        body,
        mesh=mesh,
        in_specs=placed,
        out_specs=(
            P(None, "batch", None, None),
            P(None, "batch", None, "gate"),
            P(None, "batch", None, "gate"),
            P(None, "batch", None, "gate"),
            P(None, None, ("gate", "batch")),
            P(None, "gate", "batch"),
            P("batch", None, None),
            P("batch", None, "gate"),
        ),
        check_vma=False,
    )
```

```python
import functools

import jax
import jax.numpy as jnp
from jax import lax
from jax.experimental import pallas as pl
from jax.experimental.pallas import tpu as pltpu
from jax.sharding import PartitionSpec as P

CLIP = 3.0
F32, BF16 = jnp.float32, jnp.bfloat16
QUARTERS, HALVES = 2, 2
PIECES = QUARTERS * HALVES
MIB = 2**20
LATE = 2
SHARES = (0.35, 0.3, 0.15, 0.1, 0.1)

VMEM = pl.BlockSpec(memory_space=pltpu.VMEM)
SMEM = pl.BlockSpec(memory_space=pltpu.SMEM)
ANY = pl.BlockSpec(memory_space=pl.ANY)


def pinned(array):
    return pltpu.with_memory_space_constraint(array, pltpu.VMEM)


def in_hbm(array):
    return pltpu.with_memory_space_constraint(array, pltpu.HBM)


def dot(left, right):
    return jnp.dot(left, right, preferred_element_type=F32)


def place_kernel(count, *refs):
    sources, targets, sems = refs[:count], refs[count : 2 * count], refs[2 * count]
    copies = [pltpu.make_async_copy(a, b, sems.at[i]) for i, (a, b) in enumerate(zip(sources, targets))]
    for copy in copies:
        copy.start()
    for copy in copies:
        copy.wait()


def place(*arrays):
    count = len(arrays)
    return pl.pallas_call(
        functools.partial(place_kernel, count),
        out_shape=tuple(pltpu.VMEM(x.shape, x.dtype) for x in arrays),
        in_specs=[ANY] * count,
        out_specs=[VMEM] * count,
        scratch_shapes=[pltpu.SemaphoreType.DMA((count,))],
        compiler_params=params(1),
        name="place",
    )(*(in_hbm(x) for x in arrays))


def layout_kernel(keep, which_ref, w_ref, first_ref, second_ref, buf, sems, out_sems):
    out_ref, all_ref = (first_ref, second_ref) if keep else (second_ref, first_ref)
    depth, part = w_ref.shape[1], buf.shape[1]

    def fetch(i):
        return pltpu.make_async_copy(w_ref.at[which_ref[0], pl.ds(i * part, part)], buf.at[i % 3], sems.at[i % 3])

    def store(i):
        rows = pl.ds(i * part, part)
        return pltpu.make_async_copy(out_ref.at[:, rows], all_ref.at[:, rows], out_sems.at[i])

    count = depth // part
    for i in range(min(2, count)):
        fetch(i).start()
    for i in range(count):
        if i + 2 < count:
            fetch(i + 2).start()
        fetch(i).wait()
        out_ref[:, i * part : (i + 1) * part, :] = jnp.swapaxes(buf[i % 3], 0, 1)
        store(i).start()
    for i in range(count):
        store(i).wait()


def turned_kernel(wa_ref, wb_ref, pa_ref, pb_ref, wat_ref, wbt_ref, pat_ref, pbt_ref, buf, sems, proj_buf, proj_sems):
    jobs = [(w_ref, out_ref, gate) for w_ref, out_ref in ((wa_ref, wat_ref), (wb_ref, wbt_ref)) for gate in range(4)]

    def fetch(i):
        return pltpu.make_async_copy(jobs[i][0].at[jobs[i][2]], buf.at[i % 3], sems.at[i % 3])

    proj_fetches = [pltpu.make_async_copy(x, proj_buf.at[i], proj_sems.at[i]) for i, x in enumerate((pa_ref, pb_ref))]
    fetch(0).start()
    fetch(1).start()
    for copy in proj_fetches:
        copy.start()
    for i, (_, out_ref, gate) in enumerate(jobs):
        if i + 2 < len(jobs):
            fetch(i + 2).start()
        fetch(i).wait()
        for half in range(HALVES):
            width = buf.shape[2] // HALVES
            cols = slice(half * width, (half + 1) * width)
            out_ref[gate, cols, :] = buf[i % 3, :, cols].T
    for i, out_ref in enumerate((pat_ref, pbt_ref)):
        proj_fetches[i].wait()
        out_ref[...] = proj_buf[i].T


def pass_kernel(*refs):
    pass


def after(tokens, *arrays):
    count = len(tokens)
    return pl.pallas_call(
        pass_kernel,
        out_shape=tuple(jax.ShapeDtypeStruct(x.shape, x.dtype) for x in arrays),
        in_specs=[ANY] * (count + len(arrays)),
        out_specs=[ANY] * len(arrays),
        input_output_aliases={count + i: i for i in range(len(arrays))},
        compiler_params=params(1),
        name="after",
    )(*tokens, *arrays)


def gather_kernel(lows, *refs):
    (feat_ref, prev_ref, feat_too, prev_too, kept_ref), refs = refs[:5], refs[5:]
    groups, (left_ref, right_ref, sems) = refs[:-3], refs[-3:]
    steps, _, depth = feat_ref.shape
    jobs = [
        (feat_ref, left_ref.at[:steps, :, :depth]),
        (prev_ref, left_ref.at[:steps, :, depth:]),
        (feat_too, left_ref.at[steps:, :, :depth]),
        (prev_too, left_ref.at[steps:, :, depth:]),
        (kept_ref, right_ref.at[:steps]),
    ]
    jobs += [(x, right_ref.at[steps + low : steps + low + x.shape[0]]) for x, low in zip(groups, lows)]
    copies = [pltpu.make_async_copy(a, b, sems.at[i]) for i, (a, b) in enumerate(jobs)]
    for copy in copies:
        copy.start()
    for copy in copies:
        copy.wait()


def late_kernel(lows, begin_ref, left_ref, right_in, *refs):
    groups, (right_ref, first_ref, sems) = refs[:-3], refs[-3:]
    steps = left_ref.shape[0] // 2
    copies = [
        pltpu.make_async_copy(x, right_ref.at[steps + low : steps + low + x.shape[0]], sems.at[i])
        for i, (x, low) in enumerate(zip(groups, lows))
    ]
    for copy in copies:
        copy.start()
    for copy in copies:
        copy.wait()
    if first_ref.shape[1] % 128:
        return
    share, depth = first_ref.shape[1], left_ref.shape[2] // 2
    rows = left_ref.shape[0] * left_ref.shape[1]
    left = [
        left_ref[:, :, pl.ds(pl.multiple_of(i * depth + begin_ref[0] * share, 128), share)].reshape(rows, share)
        for i in range(2)
    ]
    left = jnp.concatenate([x.T for x in left], axis=0)
    width = right_ref.shape[2] // 4

    def columns(i, _):
        cols = pl.ds(pl.multiple_of(i * width, width), width)
        total = dot(left, right_ref[:, :, cols].reshape(rows, width)).astype(BF16)
        first_ref[0, :, cols] = total[:share]
        first_ref[1, :, cols] = total[share:]
        return 0

    lax.fori_loop(0, 4, columns, 0)


def product_kernel(left_ref, right_ref, out_ref):
    rows, depth = left_ref.shape[0] * left_ref.shape[1], left_ref.shape[2] // 2
    width = right_ref.shape[2] // 4
    for which in range(2):
        left = left_ref[:, :, which * depth : (which + 1) * depth].reshape(rows, depth).T

        def columns(i, _):
            cols = pl.ds(pl.multiple_of(i * width, width), width)
            out_ref[which, :, cols] = dot(left, right_ref[:, :, cols].reshape(rows, width)).astype(BF16)
            return 0

        lax.fori_loop(0, 4, columns, 0)


def assemble_kernel(place_ref, near_a, near_b, far_a, far_b, in_ref, rec_ref):
    own, low, high = place_ref[0], place_ref[1], place_ref[2]
    width = in_ref.shape[3] // HALVES
    for direction, mine_ref, theirs_ref, index in ((own, near_a, near_b, low), (1 - own, far_a, far_b, high)):
        for which, out_ref in ((0, in_ref), (1, rec_ref)):
            mine, theirs = mine_ref[which].astype(F32), theirs_ref[which].astype(F32)
            for half in range(HALVES):
                whole = jnp.where(index == half, mine, theirs)
                gates = jnp.stack([whole[:, gate * width : (gate + 1) * width] for gate in range(4)])
                out_ref[direction, :, :, half * width : (half + 1) * width] = jnp.swapaxes(gates, 0, 1)


def order_kernel(step_ref, feat_ref, out_ref, all_ref, sems, all_sem):
    steps = feat_ref.shape[0]
    copies = [
        pltpu.make_async_copy(feat_ref.at[step_ref[0] + step_ref[1] * i], out_ref.at[i], sems.at[i]) for i in range(steps)
    ]
    for copy in copies:
        copy.start()
    for copy in copies:
        copy.wait()
    whole = pltpu.make_async_copy(out_ref, all_ref, all_sem)
    whole.start()
    whole.wait()


def pieces(refs, axis):
    for piece in range(PIECES):
        quarter, half = divmod(piece, HALVES)
        width = refs[0].shape[axis] // HALVES
        yield piece, quarter, width, slice(half * width, (half + 1) * width)


def forward_kernel(
    first, step_ref, p_ref, q_ref, start_ref, keep_ref, cell_ref, inflow_ref, wa_ref, wb_ref, pa_ref, pb_ref,
    part_ref, next_ref, gates_ref, mixed_ref, prev_ref, hidden_ref, slope_ref,
):
    keep = keep_ref[step_ref[1]][:, :1]
    if first:
        hidden = start_ref[...]
    else:
        hidden = clipped(p_ref, q_ref, hidden_ref, slope_ref)
    hidden = hidden * keep.astype(BF16)
    prev_ref[...] = hidden
    part = jnp.zeros(part_ref.shape, F32)
    for piece, quarter, width, cols in pieces((wa_ref, wb_ref), 2):
        w_ref, proj_ref = ((wa_ref, pa_ref), (wb_ref, pb_ref))[quarter]
        acts = []
        for gate in range(4):
            place = slice(gate * width, (gate + 1) * width)
            pre = dot(hidden, w_ref[gate, :, cols]) + inflow_ref[piece, :, place]
            act = jnp.tanh(pre if gate == 2 else 0.5 * pre)
            gates_ref[piece, :, place] = act.astype(BF16)
            acts.append(act if gate == 2 else 0.5 + 0.5 * act)
        ingate, forget, candidate, outgate = acts
        cell = CLIP * jnp.tanh((forget * (keep * cell_ref[piece]) + ingate * candidate) * (1.0 / CLIP))
        next_ref[piece] = cell
        mixed = (outgate * jnp.tanh(cell)).astype(BF16)
        mixed_ref[piece] = mixed
        part = part + dot(mixed, proj_ref[cols, :])
    part_ref[...] = part.astype(BF16)


def clipped(p_ref, q_ref, hidden_ref, slope_ref):
    squash = jnp.tanh((p_ref[...].astype(F32) + q_ref[...].astype(F32)) * (1.0 / CLIP))
    hidden = (CLIP * squash).astype(BF16)
    hidden_ref[...] = hidden
    slope_ref[...] = 1.0 - squash * squash
    return hidden


def between_kernel(
    first, last, passed, step_ref, feat_ref, bias_ref, wa_ref, wb_ref, cell_ref, gates_ref, mixed_ref, prev_ref, hidden_ref,
    slope_ref, *refs,
):
    refs = refs[(0 if first else 6) + passed :]
    out_ref, gates_all, cells_all, mixed_all, prev_all, hidden_all, slope_all = refs[:7]
    sems = refs[-1]
    step, time_before = step_ref[0], step_ref[2]
    copies = [pltpu.make_async_copy(gates_ref.at[i], gates_all.at[i, step], sems.at[i]) for i in range(PIECES)]
    copies += [
        pltpu.make_async_copy(mixed_ref.at[i], mixed_all.at[i, step], sems.at[PIECES + i]) for i in range(PIECES)
    ]
    copies.append(pltpu.make_async_copy(cell_ref, cells_all.at[step], sems.at[2 * PIECES]))
    copies.append(pltpu.make_async_copy(prev_ref, prev_all.at[step], sems.at[2 * PIECES + 1]))
    if not first:
        copies.append(pltpu.make_async_copy(hidden_ref, hidden_all.at[time_before], sems.at[2 * PIECES + 2]))
        copies.append(pltpu.make_async_copy(slope_ref, slope_all.at[step - 1], sems.at[2 * PIECES + 3]))
    for copy in copies:
        copy.start()
    if not last:
        inflow_into(feat_ref[step + 1], bias_ref, wa_ref, wb_ref, out_ref)
    for copy in copies:
        copy.wait()


def inflow_into(feat, bias_ref, wa_ref, wb_ref, out_ref):
    for piece, quarter, width, cols in pieces((wa_ref, wb_ref), 2):
        w_ref = (wa_ref, wb_ref)[quarter]
        for gate in range(4):
            place = slice(gate * width, (gate + 1) * width)
            out_ref[piece, :, place] = dot(feat, w_ref[gate, :, cols]) + bias_ref[piece, :, place]


def inflow_kernel(step_ref, feat_ref, bias_ref, wa_ref, wb_ref, out_ref):
    inflow_into(feat_ref[0], bias_ref, wa_ref, wb_ref, out_ref)


def backward_kernel(
    step_ref, p_ref, q_ref, keep_ref, grad_ref, bias_ref, wa_ref, wb_ref, pa_ref, pb_ref,
    gates_ref, cell_ref, prev_ref, slope_ref, up_ref, start_ref,
    part_ref, next_ref, sum_ref, raw_ref, dz_ref,
):
    step = step_ref[0]
    keep = keep_ref[step_ref[1]][:, :1]
    raw = (up_ref[...].astype(F32) + (p_ref[...].astype(F32) + q_ref[...].astype(F32))) * slope_ref[...]
    raw = raw.astype(BF16)
    raw_ref[...] = raw
    part = jnp.zeros(part_ref.shape, F32)
    for piece, quarter, width, cols in pieces((wa_ref, wb_ref), 1):
        w_ref, proj_ref = ((wa_ref, pa_ref), (wb_ref, pb_ref))[quarter]
        mixed = dot(raw, proj_ref[:, cols])
        acts = [gates_ref[piece, :, gate * width : (gate + 1) * width].astype(F32) for gate in range(4)]
        ingate, forget, outgate = (0.5 + 0.5 * acts[gate] for gate in (0, 1, 3))
        slopes = [1.0 - act * act for act in acts]
        cell = cell_ref[piece]
        prev = keep * jnp.where(step == 0, start_ref[piece], prev_ref[piece])
        squash = jnp.tanh(cell)
        total = grad_ref[piece] + mixed * outgate * (1.0 - squash * squash)
        inner = total * (1.0 - (cell * (1.0 / CLIP)) * (cell * (1.0 / CLIP)))
        next_ref[piece] = keep * inner * forget
        quart = 0.25 * inner
        pre_grads = (
            quart * acts[2] * slopes[0],
            quart * prev * slopes[1],
            inner * ingate * slopes[2],
            0.25 * mixed * squash * slopes[3],
        )
        for gate in range(4):
            low = pre_grads[gate].astype(BF16)
            place = slice(gate * width, (gate + 1) * width)
            dz_ref[piece, :, place] = low
            rows = pre_grads[gate].reshape(-1, 8, width)
            sum_ref[piece, :, place] = bias_ref[piece, :, place] + jnp.sum(rows, axis=0)
            part = part + dot(low, w_ref[gate, cols, :])
    part_ref[...] = (part * keep).astype(BF16)


def finish_kernel(
    step_ref, p_ref, q_ref, gates_all, cells_all, ups_all, hidden_in, slope_in,
    gates_ref, cell_ref, prev_ref, slope_ref, up_ref, hidden_all, slope_all,
    hidden_buf, sems, hidden_sem,
):
    copies = fetches(
        step_ref[0], step_ref[1], (gates_all, cells_all, ups_all), (gates_ref, cell_ref, prev_ref, up_ref), sems
    )
    for copy in copies:
        copy.start()
    clipped(p_ref, q_ref, hidden_buf, slope_ref)
    hidden_copy = pltpu.make_async_copy(hidden_buf, hidden_all.at[step_ref[1]], hidden_sem)
    hidden_copy.start()
    for copy in copies:
        copy.wait()
    hidden_copy.wait()


def fetches(step, time, sources, targets, sems):
    gates_all, cells_all, ups_all = sources
    gates_ref, cell_ref, prev_ref, up_ref = targets
    before = jnp.maximum(step - 1, 0)
    return [
        pltpu.make_async_copy(gates_all.at[i, step], gates_ref.at[i], sems.at[i]) for i in range(PIECES)
    ] + [
        pltpu.make_async_copy(cells_all.at[step], cell_ref, sems.at[PIECES]),
        pltpu.make_async_copy(cells_all.at[before], prev_ref, sems.at[PIECES + 1]),
        pltpu.make_async_copy(ups_all.at[time], up_ref, sems.at[PIECES + 2]),
    ]


def aside_kernel(
    first, last, opens, passed, step_ref, dz_ref, raw_ref, gates_all, cells_all, ups_all, slope_all, *refs
):
    refs = refs[(0 if first else 4) + (0 if opens else 2) + passed :]
    gates_ref, cell_ref, prev_ref, slope_ref, up_ref = refs[:5]
    dz_all, raw_all, near_all, far_all, near_out, far_out = refs[5:11]
    sems, fetch_sems = refs[-2:]
    step, time_before = step_ref[0], step_ref[2]
    slot, low, high = step_ref[4], step_ref[5], step_ref[6]
    before = jnp.maximum(step - 1, 0)
    copies = []
    if not last:
        copies += fetches(
            before, time_before, (gates_all, cells_all, ups_all), (gates_ref, cell_ref, prev_ref, up_ref), fetch_sems
        )
        copies.append(pltpu.make_async_copy(slope_all.at[before], slope_ref, fetch_sems.at[PIECES + 3]))
    copies += [pltpu.make_async_copy(dz_ref.at[i], dz_all.at[i, step], sems.at[i]) for i in range(PIECES)]
    copies.append(pltpu.make_async_copy(raw_ref, raw_all.at[step], sems.at[PIECES]))
    copies.append(pltpu.make_async_copy(dz_ref.at[low], near_all.at[step], sems.at[PIECES + 1]))
    copies.append(pltpu.make_async_copy(dz_ref.at[HALVES + high], far_all.at[step], sems.at[PIECES + 2]))
    copies.append(pltpu.make_async_copy(dz_ref.at[1 - low], near_out.at[slot], sems.at[PIECES + 3]))
    copies.append(pltpu.make_async_copy(dz_ref.at[HALVES + 1 - high], far_out.at[slot], sems.at[PIECES + 4]))
    for copy in copies:
        copy.start()
    for copy in copies:
        copy.wait()


def input_grad_kernel(step_ref, dz_ref, wa_ref, wb_ref, out_ref, acc_ref):
    piece, gate = pl.program_id(0), pl.program_id(1)
    steps, streams, width = dz_ref.shape[1:]

    @pl.when((piece == 0) & (gate == 0))
    def _():
        acc_ref[...] = jnp.zeros(acc_ref.shape, F32)

    weights = jnp.where(piece < HALVES, wa_ref[0], wb_ref[0])
    acc_ref[...] += lax.dot_general(
        dz_ref[0].reshape(steps * streams, width), weights, (((1,), (1,)), ((), ())), preferred_element_type=F32
    )

    @pl.when((piece == PIECES - 1) & (gate == 3))
    def _():
        for step in range(steps):
            time = step_ref[0] + step_ref[1] * step
            out_ref[time] = acc_ref[step * streams : (step + 1) * streams, :]


def params(mib):
    return pltpu.CompilerParams(vmem_limit_bytes=mib * MIB)


def cost(flops, size):
    return pl.CostEstimate(flops=flops, bytes_accessed=size, transcendentals=0)


def body(inputs, w_in, w_rec, bias, proj, state_h, state_c, resets, stream_doc, cotangent):
    streams, steps, depth = inputs.shape[1:]
    cells = w_in.shape[3]
    width = cells // HALVES
    rank = lax.axis_index("gate")
    own = rank % 2
    gates_size = lax.axis_size("gate")
    swap = [(i, i ^ 1) for i in range(gates_size)]
    across = [(i, i ^ 2) for i in range(gates_size)]

    def pick(stacked, index):
        return lax.dynamic_index_in_dim(stacked, index, 0, keepdims=False)

    def trade(mine, theirs):
        return (mine, lax.ppermute(theirs, "gate", swap))

    def vmem(shape, dtype):
        return pltpu.VMEM(shape, dtype)

    def hbm(shape, dtype):
        return pltpu.HBM(shape, dtype)

    def by_gate(weights, index, keep=True):
        shape = (4,) + weights.shape[1:2] + weights.shape[3:]
        kept = (vmem(shape, BF16),) if keep else ()
        part = weights.shape[1] // 8
        return pl.pallas_call(
            functools.partial(layout_kernel, keep),
            out_shape=kept + (hbm(shape, BF16),),
            in_specs=[SMEM, ANY],
            out_specs=[VMEM] * len(kept) + [ANY],
            scratch_shapes=([] if kept else [pltpu.VMEM(shape, BF16)])
            + [
                pltpu.VMEM((3, part) + weights.shape[2:], BF16),
                pltpu.SemaphoreType.DMA((3,)),
                pltpu.SemaphoreType.DMA((8,)),
            ],
            compiler_params=params(8),
            name="layout",
        )(jnp.full((1,), index, jnp.int32), in_hbm(weights))

    win_b, rec_b = (lax.ppermute(by_gate(w, 1 - own, False)[0], "gate", swap) for w in (w_in, w_rec))
    (win_av, win_a), (rec_av, rec_a) = by_gate(w_in, own), by_gate(w_rec, own)
    proj_a, proj_b = trade(pick(proj, own), pick(proj, 1 - own))
    bias_a, bias_b = trade(pick(bias, own), pick(bias, 1 - own))

    def pieces_of(pair):
        split = [x.reshape(4, HALVES, width) for x in pair]
        return jnp.transpose(jnp.stack(split), (0, 2, 1, 3)).reshape(PIECES, 1, 4 * width)

    bias_p = pieces_of((bias_a, bias_b)).astype(F32)

    def cells_to_pieces(pair):
        both = jnp.stack(pair).reshape(QUARTERS, streams, HALVES, width)
        return jnp.transpose(both, (0, 2, 1, 3)).reshape(PIECES, streams, width)

    def by_time(stacked):
        return jnp.transpose(pick(stacked, own), (1, 0, 2))

    feats = by_time(inputs)
    ups = by_time(cotangent)
    flags = resets.astype(F32)
    later = jnp.concatenate([flags[:, 1:], jnp.zeros_like(flags[:, :1])], axis=1)
    keep = 1.0 - jnp.where(own == 0, flags, later)
    keep = jnp.broadcast_to(jnp.transpose(keep)[:, :, None], (steps, streams, 128))

    docs_h = state_h[stream_doc]
    docs_c = state_c[stream_doc]
    start_h = pick(jnp.transpose(docs_h, (1, 0, 2)), own).astype(BF16)
    by_dir_c = jnp.transpose(docs_c, (1, 0, 2))
    start_c = cells_to_pieces(trade(pick(by_dir_c, own), pick(by_dir_c, 1 - own)))

    def at_step(step):
        near = jnp.array([step, step, max(step - 1, 0), min(step + 1, steps - 1)], jnp.int32)
        turned = jnp.array([step] + [steps - 1 - x for x in (step, max(step - 1, 0), min(step + 1, steps - 1))], jnp.int32)
        return jnp.where(own == 0, near, turned)

    n_batch = lax.axis_size("batch")
    spot = lax.axis_index("batch")
    low, high = spot % 2, (spot // 2) % 2
    near_swap = [(i, i ^ 1) for i in range(n_batch)]
    far_swap = [(i, i ^ 2) for i in range(n_batch)]

    def swapped(array, pairs):
        return lax.ppermute(array, "batch", pairs)

    turn = jnp.where(own == 0, jnp.array([0, 1], jnp.int32), jnp.array([steps - 1, -1], jnp.int32))
    feats_v, feat_all = pl.pallas_call(
        order_kernel,
        out_shape=(vmem(feats.shape, BF16), hbm(feats.shape, BF16)),
        in_specs=[SMEM, ANY],
        out_specs=[VMEM, ANY],
        scratch_shapes=[pltpu.SemaphoreType.DMA((steps,)), pltpu.SemaphoreType.DMA],
        compiler_params=params(1),
        name="order",
    )(turn, feats)
    feat_in = (swapped(feat_all, near_swap), swapped(feat_all, far_swap))
    keep_v, bias_v, win_bv = place(keep, bias_p, win_b)
    rec_bv, proj_av, proj_bv, start_hv, start_cv = place(rec_b, proj_a, proj_b, start_h, start_c)

    gates_shape, cell_shape = (PIECES, streams, 4 * width), (PIECES, streams, width)
    bias_shape = (PIECES, 8, 4 * width)
    inflow = pl.pallas_call(
        inflow_kernel,
        out_shape=vmem(gates_shape, F32),
        in_specs=[SMEM] + [VMEM] * 4,
        out_specs=VMEM,
        compiler_params=params(8),
        name="inflow",
    )(turn, pinned(feats_v), pinned(bias_v), pinned(win_av), pinned(win_bv))

    def forward_call(first, step, part, peer, cell, inflow):
        return pl.pallas_call(
            functools.partial(forward_kernel, first),
            out_shape=(
                vmem((streams, depth), BF16),
                vmem(cell_shape, F32),
                vmem(gates_shape, BF16),
                vmem(cell_shape, BF16),
                vmem((streams, depth), BF16),
                vmem((streams, depth), BF16),
                vmem((streams, depth), F32),
            ),
            in_specs=[SMEM] + [VMEM] * 10,
            out_specs=[VMEM] * 7,
            compiler_params=params(8),
            name="forward_step",
        )(
            at_step(step), pinned(part), pinned(peer), pinned(start_hv), pinned(keep_v), pinned(cell), pinned(inflow),
            pinned(rec_av), pinned(rec_bv), pinned(proj_av), pinned(proj_bv),
        )

    def between_call(step, fresh, stacks, passing=()):
        shapes = (
            hbm((PIECES, steps, streams, 4 * width), BF16),
            hbm((steps,) + cell_shape, F32),
            hbm((PIECES, steps, streams, width), BF16),
            hbm((steps, streams, depth), BF16),
            hbm((steps, streams, depth), BF16),
            hbm((steps, streams, depth), F32),
        )
        aliases = {11 + i: 1 + i for i in range(len(stacks))}
        aliases.update({11 + len(stacks) + i: 7 + i for i in range(len(passing))})
        inflow, *out = pl.pallas_call(
            functools.partial(between_kernel, not stacks, step == steps - 1, len(passing)),
            out_shape=(vmem(gates_shape, F32),) + shapes + tuple(hbm(x.shape, x.dtype) for x in passing),
            in_specs=[SMEM] + [VMEM] * 10 + [ANY] * (len(stacks) + len(passing)),
            out_specs=[VMEM] + [ANY] * (6 + len(passing)),
            scratch_shapes=[pltpu.SemaphoreType.DMA((2 * PIECES + 4,))],
            input_output_aliases=aliases,
            compiler_params=params(8),
            cost_estimate=cost(2 * streams * depth * 8 * cells, 8 * depth * cells * 2),
            name="between",
        )(
            at_step(step), pinned(feats_v), pinned(bias_v), pinned(win_av), pinned(win_bv),
            *(pinned(x) for x in fresh), *(in_hbm(x) for x in (*stacks, *passing)),
        )
        return inflow, tuple(out[:6]), tuple(out[6:])

    none = jnp.zeros((streams, depth), BF16)
    part, peer, cell, stacks = none, none, start_cv, ()
    for step in range(steps):
        part, cell, *fresh = forward_call(step == 0, step, part, peer, cell, inflow)
        peer = lax.ppermute(part, "gate", across)
        due = step == (2 * steps) // 3
        inflow, stacks, passed = between_call(step, (cell, *fresh), stacks, feat_in if due else ())
        feat_in = passed if due else feat_in
    gates_all, cells_all, mixed_all, prev_all, hidden_all, slope_all = stacks
    prev_in = (swapped(prev_all, near_swap), swapped(prev_all, far_swap))

    saved_shapes = (
        vmem(gates_shape, BF16),
        vmem(cell_shape, F32),
        vmem(cell_shape, F32),
        vmem((streams, depth), F32),
        vmem((streams, depth), BF16),
    )
    *saved, hidden_all, slope_all = pl.pallas_call(
        finish_kernel,
        out_shape=saved_shapes + (hbm((steps, streams, depth), BF16), hbm((steps, streams, depth), F32)),
        in_specs=[SMEM, VMEM, VMEM] + [ANY] * 5,
        out_specs=[VMEM] * 5 + [ANY] * 2,
        scratch_shapes=[
            pltpu.VMEM((streams, depth), BF16),
            pltpu.SemaphoreType.DMA((PIECES + 4,)),
            pltpu.SemaphoreType.DMA,
        ],
        input_output_aliases={6: 5, 7: 6},
        compiler_params=params(8),
        name="finish",
    )(
        at_step(steps - 1), pinned(part), pinned(peer), in_hbm(gates_all), in_hbm(cells_all), in_hbm(ups),
        in_hbm(hidden_all), in_hbm(slope_all),
    )

    rec_atv, rec_btv, proj_atv, proj_btv = pl.pallas_call(
        turned_kernel,
        out_shape=(vmem((4, cells, depth), BF16),) * 2 + (vmem((depth, cells), BF16),) * 2,
        in_specs=[ANY] * 4,
        out_specs=[VMEM] * 4,
        scratch_shapes=[
            pltpu.VMEM((3, depth, cells), BF16),
            pltpu.SemaphoreType.DMA((3,)),
            pltpu.VMEM((2, cells, depth), BF16),
            pltpu.SemaphoreType.DMA((2,)),
        ],
        compiler_params=params(8),
        name="turned",
    )(*(in_hbm(x) for x in (rec_a, rec_b, proj_a, proj_b)))

    def backward_call(step, part, peer, grad, bias, saved):
        return pl.pallas_call(
            backward_kernel,
            out_shape=(
                vmem((streams, depth), BF16),
                vmem(cell_shape, F32),
                vmem(bias_shape, F32),
                vmem((streams, depth), BF16),
                vmem(gates_shape, BF16),
            ),
            in_specs=[SMEM] + [VMEM] * 15,
            out_specs=[VMEM] * 5,
            compiler_params=params(8),
            name="backward_step",
        )(
            at_step(step), pinned(part), pinned(peer), pinned(keep_v), pinned(grad), pinned(bias),
            pinned(rec_atv), pinned(rec_btv), pinned(proj_atv), pinned(proj_btv),
            *(pinned(x) for x in saved), pinned(start_cv),
        )

    def aside_call(step, slot, slots, dz, raw, stacks, sends, passing):
        piece_shape = (streams, 4 * width)
        shapes = (
            hbm((PIECES, steps) + piece_shape, BF16),
            hbm((steps, streams, depth), BF16),
            hbm((steps,) + piece_shape, BF16),
            hbm((steps,) + piece_shape, BF16),
            hbm((slots,) + piece_shape, BF16),
            hbm((slots,) + piece_shape, BF16),
        )
        kept = len(stacks)
        aliases = {7 + i: 5 + i for i in range(kept)}
        aliases.update({7 + kept + i: 9 + i for i in range(len(sends))})
        aliases.update({7 + kept + len(sends) + i: 11 + i for i in range(len(passing))})
        out = pl.pallas_call(
            functools.partial(aside_kernel, not stacks, step == 0, not sends, len(passing)),
            out_shape=saved_shapes + shapes + tuple(hbm(x.shape, x.dtype) for x in passing),
            in_specs=[SMEM] + [VMEM] * 2 + [ANY] * (4 + kept + len(sends) + len(passing)),
            out_specs=[VMEM] * 5 + [ANY] * (6 + len(passing)),
            scratch_shapes=[
                pltpu.SemaphoreType.DMA((PIECES + 5,)),
                pltpu.SemaphoreType.DMA((PIECES + 4,)),
            ],
            input_output_aliases=aliases,
            compiler_params=params(8),
            cost_estimate=cost(0, 8 * MIB),
            name="aside",
        )(
            jnp.concatenate([at_step(step), jnp.stack([jnp.int32(slot), low, high])]), pinned(dz), pinned(raw),
            in_hbm(gates_all), in_hbm(cells_all), in_hbm(ups), in_hbm(slope_all),
            *(in_hbm(x) for x in (*stacks, *sends, *passing)),
        )
        return out[:5], tuple(out[5:9]), tuple(out[9:11]), tuple(out[11:])

    carry = (none, none, jnp.zeros(cell_shape, F32), jnp.zeros(bias_shape, F32), saved, ())
    pending, arrived, ready, top = [(steps - 1 - steps // 3, prev_in)], [], None, steps
    for index, share in enumerate(SHARES):
        slots = top if index == len(SHARES) - 1 else round(share * steps)
        sends = ()
        for step in range(top - 1, top - slots - 1, -1):
            part, peer, grad, bias_sum, saved, stacks = carry
            part, grad, bias_sum, raw, dz = backward_call(step, part, peer, grad, bias_sum, saved)
            peer = lax.ppermute(part, "gate", across)
            if ready is not None:
                due, sides = ready
                sides = after((part,), *sides) if step else sides
                pending.append((due, (swapped(sides[0], near_swap), swapped(sides[1], far_swap))))
                ready = None
            passing = pending.pop(0)[1] if pending and pending[0][0] >= step else ()
            saved, stacks, sends, passed = aside_call(
                step, step - (top - slots), slots, dz, raw, stacks, sends, passing
            )
            arrived += [passed] if passed else []
            carry = (part, peer, grad, bias_sum, saved, stacks)
        top -= slots
        ready = (max(top - 1 - (3 * slots + 3) // 4, 0 if slots > 2 else -1), sends)
    pending.append((-1, (swapped(sends[0], near_swap), swapped(sends[1], far_swap))))
    arrived += [arrays for _, arrays in pending]
    dz_all, raw_all, near_all, far_all = carry[-1]
    bias_sum = carry[3]
    prev_in, exchanged = arrived[0], arrived[1:]
    rows = steps * streams

    def by_direction(mine, theirs):
        return jnp.stack([jnp.where(own == 0, mine, theirs), jnp.where(own == 0, theirs, mine)])

    def line_sum(chunks, axis, stride, count, first=None, gates={}):
        here = (spot // stride) % count

        def chunk(index):
            return lax.dynamic_index_in_dim(chunks, jnp.clip(index, 0, count - 1), axis, keepdims=False)

        def at(device):
            return (device // stride) % count

        if count == 2:
            pairs = [(i, i + stride if at(i) == 0 else i - stride) for i in range(n_batch)]
            return (chunk(here).astype(F32) + swapped(chunk(1 - here), pairs).astype(F32)).astype(BF16)
        ends = [(i, i + stride) for i in range(n_batch) if at(i) == 0]
        ends += [(i, i - stride) for i in range(n_batch) if at(i) == count - 1]
        up = down = swapped(chunk(jnp.where(here == 0, count - 1, 0)) if first is None else first, ends)
        for slot in range(2, count):
            if slot in gates:
                up, down = gates[slot](up, down)
            rise = (chunk(here + count - slot).astype(F32) + up.astype(F32)).astype(BF16)
            fall = (chunk(here - count + slot).astype(F32) + down.astype(F32)).astype(BF16)
            up = swapped(rise, [(i, i + stride) for i in range(n_batch) if at(i) < min(slot, count - 1)])
            down = swapped(fall, [(i, i - stride) for i in range(n_batch) if at(i) > max(count - 1 - slot, 0)])
        if count in gates:
            up, down = gates[count](up, down)
        return (chunk(here).astype(F32) + up.astype(F32) + down.astype(F32)).astype(BF16)

    line = n_batch // 2
    share_rows = depth // n_batch

    def input_grad_of(dz):
        return pl.pallas_call(
            input_grad_kernel,
            out_shape=jax.ShapeDtypeStruct((steps, streams, depth), F32),
            grid_spec=pltpu.PrefetchScalarGridSpec(
                num_scalar_prefetch=1,
                grid=(PIECES, 4),
                in_specs=[
                    pl.BlockSpec((1, steps, streams, width), lambda p, g, turn: (p, 0, 0, g)),
                    pl.BlockSpec(
                        (1, depth, width), lambda p, g, turn: (jnp.where(p < 2, g, 3), 0, jnp.where(p < 2, p, 1))
                    ),
                    pl.BlockSpec(
                        (1, depth, width), lambda p, g, turn: (jnp.where(p < 2, 0, g), 0, jnp.where(p < 2, 0, p - 2))
                    ),
                ],
                out_specs=pl.BlockSpec((steps, streams, depth), lambda p, g, turn: (0, 0, 0)),
                scratch_shapes=[pltpu.VMEM((rows, depth), F32)],
            ),
            compiler_params=params(16),
            cost_estimate=cost(0, 0),
            name="input_grad",
        )(turn, dz, in_hbm(win_a), in_hbm(win_b))

    grad_proj = jnp.einsum("ptnc,tnk->pkc", mixed_all, raw_all, preferred_element_type=F32).astype(BF16)
    grad_proj = grad_proj.reshape(PIECES, line, 2, share_rows, width)
    own_cells = cells // n_batch
    bias_rows = jnp.sum(bias_sum, axis=1).reshape(QUARTERS, HALVES, 4, width)
    bias_rows = jnp.transpose(bias_rows, (0, 2, 1, 3)).reshape(QUARTERS, 4, line, 2, own_cells)
    bias_rows = jnp.transpose(bias_rows, (2, 3, 0, 1, 4)).reshape(line, 2, -1)
    bias_rows = jnp.pad(bias_rows, ((0, 0), (0, 0), (0, PIECES * width - bias_rows.shape[2])))
    bias_rows = jnp.transpose(bias_rows.reshape(line, 2, PIECES, 1, width), (2, 0, 1, 3, 4)).astype(BF16)
    grad_proj = jnp.concatenate([grad_proj, bias_rows], axis=3)

    def with_partner(grad):
        mine = lax.dynamic_index_in_dim(grad, low, grad.ndim - 3, keepdims=False)
        sent = lax.dynamic_index_in_dim(grad, 1 - low, grad.ndim - 3, keepdims=False)
        taken = swapped(sent, near_swap)
        return sent, taken, (mine.astype(F32) + taken.astype(F32)).astype(BF16)

    def across_two(grad):
        return line_sum(grad.reshape(grad.shape[:-3] + (line // 2, 2) + grad.shape[-2:]), grad.ndim - 3, 4, line // 2)

    proj_sent, proj_taken, proj_y = with_partner(grad_proj)

    lows, count = [], 0
    for x in exchanged[::-1]:
        lows.insert(0, count)
        count += x[0].shape[0]

    def gathered(kept, feat, prev, parts):
        return pl.pallas_call(
            functools.partial(gather_kernel, tuple(lows[: len(parts)])),
            out_shape=(vmem((2 * steps, streams, 2 * depth), BF16), vmem((2 * steps, streams, 4 * width), BF16)),
            in_specs=[ANY] * (5 + len(parts)),
            out_specs=[VMEM] * 2,
            scratch_shapes=[pltpu.SemaphoreType.DMA((5 + len(parts),))],
            compiler_params=params(1),
            cost_estimate=cost(0, 0),
            name="gather",
        )(*(in_hbm(x) for x in (feat_all, prev_all, feat, prev, kept, *parts)))

    def completed(begin, rows_out, left, right, parts):
        return pl.pallas_call(
            functools.partial(late_kernel, tuple(lows[len(lows) - len(parts) :])),
            out_shape=(vmem(right.shape, BF16), jax.ShapeDtypeStruct((2, max(rows_out, 8), 4 * width), BF16)),
            in_specs=[SMEM] + [VMEM] * 2 + [ANY] * len(parts),
            out_specs=[VMEM] * 2,
            scratch_shapes=[pltpu.SemaphoreType.DMA((len(parts),))],
            input_output_aliases={2: 0},
            compiler_params=params(16),
            cost_estimate=cost(0, 0),
            name="late",
        )(begin, pinned(left), pinned(right), *(in_hbm(x) for x in parts))

    def multiplied(left, right):
        return pl.pallas_call(
            product_kernel,
            out_shape=jax.ShapeDtypeStruct((2, depth, 4 * width), BF16),
            in_specs=[VMEM] * 2,
            out_specs=VMEM,
            compiler_params=params(16),
            cost_estimate=cost(0, 0),
            name="product",
        )(pinned(left), pinned(right))

    near_parts, far_parts = zip(*exchanged)
    begin = jnp.where(spot // 2 == 0, line - 1, 0)
    chunk_rows = 2 * share_rows if 2 * share_rows % 128 == 0 else 0
    near_left, near_right = gathered(near_all, feat_in[0], prev_in[0], near_parts[:-LATE])
    near_late = after((near_left, proj_sent), *near_parts[-LATE:])
    near_right, first = completed(jnp.full((1,), begin, jnp.int32), chunk_rows, near_left, near_right, near_late)
    far_all, *far_parts = after((first,), far_all, *far_parts)
    far_left, far_right = gathered(far_all, feat_in[1], prev_in[1], far_parts[:-LATE])
    far_right, _ = completed(jnp.zeros((1,), jnp.int32), 0, far_left, far_right, far_parts[-LATE:])
    far = multiplied(far_left, far_right).reshape(2, line, 2, share_rows, 4 * width)
    near = multiplied(near_left, near_right).reshape(2, line, 2, share_rows, 4 * width)
    (_, in_taken, far_in), (_, rec_taken, far_rec) = (with_partner(far[i]) for i in range(2))
    proj_two = across_two(proj_y)
    in_two, rec_two = across_two(far_in), across_two(far_rec)

    tokens = {}

    def second(up, down):
        (tokens["dz"],) = after((up,), dz_all)
        return after((far, proj_taken), up, down)

    def third(up, down):
        tokens["dx"] = input_grad_of(tokens["dz"])
        tokens["hidden"], tokens["cell"] = after((up, tokens["dx"]), hidden_all, cell)
        return after((in_taken, proj_two, tokens["dx"]), up, down)

    def final(up, down):
        return after((rec_taken, in_two), up, down)

    gates = {2: second, 3: third, line: final} if line > 3 else {}
    first = first.reshape(2, 2, share_rows, 4 * width) if chunk_rows else None
    near = line_sum(near, 1, 2, line, first, gates)
    dx_all, hidden_all, cell = (tokens[x] for x in ("dx", "hidden", "cell"))

    def halves_of(summed, index, pairs):
        mine = lax.dynamic_index_in_dim(summed, index, 1, keepdims=False)
        return mine, swapped(lax.dynamic_index_in_dim(summed, 1 - index, 1, keepdims=False), pairs)

    near_pair = halves_of(near, low, near_swap)
    far_pair = halves_of(jnp.stack([in_two, rec_two]), high, far_swap)
    far_pair = [lax.ppermute(x, "gate", swap) for x in far_pair]
    proj_mine, proj_theirs = halves_of(proj_two, high, far_swap)
    grad_proj = proj_mine.astype(F32) + proj_theirs.astype(F32)
    grad_shape = (2, share_rows, 4, cells)
    grad_w_in, grad_w_rec = pl.pallas_call(
        assemble_kernel,
        out_shape=(jax.ShapeDtypeStruct(grad_shape, F32),) * 2,
        in_specs=[SMEM] + [VMEM] * 4,
        out_specs=[VMEM] * 2,
        compiler_params=params(14),
        name="assemble",
    )(jnp.stack([own, low, high]), *near_pair, *far_pair)

    def home(mine, theirs):
        return by_direction(*trade(mine, theirs)).astype(F32)

    shaped = grad_proj[:, share_rows].reshape(-1)[: QUARTERS * 4 * own_cells].reshape(QUARTERS, 4, own_cells)
    grad_bias = home(shaped[0], shaped[1])
    grad_proj = grad_proj[:, :share_rows].reshape(QUARTERS, HALVES, share_rows, width)
    grad_proj = jnp.transpose(grad_proj, (0, 1, 3, 2)).reshape(QUARTERS, cells, share_rows).astype(BF16)
    grad_proj = home(grad_proj[0], grad_proj[1])

    both_hidden = trade(hidden_all, hidden_all)

    hidden_dirs = by_direction(*both_hidden)
    outputs = (inputs.astype(F32) + jnp.transpose(hidden_dirs, (0, 2, 1, 3)).astype(F32)).astype(BF16)
    last_h = jnp.stack([hidden_dirs[0, steps - 1], hidden_dirs[1, 0]], axis=1).astype(F32)
    final_h = jnp.zeros_like(state_h).at[stream_doc].set(last_h)
    last_c = jnp.transpose(cell.reshape(QUARTERS, HALVES, streams, width), (0, 2, 1, 3)).reshape(
        QUARTERS, streams, cells
    )
    last_dirs = by_direction(*trade(last_c[0], last_c[1]))
    final_c = jnp.zeros_like(state_c).at[stream_doc].set(jnp.transpose(last_dirs, (1, 0, 2)))

    half_cols = depth // 2
    upper = rank // 2
    keep_cols = lax.dynamic_slice_in_dim(dx_all, upper * half_cols, half_cols, 2)
    send_cols = lax.dynamic_slice_in_dim(dx_all, (1 - upper) * half_cols, half_cols, 2).astype(BF16)
    dx_half = keep_cols + lax.ppermute(send_cols, "gate", across).astype(F32)
    up_half = lax.dynamic_slice_in_dim(ups, upper * half_cols, half_cols, 2).astype(F32)
    dx_half = (dx_half + up_half).astype(BF16)
    quarter_cols = half_cols // 2
    mine = lax.dynamic_slice_in_dim(dx_half, own * quarter_cols, quarter_cols, 2)
    theirs = lax.dynamic_slice_in_dim(dx_half, (1 - own) * quarter_cols, quarter_cols, 2)
    dx_dirs = by_direction(*trade(mine, theirs))
    input_grad = jnp.transpose(dx_dirs, (0, 2, 1, 3))
    return (outputs, input_grad, grad_w_in, grad_w_rec, grad_bias, grad_proj, final_h, final_c)


def solution(mesh):
    placed = (
        P(None, "batch", None, None),
        P(None, None, None, "gate"),
        P(None, None, None, "gate"),
        P(None, None, "gate"),
        P(None, "gate", None),
        P("batch", None, None),
        P("batch", None, "gate"),
        P("batch", None),
        P("batch"),
        P(None, "batch", None, None),
    )
    return jax.shard_map(
        body,
        mesh=mesh,
        in_specs=placed,
        out_specs=(
            P(None, "batch", None, None),
            P(None, "batch", None, "gate"),
            P(None, "batch", None, "gate"),
            P(None, "batch", None, "gate"),
            P(None, None, ("gate", "batch")),
            P(None, "gate", "batch"),
            P("batch", None, None),
            P("batch", None, "gate"),
        ),
        check_vma=False,
    )
```

```python
import functools

import jax
import jax.numpy as jnp
from jax import lax
from jax.experimental import pallas as pl
from jax.experimental.pallas import tpu as pltpu
from jax.sharding import PartitionSpec as P

CLIP = 3.0
F32, BF16 = jnp.float32, jnp.bfloat16
QUARTERS, HALVES = 2, 2
PIECES = QUARTERS * HALVES
MIB = 2**20
LATE = 2
SHARES = (0.35, 0.3, 0.15, 0.1, 0.1)

VMEM = pl.BlockSpec(memory_space=pltpu.VMEM)
SMEM = pl.BlockSpec(memory_space=pltpu.SMEM)
ANY = pl.BlockSpec(memory_space=pl.ANY)


def pinned(array):
    return pltpu.with_memory_space_constraint(array, pltpu.VMEM)


def in_hbm(array):
    return pltpu.with_memory_space_constraint(array, pltpu.HBM)


def dot(left, right):
    return jnp.dot(left, right, preferred_element_type=F32)


def place_kernel(count, *refs):
    sources, targets, sems = refs[:count], refs[count : 2 * count], refs[2 * count]
    copies = [pltpu.make_async_copy(a, b, sems.at[i]) for i, (a, b) in enumerate(zip(sources, targets))]
    for copy in copies:
        copy.start()
    for copy in copies:
        copy.wait()


def place(*arrays):
    count = len(arrays)
    return pl.pallas_call(
        functools.partial(place_kernel, count),
        out_shape=tuple(pltpu.VMEM(x.shape, x.dtype) for x in arrays),
        in_specs=[ANY] * count,
        out_specs=[VMEM] * count,
        scratch_shapes=[pltpu.SemaphoreType.DMA((count,))],
        compiler_params=params(1),
        name="place",
    )(*(in_hbm(x) for x in arrays))


def layout_kernel(keep, which_ref, w_ref, first_ref, second_ref, buf, sems, out_sems):
    out_ref, all_ref = (first_ref, second_ref) if keep else (second_ref, first_ref)
    depth, part = w_ref.shape[1], buf.shape[1]

    def fetch(i):
        return pltpu.make_async_copy(w_ref.at[which_ref[0], pl.ds(i * part, part)], buf.at[i % 3], sems.at[i % 3])

    def store(i):
        rows = pl.ds(i * part, part)
        return pltpu.make_async_copy(out_ref.at[:, rows], all_ref.at[:, rows], out_sems.at[i])

    count = depth // part
    for i in range(min(2, count)):
        fetch(i).start()
    for i in range(count):
        if i + 2 < count:
            fetch(i + 2).start()
        fetch(i).wait()
        out_ref[:, i * part : (i + 1) * part, :] = jnp.swapaxes(buf[i % 3], 0, 1)
        store(i).start()
    for i in range(count):
        store(i).wait()


def turned_kernel(wa_ref, wb_ref, pa_ref, pb_ref, wat_ref, wbt_ref, pat_ref, pbt_ref, buf, sems, proj_buf, proj_sems):
    jobs = [(w_ref, out_ref, gate) for w_ref, out_ref in ((wa_ref, wat_ref), (wb_ref, wbt_ref)) for gate in range(4)]

    def fetch(i):
        return pltpu.make_async_copy(jobs[i][0].at[jobs[i][2]], buf.at[i % 3], sems.at[i % 3])

    proj_fetches = [pltpu.make_async_copy(x, proj_buf.at[i], proj_sems.at[i]) for i, x in enumerate((pa_ref, pb_ref))]
    fetch(0).start()
    fetch(1).start()
    for copy in proj_fetches:
        copy.start()
    for i, (_, out_ref, gate) in enumerate(jobs):
        if i + 2 < len(jobs):
            fetch(i + 2).start()
        fetch(i).wait()
        for half in range(HALVES):
            width = buf.shape[2] // HALVES
            cols = slice(half * width, (half + 1) * width)
            out_ref[gate, cols, :] = buf[i % 3, :, cols].T
    for i, out_ref in enumerate((pat_ref, pbt_ref)):
        proj_fetches[i].wait()
        out_ref[...] = proj_buf[i].T


def pass_kernel(*refs):
    pass


def after(tokens, *arrays):
    count = len(tokens)
    return pl.pallas_call(
        pass_kernel,
        out_shape=tuple(jax.ShapeDtypeStruct(x.shape, x.dtype) for x in arrays),
        in_specs=[ANY] * (count + len(arrays)),
        out_specs=[ANY] * len(arrays),
        input_output_aliases={count + i: i for i in range(len(arrays))},
        compiler_params=params(1),
        name="after",
    )(*tokens, *arrays)


def gather_kernel(lows, *refs):
    (feat_ref, prev_ref, feat_too, prev_too, kept_ref), refs = refs[:5], refs[5:]
    groups, (left_ref, right_ref, sems) = refs[:-3], refs[-3:]
    steps, _, depth = feat_ref.shape
    jobs = [
        (feat_ref, left_ref.at[:steps, :, :depth]),
        (prev_ref, left_ref.at[:steps, :, depth:]),
        (feat_too, left_ref.at[steps:, :, :depth]),
        (prev_too, left_ref.at[steps:, :, depth:]),
        (kept_ref, right_ref.at[:steps]),
    ]
    jobs += [(x, right_ref.at[steps + low : steps + low + x.shape[0]]) for x, low in zip(groups, lows)]
    copies = [pltpu.make_async_copy(a, b, sems.at[i]) for i, (a, b) in enumerate(jobs)]
    for copy in copies:
        copy.start()
    for copy in copies:
        copy.wait()


def late_kernel(lows, begin_ref, left_ref, right_in, *refs):
    groups, (right_ref, first_ref, sems) = refs[:-3], refs[-3:]
    steps = left_ref.shape[0] // 2
    copies = [
        pltpu.make_async_copy(x, right_ref.at[steps + low : steps + low + x.shape[0]], sems.at[i])
        for i, (x, low) in enumerate(zip(groups, lows))
    ]
    for copy in copies:
        copy.start()
    for copy in copies:
        copy.wait()
    if first_ref.shape[1] % 128:
        return
    share, depth = first_ref.shape[1], left_ref.shape[2] // 2
    rows = left_ref.shape[0] * left_ref.shape[1]
    left = [
        left_ref[:, :, pl.ds(pl.multiple_of(i * depth + begin_ref[0] * share, 128), share)].reshape(rows, share)
        for i in range(2)
    ]
    left = jnp.concatenate([x.T for x in left], axis=0)
    width = right_ref.shape[2] // 4

    def columns(i, _):
        cols = pl.ds(pl.multiple_of(i * width, width), width)
        total = dot(left, right_ref[:, :, cols].reshape(rows, width)).astype(BF16)
        first_ref[0, :, cols] = total[:share]
        first_ref[1, :, cols] = total[share:]
        return 0

    lax.fori_loop(0, 4, columns, 0)


def product_kernel(left_ref, right_ref, out_ref):
    rows, depth = left_ref.shape[0] * left_ref.shape[1], left_ref.shape[2] // 2
    width = right_ref.shape[2] // 4
    for which in range(2):
        left = left_ref[:, :, which * depth : (which + 1) * depth].reshape(rows, depth).T

        def columns(i, _):
            cols = pl.ds(pl.multiple_of(i * width, width), width)
            out_ref[which, :, cols] = dot(left, right_ref[:, :, cols].reshape(rows, width)).astype(BF16)
            return 0

        lax.fori_loop(0, 4, columns, 0)


def assemble_kernel(place_ref, near_a, near_b, far_a, far_b, in_ref, rec_ref):
    own, low, high = place_ref[0], place_ref[1], place_ref[2]
    width = in_ref.shape[3] // HALVES
    for direction, mine_ref, theirs_ref, index in ((own, near_a, near_b, low), (1 - own, far_a, far_b, high)):
        for which, out_ref in ((0, in_ref), (1, rec_ref)):
            mine, theirs = mine_ref[which].astype(F32), theirs_ref[which].astype(F32)
            for half in range(HALVES):
                whole = jnp.where(index == half, mine, theirs)
                gates = jnp.stack([whole[:, gate * width : (gate + 1) * width] for gate in range(4)])
                out_ref[direction, :, :, half * width : (half + 1) * width] = jnp.swapaxes(gates, 0, 1)


def order_kernel(step_ref, feat_ref, out_ref, all_ref, sems, all_sem):
    steps = feat_ref.shape[0]
    copies = [
        pltpu.make_async_copy(feat_ref.at[step_ref[0] + step_ref[1] * i], out_ref.at[i], sems.at[i]) for i in range(steps)
    ]
    for copy in copies:
        copy.start()
    for copy in copies:
        copy.wait()
    whole = pltpu.make_async_copy(out_ref, all_ref, all_sem)
    whole.start()
    whole.wait()


def pieces(refs, axis):
    for piece in range(PIECES):
        quarter, half = divmod(piece, HALVES)
        width = refs[0].shape[axis] // HALVES
        yield piece, quarter, width, slice(half * width, (half + 1) * width)


def forward_kernel(
    first, step_ref, p_ref, q_ref, start_ref, keep_ref, cell_ref, inflow_ref, wa_ref, wb_ref, pa_ref, pb_ref,
    part_ref, next_ref, gates_ref, mixed_ref, prev_ref, hidden_ref, slope_ref,
):
    keep = keep_ref[step_ref[1]][:, :1]
    if first:
        hidden = start_ref[...]
    else:
        hidden = clipped(p_ref, q_ref, hidden_ref, slope_ref)
    hidden = hidden * keep.astype(BF16)
    prev_ref[...] = hidden
    part = jnp.zeros(part_ref.shape, F32)
    for piece, quarter, width, cols in pieces((wa_ref, wb_ref), 2):
        w_ref, proj_ref = ((wa_ref, pa_ref), (wb_ref, pb_ref))[quarter]
        acts = []
        for gate in range(4):
            place = slice(gate * width, (gate + 1) * width)
            pre = dot(hidden, w_ref[gate, :, cols]) + inflow_ref[piece, :, place]
            act = jnp.tanh(pre if gate == 2 else 0.5 * pre)
            gates_ref[piece, :, place] = act.astype(BF16)
            acts.append(act if gate == 2 else 0.5 + 0.5 * act)
        ingate, forget, candidate, outgate = acts
        cell = CLIP * jnp.tanh((forget * (keep * cell_ref[piece]) + ingate * candidate) * (1.0 / CLIP))
        next_ref[piece] = cell
        mixed = (outgate * jnp.tanh(cell)).astype(BF16)
        mixed_ref[piece] = mixed
        part = part + dot(mixed, proj_ref[cols, :])
    part_ref[...] = part.astype(BF16)


def clipped(p_ref, q_ref, hidden_ref, slope_ref):
    squash = jnp.tanh((p_ref[...].astype(F32) + q_ref[...].astype(F32)) * (1.0 / CLIP))
    hidden = (CLIP * squash).astype(BF16)
    hidden_ref[...] = hidden
    slope_ref[...] = 1.0 - squash * squash
    return hidden


def between_kernel(
    first, last, passed, step_ref, feat_ref, bias_ref, wa_ref, wb_ref, cell_ref, gates_ref, mixed_ref, prev_ref, hidden_ref,
    slope_ref, *refs,
):
    refs = refs[(0 if first else 6) + passed :]
    out_ref, gates_all, cells_all, mixed_all, prev_all, hidden_all, slope_all = refs[:7]
    sems = refs[-1]
    step, time_before = step_ref[0], step_ref[2]
    copies = [pltpu.make_async_copy(gates_ref.at[i], gates_all.at[i, step], sems.at[i]) for i in range(PIECES)]
    copies += [
        pltpu.make_async_copy(mixed_ref.at[i], mixed_all.at[i, step], sems.at[PIECES + i]) for i in range(PIECES)
    ]
    copies.append(pltpu.make_async_copy(cell_ref, cells_all.at[step], sems.at[2 * PIECES]))
    copies.append(pltpu.make_async_copy(prev_ref, prev_all.at[step], sems.at[2 * PIECES + 1]))
    if not first:
        copies.append(pltpu.make_async_copy(hidden_ref, hidden_all.at[time_before], sems.at[2 * PIECES + 2]))
        copies.append(pltpu.make_async_copy(slope_ref, slope_all.at[step - 1], sems.at[2 * PIECES + 3]))
    for copy in copies:
        copy.start()
    if not last:
        inflow_into(feat_ref[step + 1], bias_ref, wa_ref, wb_ref, out_ref)
    for copy in copies:
        copy.wait()


def inflow_into(feat, bias_ref, wa_ref, wb_ref, out_ref):
    for piece, quarter, width, cols in pieces((wa_ref, wb_ref), 2):
        w_ref = (wa_ref, wb_ref)[quarter]
        for gate in range(4):
            place = slice(gate * width, (gate + 1) * width)
            out_ref[piece, :, place] = dot(feat, w_ref[gate, :, cols]) + bias_ref[piece, :, place]


def inflow_kernel(step_ref, feat_ref, bias_ref, wa_ref, wb_ref, out_ref):
    inflow_into(feat_ref[0], bias_ref, wa_ref, wb_ref, out_ref)


def backward_kernel(
    step_ref, p_ref, q_ref, keep_ref, grad_ref, bias_ref, wa_ref, wb_ref, pa_ref, pb_ref,
    gates_ref, cell_ref, prev_ref, slope_ref, up_ref, start_ref,
    part_ref, next_ref, sum_ref, raw_ref, dz_ref,
):
    step = step_ref[0]
    keep = keep_ref[step_ref[1]][:, :1]
    raw = (up_ref[...].astype(F32) + (p_ref[...].astype(F32) + q_ref[...].astype(F32))) * slope_ref[...]
    raw = raw.astype(BF16)
    raw_ref[...] = raw
    part = jnp.zeros(part_ref.shape, F32)
    for piece, quarter, width, cols in pieces((wa_ref, wb_ref), 1):
        w_ref, proj_ref = ((wa_ref, pa_ref), (wb_ref, pb_ref))[quarter]
        mixed = dot(raw, proj_ref[:, cols])
        acts = [gates_ref[piece, :, gate * width : (gate + 1) * width].astype(F32) for gate in range(4)]
        ingate, forget, outgate = (0.5 + 0.5 * acts[gate] for gate in (0, 1, 3))
        slopes = [1.0 - act * act for act in acts]
        cell = cell_ref[piece]
        prev = keep * jnp.where(step == 0, start_ref[piece], prev_ref[piece])
        squash = jnp.tanh(cell)
        total = grad_ref[piece] + mixed * outgate * (1.0 - squash * squash)
        inner = total * (1.0 - (cell * (1.0 / CLIP)) * (cell * (1.0 / CLIP)))
        next_ref[piece] = keep * inner * forget
        quart = 0.25 * inner
        pre_grads = (
            quart * acts[2] * slopes[0],
            quart * prev * slopes[1],
            inner * ingate * slopes[2],
            0.25 * mixed * squash * slopes[3],
        )
        for gate in range(4):
            low = pre_grads[gate].astype(BF16)
            place = slice(gate * width, (gate + 1) * width)
            dz_ref[piece, :, place] = low
            rows = pre_grads[gate].reshape(-1, 8, width)
            sum_ref[piece, :, place] = bias_ref[piece, :, place] + jnp.sum(rows, axis=0)
            part = part + dot(low, w_ref[gate, cols, :])
    part_ref[...] = (part * keep).astype(BF16)


def finish_kernel(
    step_ref, p_ref, q_ref, gates_all, cells_all, ups_all, hidden_in, slope_in,
    gates_ref, cell_ref, prev_ref, slope_ref, up_ref, hidden_all, slope_all,
    hidden_buf, sems, hidden_sem,
):
    copies = fetches(
        step_ref[0], step_ref[1], (gates_all, cells_all, ups_all), (gates_ref, cell_ref, prev_ref, up_ref), sems
    )
    for copy in copies:
        copy.start()
    clipped(p_ref, q_ref, hidden_buf, slope_ref)
    hidden_copy = pltpu.make_async_copy(hidden_buf, hidden_all.at[step_ref[1]], hidden_sem)
    hidden_copy.start()
    for copy in copies:
        copy.wait()
    hidden_copy.wait()


def fetches(step, time, sources, targets, sems):
    gates_all, cells_all, ups_all = sources
    gates_ref, cell_ref, prev_ref, up_ref = targets
    before = jnp.maximum(step - 1, 0)
    return [
        pltpu.make_async_copy(gates_all.at[i, step], gates_ref.at[i], sems.at[i]) for i in range(PIECES)
    ] + [
        pltpu.make_async_copy(cells_all.at[step], cell_ref, sems.at[PIECES]),
        pltpu.make_async_copy(cells_all.at[before], prev_ref, sems.at[PIECES + 1]),
        pltpu.make_async_copy(ups_all.at[time], up_ref, sems.at[PIECES + 2]),
    ]


def aside_kernel(
    first, last, opens, passed, step_ref, dz_ref, raw_ref, gates_all, cells_all, ups_all, slope_all, *refs
):
    refs = refs[(0 if first else 4) + (0 if opens else 2) + passed :]
    gates_ref, cell_ref, prev_ref, slope_ref, up_ref = refs[:5]
    dz_all, raw_all, near_all, far_all, near_out, far_out = refs[5:11]
    sems, fetch_sems = refs[-2:]
    step, time_before = step_ref[0], step_ref[2]
    slot, low, high = step_ref[4], step_ref[5], step_ref[6]
    before = jnp.maximum(step - 1, 0)
    copies = []
    if not last:
        copies += fetches(
            before, time_before, (gates_all, cells_all, ups_all), (gates_ref, cell_ref, prev_ref, up_ref), fetch_sems
        )
        copies.append(pltpu.make_async_copy(slope_all.at[before], slope_ref, fetch_sems.at[PIECES + 3]))
    copies += [pltpu.make_async_copy(dz_ref.at[i], dz_all.at[i, step], sems.at[i]) for i in range(PIECES)]
    copies.append(pltpu.make_async_copy(raw_ref, raw_all.at[step], sems.at[PIECES]))
    copies.append(pltpu.make_async_copy(dz_ref.at[low], near_all.at[step], sems.at[PIECES + 1]))
    copies.append(pltpu.make_async_copy(dz_ref.at[HALVES + high], far_all.at[step], sems.at[PIECES + 2]))
    copies.append(pltpu.make_async_copy(dz_ref.at[1 - low], near_out.at[slot], sems.at[PIECES + 3]))
    copies.append(pltpu.make_async_copy(dz_ref.at[HALVES + 1 - high], far_out.at[slot], sems.at[PIECES + 4]))
    for copy in copies:
        copy.start()
    for copy in copies:
        copy.wait()


def input_grad_kernel(step_ref, dz_ref, wa_ref, wb_ref, out_ref, acc_ref):
    piece, gate = pl.program_id(0), pl.program_id(1)
    steps, streams, width = dz_ref.shape[1:]

    @pl.when((piece == 0) & (gate == 0))
    def _():
        acc_ref[...] = jnp.zeros(acc_ref.shape, F32)

    weights = jnp.where(piece < HALVES, wa_ref[0], wb_ref[0])
    acc_ref[...] += lax.dot_general(
        dz_ref[0].reshape(steps * streams, width), weights, (((1,), (1,)), ((), ())), preferred_element_type=F32
    )

    @pl.when((piece == PIECES - 1) & (gate == 3))
    def _():
        for step in range(steps):
            time = step_ref[0] + step_ref[1] * step
            out_ref[time] = acc_ref[step * streams : (step + 1) * streams, :]


def params(mib):
    return pltpu.CompilerParams(vmem_limit_bytes=mib * MIB)


def cost(flops, size):
    return pl.CostEstimate(flops=flops, bytes_accessed=size, transcendentals=0)


def body(inputs, w_in, w_rec, bias, proj, state_h, state_c, resets, stream_doc, cotangent):
    streams, steps, depth = inputs.shape[1:]
    cells = w_in.shape[3]
    width = cells // HALVES
    rank = lax.axis_index("gate")
    own = rank % 2
    gates_size = lax.axis_size("gate")
    swap = [(i, i ^ 1) for i in range(gates_size)]
    across = [(i, i ^ 2) for i in range(gates_size)]

    def pick(stacked, index):
        return lax.dynamic_index_in_dim(stacked, index, 0, keepdims=False)

    def trade(mine, theirs):
        return (mine, lax.ppermute(theirs, "gate", swap))

    def vmem(shape, dtype):
        return pltpu.VMEM(shape, dtype)

    def hbm(shape, dtype):
        return pltpu.HBM(shape, dtype)

    def by_gate(weights, index, keep=True):
        shape = (4,) + weights.shape[1:2] + weights.shape[3:]
        kept = (vmem(shape, BF16),) if keep else ()
        part = weights.shape[1] // 8
        return pl.pallas_call(
            functools.partial(layout_kernel, keep),
            out_shape=kept + (hbm(shape, BF16),),
            in_specs=[SMEM, ANY],
            out_specs=[VMEM] * len(kept) + [ANY],
            scratch_shapes=([] if kept else [pltpu.VMEM(shape, BF16)])
            + [
                pltpu.VMEM((3, part) + weights.shape[2:], BF16),
                pltpu.SemaphoreType.DMA((3,)),
                pltpu.SemaphoreType.DMA((8,)),
            ],
            compiler_params=params(8),
            name="layout",
        )(jnp.full((1,), index, jnp.int32), in_hbm(weights))

    win_b, rec_b = (lax.ppermute(by_gate(w, 1 - own, False)[0], "gate", swap) for w in (w_in, w_rec))
    (win_av, win_a), (rec_av, rec_a) = by_gate(w_in, own), by_gate(w_rec, own)
    proj_a, proj_b = trade(pick(proj, own), pick(proj, 1 - own))
    bias_a, bias_b = trade(pick(bias, own), pick(bias, 1 - own))

    def pieces_of(pair):
        split = [x.reshape(4, HALVES, width) for x in pair]
        return jnp.transpose(jnp.stack(split), (0, 2, 1, 3)).reshape(PIECES, 1, 4 * width)

    bias_p = pieces_of((bias_a, bias_b)).astype(F32)

    def cells_to_pieces(pair):
        both = jnp.stack(pair).reshape(QUARTERS, streams, HALVES, width)
        return jnp.transpose(both, (0, 2, 1, 3)).reshape(PIECES, streams, width)

    def by_time(stacked):
        return jnp.transpose(pick(stacked, own), (1, 0, 2))

    feats = by_time(inputs)
    ups = by_time(cotangent)
    flags = resets.astype(F32)
    later = jnp.concatenate([flags[:, 1:], jnp.zeros_like(flags[:, :1])], axis=1)
    keep = 1.0 - jnp.where(own == 0, flags, later)
    keep = jnp.broadcast_to(jnp.transpose(keep)[:, :, None], (steps, streams, 128))

    docs_h = state_h[stream_doc]
    docs_c = state_c[stream_doc]
    start_h = pick(jnp.transpose(docs_h, (1, 0, 2)), own).astype(BF16)
    by_dir_c = jnp.transpose(docs_c, (1, 0, 2))
    start_c = cells_to_pieces(trade(pick(by_dir_c, own), pick(by_dir_c, 1 - own)))

    def at_step(step):
        near = jnp.array([step, step, max(step - 1, 0), min(step + 1, steps - 1)], jnp.int32)
        turned = jnp.array([step] + [steps - 1 - x for x in (step, max(step - 1, 0), min(step + 1, steps - 1))], jnp.int32)
        return jnp.where(own == 0, near, turned)

    n_batch = lax.axis_size("batch")
    spot = lax.axis_index("batch")
    low, high = spot % 2, (spot // 2) % 2
    near_swap = [(i, i ^ 1) for i in range(n_batch)]
    far_swap = [(i, i ^ 2) for i in range(n_batch)]

    def swapped(array, pairs):
        return lax.ppermute(array, "batch", pairs)

    turn = jnp.where(own == 0, jnp.array([0, 1], jnp.int32), jnp.array([steps - 1, -1], jnp.int32))
    feats_v, feat_all = pl.pallas_call(
        order_kernel,
        out_shape=(vmem(feats.shape, BF16), hbm(feats.shape, BF16)),
        in_specs=[SMEM, ANY],
        out_specs=[VMEM, ANY],
        scratch_shapes=[pltpu.SemaphoreType.DMA((steps,)), pltpu.SemaphoreType.DMA],
        compiler_params=params(1),
        name="order",
    )(turn, feats)
    feat_in = (swapped(feat_all, near_swap), swapped(feat_all, far_swap))
    keep_v, bias_v, win_bv = place(keep, bias_p, win_b)
    rec_bv, proj_av, proj_bv, start_hv, start_cv = place(rec_b, proj_a, proj_b, start_h, start_c)

    gates_shape, cell_shape = (PIECES, streams, 4 * width), (PIECES, streams, width)
    bias_shape = (PIECES, 8, 4 * width)
    inflow = pl.pallas_call(
        inflow_kernel,
        out_shape=vmem(gates_shape, F32),
        in_specs=[SMEM] + [VMEM] * 4,
        out_specs=VMEM,
        compiler_params=params(8),
        name="inflow",
    )(turn, pinned(feats_v), pinned(bias_v), pinned(win_av), pinned(win_bv))

    def forward_call(first, step, part, peer, cell, inflow):
        return pl.pallas_call(
            functools.partial(forward_kernel, first),
            out_shape=(
                vmem((streams, depth), BF16),
                vmem(cell_shape, F32),
                vmem(gates_shape, BF16),
                vmem(cell_shape, BF16),
                vmem((streams, depth), BF16),
                vmem((streams, depth), BF16),
                vmem((streams, depth), F32),
            ),
            in_specs=[SMEM] + [VMEM] * 10,
            out_specs=[VMEM] * 7,
            compiler_params=params(8),
            name="forward_step",
        )(
            at_step(step), pinned(part), pinned(peer), pinned(start_hv), pinned(keep_v), pinned(cell), pinned(inflow),
            pinned(rec_av), pinned(rec_bv), pinned(proj_av), pinned(proj_bv),
        )

    def between_call(step, fresh, stacks, passing=()):
        shapes = (
            hbm((PIECES, steps, streams, 4 * width), BF16),
            hbm((steps,) + cell_shape, F32),
            hbm((PIECES, steps, streams, width), BF16),
            hbm((steps, streams, depth), BF16),
            hbm((steps, streams, depth), BF16),
            hbm((steps, streams, depth), F32),
        )
        aliases = {11 + i: 1 + i for i in range(len(stacks))}
        aliases.update({11 + len(stacks) + i: 7 + i for i in range(len(passing))})
        inflow, *out = pl.pallas_call(
            functools.partial(between_kernel, not stacks, step == steps - 1, len(passing)),
            out_shape=(vmem(gates_shape, F32),) + shapes + tuple(hbm(x.shape, x.dtype) for x in passing),
            in_specs=[SMEM] + [VMEM] * 10 + [ANY] * (len(stacks) + len(passing)),
            out_specs=[VMEM] + [ANY] * (6 + len(passing)),
            scratch_shapes=[pltpu.SemaphoreType.DMA((2 * PIECES + 4,))],
            input_output_aliases=aliases,
            compiler_params=params(8),
            cost_estimate=cost(2 * streams * depth * 8 * cells, 8 * depth * cells * 2),
            name="between",
        )(
            at_step(step), pinned(feats_v), pinned(bias_v), pinned(win_av), pinned(win_bv),
            *(pinned(x) for x in fresh), *(in_hbm(x) for x in (*stacks, *passing)),
        )
        return inflow, tuple(out[:6]), tuple(out[6:])

    none = jnp.zeros((streams, depth), BF16)
    part, peer, cell, stacks = none, none, start_cv, ()
    for step in range(steps):
        part, cell, *fresh = forward_call(step == 0, step, part, peer, cell, inflow)
        peer = lax.ppermute(part, "gate", across)
        due = step == (2 * steps) // 3
        inflow, stacks, passed = between_call(step, (cell, *fresh), stacks, feat_in if due else ())
        feat_in = passed if due else feat_in
    gates_all, cells_all, mixed_all, prev_all, hidden_all, slope_all = stacks
    prev_in = (swapped(prev_all, near_swap), swapped(prev_all, far_swap))

    saved_shapes = (
        vmem(gates_shape, BF16),
        vmem(cell_shape, F32),
        vmem(cell_shape, F32),
        vmem((streams, depth), F32),
        vmem((streams, depth), BF16),
    )
    *saved, hidden_all, slope_all = pl.pallas_call(
        finish_kernel,
        out_shape=saved_shapes + (hbm((steps, streams, depth), BF16), hbm((steps, streams, depth), F32)),
        in_specs=[SMEM, VMEM, VMEM] + [ANY] * 5,
        out_specs=[VMEM] * 5 + [ANY] * 2,
        scratch_shapes=[
            pltpu.VMEM((streams, depth), BF16),
            pltpu.SemaphoreType.DMA((PIECES + 4,)),
            pltpu.SemaphoreType.DMA,
        ],
        input_output_aliases={6: 5, 7: 6},
        compiler_params=params(8),
        name="finish",
    )(
        at_step(steps - 1), pinned(part), pinned(peer), in_hbm(gates_all), in_hbm(cells_all), in_hbm(ups),
        in_hbm(hidden_all), in_hbm(slope_all),
    )

    rec_atv, rec_btv, proj_atv, proj_btv = pl.pallas_call(
        turned_kernel,
        out_shape=(vmem((4, cells, depth), BF16),) * 2 + (vmem((depth, cells), BF16),) * 2,
        in_specs=[ANY] * 4,
        out_specs=[VMEM] * 4,
        scratch_shapes=[
            pltpu.VMEM((3, depth, cells), BF16),
            pltpu.SemaphoreType.DMA((3,)),
            pltpu.VMEM((2, cells, depth), BF16),
            pltpu.SemaphoreType.DMA((2,)),
        ],
        compiler_params=params(8),
        name="turned",
    )(*(in_hbm(x) for x in (rec_a, rec_b, proj_a, proj_b)))

    def backward_call(step, part, peer, grad, bias, saved):
        return pl.pallas_call(
            backward_kernel,
            out_shape=(
                vmem((streams, depth), BF16),
                vmem(cell_shape, F32),
                vmem(bias_shape, F32),
                vmem((streams, depth), BF16),
                vmem(gates_shape, BF16),
            ),
            in_specs=[SMEM] + [VMEM] * 15,
            out_specs=[VMEM] * 5,
            compiler_params=params(8),
            name="backward_step",
        )(
            at_step(step), pinned(part), pinned(peer), pinned(keep_v), pinned(grad), pinned(bias),
            pinned(rec_atv), pinned(rec_btv), pinned(proj_atv), pinned(proj_btv),
            *(pinned(x) for x in saved), pinned(start_cv),
        )

    def aside_call(step, slot, slots, dz, raw, stacks, sends, passing):
        piece_shape = (streams, 4 * width)
        shapes = (
            hbm((PIECES, steps) + piece_shape, BF16),
            hbm((steps, streams, depth), BF16),
            hbm((steps,) + piece_shape, BF16),
            hbm((steps,) + piece_shape, BF16),
            hbm((slots,) + piece_shape, BF16),
            hbm((slots,) + piece_shape, BF16),
        )
        kept = len(stacks)
        aliases = {7 + i: 5 + i for i in range(kept)}
        aliases.update({7 + kept + i: 9 + i for i in range(len(sends))})
        aliases.update({7 + kept + len(sends) + i: 11 + i for i in range(len(passing))})
        out = pl.pallas_call(
            functools.partial(aside_kernel, not stacks, step == 0, not sends, len(passing)),
            out_shape=saved_shapes + shapes + tuple(hbm(x.shape, x.dtype) for x in passing),
            in_specs=[SMEM] + [VMEM] * 2 + [ANY] * (4 + kept + len(sends) + len(passing)),
            out_specs=[VMEM] * 5 + [ANY] * (6 + len(passing)),
            scratch_shapes=[
                pltpu.SemaphoreType.DMA((PIECES + 5,)),
                pltpu.SemaphoreType.DMA((PIECES + 4,)),
            ],
            input_output_aliases=aliases,
            compiler_params=params(8),
            cost_estimate=cost(0, 8 * MIB),
            name="aside",
        )(
            jnp.concatenate([at_step(step), jnp.stack([jnp.int32(slot), low, high])]), pinned(dz), pinned(raw),
            in_hbm(gates_all), in_hbm(cells_all), in_hbm(ups), in_hbm(slope_all),
            *(in_hbm(x) for x in (*stacks, *sends, *passing)),
        )
        return out[:5], tuple(out[5:9]), tuple(out[9:11]), tuple(out[11:])

    carry = (none, none, jnp.zeros(cell_shape, F32), jnp.zeros(bias_shape, F32), saved, ())
    pending, arrived, ready, top = [(steps - 1 - steps // 3, prev_in)], [], None, steps
    for index, share in enumerate(SHARES):
        slots = top if index == len(SHARES) - 1 else round(share * steps)
        sends = ()
        for step in range(top - 1, top - slots - 1, -1):
            part, peer, grad, bias_sum, saved, stacks = carry
            part, grad, bias_sum, raw, dz = backward_call(step, part, peer, grad, bias_sum, saved)
            peer = lax.ppermute(part, "gate", across)
            if ready is not None:
                due, sides = ready
                sides = after((part,), *sides) if step else sides
                pending.append((due, (swapped(sides[0], near_swap), swapped(sides[1], far_swap))))
                ready = None
            passing = pending.pop(0)[1] if pending and pending[0][0] >= step else ()
            saved, stacks, sends, passed = aside_call(
                step, step - (top - slots), slots, dz, raw, stacks, sends, passing
            )
            arrived += [passed] if passed else []
            carry = (part, peer, grad, bias_sum, saved, stacks)
        top -= slots
        ready = (max(top - 1 - (3 * slots + 3) // 4, 0 if slots > 2 else -1), sends)
    pending.append((-1, (swapped(sends[0], near_swap), swapped(sends[1], far_swap))))
    arrived += [arrays for _, arrays in pending]
    dz_all, raw_all, near_all, far_all = carry[-1]
    bias_sum = carry[3]
    prev_in, exchanged = arrived[0], arrived[1:]
    rows = steps * streams

    def by_direction(mine, theirs):
        return jnp.stack([jnp.where(own == 0, mine, theirs), jnp.where(own == 0, theirs, mine)])

    def line_sum(chunks, axis, stride, count, first=None, gates={}):
        here = (spot // stride) % count

        def chunk(index):
            return lax.dynamic_index_in_dim(chunks, jnp.clip(index, 0, count - 1), axis, keepdims=False)

        def at(device):
            return (device // stride) % count

        if count == 2:
            pairs = [(i, i + stride if at(i) == 0 else i - stride) for i in range(n_batch)]
            return (chunk(here).astype(F32) + swapped(chunk(1 - here), pairs).astype(F32)).astype(BF16)
        ends = [(i, i + stride) for i in range(n_batch) if at(i) == 0]
        ends += [(i, i - stride) for i in range(n_batch) if at(i) == count - 1]
        up = down = swapped(chunk(jnp.where(here == 0, count - 1, 0)) if first is None else first, ends)
        for slot in range(2, count):
            if slot in gates:
                up, down = gates[slot](up, down)
            rise = (chunk(here + count - slot).astype(F32) + up.astype(F32)).astype(BF16)
            fall = (chunk(here - count + slot).astype(F32) + down.astype(F32)).astype(BF16)
            up = swapped(rise, [(i, i + stride) for i in range(n_batch) if at(i) < min(slot, count - 1)])
            down = swapped(fall, [(i, i - stride) for i in range(n_batch) if at(i) > max(count - 1 - slot, 0)])
        if count in gates:
            up, down = gates[count](up, down)
        return (chunk(here).astype(F32) + up.astype(F32) + down.astype(F32)).astype(BF16)

    line = n_batch // 2
    share_rows = depth // n_batch

    def input_grad_of(dz):
        return pl.pallas_call(
            input_grad_kernel,
            out_shape=jax.ShapeDtypeStruct((steps, streams, depth), F32),
            grid_spec=pltpu.PrefetchScalarGridSpec(
                num_scalar_prefetch=1,
                grid=(PIECES, 4),
                in_specs=[
                    pl.BlockSpec((1, steps, streams, width), lambda p, g, turn: (p, 0, 0, g)),
                    pl.BlockSpec(
                        (1, depth, width), lambda p, g, turn: (jnp.where(p < 2, g, 3), 0, jnp.where(p < 2, p, 1))
                    ),
                    pl.BlockSpec(
                        (1, depth, width), lambda p, g, turn: (jnp.where(p < 2, 0, g), 0, jnp.where(p < 2, 0, p - 2))
                    ),
                ],
                out_specs=pl.BlockSpec((steps, streams, depth), lambda p, g, turn: (0, 0, 0)),
                scratch_shapes=[pltpu.VMEM((rows, depth), F32)],
            ),
            compiler_params=params(16),
            cost_estimate=cost(0, 0),
            name="input_grad",
        )(turn, dz, in_hbm(win_a), in_hbm(win_b))

    grad_proj = jnp.einsum("ptnc,tnk->pkc", mixed_all, raw_all, preferred_element_type=F32).astype(BF16)
    grad_proj = grad_proj.reshape(PIECES, line, 2, share_rows, width)
    own_cells = cells // n_batch
    bias_rows = jnp.sum(bias_sum, axis=1).reshape(QUARTERS, HALVES, 4, width)
    bias_rows = jnp.transpose(bias_rows, (0, 2, 1, 3)).reshape(QUARTERS, 4, line, 2, own_cells)
    bias_rows = jnp.transpose(bias_rows, (2, 3, 0, 1, 4)).reshape(line, 2, -1)
    bias_rows = jnp.pad(bias_rows, ((0, 0), (0, 0), (0, PIECES * width - bias_rows.shape[2])))
    bias_rows = jnp.transpose(bias_rows.reshape(line, 2, PIECES, 1, width), (2, 0, 1, 3, 4)).astype(BF16)
    grad_proj = jnp.concatenate([grad_proj, bias_rows], axis=3)

    def with_partner(grad):
        mine = lax.dynamic_index_in_dim(grad, low, grad.ndim - 3, keepdims=False)
        sent = lax.dynamic_index_in_dim(grad, 1 - low, grad.ndim - 3, keepdims=False)
        taken = swapped(sent, near_swap)
        return sent, taken, (mine.astype(F32) + taken.astype(F32)).astype(BF16)

    def across_two(grad):
        return line_sum(grad.reshape(grad.shape[:-3] + (line // 2, 2) + grad.shape[-2:]), grad.ndim - 3, 4, line // 2)

    proj_sent, proj_taken, proj_y = with_partner(grad_proj)

    lows, count = [], 0
    for x in exchanged[::-1]:
        lows.insert(0, count)
        count += x[0].shape[0]

    def gathered(kept, feat, prev, parts):
        return pl.pallas_call(
            functools.partial(gather_kernel, tuple(lows[: len(parts)])),
            out_shape=(vmem((2 * steps, streams, 2 * depth), BF16), vmem((2 * steps, streams, 4 * width), BF16)),
            in_specs=[ANY] * (5 + len(parts)),
            out_specs=[VMEM] * 2,
            scratch_shapes=[pltpu.SemaphoreType.DMA((5 + len(parts),))],
            compiler_params=params(1),
            cost_estimate=cost(0, 0),
            name="gather",
        )(*(in_hbm(x) for x in (feat_all, prev_all, feat, prev, kept, *parts)))

    def completed(begin, rows_out, left, right, parts):
        return pl.pallas_call(
            functools.partial(late_kernel, tuple(lows[len(lows) - len(parts) :])),
            out_shape=(vmem(right.shape, BF16), jax.ShapeDtypeStruct((2, max(rows_out, 8), 4 * width), BF16)),
            in_specs=[SMEM] + [VMEM] * 2 + [ANY] * len(parts),
            out_specs=[VMEM] * 2,
            scratch_shapes=[pltpu.SemaphoreType.DMA((len(parts),))],
            input_output_aliases={2: 0},
            compiler_params=params(16),
            cost_estimate=cost(0, 0),
            name="late",
        )(begin, pinned(left), pinned(right), *(in_hbm(x) for x in parts))

    def multiplied(left, right):
        return pl.pallas_call(
            product_kernel,
            out_shape=jax.ShapeDtypeStruct((2, depth, 4 * width), BF16),
            in_specs=[VMEM] * 2,
            out_specs=VMEM,
            compiler_params=params(16),
            cost_estimate=cost(0, 0),
            name="product",
        )(pinned(left), pinned(right))

    near_parts, far_parts = zip(*exchanged)
    begin = jnp.where(spot // 2 == 0, line - 1, 0)
    chunk_rows = 2 * share_rows if 2 * share_rows % 128 == 0 else 0
    near_left, near_right = gathered(near_all, feat_in[0], prev_in[0], near_parts[:-LATE])
    near_late = after((near_left, proj_sent, *far_parts[-LATE:]), *near_parts[-LATE:])
    near_right, first = completed(jnp.full((1,), begin, jnp.int32), chunk_rows, near_left, near_right, near_late)
    far_all, *far_parts = after((first,), far_all, *far_parts)
    far_left, far_right = gathered(far_all, feat_in[1], prev_in[1], far_parts[:-LATE])
    far_right, _ = completed(jnp.zeros((1,), jnp.int32), 0, far_left, far_right, far_parts[-LATE:])
    far = multiplied(far_left, far_right).reshape(2, line, 2, share_rows, 4 * width)
    near = multiplied(near_left, near_right).reshape(2, line, 2, share_rows, 4 * width)

    def states_of(hidden, cell):
        both_hidden = trade(hidden, hidden)

        hidden_dirs = by_direction(*both_hidden)
        outputs = (inputs.astype(F32) + jnp.transpose(hidden_dirs, (0, 2, 1, 3)).astype(F32)).astype(BF16)
        last_h = jnp.stack([hidden_dirs[0, steps - 1], hidden_dirs[1, 0]], axis=1).astype(F32)
        final_h = jnp.zeros_like(state_h).at[stream_doc].set(last_h)
        last_c = jnp.transpose(cell.reshape(QUARTERS, HALVES, streams, width), (0, 2, 1, 3)).reshape(
            QUARTERS, streams, cells
        )
        last_dirs = by_direction(*trade(last_c[0], last_c[1]))
        final_c = jnp.zeros_like(state_c).at[stream_doc].set(jnp.transpose(last_dirs, (1, 0, 2)))
        return outputs, final_h, final_c

    tokens = {}

    def second(up, down):
        up, sent, tokens["dz"], proj_sum = after((), up, far, dz_all, proj_y)
        tokens["in"], tokens["rec"] = (with_partner(sent[i])[2] for i in range(2))
        tokens["proj"] = across_two(proj_sum)
        return up, up

    def third(up, down):
        dx = input_grad_of(tokens["dz"])
        up, down, tokens["dx"], in_sum, tokens["proj"], hidden, last_cell = after(
            (), up, down, dx, tokens["in"], tokens["proj"], hidden_all, cell
        )
        tokens["in"] = across_two(in_sum)
        tokens["states"] = states_of(hidden, last_cell)
        return up, down

    def final(up, down):
        up, down, tokens["in"], rec_sum = after(tokens["states"], up, down, tokens["in"], tokens["rec"])
        tokens["rec"] = across_two(rec_sum)
        return up, down

    gates = {2: second, 3: third, line: final} if line > 3 else {}
    first = first.reshape(2, 2, share_rows, 4 * width) if chunk_rows else None
    near = line_sum(near, 1, 2, line, first, gates)
    dx_all, (outputs, final_h, final_c) = tokens["dx"], tokens["states"]
    in_two, rec_two, proj_two = tokens["in"], tokens["rec"], tokens["proj"]

    def halves_of(summed, index, pairs):
        mine = lax.dynamic_index_in_dim(summed, index, 1, keepdims=False)
        return mine, swapped(lax.dynamic_index_in_dim(summed, 1 - index, 1, keepdims=False), pairs)

    near_pair = halves_of(near, low, near_swap)
    far_pair = halves_of(jnp.stack([in_two, rec_two]), high, far_swap)
    far_pair = [lax.ppermute(x, "gate", swap) for x in far_pair]
    proj_mine, proj_theirs = halves_of(proj_two, high, far_swap)
    grad_proj = proj_mine.astype(F32) + proj_theirs.astype(F32)
    grad_shape = (2, share_rows, 4, cells)
    grad_w_in, grad_w_rec = pl.pallas_call(
        assemble_kernel,
        out_shape=(jax.ShapeDtypeStruct(grad_shape, F32),) * 2,
        in_specs=[SMEM] + [VMEM] * 4,
        out_specs=[VMEM] * 2,
        compiler_params=params(14),
        name="assemble",
    )(jnp.stack([own, low, high]), *near_pair, *far_pair)

    def home(mine, theirs):
        return by_direction(*trade(mine, theirs)).astype(F32)

    shaped = grad_proj[:, share_rows].reshape(-1)[: QUARTERS * 4 * own_cells].reshape(QUARTERS, 4, own_cells)
    grad_bias = home(shaped[0], shaped[1])
    grad_proj = grad_proj[:, :share_rows].reshape(QUARTERS, HALVES, share_rows, width)
    grad_proj = jnp.transpose(grad_proj, (0, 1, 3, 2)).reshape(QUARTERS, cells, share_rows).astype(BF16)
    grad_proj = home(grad_proj[0], grad_proj[1])

    half_cols = depth // 2
    upper = rank // 2
    keep_cols = lax.dynamic_slice_in_dim(dx_all, upper * half_cols, half_cols, 2)
    send_cols = lax.dynamic_slice_in_dim(dx_all, (1 - upper) * half_cols, half_cols, 2).astype(BF16)
    dx_half = keep_cols + lax.ppermute(send_cols, "gate", across).astype(F32)
    up_half = lax.dynamic_slice_in_dim(ups, upper * half_cols, half_cols, 2).astype(F32)
    dx_half = (dx_half + up_half).astype(BF16)
    quarter_cols = half_cols // 2
    mine = lax.dynamic_slice_in_dim(dx_half, own * quarter_cols, quarter_cols, 2)
    theirs = lax.dynamic_slice_in_dim(dx_half, (1 - own) * quarter_cols, quarter_cols, 2)
    dx_dirs = by_direction(*trade(mine, theirs))
    input_grad = jnp.transpose(dx_dirs, (0, 2, 1, 3))
    return (outputs, input_grad, grad_w_in, grad_w_rec, grad_bias, grad_proj, final_h, final_c)


def solution(mesh):
    placed = (
        P(None, "batch", None, None),
        P(None, None, None, "gate"),
        P(None, None, None, "gate"),
        P(None, None, "gate"),
        P(None, "gate", None),
        P("batch", None, None),
        P("batch", None, "gate"),
        P("batch", None),
        P("batch"),
        P(None, "batch", None, None),
    )
    return jax.shard_map(
        body,
        mesh=mesh,
        in_specs=placed,
        out_specs=(
            P(None, "batch", None, None),
            P(None, "batch", None, "gate"),
            P(None, "batch", None, "gate"),
            P(None, "batch", None, "gate"),
            P(None, None, ("gate", "batch")),
            P(None, "gate", "batch"),
            P("batch", None, None),
            P("batch", None, "gate"),
        ),
        check_vma=False,
    )
```

```python
import functools

import jax
import jax.numpy as jnp
from jax import lax
from jax.experimental import pallas as pl
from jax.experimental.pallas import tpu as pltpu
from jax.sharding import PartitionSpec as P

CLIP = 3.0
F32, BF16 = jnp.float32, jnp.bfloat16
QUARTERS, HALVES = 2, 2
PIECES = QUARTERS * HALVES
MIB = 2**20
LATE = 2
SHARES = (0.35, 0.3, 0.15, 0.1, 0.1)

VMEM = pl.BlockSpec(memory_space=pltpu.VMEM)
SMEM = pl.BlockSpec(memory_space=pltpu.SMEM)
ANY = pl.BlockSpec(memory_space=pl.ANY)


def pinned(array):
    return pltpu.with_memory_space_constraint(array, pltpu.VMEM)


def in_hbm(array):
    return pltpu.with_memory_space_constraint(array, pltpu.HBM)


def dot(left, right):
    return jnp.dot(left, right, preferred_element_type=F32)


def place_kernel(count, *refs):
    sources, targets, sems = refs[:count], refs[count : 2 * count], refs[2 * count]
    copies = [pltpu.make_async_copy(a, b, sems.at[i]) for i, (a, b) in enumerate(zip(sources, targets))]
    for copy in copies:
        copy.start()
    for copy in copies:
        copy.wait()


def place(*arrays):
    count = len(arrays)
    return pl.pallas_call(
        functools.partial(place_kernel, count),
        out_shape=tuple(pltpu.VMEM(x.shape, x.dtype) for x in arrays),
        in_specs=[ANY] * count,
        out_specs=[VMEM] * count,
        scratch_shapes=[pltpu.SemaphoreType.DMA((count,))],
        compiler_params=params(1),
        name="place",
    )(*(in_hbm(x) for x in arrays))


def layout_kernel(keep, which_ref, w_ref, first_ref, second_ref, buf, sems, out_sems):
    out_ref, all_ref = (first_ref, second_ref) if keep else (second_ref, first_ref)
    depth, part = w_ref.shape[1], buf.shape[1]

    def fetch(i):
        return pltpu.make_async_copy(w_ref.at[which_ref[0], pl.ds(i * part, part)], buf.at[i % 3], sems.at[i % 3])

    def store(i):
        rows = pl.ds(i * part, part)
        return pltpu.make_async_copy(out_ref.at[:, rows], all_ref.at[:, rows], out_sems.at[i])

    count = depth // part
    for i in range(min(2, count)):
        fetch(i).start()
    for i in range(count):
        if i + 2 < count:
            fetch(i + 2).start()
        fetch(i).wait()
        out_ref[:, i * part : (i + 1) * part, :] = jnp.swapaxes(buf[i % 3], 0, 1)
        store(i).start()
    for i in range(count):
        store(i).wait()


def turned_kernel(wa_ref, wb_ref, pa_ref, pb_ref, wat_ref, wbt_ref, pat_ref, pbt_ref, buf, sems, proj_buf, proj_sems):
    jobs = [(w_ref, out_ref, gate) for w_ref, out_ref in ((wa_ref, wat_ref), (wb_ref, wbt_ref)) for gate in range(4)]

    def fetch(i):
        return pltpu.make_async_copy(jobs[i][0].at[jobs[i][2]], buf.at[i % 3], sems.at[i % 3])

    proj_fetches = [pltpu.make_async_copy(x, proj_buf.at[i], proj_sems.at[i]) for i, x in enumerate((pa_ref, pb_ref))]
    fetch(0).start()
    fetch(1).start()
    for copy in proj_fetches:
        copy.start()
    for i, (_, out_ref, gate) in enumerate(jobs):
        if i + 2 < len(jobs):
            fetch(i + 2).start()
        fetch(i).wait()
        for half in range(HALVES):
            width = buf.shape[2] // HALVES
            cols = slice(half * width, (half + 1) * width)
            out_ref[gate, cols, :] = buf[i % 3, :, cols].T
    for i, out_ref in enumerate((pat_ref, pbt_ref)):
        proj_fetches[i].wait()
        out_ref[...] = proj_buf[i].T


def pass_kernel(*refs):
    pass


def after(tokens, *arrays, free=0):
    count = len(tokens)
    return pl.pallas_call(
        pass_kernel,
        out_shape=tuple(jax.ShapeDtypeStruct(x.shape, x.dtype) for x in arrays),
        in_specs=[ANY] * (count + len(arrays)),
        out_specs=[ANY] * len(arrays),
        input_output_aliases={count + i: i for i in range(len(arrays))},
        compiler_params=params(1),
        name="after",
    )(*tokens, *(in_hbm(x) if x.size * x.dtype.itemsize > free else x for x in arrays))


def gather_kernel(lows, *refs):
    (feat_ref, prev_ref, feat_too, prev_too, kept_ref), refs = refs[:5], refs[5:]
    groups, (left_ref, right_ref, sems) = refs[:-3], refs[-3:]
    steps, _, depth = feat_ref.shape
    jobs = [
        (feat_ref, left_ref.at[:steps, :, :depth]),
        (prev_ref, left_ref.at[:steps, :, depth:]),
        (feat_too, left_ref.at[steps:, :, :depth]),
        (prev_too, left_ref.at[steps:, :, depth:]),
        (kept_ref, right_ref.at[:steps]),
    ]
    jobs += [(x, right_ref.at[steps + low : steps + low + x.shape[0]]) for x, low in zip(groups, lows)]
    copies = [pltpu.make_async_copy(a, b, sems.at[i]) for i, (a, b) in enumerate(jobs)]
    for copy in copies:
        copy.start()
    for copy in copies:
        copy.wait()


def late_kernel(lows, begin_ref, left_ref, right_in, *refs):
    groups, (right_ref, first_ref, sems) = refs[:-3], refs[-3:]
    steps = left_ref.shape[0] // 2
    copies = [
        pltpu.make_async_copy(x, right_ref.at[steps + low : steps + low + x.shape[0]], sems.at[i])
        for i, (x, low) in enumerate(zip(groups, lows))
    ]
    for copy in copies:
        copy.start()
    for copy in copies:
        copy.wait()
    if first_ref.shape[1] % 128:
        return
    share, depth = first_ref.shape[1], left_ref.shape[2] // 2
    rows = left_ref.shape[0] * left_ref.shape[1]
    left = [
        left_ref[:, :, pl.ds(pl.multiple_of(i * depth + begin_ref[0] * share, 128), share)].reshape(rows, share)
        for i in range(2)
    ]
    left = jnp.concatenate([x.T for x in left], axis=0)
    width = right_ref.shape[2] // 4

    def columns(i, _):
        cols = pl.ds(pl.multiple_of(i * width, width), width)
        total = dot(left, right_ref[:, :, cols].reshape(rows, width)).astype(BF16)
        first_ref[0, :, cols] = total[:share]
        first_ref[1, :, cols] = total[share:]
        return 0

    lax.fori_loop(0, 4, columns, 0)


def product_kernel(left_ref, right_ref, out_ref):
    rows, depth = left_ref.shape[0] * left_ref.shape[1], left_ref.shape[2] // 2
    width = right_ref.shape[2] // 4
    for which in range(2):
        left = left_ref[:, :, which * depth : (which + 1) * depth].reshape(rows, depth).T

        def columns(i, _):
            cols = pl.ds(pl.multiple_of(i * width, width), width)
            out_ref[which, :, cols] = dot(left, right_ref[:, :, cols].reshape(rows, width)).astype(BF16)
            return 0

        lax.fori_loop(0, 4, columns, 0)


def assemble_kernel(place_ref, near_a, near_b, far_a, far_b, in_ref, rec_ref):
    own, low, high = place_ref[0], place_ref[1], place_ref[2]
    width = in_ref.shape[3] // HALVES
    for direction, mine_ref, theirs_ref, index in ((own, near_a, near_b, low), (1 - own, far_a, far_b, high)):
        for which, out_ref in ((0, in_ref), (1, rec_ref)):
            mine, theirs = mine_ref[which].astype(F32), theirs_ref[which].astype(F32)
            for half in range(HALVES):
                whole = jnp.where(index == half, mine, theirs)
                gates = jnp.stack([whole[:, gate * width : (gate + 1) * width] for gate in range(4)])
                out_ref[direction, :, :, half * width : (half + 1) * width] = jnp.swapaxes(gates, 0, 1)


def order_kernel(step_ref, feat_ref, out_ref, all_ref, sems):
    copies = []
    for i in range(feat_ref.shape[0]):
        source = feat_ref.at[step_ref[0] + step_ref[1] * i]
        copies.append(pltpu.make_async_copy(source, out_ref.at[i], sems.at[2 * i]))
        copies.append(pltpu.make_async_copy(source, all_ref.at[i], sems.at[2 * i + 1]))
    for copy in copies:
        copy.start()
    for copy in copies:
        copy.wait()


def numbers_kernel(in_ref, out_ref):
    for i in range(in_ref.shape[0]):
        out_ref[i] = in_ref[i]


def bias_kernel(sum_ref, out_ref):
    width = sum_ref.shape[2] // 4
    for piece in range(PIECES):
        for gate in range(4):
            out_ref[piece, gate : gate + 1, :] = jnp.sum(
                sum_ref[piece, :, gate * width : (gate + 1) * width], axis=0, keepdims=True
            )


def pieces(refs, axis):
    for piece in range(PIECES):
        quarter, half = divmod(piece, HALVES)
        width = refs[0].shape[axis] // HALVES
        yield piece, quarter, width, slice(half * width, (half + 1) * width)


def forward_kernel(
    first, step_ref, p_ref, q_ref, start_ref, keep_ref, cell_ref, inflow_ref, wa_ref, wb_ref, pa_ref, pb_ref,
    part_ref, next_ref, gates_ref, mixed_ref, prev_ref, hidden_ref, slope_ref,
):
    keep = keep_ref[step_ref[1]][:, :1]
    if first:
        hidden = start_ref[...]
    else:
        hidden = clipped(p_ref, q_ref, hidden_ref, slope_ref)
    hidden = hidden * keep.astype(BF16)
    prev_ref[...] = hidden
    part = jnp.zeros(part_ref.shape, F32)
    for piece, quarter, width, cols in pieces((wa_ref, wb_ref), 2):
        w_ref, proj_ref = ((wa_ref, pa_ref), (wb_ref, pb_ref))[quarter]
        acts = []
        for gate in range(4):
            place = slice(gate * width, (gate + 1) * width)
            pre = dot(hidden, w_ref[gate, :, cols]) + inflow_ref[piece, :, place]
            act = jnp.tanh(pre if gate == 2 else 0.5 * pre)
            gates_ref[piece, :, place] = act.astype(BF16)
            acts.append(act if gate == 2 else 0.5 + 0.5 * act)
        ingate, forget, candidate, outgate = acts
        cell = CLIP * jnp.tanh((forget * (keep * cell_ref[piece]) + ingate * candidate) * (1.0 / CLIP))
        next_ref[piece] = cell
        mixed = (outgate * jnp.tanh(cell)).astype(BF16)
        mixed_ref[piece] = mixed
        part = part + dot(mixed, proj_ref[cols, :])
    part_ref[...] = part.astype(BF16)


def clipped(p_ref, q_ref, hidden_ref, slope_ref):
    squash = jnp.tanh((p_ref[...].astype(F32) + q_ref[...].astype(F32)) * (1.0 / CLIP))
    hidden = (CLIP * squash).astype(BF16)
    hidden_ref[...] = hidden
    slope_ref[...] = 1.0 - squash * squash
    return hidden


def between_kernel(
    first, last, passed, step_ref, feat_ref, ba_ref, bb_ref, wa_ref, wb_ref, cell_ref, gates_ref, mixed_ref, prev_ref, hidden_ref,
    slope_ref, *refs,
):
    refs = refs[(0 if first else 6) + passed :]
    out_ref, gates_all, cells_all, mixed_all, prev_all, hidden_all, slope_all = refs[:7]
    sems = refs[-1]
    step, time_before = step_ref[0], step_ref[2]
    copies = [pltpu.make_async_copy(gates_ref.at[i], gates_all.at[i, step], sems.at[i]) for i in range(PIECES)]
    copies += [
        pltpu.make_async_copy(mixed_ref.at[i], mixed_all.at[i, step], sems.at[PIECES + i]) for i in range(PIECES)
    ]
    copies.append(pltpu.make_async_copy(cell_ref, cells_all.at[step], sems.at[2 * PIECES]))
    copies.append(pltpu.make_async_copy(prev_ref, prev_all.at[step], sems.at[2 * PIECES + 1]))
    if not first:
        copies.append(pltpu.make_async_copy(hidden_ref, hidden_all.at[time_before], sems.at[2 * PIECES + 2]))
        copies.append(pltpu.make_async_copy(slope_ref, slope_all.at[step - 1], sems.at[2 * PIECES + 3]))
    for copy in copies:
        copy.start()
    if not last:
        inflow_into(feat_ref[step + 1], ba_ref, bb_ref, wa_ref, wb_ref, out_ref)
    for copy in copies:
        copy.wait()


def inflow_into(feat, ba_ref, bb_ref, wa_ref, wb_ref, out_ref):
    for piece, quarter, width, cols in pieces((wa_ref, wb_ref), 2):
        w_ref, bias_ref = ((wa_ref, ba_ref), (wb_ref, bb_ref))[quarter]
        for gate in range(4):
            place = slice(gate * width, (gate + 1) * width)
            out_ref[piece, :, place] = dot(feat, w_ref[gate, :, cols]) + bias_ref[gate : gate + 1, cols]


def inflow_kernel(feat_ref, ba_ref, bb_ref, wa_ref, wb_ref, out_ref):
    inflow_into(feat_ref[0], ba_ref, bb_ref, wa_ref, wb_ref, out_ref)


def backward_kernel(
    step_ref, p_ref, q_ref, keep_ref, grad_ref, bias_ref, wa_ref, wb_ref, pa_ref, pb_ref,
    gates_ref, cell_ref, prev_ref, slope_ref, up_ref, start_ref,
    part_ref, next_ref, sum_ref, raw_ref, dz_ref,
):
    step = step_ref[0]
    keep = keep_ref[step_ref[1]][:, :1]
    raw = (up_ref[...].astype(F32) + (p_ref[...].astype(F32) + q_ref[...].astype(F32))) * slope_ref[...]
    raw = raw.astype(BF16)
    raw_ref[...] = raw
    part = jnp.zeros(part_ref.shape, F32)
    for piece, quarter, width, cols in pieces((wa_ref, wb_ref), 1):
        w_ref, proj_ref = ((wa_ref, pa_ref), (wb_ref, pb_ref))[quarter]
        mixed = dot(raw, proj_ref[:, cols])
        acts = [gates_ref[piece, :, gate * width : (gate + 1) * width].astype(F32) for gate in range(4)]
        ingate, forget, outgate = (0.5 + 0.5 * acts[gate] for gate in (0, 1, 3))
        slopes = [1.0 - act * act for act in acts]
        cell = cell_ref[piece]
        prev = keep * jnp.where(step == 0, start_ref[piece], prev_ref[piece])
        squash = jnp.tanh(cell)
        total = grad_ref[piece] + mixed * outgate * (1.0 - squash * squash)
        inner = total * (1.0 - (cell * (1.0 / CLIP)) * (cell * (1.0 / CLIP)))
        next_ref[piece] = keep * inner * forget
        quart = 0.25 * inner
        pre_grads = (
            quart * acts[2] * slopes[0],
            quart * prev * slopes[1],
            inner * ingate * slopes[2],
            0.25 * mixed * squash * slopes[3],
        )
        for gate in range(4):
            low = pre_grads[gate].astype(BF16)
            place = slice(gate * width, (gate + 1) * width)
            dz_ref[piece, :, place] = low
            rows = pre_grads[gate].reshape(-1, 8, width)
            sum_ref[piece, :, place] = bias_ref[piece, :, place] + jnp.sum(rows, axis=0)
            part = part + dot(low, w_ref[gate, cols, :])
    part_ref[...] = (part * keep).astype(BF16)


def finish_kernel(
    step_ref, p_ref, q_ref, gates_all, cells_all, ups_all, hidden_in, slope_in,
    gates_ref, cell_ref, prev_ref, slope_ref, up_ref, hidden_all, slope_all,
    hidden_buf, sems, hidden_sem,
):
    copies = fetches(
        step_ref[0], step_ref[1], (gates_all, cells_all, ups_all), (gates_ref, cell_ref, prev_ref, up_ref), sems
    )
    for copy in copies:
        copy.start()
    clipped(p_ref, q_ref, hidden_buf, slope_ref)
    hidden_copy = pltpu.make_async_copy(hidden_buf, hidden_all.at[step_ref[1]], hidden_sem)
    hidden_copy.start()
    for copy in copies:
        copy.wait()
    hidden_copy.wait()


def fetches(step, time, sources, targets, sems):
    gates_all, cells_all, ups_all = sources
    gates_ref, cell_ref, prev_ref, up_ref = targets
    before = jnp.maximum(step - 1, 0)
    return [
        pltpu.make_async_copy(gates_all.at[i, step], gates_ref.at[i], sems.at[i]) for i in range(PIECES)
    ] + [
        pltpu.make_async_copy(cells_all.at[step], cell_ref, sems.at[PIECES]),
        pltpu.make_async_copy(cells_all.at[before], prev_ref, sems.at[PIECES + 1]),
        pltpu.make_async_copy(ups_all.at[time], up_ref, sems.at[PIECES + 2]),
    ]


def aside_kernel(
    first, last, opens, passed, step_ref, dz_ref, raw_ref, gates_all, cells_all, ups_all, slope_all, *refs
):
    refs = refs[(0 if first else 4) + (0 if opens else 2) + passed :]
    gates_ref, cell_ref, prev_ref, slope_ref, up_ref = refs[:5]
    dz_all, raw_all, near_all, far_all, near_out, far_out = refs[5:11]
    sems, fetch_sems = refs[-2:]
    step, time_before = step_ref[0], step_ref[2]
    slot, low, high = step_ref[4], step_ref[5], step_ref[6]
    before = jnp.maximum(step - 1, 0)
    copies = []
    if not last:
        copies += fetches(
            before, time_before, (gates_all, cells_all, ups_all), (gates_ref, cell_ref, prev_ref, up_ref), fetch_sems
        )
        copies.append(pltpu.make_async_copy(slope_all.at[before], slope_ref, fetch_sems.at[PIECES + 3]))
    copies += [pltpu.make_async_copy(dz_ref.at[i], dz_all.at[i, step], sems.at[i]) for i in range(PIECES)]
    copies.append(pltpu.make_async_copy(raw_ref, raw_all.at[step], sems.at[PIECES]))
    copies.append(pltpu.make_async_copy(dz_ref.at[low], near_all.at[step], sems.at[PIECES + 1]))
    copies.append(pltpu.make_async_copy(dz_ref.at[HALVES + high], far_all.at[step], sems.at[PIECES + 2]))
    copies.append(pltpu.make_async_copy(dz_ref.at[1 - low], near_out.at[slot], sems.at[PIECES + 3]))
    copies.append(pltpu.make_async_copy(dz_ref.at[HALVES + 1 - high], far_out.at[slot], sems.at[PIECES + 4]))
    for copy in copies:
        copy.start()
    for copy in copies:
        copy.wait()


def input_grad_kernel(step_ref, dz_ref, wa_ref, wb_ref, out_ref, acc_ref):
    piece, gate = pl.program_id(0), pl.program_id(1)
    steps, streams, width = dz_ref.shape[1:]

    @pl.when((piece == 0) & (gate == 0))
    def _():
        acc_ref[...] = jnp.zeros(acc_ref.shape, F32)

    weights = jnp.where(piece < HALVES, wa_ref[0], wb_ref[0])
    acc_ref[...] += lax.dot_general(
        dz_ref[0].reshape(steps * streams, width), weights, (((1,), (1,)), ((), ())), preferred_element_type=F32
    )

    @pl.when((piece == PIECES - 1) & (gate == 3))
    def _():
        for step in range(steps):
            time = step_ref[0] + step_ref[1] * step
            out_ref[time] = acc_ref[step * streams : (step + 1) * streams, :]


def params(mib):
    return pltpu.CompilerParams(vmem_limit_bytes=mib * MIB)


def cost(flops, size):
    return pl.CostEstimate(flops=flops, bytes_accessed=size, transcendentals=0)


def body(inputs, w_in, w_rec, bias, proj, state_h, state_c, resets, stream_doc, cotangent):
    streams, steps, depth = inputs.shape[1:]
    cells = w_in.shape[3]
    width = cells // HALVES
    n_batch = lax.axis_size("batch")
    gates_size = lax.axis_size("gate")
    line = n_batch // 2
    swap = [(i, i ^ 1) for i in range(gates_size)]
    across = [(i, i ^ 2) for i in range(gates_size)]
    near_swap = [(i, i ^ 1) for i in range(n_batch)]
    far_swap = [(i, i ^ 2) for i in range(n_batch)]

    rank, spot = lax.axis_index("gate"), lax.axis_index("batch")
    half_cols, quarter_cols = depth // 2, depth // 4
    place_numbers = {
        "own": rank % 2,
        "other": 1 - rank % 2,
        "low": spot % 2,
        "not_low": 1 - spot % 2,
        "high": (spot // 2) % 2,
        "not_high": 1 - (spot // 2) % 2,
        "spot": spot,
        "begin": jnp.where(spot // 2 == 0, line - 1, 0),
        "cols": (rank // 2) * half_cols,
        "other_cols": (1 - rank // 2) * half_cols,
    }
    for stride, count in {(2, line), (4, line // 2)}:
        here = (spot // stride) % count
        place_numbers[stride, "here"] = here
        place_numbers[stride, "not_here"] = jnp.maximum(1 - here, 0)
        for slot in range(2, count):
            place_numbers[stride, "rise", slot] = jnp.minimum(here + count - slot, count - 1)
            place_numbers[stride, "fall", slot] = jnp.maximum(here - count + slot, 0)
        if count > 2:
            place_numbers[stride, "begin"] = jnp.where(here == 0, count - 1, 0)
    names = sorted(place_numbers, key=str)
    gathered_numbers = pl.pallas_call(
        numbers_kernel,
        out_shape=jax.ShapeDtypeStruct((len(names),), jnp.int32),
        in_specs=[SMEM],
        out_specs=SMEM,
        name="numbers",
    )(jnp.stack([place_numbers[x] for x in names]).astype(jnp.int32))
    number = {x: gathered_numbers[i] for i, x in enumerate(names)}
    own, low, high = number["own"], number["low"], number["high"]

    def pick(stacked, index, axis=0):
        return lax.dynamic_index_in_dim(stacked, index, axis, keepdims=False, allow_negative_indices=False)

    def trade(mine, theirs):
        return (mine, lax.ppermute(theirs, "gate", swap))

    def vmem(shape, dtype):
        return pltpu.VMEM(shape, dtype)

    def hbm(shape, dtype):
        return pltpu.HBM(shape, dtype)

    def by_gate(weights, index, keep=True):
        shape = (4,) + weights.shape[1:2] + weights.shape[3:]
        kept = (vmem(shape, BF16),) if keep else ()
        part = weights.shape[1] // 8
        return pl.pallas_call(
            functools.partial(layout_kernel, keep),
            out_shape=kept + (hbm(shape, BF16),),
            in_specs=[SMEM, ANY],
            out_specs=[VMEM] * len(kept) + [ANY],
            scratch_shapes=([] if kept else [pltpu.VMEM(shape, BF16)])
            + [
                pltpu.VMEM((3, part) + weights.shape[2:], BF16),
                pltpu.SemaphoreType.DMA((3,)),
                pltpu.SemaphoreType.DMA((8,)),
            ],
            compiler_params=params(8),
            name="layout",
        )(jnp.full((1,), index, jnp.int32), in_hbm(weights))

    win_b, rec_b = (lax.ppermute(by_gate(w, number["other"], False)[0], "gate", swap) for w in (w_in, w_rec))
    (win_av, win_a), (rec_av, rec_a) = by_gate(w_in, own), by_gate(w_rec, own)
    proj_a, proj_b = trade(pick(proj, own), pick(proj, number["other"]))
    bias_a, bias_b = trade(pick(bias, own), pick(bias, number["other"]))

    def cells_to_pieces(pair):
        both = jnp.stack(pair).reshape(QUARTERS, streams, HALVES, width)
        return jnp.transpose(both, (0, 2, 1, 3)).reshape(PIECES, streams, width)

    def by_time(stacked):
        return jnp.transpose(pick(stacked, own), (1, 0, 2))

    feats = by_time(inputs)
    ups = by_time(cotangent)
    flags = resets.astype(F32)
    later = jnp.concatenate([flags[:, 1:], jnp.zeros_like(flags[:, :1])], axis=1)
    keep = 1.0 - jnp.where(own == 0, flags, later)
    keep = jnp.broadcast_to(jnp.transpose(keep)[:, :, None], (steps, streams, 128))

    docs_h = state_h[stream_doc]
    docs_c = state_c[stream_doc]
    start_h = pick(jnp.transpose(docs_h, (1, 0, 2)), own).astype(BF16)
    by_dir_c = jnp.transpose(docs_c, (1, 0, 2))
    start_c = cells_to_pieces(trade(pick(by_dir_c, own), pick(by_dir_c, number["other"])))

    def at_step(step):
        near = jnp.array([step, step, max(step - 1, 0), min(step + 1, steps - 1)], jnp.int32)
        turned = jnp.array([step] + [steps - 1 - x for x in (step, max(step - 1, 0), min(step + 1, steps - 1))], jnp.int32)
        return jnp.where(own == 0, near, turned)

    def swapped(array, pairs):
        return lax.ppermute(array, "batch", pairs)

    turn = jnp.where(own == 0, jnp.array([0, 1], jnp.int32), jnp.array([steps - 1, -1], jnp.int32))
    feats_v, feat_all = pl.pallas_call(
        order_kernel,
        out_shape=(vmem(feats.shape, BF16), hbm(feats.shape, BF16)),
        in_specs=[SMEM, ANY],
        out_specs=[VMEM, ANY],
        scratch_shapes=[pltpu.SemaphoreType.DMA((2 * steps,))],
        compiler_params=params(1),
        name="order",
    )(turn, feats)
    feat_in = (swapped(feat_all, near_swap), swapped(feat_all, far_swap))
    keep_v, bias_av, bias_bv, win_bv = place(keep, bias_a.astype(F32), bias_b.astype(F32), win_b)
    rec_bv, proj_av, proj_bv, start_hv, start_cv = place(rec_b, proj_a, proj_b, start_h, start_c)

    gates_shape, cell_shape = (PIECES, streams, 4 * width), (PIECES, streams, width)
    bias_shape = (PIECES, 8, 4 * width)
    inflow = pl.pallas_call(
        inflow_kernel,
        out_shape=vmem(gates_shape, F32),
        in_specs=[VMEM] * 5,
        out_specs=VMEM,
        compiler_params=params(8),
        name="inflow",
    )(pinned(feats_v), pinned(bias_av), pinned(bias_bv), pinned(win_av), pinned(win_bv))

    def forward_call(first, step, part, peer, cell, inflow):
        return pl.pallas_call(
            functools.partial(forward_kernel, first),
            out_shape=(
                vmem((streams, depth), BF16),
                vmem(cell_shape, F32),
                vmem(gates_shape, BF16),
                vmem(cell_shape, BF16),
                vmem((streams, depth), BF16),
                vmem((streams, depth), BF16),
                vmem((streams, depth), F32),
            ),
            in_specs=[SMEM] + [VMEM] * 10,
            out_specs=[VMEM] * 7,
            compiler_params=params(8),
            name="forward_step",
        )(
            at_step(step), pinned(part), pinned(peer), pinned(start_hv), pinned(keep_v), pinned(cell), pinned(inflow),
            pinned(rec_av), pinned(rec_bv), pinned(proj_av), pinned(proj_bv),
        )

    def between_call(step, fresh, stacks, passing=()):
        shapes = (
            hbm((PIECES, steps, streams, 4 * width), BF16),
            hbm((steps,) + cell_shape, F32),
            hbm((PIECES, steps, streams, width), BF16),
            hbm((steps, streams, depth), BF16),
            hbm((steps, streams, depth), BF16),
            hbm((steps, streams, depth), F32),
        )
        aliases = {12 + i: 1 + i for i in range(len(stacks))}
        aliases.update({12 + len(stacks) + i: 7 + i for i in range(len(passing))})
        inflow, *out = pl.pallas_call(
            functools.partial(between_kernel, not stacks, step == steps - 1, len(passing)),
            out_shape=(vmem(gates_shape, F32),) + shapes + tuple(hbm(x.shape, x.dtype) for x in passing),
            in_specs=[SMEM] + [VMEM] * 11 + [ANY] * (len(stacks) + len(passing)),
            out_specs=[VMEM] + [ANY] * (6 + len(passing)),
            scratch_shapes=[pltpu.SemaphoreType.DMA((2 * PIECES + 4,))],
            input_output_aliases=aliases,
            compiler_params=params(8),
            cost_estimate=cost(2 * streams * depth * 8 * cells, 8 * depth * cells * 2),
            name="between",
        )(
            at_step(step), pinned(feats_v), pinned(bias_av), pinned(bias_bv), pinned(win_av), pinned(win_bv),
            *(pinned(x) for x in fresh), *(in_hbm(x) for x in (*stacks, *passing)),
        )
        return inflow, tuple(out[:6]), tuple(out[6:])

    none = jnp.zeros((streams, depth), BF16)
    part, peer, cell, stacks = none, none, start_cv, ()
    for step in range(steps):
        part, cell, *fresh = forward_call(step == 0, step, part, peer, cell, inflow)
        peer = lax.ppermute(part, "gate", across)
        due = step == (2 * steps) // 3
        inflow, stacks, passed = between_call(step, (cell, *fresh), stacks, feat_in if due else ())
        feat_in = passed if due else feat_in
    gates_all, cells_all, mixed_all, prev_all, hidden_all, slope_all = stacks
    prev_in = (swapped(prev_all, near_swap), swapped(prev_all, far_swap))

    saved_shapes = (
        vmem(gates_shape, BF16),
        vmem(cell_shape, F32),
        vmem(cell_shape, F32),
        vmem((streams, depth), F32),
        vmem((streams, depth), BF16),
    )
    *saved, hidden_all, slope_all = pl.pallas_call(
        finish_kernel,
        out_shape=saved_shapes + (hbm((steps, streams, depth), BF16), hbm((steps, streams, depth), F32)),
        in_specs=[SMEM, VMEM, VMEM] + [ANY] * 5,
        out_specs=[VMEM] * 5 + [ANY] * 2,
        scratch_shapes=[
            pltpu.VMEM((streams, depth), BF16),
            pltpu.SemaphoreType.DMA((PIECES + 4,)),
            pltpu.SemaphoreType.DMA,
        ],
        input_output_aliases={6: 5, 7: 6},
        compiler_params=params(8),
        name="finish",
    )(
        at_step(steps - 1), pinned(part), pinned(peer), in_hbm(gates_all), in_hbm(cells_all), in_hbm(ups),
        in_hbm(hidden_all), in_hbm(slope_all),
    )

    rec_atv, rec_btv, proj_atv, proj_btv = pl.pallas_call(
        turned_kernel,
        out_shape=(vmem((4, cells, depth), BF16),) * 2 + (vmem((depth, cells), BF16),) * 2,
        in_specs=[ANY] * 4,
        out_specs=[VMEM] * 4,
        scratch_shapes=[
            pltpu.VMEM((3, depth, cells), BF16),
            pltpu.SemaphoreType.DMA((3,)),
            pltpu.VMEM((2, cells, depth), BF16),
            pltpu.SemaphoreType.DMA((2,)),
        ],
        compiler_params=params(8),
        name="turned",
    )(*(in_hbm(x) for x in (rec_a, rec_b, proj_a, proj_b)))

    def backward_call(step, part, peer, grad, bias, saved):
        return pl.pallas_call(
            backward_kernel,
            out_shape=(
                vmem((streams, depth), BF16),
                vmem(cell_shape, F32),
                vmem(bias_shape, F32),
                vmem((streams, depth), BF16),
                vmem(gates_shape, BF16),
            ),
            in_specs=[SMEM] + [VMEM] * 15,
            out_specs=[VMEM] * 5,
            compiler_params=params(8),
            name="backward_step",
        )(
            at_step(step), pinned(part), pinned(peer), pinned(keep_v), pinned(grad), pinned(bias),
            pinned(rec_atv), pinned(rec_btv), pinned(proj_atv), pinned(proj_btv),
            *(pinned(x) for x in saved), pinned(start_cv),
        )

    def aside_call(step, slot, slots, dz, raw, stacks, sends, passing):
        piece_shape = (streams, 4 * width)
        shapes = (
            hbm((PIECES, steps) + piece_shape, BF16),
            hbm((steps, streams, depth), BF16),
            hbm((steps,) + piece_shape, BF16),
            hbm((steps,) + piece_shape, BF16),
            hbm((slots,) + piece_shape, BF16),
            hbm((slots,) + piece_shape, BF16),
        )
        kept = len(stacks)
        aliases = {7 + i: 5 + i for i in range(kept)}
        aliases.update({7 + kept + i: 9 + i for i in range(len(sends))})
        aliases.update({7 + kept + len(sends) + i: 11 + i for i in range(len(passing))})
        out = pl.pallas_call(
            functools.partial(aside_kernel, not stacks, step == 0, not sends, len(passing)),
            out_shape=saved_shapes + shapes + tuple(hbm(x.shape, x.dtype) for x in passing),
            in_specs=[SMEM] + [VMEM] * 2 + [ANY] * (4 + kept + len(sends) + len(passing)),
            out_specs=[VMEM] * 5 + [ANY] * (6 + len(passing)),
            scratch_shapes=[
                pltpu.SemaphoreType.DMA((PIECES + 5,)),
                pltpu.SemaphoreType.DMA((PIECES + 4,)),
            ],
            input_output_aliases=aliases,
            compiler_params=params(8),
            cost_estimate=cost(0, 8 * MIB),
            name="aside",
        )(
            jnp.concatenate([at_step(step), jnp.stack([jnp.int32(slot), low, high])]), pinned(dz), pinned(raw),
            in_hbm(gates_all), in_hbm(cells_all), in_hbm(ups), in_hbm(slope_all),
            *(in_hbm(x) for x in (*stacks, *sends, *passing)),
        )
        return out[:5], tuple(out[5:9]), tuple(out[9:11]), tuple(out[11:])

    carry = (none, none, jnp.zeros(cell_shape, F32), jnp.zeros(bias_shape, F32), saved, ())
    pending, arrived, ready, top = [(steps - 1 - steps // 3, prev_in)], [], None, steps
    for index, share in enumerate(SHARES):
        slots = top if index == len(SHARES) - 1 else round(share * steps)
        sends = ()
        for step in range(top - 1, top - slots - 1, -1):
            part, peer, grad, bias_sum, saved, stacks = carry
            part, grad, bias_sum, raw, dz = backward_call(step, part, peer, grad, bias_sum, saved)
            peer = lax.ppermute(part, "gate", across)
            if ready is not None:
                due, sides = ready
                sides = after((part,), *sides) if step else sides
                pending.append((due, (swapped(sides[0], near_swap), swapped(sides[1], far_swap))))
                ready = None
            passing = pending.pop(0)[1] if pending and pending[0][0] >= step else ()
            saved, stacks, sends, passed = aside_call(
                step, step - (top - slots), slots, dz, raw, stacks, sends, passing
            )
            arrived += [passed] if passed else []
            carry = (part, peer, grad, bias_sum, saved, stacks)
        top -= slots
        ready = (max(top - 1 - (3 * slots + 3) // 4, 0 if slots > 2 else -1), sends)
    pending.append((-1, (swapped(sends[0], near_swap), swapped(sends[1], far_swap))))
    arrived += [arrays for _, arrays in pending]
    dz_all, raw_all, near_all, far_all = carry[-1]
    bias_sum = carry[3]
    prev_in, exchanged = arrived[0], arrived[1:]
    rows = steps * streams

    def by_direction(mine, theirs):
        return jnp.stack([jnp.where(own == 0, mine, theirs), jnp.where(own == 0, theirs, mine)])

    def line_sum(chunks, axis, stride, count, first=None, gates={}):
        def chunk(*name):
            return pick(chunks, number[(stride, *name)], axis)

        def at(device):
            return (device // stride) % count

        if count == 2:
            pairs = [(i, i + stride if at(i) == 0 else i - stride) for i in range(n_batch)]
            return (chunk("here").astype(F32) + swapped(chunk("not_here"), pairs).astype(F32)).astype(BF16)
        ends = [(i, i + stride) for i in range(n_batch) if at(i) == 0]
        ends += [(i, i - stride) for i in range(n_batch) if at(i) == count - 1]
        up = down = swapped(chunk("begin") if first is None else first, ends)
        for slot in range(2, count):
            if slot in gates:
                up, down = gates[slot](up, down)
            rise = (chunk("rise", slot).astype(F32) + up.astype(F32)).astype(BF16)
            fall = (chunk("fall", slot).astype(F32) + down.astype(F32)).astype(BF16)
            up = swapped(rise, [(i, i + stride) for i in range(n_batch) if at(i) < min(slot, count - 1)])
            down = swapped(fall, [(i, i - stride) for i in range(n_batch) if at(i) > max(count - 1 - slot, 0)])
        if count in gates:
            up, down = gates[count](up, down)
        return (chunk("here").astype(F32) + up.astype(F32) + down.astype(F32)).astype(BF16)

    share_rows = depth // n_batch

    def input_grad_of(dz):
        return pl.pallas_call(
            input_grad_kernel,
            out_shape=jax.ShapeDtypeStruct((steps, streams, depth), F32),
            grid_spec=pltpu.PrefetchScalarGridSpec(
                num_scalar_prefetch=1,
                grid=(PIECES, 4),
                in_specs=[
                    pl.BlockSpec((1, steps, streams, width), lambda p, g, turn: (p, 0, 0, g)),
                    pl.BlockSpec(
                        (1, depth, width), lambda p, g, turn: (jnp.where(p < 2, g, 3), 0, jnp.where(p < 2, p, 1))
                    ),
                    pl.BlockSpec(
                        (1, depth, width), lambda p, g, turn: (jnp.where(p < 2, 0, g), 0, jnp.where(p < 2, 0, p - 2))
                    ),
                ],
                out_specs=pl.BlockSpec((steps, streams, depth), lambda p, g, turn: (0, 0, 0)),
                scratch_shapes=[pltpu.VMEM((rows, depth), F32)],
            ),
            compiler_params=params(16),
            cost_estimate=cost(0, 0),
            name="input_grad",
        )(turn, in_hbm(dz), in_hbm(win_a), in_hbm(win_b))

    grad_proj = jnp.einsum("ptnc,tnk->pkc", mixed_all, raw_all, preferred_element_type=F32).astype(BF16)
    grad_proj = grad_proj.reshape(PIECES, line, 2, share_rows, width)
    bias_rows = pl.pallas_call(
        bias_kernel,
        out_shape=jax.ShapeDtypeStruct((PIECES, 4, width), F32),
        in_specs=[VMEM],
        out_specs=VMEM,
        compiler_params=params(1),
        name="bias",
    )(pinned(bias_sum))
    bias_rows = jnp.broadcast_to(bias_rows[:, None, None].astype(BF16), (PIECES, line, 2, 4, width))
    grad_proj = jnp.concatenate([grad_proj, bias_rows], axis=3)

    def with_partner(grad):
        mine, sent = (pick(grad, number[x], grad.ndim - 3) for x in ("low", "not_low"))
        taken = swapped(sent, near_swap)
        return sent, taken, (mine.astype(F32) + taken.astype(F32)).astype(BF16)

    def across_two(grad):
        return line_sum(grad.reshape(grad.shape[:-3] + (line // 2, 2) + grad.shape[-2:]), grad.ndim - 3, 4, line // 2)

    proj_sent, proj_taken, proj_y = with_partner(grad_proj)

    lows, count = [], 0
    for x in exchanged[::-1]:
        lows.insert(0, count)
        count += x[0].shape[0]

    def gathered(kept, feat, prev, parts):
        return pl.pallas_call(
            functools.partial(gather_kernel, tuple(lows[: len(parts)])),
            out_shape=(vmem((2 * steps, streams, 2 * depth), BF16), vmem((2 * steps, streams, 4 * width), BF16)),
            in_specs=[ANY] * (5 + len(parts)),
            out_specs=[VMEM] * 2,
            scratch_shapes=[pltpu.SemaphoreType.DMA((5 + len(parts),))],
            compiler_params=params(1),
            cost_estimate=cost(0, 0),
            name="gather",
        )(*(in_hbm(x) for x in (feat_all, prev_all, feat, prev, kept, *parts)))

    def completed(begin, rows_out, left, right, parts):
        return pl.pallas_call(
            functools.partial(late_kernel, tuple(lows[len(lows) - len(parts) :])),
            out_shape=(vmem(right.shape, BF16), jax.ShapeDtypeStruct((2, max(rows_out, 8), 4 * width), BF16)),
            in_specs=[SMEM] + [VMEM] * 2 + [ANY] * len(parts),
            out_specs=[VMEM] * 2,
            scratch_shapes=[pltpu.SemaphoreType.DMA((len(parts),))],
            input_output_aliases={2: 0},
            compiler_params=params(16),
            cost_estimate=cost(0, 0),
            name="late",
        )(begin, pinned(left), pinned(right), *(in_hbm(x) for x in parts))

    def multiplied(left, right):
        return pl.pallas_call(
            product_kernel,
            out_shape=jax.ShapeDtypeStruct((2, depth, 4 * width), BF16),
            in_specs=[VMEM] * 2,
            out_specs=VMEM,
            compiler_params=params(16),
            cost_estimate=cost(0, 0),
            name="product",
        )(pinned(left), pinned(right))

    near_parts, far_parts = zip(*exchanged)
    chunk_rows = 2 * share_rows if 2 * share_rows % 128 == 0 else 0
    near_left, near_right = gathered(near_all, feat_in[0], prev_in[0], near_parts[:-LATE])
    near_late = after((near_left, proj_sent, *far_parts[-LATE:]), *near_parts[-LATE:])
    near_right, first = completed(jnp.full((1,), number["begin"], jnp.int32), chunk_rows, near_left, near_right, near_late)
    far_all, *far_parts = after((first,), far_all, *far_parts)
    far_left, far_right = gathered(far_all, feat_in[1], prev_in[1], far_parts[:-LATE])
    far_right, _ = completed(jnp.zeros((1,), jnp.int32), 0, far_left, far_right, far_parts[-LATE:])
    far = multiplied(far_left, far_right).reshape(2, line, 2, share_rows, 4 * width)
    near = multiplied(near_left, near_right).reshape(2, line, 2, share_rows, 4 * width)

    def states_of(hidden, cell):
        both_hidden = trade(hidden, hidden)

        hidden_dirs = by_direction(*both_hidden)
        outputs = (inputs.astype(F32) + jnp.transpose(hidden_dirs, (0, 2, 1, 3)).astype(F32)).astype(BF16)
        last_h = jnp.stack([hidden_dirs[0, steps - 1], hidden_dirs[1, 0]], axis=1).astype(F32)
        final_h = jnp.zeros_like(state_h).at[stream_doc].set(last_h)
        last_c = jnp.transpose(cell.reshape(QUARTERS, HALVES, streams, width), (0, 2, 1, 3)).reshape(
            QUARTERS, streams, cells
        )
        last_dirs = by_direction(*trade(last_c[0], last_c[1]))
        final_c = jnp.zeros_like(state_c).at[stream_doc].set(jnp.transpose(last_dirs, (1, 0, 2)))
        return outputs, final_h, final_c

    tokens = {}

    def second(up, down):
        up, sent, tokens["dz"], proj_sum = after((), up, far, dz_all, proj_y, free=2 * MIB)
        tokens["in"], tokens["rec"] = (with_partner(sent[i])[2] for i in range(2))
        tokens["proj"] = across_two(proj_sum)
        return up, up

    def third(up, down):
        dx = input_grad_of(tokens["dz"])
        up, down, tokens["dx"], in_sum, tokens["proj"], hidden, last_cell = after(
            (), up, down, dx, tokens["in"], tokens["proj"], hidden_all, cell, free=2 * MIB
        )
        tokens["in"] = across_two(in_sum)
        tokens["states"] = states_of(hidden, last_cell)
        return up, down

    def final(up, down):
        up, down, tokens["in"], rec_sum = after(tokens["states"], up, down, tokens["in"], tokens["rec"], free=2 * MIB)
        tokens["rec"] = across_two(rec_sum)
        return up, down

    gates = {2: second, 3: third, line: final} if line > 3 else {}
    first = first.reshape(2, 2, share_rows, 4 * width) if chunk_rows else None
    near = line_sum(near, 1, 2, line, first, gates)
    dx_all, (outputs, final_h, final_c) = tokens["dx"], tokens["states"]
    in_two, rec_two, proj_two = tokens["in"], tokens["rec"], tokens["proj"]

    def halves_of(summed, name, pairs):
        return pick(summed, number[name], 1), swapped(pick(summed, number["not_" + name], 1), pairs)

    near_pair = halves_of(near, "low", near_swap)
    far_pair = halves_of(jnp.stack([in_two, rec_two]), "high", far_swap)
    far_pair = [lax.ppermute(x, "gate", swap) for x in far_pair]
    proj_mine, proj_theirs = halves_of(proj_two, "high", far_swap)
    grad_proj = proj_mine.astype(F32) + proj_theirs.astype(F32)
    grad_shape = (2, share_rows, 4, cells)
    grad_w_in, grad_w_rec = pl.pallas_call(
        assemble_kernel,
        out_shape=(jax.ShapeDtypeStruct(grad_shape, F32),) * 2,
        in_specs=[SMEM] + [VMEM] * 4,
        out_specs=[VMEM] * 2,
        compiler_params=params(14),
        name="assemble",
    )(jnp.stack([own, low, high]), *near_pair, *far_pair)

    def home(mine, theirs):
        return by_direction(*trade(mine, theirs)).astype(F32)

    own_cells = cells // n_batch
    shaped = jnp.transpose(grad_proj[:, share_rows:].reshape(QUARTERS, HALVES, 4, width), (0, 2, 1, 3))
    shaped = pick(shaped.reshape(QUARTERS, 4, n_batch, own_cells), number["spot"], 2)
    grad_bias = home(shaped[0], shaped[1])
    grad_proj = grad_proj[:, :share_rows].reshape(QUARTERS, HALVES, share_rows, width)
    grad_proj = jnp.transpose(grad_proj, (0, 1, 3, 2)).reshape(QUARTERS, cells, share_rows).astype(BF16)
    grad_proj = home(grad_proj[0], grad_proj[1])

    def columns(array, name, size):
        return lax.dynamic_slice_in_dim(array, number[name], size, 2, allow_negative_indices=False)

    dx_half = columns(dx_all, "cols", half_cols)
    dx_sent = columns(dx_all, "other_cols", half_cols).astype(BF16)
    dx_half = dx_half + lax.ppermute(dx_sent, "gate", across).astype(F32)
    dx_half = (dx_half + columns(ups, "cols", half_cols).astype(F32)).astype(BF16)
    dx_half = dx_half.reshape(steps, streams, 2, quarter_cols)
    dx_dirs = by_direction(*trade(pick(dx_half, own, 2), pick(dx_half, number["other"], 2)))
    input_grad = jnp.transpose(dx_dirs, (0, 2, 1, 3))
    return (outputs, input_grad, grad_w_in, grad_w_rec, grad_bias, grad_proj, final_h, final_c)


def solution(mesh):
    placed = (
        P(None, "batch", None, None),
        P(None, None, None, "gate"),
        P(None, None, None, "gate"),
        P(None, None, "gate"),
        P(None, "gate", None),
        P("batch", None, None),
        P("batch", None, "gate"),
        P("batch", None),
        P("batch"),
        P(None, "batch", None, None),
    )
    return jax.shard_map(
        body,
        mesh=mesh,
        in_specs=placed,
        out_specs=(
            P(None, "batch", None, None),
            P(None, "batch", None, "gate"),
            P(None, "batch", None, "gate"),
            P(None, "batch", None, "gate"),
            P(None, None, ("gate", "batch")),
            P(None, "gate", "batch"),
            P("batch", None, None),
            P("batch", None, "gate"),
        ),
        check_vma=False,
    )
```

```python
import functools

import jax
import jax.numpy as jnp
from jax import lax
from jax.experimental import pallas as pl
from jax.experimental.pallas import tpu as pltpu
from jax.sharding import PartitionSpec as P

CLIP = 3.0
F32, BF16 = jnp.float32, jnp.bfloat16
QUARTERS, HALVES = 2, 2
PIECES = QUARTERS * HALVES
MIB = 2**20
LATE = 2
SHARES = (0.35, 0.3, 0.15, 0.1, 0.1)

VMEM = pl.BlockSpec(memory_space=pltpu.VMEM)
SMEM = pl.BlockSpec(memory_space=pltpu.SMEM)
ANY = pl.BlockSpec(memory_space=pl.ANY)


def pinned(array):
    return pltpu.with_memory_space_constraint(array, pltpu.VMEM)


def in_hbm(array):
    return pltpu.with_memory_space_constraint(array, pltpu.HBM)


def dot(left, right):
    return jnp.dot(left, right, preferred_element_type=F32)


def place_kernel(count, *refs):
    sources, targets, sems = refs[:count], refs[count : 2 * count], refs[2 * count]
    copies = [pltpu.make_async_copy(a, b, sems.at[i]) for i, (a, b) in enumerate(zip(sources, targets))]
    for copy in copies:
        copy.start()
    for copy in copies:
        copy.wait()


def place(*arrays):
    count = len(arrays)
    return pl.pallas_call(
        functools.partial(place_kernel, count),
        out_shape=tuple(pltpu.VMEM(x.shape, x.dtype) for x in arrays),
        in_specs=[ANY] * count,
        out_specs=[VMEM] * count,
        scratch_shapes=[pltpu.SemaphoreType.DMA((count,))],
        compiler_params=params(1),
        name="place",
    )(*(in_hbm(x) for x in arrays))


def layout_kernel(keep, which_ref, w_ref, first_ref, second_ref, buf, sems, out_sems):
    out_ref, all_ref = (first_ref, second_ref) if keep else (second_ref, first_ref)
    depth, part = w_ref.shape[1], buf.shape[1]

    def fetch(i):
        return pltpu.make_async_copy(w_ref.at[which_ref[0], pl.ds(i * part, part)], buf.at[i % 3], sems.at[i % 3])

    def store(i):
        rows = pl.ds(i * part, part)
        return pltpu.make_async_copy(out_ref.at[:, rows], all_ref.at[:, rows], out_sems.at[i])

    count = depth // part
    for i in range(min(2, count)):
        fetch(i).start()
    for i in range(count):
        if i + 2 < count:
            fetch(i + 2).start()
        fetch(i).wait()
        out_ref[:, i * part : (i + 1) * part, :] = jnp.swapaxes(buf[i % 3], 0, 1)
        store(i).start()
    for i in range(count):
        store(i).wait()


def turned_kernel(wa_ref, wb_ref, pa_ref, pb_ref, wat_ref, wbt_ref, pat_ref, pbt_ref, buf, sems, proj_buf, proj_sems):
    jobs = [(w_ref, out_ref, gate) for w_ref, out_ref in ((wa_ref, wat_ref), (wb_ref, wbt_ref)) for gate in range(4)]

    def fetch(i):
        return pltpu.make_async_copy(jobs[i][0].at[jobs[i][2]], buf.at[i % 3], sems.at[i % 3])

    proj_fetches = [pltpu.make_async_copy(x, proj_buf.at[i], proj_sems.at[i]) for i, x in enumerate((pa_ref, pb_ref))]
    fetch(0).start()
    fetch(1).start()
    for copy in proj_fetches:
        copy.start()
    for i, (_, out_ref, gate) in enumerate(jobs):
        if i + 2 < len(jobs):
            fetch(i + 2).start()
        fetch(i).wait()
        for half in range(HALVES):
            width = buf.shape[2] // HALVES
            cols = slice(half * width, (half + 1) * width)
            out_ref[gate, cols, :] = buf[i % 3, :, cols].T
    for i, out_ref in enumerate((pat_ref, pbt_ref)):
        proj_fetches[i].wait()
        out_ref[...] = proj_buf[i].T


def pass_kernel(*refs):
    pass


def after(tokens, *arrays, free=0):
    count = len(tokens)
    return pl.pallas_call(
        pass_kernel,
        out_shape=tuple(jax.ShapeDtypeStruct(x.shape, x.dtype) for x in arrays),
        in_specs=[ANY] * (count + len(arrays)),
        out_specs=[ANY] * len(arrays),
        input_output_aliases={count + i: i for i in range(len(arrays))},
        compiler_params=params(1),
        name="after",
    )(*tokens, *(in_hbm(x) if x.size * x.dtype.itemsize > free else x for x in arrays))


def gather_kernel(lows, *refs):
    (feat_ref, prev_ref, feat_too, prev_too, kept_ref), refs = refs[:5], refs[5:]
    groups, (left_ref, right_ref, sems) = refs[:-3], refs[-3:]
    steps, _, depth = feat_ref.shape
    jobs = [
        (feat_ref, left_ref.at[:steps, :, :depth]),
        (prev_ref, left_ref.at[:steps, :, depth:]),
        (feat_too, left_ref.at[steps:, :, :depth]),
        (prev_too, left_ref.at[steps:, :, depth:]),
        (kept_ref, right_ref.at[:steps]),
    ]
    jobs += [(x, right_ref.at[steps + low : steps + low + x.shape[0]]) for x, low in zip(groups, lows)]
    copies = [pltpu.make_async_copy(a, b, sems.at[i]) for i, (a, b) in enumerate(jobs)]
    for copy in copies:
        copy.start()
    for copy in copies:
        copy.wait()


def late_kernel(lows, begin_ref, left_ref, right_in, *refs):
    groups, (right_ref, first_ref, sems) = refs[:-3], refs[-3:]
    steps = left_ref.shape[0] // 2
    copies = [
        pltpu.make_async_copy(x, right_ref.at[steps + low : steps + low + x.shape[0]], sems.at[i])
        for i, (x, low) in enumerate(zip(groups, lows))
    ]
    for copy in copies:
        copy.start()
    for copy in copies:
        copy.wait()
    if first_ref.shape[1] % 128:
        return
    share, depth = first_ref.shape[1], left_ref.shape[2] // 2
    rows = left_ref.shape[0] * left_ref.shape[1]
    left = [
        left_ref[:, :, pl.ds(pl.multiple_of(i * depth + begin_ref[0] * share, 128), share)].reshape(rows, share)
        for i in range(2)
    ]
    left = jnp.concatenate([x.T for x in left], axis=0)
    width = right_ref.shape[2] // 4

    def columns(i, _):
        cols = pl.ds(pl.multiple_of(i * width, width), width)
        total = dot(left, right_ref[:, :, cols].reshape(rows, width)).astype(BF16)
        first_ref[0, :, cols] = total[:share]
        first_ref[1, :, cols] = total[share:]
        return 0

    lax.fori_loop(0, 4, columns, 0)


def product_kernel(left_ref, right_ref, out_ref):
    rows, depth = left_ref.shape[0] * left_ref.shape[1], left_ref.shape[2] // 2
    width = right_ref.shape[2] // 4
    for which in range(2):
        left = left_ref[:, :, which * depth : (which + 1) * depth].reshape(rows, depth).T

        def columns(i, _):
            cols = pl.ds(pl.multiple_of(i * width, width), width)
            out_ref[which, :, cols] = dot(left, right_ref[:, :, cols].reshape(rows, width)).astype(BF16)
            return 0

        lax.fori_loop(0, 4, columns, 0)


def assemble_kernel(place_ref, near_a, near_b, far_a, far_b, in_ref, rec_ref):
    own, low, high = place_ref[0], place_ref[1], place_ref[2]
    width = in_ref.shape[3] // HALVES
    for direction, mine_ref, theirs_ref, index in ((own, near_a, near_b, low), (1 - own, far_a, far_b, high)):
        for which, out_ref in ((0, in_ref), (1, rec_ref)):
            mine, theirs = mine_ref[which].astype(F32), theirs_ref[which].astype(F32)
            for half in range(HALVES):
                whole = jnp.where(index == half, mine, theirs)
                gates = jnp.stack([whole[:, gate * width : (gate + 1) * width] for gate in range(4)])
                out_ref[direction, :, :, half * width : (half + 1) * width] = jnp.swapaxes(gates, 0, 1)


def order_kernel(step_ref, feat_ref, out_ref, all_ref, sems):
    copies = []
    for i in range(feat_ref.shape[0]):
        source = feat_ref.at[step_ref[0] + step_ref[1] * i]
        copies.append(pltpu.make_async_copy(source, out_ref.at[i], sems.at[2 * i]))
        copies.append(pltpu.make_async_copy(source, all_ref.at[i], sems.at[2 * i + 1]))
    for copy in copies:
        copy.start()
    for copy in copies:
        copy.wait()


def numbers_kernel(in_ref, out_ref):
    for i in range(in_ref.shape[0]):
        out_ref[i] = in_ref[i]


def bias_kernel(sum_ref, out_ref):
    width = sum_ref.shape[2] // 4
    for piece in range(PIECES):
        for gate in range(4):
            out_ref[piece, gate : gate + 1, :] = jnp.sum(
                sum_ref[piece, :, gate * width : (gate + 1) * width], axis=0, keepdims=True
            )


def pieces(refs, axis):
    for piece in range(PIECES):
        quarter, half = divmod(piece, HALVES)
        width = refs[0].shape[axis] // HALVES
        yield piece, quarter, width, slice(half * width, (half + 1) * width)


def forward_kernel(
    first, step_ref, p_ref, q_ref, start_ref, keep_ref, cell_ref, inflow_ref, wa_ref, wb_ref, pa_ref, pb_ref,
    part_ref, next_ref, gates_ref, mixed_ref, prev_ref, hidden_ref, slope_ref,
):
    keep = keep_ref[step_ref[1]][:, :1]
    if first:
        hidden = start_ref[...]
    else:
        hidden = clipped(p_ref, q_ref, hidden_ref, slope_ref)
    hidden = hidden * keep.astype(BF16)
    prev_ref[...] = hidden
    part = jnp.zeros(part_ref.shape, F32)
    for piece, quarter, width, cols in pieces((wa_ref, wb_ref), 2):
        w_ref, proj_ref = ((wa_ref, pa_ref), (wb_ref, pb_ref))[quarter]
        acts = []
        for gate in range(4):
            place = slice(gate * width, (gate + 1) * width)
            pre = dot(hidden, w_ref[gate, :, cols]) + inflow_ref[piece, :, place]
            act = jnp.tanh(pre if gate == 2 else 0.5 * pre)
            gates_ref[piece, :, place] = act.astype(BF16)
            acts.append(act if gate == 2 else 0.5 + 0.5 * act)
        ingate, forget, candidate, outgate = acts
        cell = CLIP * jnp.tanh((forget * (keep * cell_ref[piece]) + ingate * candidate) * (1.0 / CLIP))
        next_ref[piece] = cell
        mixed = (outgate * jnp.tanh(cell)).astype(BF16)
        mixed_ref[piece] = mixed
        part = part + dot(mixed, proj_ref[cols, :])
    part_ref[...] = part.astype(BF16)


def clipped(p_ref, q_ref, hidden_ref, slope_ref):
    squash = jnp.tanh((p_ref[...].astype(F32) + q_ref[...].astype(F32)) * (1.0 / CLIP))
    hidden = (CLIP * squash).astype(BF16)
    hidden_ref[...] = hidden
    slope_ref[...] = 1.0 - squash * squash
    return hidden


def between_kernel(
    first, last, passed, step_ref, feat_ref, ba_ref, bb_ref, wa_ref, wb_ref, cell_ref, gates_ref, mixed_ref, prev_ref, hidden_ref,
    slope_ref, *refs,
):
    refs = refs[(0 if first else 6) + passed :]
    out_ref, gates_all, cells_all, mixed_all, prev_all, hidden_all, slope_all = refs[:7]
    sems = refs[-1]
    step, time_before = step_ref[0], step_ref[2]
    copies = [pltpu.make_async_copy(gates_ref.at[i], gates_all.at[i, step], sems.at[i]) for i in range(PIECES)]
    copies += [
        pltpu.make_async_copy(mixed_ref.at[i], mixed_all.at[i, step], sems.at[PIECES + i]) for i in range(PIECES)
    ]
    copies.append(pltpu.make_async_copy(cell_ref, cells_all.at[step], sems.at[2 * PIECES]))
    copies.append(pltpu.make_async_copy(prev_ref, prev_all.at[step], sems.at[2 * PIECES + 1]))
    if not first:
        copies.append(pltpu.make_async_copy(hidden_ref, hidden_all.at[time_before], sems.at[2 * PIECES + 2]))
        copies.append(pltpu.make_async_copy(slope_ref, slope_all.at[step - 1], sems.at[2 * PIECES + 3]))
    for copy in copies:
        copy.start()
    if not last:
        inflow_into(feat_ref[step + 1], ba_ref, bb_ref, wa_ref, wb_ref, out_ref)
    for copy in copies:
        copy.wait()


def inflow_into(feat, ba_ref, bb_ref, wa_ref, wb_ref, out_ref):
    for piece, quarter, width, cols in pieces((wa_ref, wb_ref), 2):
        w_ref, bias_ref = ((wa_ref, ba_ref), (wb_ref, bb_ref))[quarter]
        for gate in range(4):
            place = slice(gate * width, (gate + 1) * width)
            out_ref[piece, :, place] = dot(feat, w_ref[gate, :, cols]) + bias_ref[gate : gate + 1, cols]


def inflow_kernel(feat_ref, ba_ref, bb_ref, wa_ref, wb_ref, out_ref):
    inflow_into(feat_ref[0], ba_ref, bb_ref, wa_ref, wb_ref, out_ref)


def backward_kernel(
    step_ref, p_ref, q_ref, keep_ref, grad_ref, bias_ref, wa_ref, wb_ref, pa_ref, pb_ref,
    gates_ref, cell_ref, prev_ref, slope_ref, up_ref, start_ref,
    part_ref, next_ref, sum_ref, raw_ref, dz_ref,
):
    step = step_ref[0]
    keep = keep_ref[step_ref[1]][:, :1]
    raw = (up_ref[...].astype(F32) + (p_ref[...].astype(F32) + q_ref[...].astype(F32))) * slope_ref[...]
    raw = raw.astype(BF16)
    raw_ref[...] = raw
    part = jnp.zeros(part_ref.shape, F32)
    for piece, quarter, width, cols in pieces((wa_ref, wb_ref), 1):
        w_ref, proj_ref = ((wa_ref, pa_ref), (wb_ref, pb_ref))[quarter]
        mixed = dot(raw, proj_ref[:, cols])
        acts = [gates_ref[piece, :, gate * width : (gate + 1) * width].astype(F32) for gate in range(4)]
        ingate, forget, outgate = (0.5 + 0.5 * acts[gate] for gate in (0, 1, 3))
        slopes = [1.0 - act * act for act in acts]
        cell = cell_ref[piece]
        prev = keep * jnp.where(step == 0, start_ref[piece], prev_ref[piece])
        squash = jnp.tanh(cell)
        total = grad_ref[piece] + mixed * outgate * (1.0 - squash * squash)
        inner = total * (1.0 - (cell * (1.0 / CLIP)) * (cell * (1.0 / CLIP)))
        next_ref[piece] = keep * inner * forget
        quart = 0.25 * inner
        pre_grads = (
            quart * acts[2] * slopes[0],
            quart * prev * slopes[1],
            inner * ingate * slopes[2],
            0.25 * mixed * squash * slopes[3],
        )
        for gate in range(4):
            low = pre_grads[gate].astype(BF16)
            place = slice(gate * width, (gate + 1) * width)
            dz_ref[piece, :, place] = low
            rows = pre_grads[gate].reshape(-1, 8, width)
            sum_ref[piece, :, place] = bias_ref[piece, :, place] + jnp.sum(rows, axis=0)
            part = part + dot(low, w_ref[gate, cols, :])
    part_ref[...] = (part * keep).astype(BF16)


def finish_kernel(
    step_ref, p_ref, q_ref, gates_all, cells_all, ups_all, hidden_in, slope_in,
    gates_ref, cell_ref, prev_ref, slope_ref, up_ref, hidden_all, slope_all,
    hidden_buf, sems, hidden_sem,
):
    copies = fetches(
        step_ref[0], step_ref[1], (gates_all, cells_all, ups_all), (gates_ref, cell_ref, prev_ref, up_ref), sems
    )
    for copy in copies:
        copy.start()
    clipped(p_ref, q_ref, hidden_buf, slope_ref)
    hidden_copy = pltpu.make_async_copy(hidden_buf, hidden_all.at[step_ref[1]], hidden_sem)
    hidden_copy.start()
    for copy in copies:
        copy.wait()
    hidden_copy.wait()


def fetches(step, time, sources, targets, sems):
    gates_all, cells_all, ups_all = sources
    gates_ref, cell_ref, prev_ref, up_ref = targets
    before = jnp.maximum(step - 1, 0)
    return [
        pltpu.make_async_copy(gates_all.at[i, step], gates_ref.at[i], sems.at[i]) for i in range(PIECES)
    ] + [
        pltpu.make_async_copy(cells_all.at[step], cell_ref, sems.at[PIECES]),
        pltpu.make_async_copy(cells_all.at[before], prev_ref, sems.at[PIECES + 1]),
        pltpu.make_async_copy(ups_all.at[time], up_ref, sems.at[PIECES + 2]),
    ]


def aside_kernel(
    first, last, opens, passed, step_ref, dz_ref, raw_ref, gates_all, cells_all, ups_all, slope_all, *refs
):
    refs = refs[(0 if first else 4) + (0 if opens else 2) + passed :]
    gates_ref, cell_ref, prev_ref, slope_ref, up_ref = refs[:5]
    dz_all, raw_all, near_all, far_all, near_out, far_out = refs[5:11]
    sems, fetch_sems = refs[-2:]
    step, time_before = step_ref[0], step_ref[2]
    slot, low, high = step_ref[4], step_ref[5], step_ref[6]
    before = jnp.maximum(step - 1, 0)
    copies = []
    if not last:
        copies += fetches(
            before, time_before, (gates_all, cells_all, ups_all), (gates_ref, cell_ref, prev_ref, up_ref), fetch_sems
        )
        copies.append(pltpu.make_async_copy(slope_all.at[before], slope_ref, fetch_sems.at[PIECES + 3]))
    copies += [pltpu.make_async_copy(dz_ref.at[i], dz_all.at[i, step], sems.at[i]) for i in range(PIECES)]
    copies.append(pltpu.make_async_copy(raw_ref, raw_all.at[step], sems.at[PIECES]))
    copies.append(pltpu.make_async_copy(dz_ref.at[low], near_all.at[step], sems.at[PIECES + 1]))
    copies.append(pltpu.make_async_copy(dz_ref.at[HALVES + high], far_all.at[step], sems.at[PIECES + 2]))
    copies.append(pltpu.make_async_copy(dz_ref.at[1 - low], near_out.at[slot], sems.at[PIECES + 3]))
    copies.append(pltpu.make_async_copy(dz_ref.at[HALVES + 1 - high], far_out.at[slot], sems.at[PIECES + 4]))
    for copy in copies:
        copy.start()
    for copy in copies:
        copy.wait()


def input_grad_kernel(step_ref, dz_ref, wa_ref, wb_ref, out_ref, acc_ref):
    piece, gate = pl.program_id(0), pl.program_id(1)
    steps, streams, width = dz_ref.shape[1:]

    @pl.when((piece == 0) & (gate == 0))
    def _():
        acc_ref[...] = jnp.zeros(acc_ref.shape, F32)

    weights = jnp.where(piece < HALVES, wa_ref[0], wb_ref[0])
    acc_ref[...] += lax.dot_general(
        dz_ref[0].reshape(steps * streams, width), weights, (((1,), (1,)), ((), ())), preferred_element_type=F32
    )

    @pl.when((piece == PIECES - 1) & (gate == 3))
    def _():
        for step in range(steps):
            time = step_ref[0] + step_ref[1] * step
            out_ref[time] = acc_ref[step * streams : (step + 1) * streams, :]


def params(mib):
    return pltpu.CompilerParams(vmem_limit_bytes=mib * MIB)


def cost(flops, size):
    return pl.CostEstimate(flops=flops, bytes_accessed=size, transcendentals=0)


def body(inputs, w_in, w_rec, bias, proj, state_h, state_c, resets, stream_doc, cotangent):
    streams, steps, depth = inputs.shape[1:]
    cells = w_in.shape[3]
    width = cells // HALVES
    n_batch = lax.axis_size("batch")
    gates_size = lax.axis_size("gate")
    line = n_batch // 2
    swap = [(i, i ^ 1) for i in range(gates_size)]
    across = [(i, i ^ 2) for i in range(gates_size)]
    near_swap = [(i, i ^ 1) for i in range(n_batch)]
    far_swap = [(i, i ^ 2) for i in range(n_batch)]

    rank, spot = lax.axis_index("gate"), lax.axis_index("batch")
    half_cols, quarter_cols = depth // 2, depth // 4
    place_numbers = {
        "own": rank % 2,
        "other": 1 - rank % 2,
        "low": spot % 2,
        "not_low": 1 - spot % 2,
        "high": (spot // 2) % 2,
        "not_high": 1 - (spot // 2) % 2,
        "spot": spot,
        "begin": jnp.where(spot // 2 == 0, line - 1, 0),
        "cols": (rank // 2) * half_cols,
        "other_cols": (1 - rank // 2) * half_cols,
    }
    for stride, count in {(2, line), (4, line // 2)}:
        here = (spot // stride) % count
        place_numbers[stride, "here"] = here
        place_numbers[stride, "not_here"] = jnp.maximum(1 - here, 0)
        for slot in range(2, count):
            place_numbers[stride, "rise", slot] = jnp.minimum(here + count - slot, count - 1)
            place_numbers[stride, "fall", slot] = jnp.maximum(here - count + slot, 0)
        if count > 2:
            place_numbers[stride, "begin"] = jnp.where(here == 0, count - 1, 0)
    names = sorted(place_numbers, key=str)
    gathered_numbers = pl.pallas_call(
        numbers_kernel,
        out_shape=jax.ShapeDtypeStruct((len(names),), jnp.int32),
        in_specs=[SMEM],
        out_specs=SMEM,
        name="numbers",
    )(jnp.stack([place_numbers[x] for x in names]).astype(jnp.int32))
    number = {x: place_numbers[x].astype(jnp.int32) for x in names}
    own, low, high = number["own"], number["low"], number["high"]
    which = {x: lax.slice_in_dim(gathered_numbers, names.index(x), names.index(x) + 1) for x in ("own", "other")}

    def pick(stacked, index, axis=0):
        return lax.dynamic_index_in_dim(stacked, index, axis, keepdims=False, allow_negative_indices=False)

    def trade(mine, theirs):
        return (mine, lax.ppermute(theirs, "gate", swap))

    def vmem(shape, dtype):
        return pltpu.VMEM(shape, dtype)

    def hbm(shape, dtype):
        return pltpu.HBM(shape, dtype)

    def by_gate(weights, index, keep=True):
        shape = (4,) + weights.shape[1:2] + weights.shape[3:]
        kept = (vmem(shape, BF16),) if keep else ()
        part = weights.shape[1] // 8
        return pl.pallas_call(
            functools.partial(layout_kernel, keep),
            out_shape=kept + (hbm(shape, BF16),),
            in_specs=[SMEM, ANY],
            out_specs=[VMEM] * len(kept) + [ANY],
            scratch_shapes=([] if kept else [pltpu.VMEM(shape, BF16)])
            + [
                pltpu.VMEM((3, part) + weights.shape[2:], BF16),
                pltpu.SemaphoreType.DMA((3,)),
                pltpu.SemaphoreType.DMA((8,)),
            ],
            compiler_params=params(8),
            name="layout",
        )(index, in_hbm(weights))

    win_b, rec_b = (lax.ppermute(by_gate(w, which["other"], False)[0], "gate", swap) for w in (w_in, w_rec))
    (win_av, win_a), (rec_av, rec_a) = by_gate(w_in, which["own"]), by_gate(w_rec, which["own"])
    proj_a, proj_b = trade(pick(proj, own), pick(proj, number["other"]))
    bias_a, bias_b = trade(pick(bias, own), pick(bias, number["other"]))

    def cells_to_pieces(pair):
        both = jnp.stack(pair).reshape(QUARTERS, streams, HALVES, width)
        return jnp.transpose(both, (0, 2, 1, 3)).reshape(PIECES, streams, width)

    def by_time(stacked):
        return jnp.transpose(pick(stacked, own), (1, 0, 2))

    feats = by_time(inputs)
    ups = by_time(cotangent)
    flags = resets.astype(F32)
    later = jnp.concatenate([flags[:, 1:], jnp.zeros_like(flags[:, :1])], axis=1)
    keep = 1.0 - jnp.where(own == 0, flags, later)
    keep = jnp.broadcast_to(jnp.transpose(keep)[:, :, None], (steps, streams, 128))

    docs_h = state_h[stream_doc]
    docs_c = state_c[stream_doc]
    start_h = pick(jnp.transpose(docs_h, (1, 0, 2)), own).astype(BF16)
    by_dir_c = jnp.transpose(docs_c, (1, 0, 2))
    start_c = cells_to_pieces(trade(pick(by_dir_c, own), pick(by_dir_c, number["other"])))

    def at_step(step):
        near = jnp.array([step, step, max(step - 1, 0), min(step + 1, steps - 1)], jnp.int32)
        turned = jnp.array([step] + [steps - 1 - x for x in (step, max(step - 1, 0), min(step + 1, steps - 1))], jnp.int32)
        return jnp.where(own == 0, near, turned)

    def swapped(array, pairs):
        return lax.ppermute(array, "batch", pairs)

    turn = jnp.where(own == 0, jnp.array([0, 1], jnp.int32), jnp.array([steps - 1, -1], jnp.int32))
    feats_v, feat_all = pl.pallas_call(
        order_kernel,
        out_shape=(vmem(feats.shape, BF16), hbm(feats.shape, BF16)),
        in_specs=[SMEM, ANY],
        out_specs=[VMEM, ANY],
        scratch_shapes=[pltpu.SemaphoreType.DMA((2 * steps,))],
        compiler_params=params(1),
        name="order",
    )(turn, feats)
    feat_in = (swapped(feat_all, near_swap), swapped(feat_all, far_swap))
    keep_v, bias_av, bias_bv, win_bv = place(keep, bias_a.astype(F32), bias_b.astype(F32), win_b)
    rec_bv, proj_av, proj_bv, start_hv, start_cv = place(rec_b, proj_a, proj_b, start_h, start_c)

    gates_shape, cell_shape = (PIECES, streams, 4 * width), (PIECES, streams, width)
    bias_shape = (PIECES, 8, 4 * width)
    inflow = pl.pallas_call(
        inflow_kernel,
        out_shape=vmem(gates_shape, F32),
        in_specs=[VMEM] * 5,
        out_specs=VMEM,
        compiler_params=params(8),
        name="inflow",
    )(pinned(feats_v), pinned(bias_av), pinned(bias_bv), pinned(win_av), pinned(win_bv))

    def forward_call(first, step, part, peer, cell, inflow):
        return pl.pallas_call(
            functools.partial(forward_kernel, first),
            out_shape=(
                vmem((streams, depth), BF16),
                vmem(cell_shape, F32),
                vmem(gates_shape, BF16),
                vmem(cell_shape, BF16),
                vmem((streams, depth), BF16),
                vmem((streams, depth), BF16),
                vmem((streams, depth), F32),
            ),
            in_specs=[SMEM] + [VMEM] * 10,
            out_specs=[VMEM] * 7,
            compiler_params=params(8),
            name="forward_step",
        )(
            at_step(step), pinned(part), pinned(peer), pinned(start_hv), pinned(keep_v), pinned(cell), pinned(inflow),
            pinned(rec_av), pinned(rec_bv), pinned(proj_av), pinned(proj_bv),
        )

    def between_call(step, fresh, stacks, passing=()):
        shapes = (
            hbm((PIECES, steps, streams, 4 * width), BF16),
            hbm((steps,) + cell_shape, F32),
            hbm((PIECES, steps, streams, width), BF16),
            hbm((steps, streams, depth), BF16),
            hbm((steps, streams, depth), BF16),
            hbm((steps, streams, depth), F32),
        )
        aliases = {12 + i: 1 + i for i in range(len(stacks))}
        aliases.update({12 + len(stacks) + i: 7 + i for i in range(len(passing))})
        inflow, *out = pl.pallas_call(
            functools.partial(between_kernel, not stacks, step == steps - 1, len(passing)),
            out_shape=(vmem(gates_shape, F32),) + shapes + tuple(hbm(x.shape, x.dtype) for x in passing),
            in_specs=[SMEM] + [VMEM] * 11 + [ANY] * (len(stacks) + len(passing)),
            out_specs=[VMEM] + [ANY] * (6 + len(passing)),
            scratch_shapes=[pltpu.SemaphoreType.DMA((2 * PIECES + 4,))],
            input_output_aliases=aliases,
            compiler_params=params(8),
            cost_estimate=cost(2 * streams * depth * 8 * cells, 8 * depth * cells * 2),
            name="between",
        )(
            at_step(step), pinned(feats_v), pinned(bias_av), pinned(bias_bv), pinned(win_av), pinned(win_bv),
            *(pinned(x) for x in fresh), *(in_hbm(x) for x in (*stacks, *passing)),
        )
        return inflow, tuple(out[:6]), tuple(out[6:])

    none = jnp.zeros((streams, depth), BF16)
    part, peer, cell, stacks = none, none, start_cv, ()
    for step in range(steps):
        part, cell, *fresh = forward_call(step == 0, step, part, peer, cell, inflow)
        peer = lax.ppermute(part, "gate", across)
        due = step == (2 * steps) // 3
        inflow, stacks, passed = between_call(step, (cell, *fresh), stacks, feat_in if due else ())
        feat_in = passed if due else feat_in
    gates_all, cells_all, mixed_all, prev_all, hidden_all, slope_all = stacks
    prev_in = (swapped(prev_all, near_swap), swapped(prev_all, far_swap))

    saved_shapes = (
        vmem(gates_shape, BF16),
        vmem(cell_shape, F32),
        vmem(cell_shape, F32),
        vmem((streams, depth), F32),
        vmem((streams, depth), BF16),
    )
    *saved, hidden_all, slope_all = pl.pallas_call(
        finish_kernel,
        out_shape=saved_shapes + (hbm((steps, streams, depth), BF16), hbm((steps, streams, depth), F32)),
        in_specs=[SMEM, VMEM, VMEM] + [ANY] * 5,
        out_specs=[VMEM] * 5 + [ANY] * 2,
        scratch_shapes=[
            pltpu.VMEM((streams, depth), BF16),
            pltpu.SemaphoreType.DMA((PIECES + 4,)),
            pltpu.SemaphoreType.DMA,
        ],
        input_output_aliases={6: 5, 7: 6},
        compiler_params=params(8),
        name="finish",
    )(
        at_step(steps - 1), pinned(part), pinned(peer), in_hbm(gates_all), in_hbm(cells_all), in_hbm(ups),
        in_hbm(hidden_all), in_hbm(slope_all),
    )

    rec_atv, rec_btv, proj_atv, proj_btv = pl.pallas_call(
        turned_kernel,
        out_shape=(vmem((4, cells, depth), BF16),) * 2 + (vmem((depth, cells), BF16),) * 2,
        in_specs=[ANY] * 4,
        out_specs=[VMEM] * 4,
        scratch_shapes=[
            pltpu.VMEM((3, depth, cells), BF16),
            pltpu.SemaphoreType.DMA((3,)),
            pltpu.VMEM((2, cells, depth), BF16),
            pltpu.SemaphoreType.DMA((2,)),
        ],
        compiler_params=params(8),
        name="turned",
    )(*(in_hbm(x) for x in (rec_a, rec_b, proj_a, proj_b)))

    def backward_call(step, part, peer, grad, bias, saved):
        return pl.pallas_call(
            backward_kernel,
            out_shape=(
                vmem((streams, depth), BF16),
                vmem(cell_shape, F32),
                vmem(bias_shape, F32),
                vmem((streams, depth), BF16),
                vmem(gates_shape, BF16),
            ),
            in_specs=[SMEM] + [VMEM] * 15,
            out_specs=[VMEM] * 5,
            compiler_params=params(8),
            name="backward_step",
        )(
            at_step(step), pinned(part), pinned(peer), pinned(keep_v), pinned(grad), pinned(bias),
            pinned(rec_atv), pinned(rec_btv), pinned(proj_atv), pinned(proj_btv),
            *(pinned(x) for x in saved), pinned(start_cv),
        )

    def aside_call(step, slot, slots, dz, raw, stacks, sends, passing):
        piece_shape = (streams, 4 * width)
        shapes = (
            hbm((PIECES, steps) + piece_shape, BF16),
            hbm((steps, streams, depth), BF16),
            hbm((steps,) + piece_shape, BF16),
            hbm((steps,) + piece_shape, BF16),
            hbm((slots,) + piece_shape, BF16),
            hbm((slots,) + piece_shape, BF16),
        )
        kept = len(stacks)
        aliases = {7 + i: 5 + i for i in range(kept)}
        aliases.update({7 + kept + i: 9 + i for i in range(len(sends))})
        aliases.update({7 + kept + len(sends) + i: 11 + i for i in range(len(passing))})
        out = pl.pallas_call(
            functools.partial(aside_kernel, not stacks, step == 0, not sends, len(passing)),
            out_shape=saved_shapes + shapes + tuple(hbm(x.shape, x.dtype) for x in passing),
            in_specs=[SMEM] + [VMEM] * 2 + [ANY] * (4 + kept + len(sends) + len(passing)),
            out_specs=[VMEM] * 5 + [ANY] * (6 + len(passing)),
            scratch_shapes=[
                pltpu.SemaphoreType.DMA((PIECES + 5,)),
                pltpu.SemaphoreType.DMA((PIECES + 4,)),
            ],
            input_output_aliases=aliases,
            compiler_params=params(8),
            cost_estimate=cost(0, 8 * MIB),
            name="aside",
        )(
            jnp.concatenate([at_step(step), jnp.stack([jnp.int32(slot), low, high])]), pinned(dz), pinned(raw),
            in_hbm(gates_all), in_hbm(cells_all), in_hbm(ups), in_hbm(slope_all),
            *(in_hbm(x) for x in (*stacks, *sends, *passing)),
        )
        return out[:5], tuple(out[5:9]), tuple(out[9:11]), tuple(out[11:])

    carry = (none, none, jnp.zeros(cell_shape, F32), jnp.zeros(bias_shape, F32), saved, ())
    pending, arrived, ready, top = [(steps - 1 - steps // 3, prev_in)], [], None, steps
    for index, share in enumerate(SHARES):
        slots = top if index == len(SHARES) - 1 else round(share * steps)
        sends = ()
        for step in range(top - 1, top - slots - 1, -1):
            part, peer, grad, bias_sum, saved, stacks = carry
            part, grad, bias_sum, raw, dz = backward_call(step, part, peer, grad, bias_sum, saved)
            peer = lax.ppermute(part, "gate", across)
            if ready is not None:
                due, sides = ready
                sides = after((part,), *sides) if step else sides
                pending.append((due, (swapped(sides[0], near_swap), swapped(sides[1], far_swap))))
                ready = None
            passing = ()
            while pending and pending[0][0] >= step:
                passing += pending.pop(0)[1]
            saved, stacks, sends, passed = aside_call(
                step, step - (top - slots), slots, dz, raw, stacks, sends, passing
            )
            arrived += [passed[i : i + 2] for i in range(0, len(passed), 2)]
            carry = (part, peer, grad, bias_sum, saved, stacks)
        top -= slots
        ready = (max(top - 1 - (3 * slots + 3) // 4, 0 if slots > 2 else -1), sends)
    pending.append((-1, (swapped(sends[0], near_swap), swapped(sends[1], far_swap))))
    arrived += [arrays for _, arrays in pending]
    dz_all, raw_all, near_all, far_all = carry[-1]
    bias_sum = carry[3]
    prev_in, exchanged = arrived[0], arrived[1:]
    rows = steps * streams

    def by_direction(mine, theirs):
        return jnp.stack([jnp.where(own == 0, mine, theirs), jnp.where(own == 0, theirs, mine)])

    def line_sum(chunks, axis, stride, count, first=None, gates={}):
        def chunk(*name):
            return pick(chunks, number[(stride, *name)], axis)

        def at(device):
            return (device // stride) % count

        if count == 2:
            pairs = [(i, i + stride if at(i) == 0 else i - stride) for i in range(n_batch)]
            return (chunk("here").astype(F32) + swapped(chunk("not_here"), pairs).astype(F32)).astype(BF16)
        ends = [(i, i + stride) for i in range(n_batch) if at(i) == 0]
        ends += [(i, i - stride) for i in range(n_batch) if at(i) == count - 1]
        up = down = swapped(chunk("begin") if first is None else first, ends)
        for slot in range(2, count):
            if slot in gates:
                up, down = gates[slot](up, down)
            rise = (chunk("rise", slot).astype(F32) + up.astype(F32)).astype(BF16)
            fall = (chunk("fall", slot).astype(F32) + down.astype(F32)).astype(BF16)
            up = swapped(rise, [(i, i + stride) for i in range(n_batch) if at(i) < min(slot, count - 1)])
            down = swapped(fall, [(i, i - stride) for i in range(n_batch) if at(i) > max(count - 1 - slot, 0)])
        if count in gates:
            up, down = gates[count](up, down)
        return (chunk("here").astype(F32) + up.astype(F32) + down.astype(F32)).astype(BF16)

    share_rows = depth // n_batch

    def input_grad_of(dz):
        return pl.pallas_call(
            input_grad_kernel,
            out_shape=jax.ShapeDtypeStruct((steps, streams, depth), F32),
            grid_spec=pltpu.PrefetchScalarGridSpec(
                num_scalar_prefetch=1,
                grid=(PIECES, 4),
                in_specs=[
                    pl.BlockSpec((1, steps, streams, width), lambda p, g, turn: (p, 0, 0, g)),
                    pl.BlockSpec(
                        (1, depth, width), lambda p, g, turn: (jnp.where(p < 2, g, 3), 0, jnp.where(p < 2, p, 1))
                    ),
                    pl.BlockSpec(
                        (1, depth, width), lambda p, g, turn: (jnp.where(p < 2, 0, g), 0, jnp.where(p < 2, 0, p - 2))
                    ),
                ],
                out_specs=pl.BlockSpec((steps, streams, depth), lambda p, g, turn: (0, 0, 0)),
                scratch_shapes=[pltpu.VMEM((rows, depth), F32)],
            ),
            compiler_params=params(16),
            cost_estimate=cost(0, 0),
            name="input_grad",
        )(turn, in_hbm(dz), in_hbm(win_a), in_hbm(win_b))

    grad_proj = jnp.einsum("ptnc,tnk->pkc", mixed_all, raw_all, preferred_element_type=F32).astype(BF16)
    grad_proj = grad_proj.reshape(PIECES, line, 2, share_rows, width)
    bias_rows = pl.pallas_call(
        bias_kernel,
        out_shape=jax.ShapeDtypeStruct((PIECES, 4, width), F32),
        in_specs=[VMEM],
        out_specs=VMEM,
        compiler_params=params(1),
        name="bias",
    )(pinned(bias_sum))
    bias_rows = jnp.broadcast_to(bias_rows[:, None, None].astype(BF16), (PIECES, line, 2, 4, width))
    grad_proj = jnp.concatenate([grad_proj, bias_rows], axis=3)

    def with_partner(grad):
        mine, sent = (pick(grad, number[x], grad.ndim - 3) for x in ("low", "not_low"))
        taken = swapped(sent, near_swap)
        return sent, taken, (mine.astype(F32) + taken.astype(F32)).astype(BF16)

    def across_two(grad):
        return line_sum(grad.reshape(grad.shape[:-3] + (line // 2, 2) + grad.shape[-2:]), grad.ndim - 3, 4, line // 2)

    proj_sent, proj_taken, proj_y = with_partner(grad_proj)

    lows, count = [], 0
    for x in exchanged[::-1]:
        lows.insert(0, count)
        count += x[0].shape[0]

    def gathered(kept, feat, prev, parts):
        return pl.pallas_call(
            functools.partial(gather_kernel, tuple(lows[: len(parts)])),
            out_shape=(vmem((2 * steps, streams, 2 * depth), BF16), vmem((2 * steps, streams, 4 * width), BF16)),
            in_specs=[ANY] * (5 + len(parts)),
            out_specs=[VMEM] * 2,
            scratch_shapes=[pltpu.SemaphoreType.DMA((5 + len(parts),))],
            compiler_params=params(1),
            cost_estimate=cost(0, 0),
            name="gather",
        )(*(in_hbm(x) for x in (feat_all, prev_all, feat, prev, kept, *parts)))

    def completed(begin, rows_out, left, right, parts):
        return pl.pallas_call(
            functools.partial(late_kernel, tuple(lows[len(lows) - len(parts) :])),
            out_shape=(vmem(right.shape, BF16), jax.ShapeDtypeStruct((2, max(rows_out, 8), 4 * width), BF16)),
            in_specs=[SMEM] + [VMEM] * 2 + [ANY] * len(parts),
            out_specs=[VMEM] * 2,
            scratch_shapes=[pltpu.SemaphoreType.DMA((len(parts),))],
            input_output_aliases={2: 0},
            compiler_params=params(16),
            cost_estimate=cost(0, 0),
            name="late",
        )(begin, pinned(left), pinned(right), *(in_hbm(x) for x in parts))

    def multiplied(left, right):
        return pl.pallas_call(
            product_kernel,
            out_shape=jax.ShapeDtypeStruct((2, depth, 4 * width), BF16),
            in_specs=[VMEM] * 2,
            out_specs=VMEM,
            compiler_params=params(16),
            cost_estimate=cost(0, 0),
            name="product",
        )(pinned(left), pinned(right))

    near_parts, far_parts = zip(*exchanged)
    chunk_rows = 2 * share_rows if 2 * share_rows % 128 == 0 else 0
    near_left, near_right = gathered(near_all, feat_in[0], prev_in[0], near_parts[:-LATE])
    near_late = after((near_left, proj_sent, *far_parts[-LATE:]), *near_parts[-LATE:])
    near_right, first = completed(jnp.full((1,), number["begin"], jnp.int32), chunk_rows, near_left, near_right, near_late)
    far_all, *far_parts = after((first,), far_all, *far_parts)
    far_left, far_right = gathered(far_all, feat_in[1], prev_in[1], far_parts[:-LATE])
    far_right, _ = completed(jnp.zeros((1,), jnp.int32), 0, far_left, far_right, far_parts[-LATE:])
    far = multiplied(far_left, far_right).reshape(2, line, 2, share_rows, 4 * width)
    near = multiplied(near_left, near_right).reshape(2, line, 2, share_rows, 4 * width)

    def states_of(hidden, cell):
        both_hidden = trade(hidden, hidden)

        hidden_dirs = by_direction(*both_hidden)
        outputs = (inputs.astype(F32) + jnp.transpose(hidden_dirs, (0, 2, 1, 3)).astype(F32)).astype(BF16)
        last_h = jnp.stack([hidden_dirs[0, steps - 1], hidden_dirs[1, 0]], axis=1).astype(F32)
        final_h = jnp.zeros_like(state_h).at[stream_doc].set(last_h)
        last_c = jnp.transpose(cell.reshape(QUARTERS, HALVES, streams, width), (0, 2, 1, 3)).reshape(
            QUARTERS, streams, cells
        )
        last_dirs = by_direction(*trade(last_c[0], last_c[1]))
        final_c = jnp.zeros_like(state_c).at[stream_doc].set(jnp.transpose(last_dirs, (1, 0, 2)))
        return outputs, final_h, final_c

    tokens = {}

    def second(up, down):
        up, sent, tokens["dz"], proj_sum = after((), up, far, dz_all, proj_y, free=2 * MIB)
        tokens["in"], tokens["rec"] = (with_partner(sent[i])[2] for i in range(2))
        tokens["proj"] = across_two(proj_sum)
        return up, up

    def third(up, down):
        dx = input_grad_of(tokens["dz"])
        up, down, tokens["dx"], in_sum, tokens["proj"], hidden, last_cell = after(
            (), up, down, dx, tokens["in"], tokens["proj"], hidden_all, cell, free=2 * MIB
        )
        tokens["in"] = across_two(in_sum)
        tokens["states"] = states_of(hidden, last_cell)
        return up, down

    def final(up, down):
        up, down, tokens["in"], rec_sum = after(tokens["states"], up, down, tokens["in"], tokens["rec"], free=2 * MIB)
        tokens["rec"] = across_two(rec_sum)
        return up, down

    gates = {2: second, 3: third, line: final} if line > 3 else {}
    first = first.reshape(2, 2, share_rows, 4 * width) if chunk_rows else None
    near = line_sum(near, 1, 2, line, first, gates)
    dx_all, (outputs, final_h, final_c) = tokens["dx"], tokens["states"]
    in_two, rec_two, proj_two = tokens["in"], tokens["rec"], tokens["proj"]

    def halves_of(summed, name, pairs):
        return pick(summed, number[name], 1), swapped(pick(summed, number["not_" + name], 1), pairs)

    near_pair = halves_of(near, "low", near_swap)
    far_pair = halves_of(jnp.stack([in_two, rec_two]), "high", far_swap)
    far_pair = [lax.ppermute(x, "gate", swap) for x in far_pair]
    proj_mine, proj_theirs = halves_of(proj_two, "high", far_swap)
    grad_proj = proj_mine.astype(F32) + proj_theirs.astype(F32)
    grad_shape = (2, share_rows, 4, cells)
    grad_w_in, grad_w_rec = pl.pallas_call(
        assemble_kernel,
        out_shape=(jax.ShapeDtypeStruct(grad_shape, F32),) * 2,
        in_specs=[SMEM] + [VMEM] * 4,
        out_specs=[VMEM] * 2,
        compiler_params=params(14),
        name="assemble",
    )(jnp.stack([own, low, high]), *near_pair, *far_pair)

    def home(mine, theirs):
        return by_direction(*trade(mine, theirs)).astype(F32)

    own_cells = cells // n_batch
    shaped = jnp.transpose(grad_proj[:, share_rows:].reshape(QUARTERS, HALVES, 4, width), (0, 2, 1, 3))
    shaped = pick(shaped.reshape(QUARTERS, 4, n_batch, own_cells), number["spot"], 2)
    grad_bias = home(shaped[0], shaped[1])
    grad_proj = grad_proj[:, :share_rows].reshape(QUARTERS, HALVES, share_rows, width)
    grad_proj = jnp.transpose(grad_proj, (0, 1, 3, 2)).reshape(QUARTERS, cells, share_rows).astype(BF16)
    grad_proj = home(grad_proj[0], grad_proj[1])

    def columns(array, name, size):
        return lax.dynamic_slice_in_dim(array, number[name], size, 2, allow_negative_indices=False)

    dx_half = columns(dx_all, "cols", half_cols)
    dx_sent = columns(dx_all, "other_cols", half_cols).astype(BF16)
    dx_half = dx_half + lax.ppermute(dx_sent, "gate", across).astype(F32)
    dx_half = (dx_half + columns(ups, "cols", half_cols).astype(F32)).astype(BF16)
    dx_half = dx_half.reshape(steps, streams, 2, quarter_cols)
    dx_dirs = by_direction(*trade(pick(dx_half, own, 2), pick(dx_half, number["other"], 2)))
    input_grad = jnp.transpose(dx_dirs, (0, 2, 1, 3))
    return (outputs, input_grad, grad_w_in, grad_w_rec, grad_bias, grad_proj, final_h, final_c)


def solution(mesh):
    placed = (
        P(None, "batch", None, None),
        P(None, None, None, "gate"),
        P(None, None, None, "gate"),
        P(None, None, "gate"),
        P(None, "gate", None),
        P("batch", None, None),
        P("batch", None, "gate"),
        P("batch", None),
        P("batch"),
        P(None, "batch", None, None),
    )
    return jax.shard_map(
        body,
        mesh=mesh,
        in_specs=placed,
        out_specs=(
            P(None, "batch", None, None),
            P(None, "batch", None, "gate"),
            P(None, "batch", None, "gate"),
            P(None, "batch", None, "gate"),
            P(None, None, ("gate", "batch")),
            P(None, "gate", "batch"),
            P("batch", None, None),
            P("batch", None, "gate"),
        ),
        check_vma=False,
    )
```

```python
import functools

import jax
import jax.numpy as jnp
from jax import lax
from jax.experimental import pallas as pl
from jax.experimental.pallas import tpu as pltpu
from jax.sharding import PartitionSpec as P

CLIP = 3.0
F32, BF16 = jnp.float32, jnp.bfloat16
QUARTERS, HALVES = 2, 2
PIECES = QUARTERS * HALVES
MIB = 2**20
LATE = 2
SHARES = (0.35, 0.3, 0.15, 0.1, 0.1)

VMEM = pl.BlockSpec(memory_space=pltpu.VMEM)
SMEM = pl.BlockSpec(memory_space=pltpu.SMEM)
ANY = pl.BlockSpec(memory_space=pl.ANY)


def pinned(array):
    return pltpu.with_memory_space_constraint(array, pltpu.VMEM)


def in_hbm(array):
    return pltpu.with_memory_space_constraint(array, pltpu.HBM)


def dot(left, right):
    return jnp.dot(left, right, preferred_element_type=F32)


def layout_kernel(keep, spread, which_ref, w_ref, *refs):
    buf, sems, out_sems = refs[-3:]
    out_ref = refs[0] if keep else refs[1]
    all_ref = refs[1] if keep else refs[0]
    depth, ahead, part = w_ref.shape[1], buf.shape[0], buf.shape[1]
    count = depth // part

    def fetch(i):
        return pltpu.make_async_copy(w_ref.at[which_ref[0], pl.ds(i * part, part)], buf.at[i % ahead], sems.at[i % ahead])

    def store(i):
        rows = pl.ds(i * part, part)
        return pltpu.make_async_copy(out_ref.at[:, rows], all_ref.at[:, rows], out_sems.at[i])

    for i in range(min(ahead - 1, count)):
        fetch(i).start()
    for i in range(count):
        if i + ahead - 1 < count:
            fetch(i + ahead - 1).start()
        fetch(i).wait()
        out_ref[:, i * part : (i + 1) * part, :] = jnp.swapaxes(buf[i % ahead], 0, 1)
        if spread:
            store(i).start()
    for i in range(count if spread else 0):
        store(i).wait()


def turned_kernel(wa_ref, wb_ref, pa_ref, pb_ref, wat_ref, wbt_ref, pat_ref, pbt_ref):
    for w_ref, out_ref in ((wa_ref, wat_ref), (wb_ref, wbt_ref)):
        for gate in range(4):
            for half in range(HALVES):
                width = w_ref.shape[2] // HALVES
                cols = slice(half * width, (half + 1) * width)
                out_ref[gate, cols, :] = w_ref[gate, :, cols].T
    pat_ref[...] = pa_ref[...].T
    pbt_ref[...] = pb_ref[...].T


def pass_kernel(*refs):
    pass


def after(tokens, *arrays, free=0):
    count = len(tokens)
    return pl.pallas_call(
        pass_kernel,
        out_shape=tuple(jax.ShapeDtypeStruct(x.shape, x.dtype) for x in arrays),
        in_specs=[ANY] * (count + len(arrays)),
        out_specs=[ANY] * len(arrays),
        input_output_aliases={count + i: i for i in range(len(arrays))},
        compiler_params=params(1),
        name="after",
    )(*tokens, *(in_hbm(x) if x.size * x.dtype.itemsize > free else x for x in arrays))


def gather_kernel(lows, *refs):
    (feat_ref, prev_ref, feat_too, prev_too, kept_ref), refs = refs[:5], refs[5:]
    groups, (left_ref, right_ref, sems) = refs[:-3], refs[-3:]
    steps, _, depth = feat_ref.shape
    jobs = [
        (feat_ref, left_ref.at[:steps, :, :depth]),
        (prev_ref, left_ref.at[:steps, :, depth:]),
        (feat_too, left_ref.at[steps:, :, :depth]),
        (prev_too, left_ref.at[steps:, :, depth:]),
        (kept_ref, right_ref.at[:steps]),
    ]
    jobs += [(x, right_ref.at[steps + low : steps + low + x.shape[0]]) for x, low in zip(groups, lows)]
    copies = [pltpu.make_async_copy(a, b, sems.at[i]) for i, (a, b) in enumerate(jobs)]
    for copy in copies:
        copy.start()
    for copy in copies:
        copy.wait()


def late_kernel(lows, begin_ref, left_ref, right_in, *refs):
    groups, (right_ref, first_ref, sems) = refs[:-3], refs[-3:]
    steps = left_ref.shape[0] // 2
    copies = [
        pltpu.make_async_copy(x, right_ref.at[steps + low : steps + low + x.shape[0]], sems.at[i])
        for i, (x, low) in enumerate(zip(groups, lows))
    ]
    for copy in copies:
        copy.start()
    for copy in copies:
        copy.wait()
    if first_ref.shape[1] % 128:
        return
    share, depth = first_ref.shape[1], left_ref.shape[2] // 2
    rows = left_ref.shape[0] * left_ref.shape[1]
    left = [
        left_ref[:, :, pl.ds(pl.multiple_of(i * depth + begin_ref[0] * share, 128), share)].reshape(rows, share)
        for i in range(2)
    ]
    left = jnp.concatenate([x.T for x in left], axis=0)
    width = right_ref.shape[2] // 4

    def columns(i, _):
        cols = pl.ds(pl.multiple_of(i * width, width), width)
        total = dot(left, right_ref[:, :, cols].reshape(rows, width)).astype(BF16)
        first_ref[0, :, cols] = total[:share]
        first_ref[1, :, cols] = total[share:]
        return 0

    lax.fori_loop(0, 4, columns, 0)


def product_kernel(left_ref, right_ref, out_ref):
    rows, depth = left_ref.shape[0] * left_ref.shape[1], left_ref.shape[2] // 2
    width = right_ref.shape[2] // 4
    for which in range(2):
        left = left_ref[:, :, which * depth : (which + 1) * depth].reshape(rows, depth).T

        def columns(i, _):
            cols = pl.ds(pl.multiple_of(i * width, width), width)
            out_ref[which, :, cols] = dot(left, right_ref[:, :, cols].reshape(rows, width)).astype(BF16)
            return 0

        lax.fori_loop(0, 4, columns, 0)


def assemble_kernel(place_ref, near_a, near_b, far_a, far_b, in_ref, rec_ref):
    own, low, high = place_ref[0], place_ref[1], place_ref[2]
    width = in_ref.shape[3] // HALVES
    for direction, mine_ref, theirs_ref, index in ((own, near_a, near_b, low), (1 - own, far_a, far_b, high)):
        for which, out_ref in ((0, in_ref), (1, rec_ref)):
            mine, theirs = mine_ref[which].astype(F32), theirs_ref[which].astype(F32)
            for half in range(HALVES):
                whole = jnp.where(index == half, mine, theirs)
                gates = jnp.stack([whole[:, gate * width : (gate + 1) * width] for gate in range(4)])
                out_ref[direction, :, :, half * width : (half + 1) * width] = jnp.swapaxes(gates, 0, 1)


def order_kernel(step_ref, feat_ref, out_ref, all_ref, sems):
    copies = []
    for i in range(feat_ref.shape[0]):
        source = feat_ref.at[step_ref[0] + step_ref[1] * i]
        copies.append(pltpu.make_async_copy(source, out_ref.at[i], sems.at[2 * i]))
        copies.append(pltpu.make_async_copy(source, all_ref.at[i], sems.at[2 * i + 1]))
    for copy in copies:
        copy.start()
    for copy in copies:
        copy.wait()


def numbers_kernel(in_ref, out_ref):
    for i in range(in_ref.shape[0]):
        out_ref[i] = in_ref[i]


def bias_kernel(sum_ref, out_ref):
    width = sum_ref.shape[2] // 4
    for piece in range(PIECES):
        for gate in range(4):
            out_ref[piece, gate : gate + 1, :] = jnp.sum(
                sum_ref[piece, :, gate * width : (gate + 1) * width], axis=0, keepdims=True
            )


def pieces(refs, axis):
    for piece in range(PIECES):
        quarter, half = divmod(piece, HALVES)
        width = refs[0].shape[axis] // HALVES
        yield piece, quarter, width, slice(half * width, (half + 1) * width)


def forward_kernel(
    first, step_ref, p_ref, q_ref, start_ref, keep_ref, cell_ref, inflow_ref, wa_ref, wb_ref, pa_ref, pb_ref,
    part_ref, next_ref, gates_ref, mixed_ref, prev_ref, hidden_ref, slope_ref,
):
    keep = keep_ref[step_ref[1]][:, :1]
    if first:
        hidden = start_ref[...]
    else:
        hidden = clipped(p_ref, q_ref, hidden_ref, slope_ref)
    hidden = hidden * keep.astype(BF16)
    prev_ref[...] = hidden
    part = jnp.zeros(part_ref.shape, F32)
    for piece, quarter, width, cols in pieces((wa_ref, wb_ref), 2):
        w_ref, proj_ref = ((wa_ref, pa_ref), (wb_ref, pb_ref))[quarter]
        acts = []
        for gate in range(4):
            place = slice(gate * width, (gate + 1) * width)
            pre = dot(hidden, w_ref[gate, :, cols]) + inflow_ref[piece, :, place]
            act = jnp.tanh(pre if gate == 2 else 0.5 * pre)
            gates_ref[piece, :, place] = act.astype(BF16)
            acts.append(act if gate == 2 else 0.5 + 0.5 * act)
        ingate, forget, candidate, outgate = acts
        cell = CLIP * jnp.tanh((forget * (keep * cell_ref[piece]) + ingate * candidate) * (1.0 / CLIP))
        next_ref[piece] = cell
        mixed = (outgate * jnp.tanh(cell)).astype(BF16)
        mixed_ref[piece] = mixed
        part = part + dot(mixed, proj_ref[cols, :])
    part_ref[...] = part.astype(BF16)


def clipped(p_ref, q_ref, hidden_ref, slope_ref):
    squash = jnp.tanh((p_ref[...].astype(F32) + q_ref[...].astype(F32)) * (1.0 / CLIP))
    hidden = (CLIP * squash).astype(BF16)
    hidden_ref[...] = hidden
    slope_ref[...] = 1.0 - squash * squash
    return hidden


def between_kernel(
    first, last, passed, step_ref, feat_ref, ba_ref, bb_ref, wa_ref, wb_ref, cell_ref, gates_ref, mixed_ref, prev_ref, hidden_ref,
    slope_ref, *refs,
):
    refs = refs[(0 if first else 6) + passed :]
    out_ref, gates_all, cells_all, mixed_all, prev_all, hidden_all, slope_all = refs[:7]
    sems = refs[-1]
    step, time_before = step_ref[0], step_ref[2]
    copies = [pltpu.make_async_copy(gates_ref.at[i], gates_all.at[i, step], sems.at[i]) for i in range(PIECES)]
    copies += [
        pltpu.make_async_copy(mixed_ref.at[i], mixed_all.at[i, step], sems.at[PIECES + i]) for i in range(PIECES)
    ]
    copies.append(pltpu.make_async_copy(cell_ref, cells_all.at[step], sems.at[2 * PIECES]))
    copies.append(pltpu.make_async_copy(prev_ref, prev_all.at[step], sems.at[2 * PIECES + 1]))
    if not first:
        copies.append(pltpu.make_async_copy(hidden_ref, hidden_all.at[time_before], sems.at[2 * PIECES + 2]))
        copies.append(pltpu.make_async_copy(slope_ref, slope_all.at[step - 1], sems.at[2 * PIECES + 3]))
    for copy in copies:
        copy.start()
    if not last:
        inflow_into(feat_ref[step + 1], ba_ref, bb_ref, wa_ref, wb_ref, out_ref)
    for copy in copies:
        copy.wait()


def inflow_into(feat, ba_ref, bb_ref, wa_ref, wb_ref, out_ref):
    for piece, quarter, width, cols in pieces((wa_ref, wb_ref), 2):
        w_ref, bias_ref = ((wa_ref, ba_ref), (wb_ref, bb_ref))[quarter]
        for gate in range(4):
            place = slice(gate * width, (gate + 1) * width)
            out_ref[piece, :, place] = dot(feat, w_ref[gate, :, cols]) + bias_ref[gate : gate + 1, cols]


def begin_kernel(which_ref, feat_ref, wa_ref, wb_ref, proj_ref, *refs):
    sems = refs[-1]
    out_ref, pa_ref, *placed = refs[-8:-1]
    copies = [pltpu.make_async_copy(x, y, sems.at[i]) for i, (x, y) in enumerate(zip(refs[:-8], placed))]
    copies.append(pltpu.make_async_copy(proj_ref.at[which_ref[0]], pa_ref, sems.at[len(copies)]))
    for copy in copies:
        copy.start()
    for copy in copies[:2]:
        copy.wait()
    inflow_into(feat_ref[0], *placed[:2], wa_ref, wb_ref, out_ref)
    for copy in copies[2:]:
        copy.wait()


def backward_kernel(
    step_ref, p_ref, q_ref, keep_ref, grad_ref, bias_ref, wa_ref, wb_ref, pa_ref, pb_ref,
    gates_ref, cell_ref, prev_ref, slope_ref, up_ref, start_ref,
    part_ref, next_ref, sum_ref, raw_ref, dz_ref,
):
    step = step_ref[0]
    keep = keep_ref[step_ref[1]][:, :1]
    raw = (up_ref[...].astype(F32) + (p_ref[...].astype(F32) + q_ref[...].astype(F32))) * slope_ref[...]
    raw = raw.astype(BF16)
    raw_ref[...] = raw
    part = jnp.zeros(part_ref.shape, F32)
    for piece, quarter, width, cols in pieces((wa_ref, wb_ref), 1):
        w_ref, proj_ref = ((wa_ref, pa_ref), (wb_ref, pb_ref))[quarter]
        mixed = dot(raw, proj_ref[:, cols])
        acts = [gates_ref[piece, :, gate * width : (gate + 1) * width].astype(F32) for gate in range(4)]
        ingate, forget, outgate = (0.5 + 0.5 * acts[gate] for gate in (0, 1, 3))
        slopes = [1.0 - act * act for act in acts]
        cell = cell_ref[piece]
        prev = keep * jnp.where(step == 0, start_ref[piece], prev_ref[piece])
        squash = jnp.tanh(cell)
        total = grad_ref[piece] + mixed * outgate * (1.0 - squash * squash)
        inner = total * (1.0 - (cell * (1.0 / CLIP)) * (cell * (1.0 / CLIP)))
        next_ref[piece] = keep * inner * forget
        quart = 0.25 * inner
        pre_grads = (
            quart * acts[2] * slopes[0],
            quart * prev * slopes[1],
            inner * ingate * slopes[2],
            0.25 * mixed * squash * slopes[3],
        )
        for gate in range(4):
            low = pre_grads[gate].astype(BF16)
            place = slice(gate * width, (gate + 1) * width)
            dz_ref[piece, :, place] = low
            rows = pre_grads[gate].reshape(-1, 8, width)
            sum_ref[piece, :, place] = bias_ref[piece, :, place] + jnp.sum(rows, axis=0)
            part = part + dot(low, w_ref[gate, cols, :])
    part_ref[...] = (part * keep).astype(BF16)


def finish_kernel(
    step_ref, p_ref, q_ref, mixed_ref, prev_ref, hidden_ref, before_ref, ups_all, mixed_in, prev_in, hidden_in, slope_in,
    slope_ref, up_ref, mixed_all, prev_all, hidden_all, slope_all, hidden_buf, sems,
):
    step, time, time_before = step_ref[0], step_ref[1], step_ref[2]
    jobs = [(mixed_ref.at[i], mixed_all.at[i, step]) for i in range(PIECES)]
    jobs += [
        (ups_all.at[time], up_ref),
        (prev_ref, prev_all.at[step]),
        (hidden_ref, hidden_all.at[time_before]),
        (before_ref, slope_all.at[step - 1]),
        (hidden_buf, hidden_all.at[time]),
    ]
    copies = [pltpu.make_async_copy(x, y, sems.at[i]) for i, (x, y) in enumerate(jobs)]
    for copy in copies[:-1]:
        copy.start()
    clipped(p_ref, q_ref, hidden_buf, slope_ref)
    copies[-1].start()
    for copy in copies:
        copy.wait()


def fetches(step, time, sources, targets, sems):
    gates_all, cells_all, ups_all = sources
    gates_ref, cell_ref, prev_ref, up_ref = targets
    before = jnp.maximum(step - 1, 0)
    return [
        pltpu.make_async_copy(gates_all.at[i, step], gates_ref.at[i], sems.at[i]) for i in range(PIECES)
    ] + [
        pltpu.make_async_copy(cells_all.at[step], cell_ref, sems.at[PIECES]),
        pltpu.make_async_copy(cells_all.at[before], prev_ref, sems.at[PIECES + 1]),
        pltpu.make_async_copy(ups_all.at[time], up_ref, sems.at[PIECES + 2]),
    ]


def aside_kernel(
    first, last, opens, passed, step_ref, dz_ref, raw_ref, gates_all, cells_all, ups_all, slope_all, *refs
):
    refs = refs[(0 if first else 4) + (0 if opens else 2) + passed :]
    gates_ref, cell_ref, prev_ref, slope_ref, up_ref = refs[:5]
    dz_all, raw_all, near_all, far_all, near_out, far_out = refs[5:11]
    sems, fetch_sems = refs[-2:]
    step, time_before = step_ref[0], step_ref[2]
    slot, low, high = step_ref[4], step_ref[5], step_ref[6]
    before = jnp.maximum(step - 1, 0)
    copies = []
    if not last:
        copies += fetches(
            before, time_before, (gates_all, cells_all, ups_all), (gates_ref, cell_ref, prev_ref, up_ref), fetch_sems
        )
        copies.append(pltpu.make_async_copy(slope_all.at[before], slope_ref, fetch_sems.at[PIECES + 3]))
    copies += [pltpu.make_async_copy(dz_ref.at[i], dz_all.at[i, step], sems.at[i]) for i in range(PIECES)]
    copies.append(pltpu.make_async_copy(raw_ref, raw_all.at[step], sems.at[PIECES]))
    copies.append(pltpu.make_async_copy(dz_ref.at[low], near_all.at[step], sems.at[PIECES + 1]))
    copies.append(pltpu.make_async_copy(dz_ref.at[HALVES + high], far_all.at[step], sems.at[PIECES + 2]))
    copies.append(pltpu.make_async_copy(dz_ref.at[1 - low], near_out.at[slot], sems.at[PIECES + 3]))
    copies.append(pltpu.make_async_copy(dz_ref.at[HALVES + 1 - high], far_out.at[slot], sems.at[PIECES + 4]))
    for copy in copies:
        copy.start()
    for copy in copies:
        copy.wait()


def input_grad_kernel(step_ref, dz_ref, wa_ref, wb_ref, out_ref, acc_ref):
    piece, gate = pl.program_id(0), pl.program_id(1)
    steps, streams, width = dz_ref.shape[1:]

    @pl.when((piece == 0) & (gate == 0))
    def _():
        acc_ref[...] = jnp.zeros(acc_ref.shape, F32)

    weights = jnp.where(piece < HALVES, wa_ref[0], wb_ref[0])
    acc_ref[...] += lax.dot_general(
        dz_ref[0].reshape(steps * streams, width), weights, (((1,), (1,)), ((), ())), preferred_element_type=F32
    )

    @pl.when((piece == PIECES - 1) & (gate == 3))
    def _():
        for step in range(steps):
            time = step_ref[0] + step_ref[1] * step
            out_ref[time] = acc_ref[step * streams : (step + 1) * streams, :]


def params(mib):
    return pltpu.CompilerParams(vmem_limit_bytes=mib * MIB)


def cost(flops, size):
    return pl.CostEstimate(flops=flops, bytes_accessed=size, transcendentals=0)


def body(inputs, w_in, w_rec, bias, proj, state_h, state_c, resets, stream_doc, cotangent):
    streams, steps, depth = inputs.shape[1:]
    cells = w_in.shape[3]
    width = cells // HALVES
    n_batch = lax.axis_size("batch")
    gates_size = lax.axis_size("gate")
    line = n_batch // 2
    swap = [(i, i ^ 1) for i in range(gates_size)]
    across = [(i, i ^ 2) for i in range(gates_size)]
    near_swap = [(i, i ^ 1) for i in range(n_batch)]
    far_swap = [(i, i ^ 2) for i in range(n_batch)]

    rank, spot = lax.axis_index("gate"), lax.axis_index("batch")
    half_cols, quarter_cols = depth // 2, depth // 4
    place_numbers = {
        "own": rank % 2,
        "other": 1 - rank % 2,
        "low": spot % 2,
        "not_low": 1 - spot % 2,
        "high": (spot // 2) % 2,
        "not_high": 1 - (spot // 2) % 2,
        "spot": spot,
        "begin": jnp.where(spot // 2 == 0, line - 1, 0),
        "cols": (rank // 2) * half_cols,
        "other_cols": (1 - rank // 2) * half_cols,
    }
    for stride, count in {(2, line), (4, line // 2)}:
        here = (spot // stride) % count
        place_numbers[stride, "here"] = here
        place_numbers[stride, "not_here"] = jnp.maximum(1 - here, 0)
        for slot in range(2, count):
            place_numbers[stride, "rise", slot] = jnp.minimum(here + count - slot, count - 1)
            place_numbers[stride, "fall", slot] = jnp.maximum(here - count + slot, 0)
        if count > 2:
            place_numbers[stride, "begin"] = jnp.where(here == 0, count - 1, 0)
    names = sorted(place_numbers, key=str)
    gathered_numbers = pl.pallas_call(
        numbers_kernel,
        out_shape=jax.ShapeDtypeStruct((len(names),), jnp.int32),
        in_specs=[SMEM],
        out_specs=SMEM,
        name="numbers",
    )(jnp.stack([place_numbers[x] for x in names]).astype(jnp.int32))
    number = {x: place_numbers[x].astype(jnp.int32) for x in names}
    own, low, high = number["own"], number["low"], number["high"]
    which = lax.slice_in_dim(gathered_numbers, names.index("own"), names.index("own") + 1)

    def pick(stacked, index, axis=0):
        return lax.dynamic_index_in_dim(stacked, index, axis, keepdims=False, allow_negative_indices=False)

    def trade(mine, theirs):
        return (mine, lax.ppermute(theirs, "gate", swap))

    def vmem(shape, dtype):
        return pltpu.VMEM(shape, dtype)

    def hbm(shape, dtype):
        return pltpu.HBM(shape, dtype)

    def by_gate(weights, index, keep, spread):
        shape = (4,) + weights.shape[1:2] + weights.shape[3:]
        count = 16
        kept, spreads = (vmem(shape, BF16),) * keep, (hbm(shape, BF16),) * spread
        return pl.pallas_call(
            functools.partial(layout_kernel, keep, spread),
            out_shape=kept + spreads,
            in_specs=[SMEM, ANY],
            out_specs=[VMEM] * keep + [ANY] * spread,
            scratch_shapes=[pltpu.VMEM(shape, BF16)] * (1 - keep)
            + [
                pltpu.VMEM((4, weights.shape[1] // count) + weights.shape[2:], BF16),
                pltpu.SemaphoreType.DMA((4,)),
                pltpu.SemaphoreType.DMA((count,)),
            ],
            compiler_params=params(8),
            name="layout",
        )(index, in_hbm(weights))

    away = jnp.full((1,), number["other"], jnp.int32)
    win_b, rec_b = (lax.ppermute(by_gate(w, away, False, True)[0], "gate", swap) for w in (w_in, w_rec))
    (win_av, win_a), (rec_av,) = by_gate(w_in, which, True, True), by_gate(w_rec, which, True, False)
    proj_b = lax.ppermute(pick(proj, number["other"]), "gate", swap)
    bias_a, bias_b = trade(pick(bias, own), pick(bias, number["other"]))

    def cells_to_pieces(pair):
        both = jnp.stack(pair).reshape(QUARTERS, streams, HALVES, width)
        return jnp.transpose(both, (0, 2, 1, 3)).reshape(PIECES, streams, width)

    def by_time(stacked):
        return jnp.transpose(pick(stacked, own), (1, 0, 2))

    feats = by_time(inputs)
    ups = by_time(cotangent)
    flags = resets.astype(F32)
    later = jnp.concatenate([flags[:, 1:], jnp.zeros_like(flags[:, :1])], axis=1)
    keep = 1.0 - jnp.where(own == 0, flags, later)
    keep = jnp.broadcast_to(jnp.transpose(keep)[:, :, None], (steps, streams, 128))

    docs_h = state_h[stream_doc]
    docs_c = state_c[stream_doc]
    start_h = pick(jnp.transpose(docs_h, (1, 0, 2)), own).astype(BF16)
    by_dir_c = jnp.transpose(docs_c, (1, 0, 2))
    start_c = cells_to_pieces(trade(pick(by_dir_c, own), pick(by_dir_c, number["other"])))

    def at_step(step):
        near = jnp.array([step, step, max(step - 1, 0), min(step + 1, steps - 1)], jnp.int32)
        turned = jnp.array([step] + [steps - 1 - x for x in (step, max(step - 1, 0), min(step + 1, steps - 1))], jnp.int32)
        return jnp.where(own == 0, near, turned)

    def swapped(array, pairs):
        return lax.ppermute(array, "batch", pairs)

    turn = jnp.where(own == 0, jnp.array([0, 1], jnp.int32), jnp.array([steps - 1, -1], jnp.int32))
    feats_v, feat_all = pl.pallas_call(
        order_kernel,
        out_shape=(vmem(feats.shape, BF16), hbm(feats.shape, BF16)),
        in_specs=[SMEM, ANY],
        out_specs=[VMEM, ANY],
        scratch_shapes=[pltpu.SemaphoreType.DMA((2 * steps,))],
        compiler_params=params(1),
        name="order",
    )(turn, feats)
    gates_shape, cell_shape = (PIECES, streams, 4 * width), (PIECES, streams, width)
    bias_shape = (PIECES, 8, 4 * width)
    win_bv, rec_bv, proj_bv = win_b, rec_b, proj_b
    sources = (bias_a.astype(F32), bias_b.astype(F32), keep, start_h, start_c)
    inflow, proj_av, bias_av, bias_bv, keep_v, start_hv, start_cv = pl.pallas_call(
        begin_kernel,
        out_shape=(vmem(gates_shape, F32), vmem((cells, depth), BF16)) + tuple(vmem(x.shape, x.dtype) for x in sources),
        in_specs=[SMEM, VMEM, VMEM, VMEM] + [ANY] * (1 + len(sources)),
        out_specs=[VMEM] * (2 + len(sources)),
        scratch_shapes=[pltpu.SemaphoreType.DMA((1 + len(sources),))],
        compiler_params=params(8),
        name="begin",
    )(which, pinned(feats_v), pinned(win_av), pinned(win_bv), in_hbm(proj), *sources)

    def forward_call(first, step, part, peer, cell, inflow):
        return pl.pallas_call(
            functools.partial(forward_kernel, first),
            out_shape=(
                vmem((streams, depth), BF16),
                vmem(cell_shape, F32),
                vmem(gates_shape, BF16),
                vmem(cell_shape, BF16),
                vmem((streams, depth), BF16),
                vmem((streams, depth), BF16),
                vmem((streams, depth), F32),
            ),
            in_specs=[SMEM] + [VMEM] * 10,
            out_specs=[VMEM] * 7,
            compiler_params=params(8),
            name="forward_step",
        )(
            at_step(step), pinned(part), pinned(peer), pinned(start_hv), pinned(keep_v), pinned(cell), pinned(inflow),
            pinned(rec_av), pinned(rec_bv), pinned(proj_av), pinned(proj_bv),
        )

    def between_call(step, fresh, stacks, passing=()):
        shapes = (
            hbm((PIECES, steps, streams, 4 * width), BF16),
            hbm((steps,) + cell_shape, F32),
            hbm((PIECES, steps, streams, width), BF16),
            hbm((steps, streams, depth), BF16),
            hbm((steps, streams, depth), BF16),
            hbm((steps, streams, depth), F32),
        )
        aliases = {12 + i: 1 + i for i in range(len(stacks))}
        aliases.update({12 + len(stacks) + i: 7 + i for i in range(len(passing))})
        inflow, *out = pl.pallas_call(
            functools.partial(between_kernel, not stacks, step == steps - 1, len(passing)),
            out_shape=(vmem(gates_shape, F32),) + shapes + tuple(hbm(x.shape, x.dtype) for x in passing),
            in_specs=[SMEM] + [VMEM] * 11 + [ANY] * (len(stacks) + len(passing)),
            out_specs=[VMEM] + [ANY] * (6 + len(passing)),
            scratch_shapes=[pltpu.SemaphoreType.DMA((2 * PIECES + 4,))],
            input_output_aliases=aliases,
            compiler_params=params(8),
            cost_estimate=cost(2 * streams * depth * 8 * cells, 8 * depth * cells * 2),
            name="between",
        )(
            at_step(step), pinned(feats_v), pinned(bias_av), pinned(bias_bv), pinned(win_av), pinned(win_bv),
            *(pinned(x) for x in fresh), *(in_hbm(x) for x in (*stacks, *passing)),
        )
        return inflow, tuple(out[:6]), tuple(out[6:])

    none = jnp.zeros((streams, depth), BF16)
    part, peer, cell, stacks = none, none, start_cv, ()
    for step in range(steps):
        cell_before = cell
        part, cell, *fresh = forward_call(step == 0, step, part, peer, cell, inflow)
        peer = lax.ppermute(part, "gate", across)
        if step == steps - 1:
            break
        if step == 2:
            (early_feat,) = after((part,), feat_all)
            feat_in = (swapped(early_feat, near_swap), swapped(early_feat, far_swap))
        due = step == (3 * steps) // 4
        inflow, stacks, passed = between_call(step, (cell, *fresh), stacks, feat_in if due else ())
        feat_in = passed if due else (feat_in if step >= 2 else None)
    gates, mixed, prev, hidden, slope = fresh
    gates_all, cells_all, mixed_all, prev_all, hidden_all, slope_all = stacks

    slope_now, up_now, mixed_all, prev_all, hidden_all, slope_all = pl.pallas_call(
        finish_kernel,
        out_shape=(vmem((streams, depth), F32), vmem((streams, depth), BF16))
        + tuple(hbm(x.shape, x.dtype) for x in (mixed_all, prev_all, hidden_all, slope_all)),
        in_specs=[SMEM] + [VMEM] * 6 + [ANY] * 5,
        out_specs=[VMEM] * 2 + [ANY] * 4,
        scratch_shapes=[pltpu.VMEM((streams, depth), BF16), pltpu.SemaphoreType.DMA((PIECES + 5,))],
        input_output_aliases={8 + i: 2 + i for i in range(4)},
        compiler_params=params(8),
        name="finish",
    )(
        at_step(steps - 1), pinned(part), pinned(peer), *(pinned(x) for x in (mixed, prev, hidden, slope)), in_hbm(ups),
        *(in_hbm(x) for x in (mixed_all, prev_all, hidden_all, slope_all)),
    )
    saved = (gates, cell, cell_before, slope_now, up_now)
    saved_shapes = (
        vmem(gates_shape, BF16),
        vmem(cell_shape, F32),
        vmem(cell_shape, F32),
        vmem((streams, depth), F32),
        vmem((streams, depth), BF16),
    )

    rec_atv, rec_btv, proj_atv, proj_btv = pl.pallas_call(
        turned_kernel,
        out_shape=(vmem((4, cells, depth), BF16),) * 2 + (vmem((depth, cells), BF16),) * 2,
        in_specs=[VMEM] * 4,
        out_specs=[VMEM] * 4,
        compiler_params=params(8),
        name="turned",
    )(pinned(rec_av), pinned(rec_bv), pinned(proj_av), pinned(proj_bv))

    def backward_call(step, part, peer, grad, bias, saved):
        return pl.pallas_call(
            backward_kernel,
            out_shape=(
                vmem((streams, depth), BF16),
                vmem(cell_shape, F32),
                vmem(bias_shape, F32),
                vmem((streams, depth), BF16),
                vmem(gates_shape, BF16),
            ),
            in_specs=[SMEM] + [VMEM] * 15,
            out_specs=[VMEM] * 5,
            compiler_params=params(8),
            name="backward_step",
        )(
            at_step(step), pinned(part), pinned(peer), pinned(keep_v), pinned(grad), pinned(bias),
            pinned(rec_atv), pinned(rec_btv), pinned(proj_atv), pinned(proj_btv),
            *(pinned(x) for x in saved), pinned(start_cv),
        )

    def aside_call(step, slot, slots, dz, raw, stacks, sends, passing):
        piece_shape = (streams, 4 * width)
        shapes = (
            hbm((PIECES, steps) + piece_shape, BF16),
            hbm((steps, streams, depth), BF16),
            hbm((steps,) + piece_shape, BF16),
            hbm((steps,) + piece_shape, BF16),
            hbm((slots,) + piece_shape, BF16),
            hbm((slots,) + piece_shape, BF16),
        )
        kept = len(stacks)
        aliases = {7 + i: 5 + i for i in range(kept)}
        aliases.update({7 + kept + i: 9 + i for i in range(len(sends))})
        aliases.update({7 + kept + len(sends) + i: 11 + i for i in range(len(passing))})
        out = pl.pallas_call(
            functools.partial(aside_kernel, not stacks, step == 0, not sends, len(passing)),
            out_shape=saved_shapes + shapes + tuple(hbm(x.shape, x.dtype) for x in passing),
            in_specs=[SMEM] + [VMEM] * 2 + [ANY] * (4 + kept + len(sends) + len(passing)),
            out_specs=[VMEM] * 5 + [ANY] * (6 + len(passing)),
            scratch_shapes=[
                pltpu.SemaphoreType.DMA((PIECES + 5,)),
                pltpu.SemaphoreType.DMA((PIECES + 4,)),
            ],
            input_output_aliases=aliases,
            compiler_params=params(8),
            cost_estimate=cost(0, 8 * MIB),
            name="aside",
        )(
            jnp.concatenate([at_step(step), jnp.stack([jnp.int32(slot), low, high])]), pinned(dz), pinned(raw),
            in_hbm(gates_all), in_hbm(cells_all), in_hbm(ups), in_hbm(slope_all),
            *(in_hbm(x) for x in (*stacks, *sends, *passing)),
        )
        return out[:5], tuple(out[5:9]), tuple(out[9:11]), tuple(out[11:])

    carry = (none, none, jnp.zeros(cell_shape, F32), jnp.zeros(bias_shape, F32), saved, ())
    pending, arrived, ready, top = [], [], None, steps
    for index, share in enumerate(SHARES):
        slots = top if index == len(SHARES) - 1 else round(share * steps)
        sends = ()
        for step in range(top - 1, top - slots - 1, -1):
            part, peer, grad, bias_sum, saved, stacks = carry
            part, grad, bias_sum, raw, dz = backward_call(step, part, peer, grad, bias_sum, saved)
            peer = lax.ppermute(part, "gate", across)
            if step == steps - 1:
                (early_prev,) = after((part,), prev_all)
                pending.append((step - steps // 3, (swapped(early_prev, near_swap), swapped(early_prev, far_swap))))
            if ready is not None:
                due, sides = ready
                sides = after((part,), *sides) if step else sides
                pending.append((due, (swapped(sides[0], near_swap), swapped(sides[1], far_swap))))
                ready = None
            passing = ()
            while pending and pending[0][0] >= step:
                passing += pending.pop(0)[1]
            saved, stacks, sends, passed = aside_call(
                step, step - (top - slots), slots, dz, raw, stacks, sends, passing
            )
            arrived += [passed[i : i + 2] for i in range(0, len(passed), 2)]
            carry = (part, peer, grad, bias_sum, saved, stacks)
        top -= slots
        ready = (max(top - 1 - (3 * slots + 3) // 4, 0 if slots > 2 else -1), sends)
    pending.append((-1, (swapped(sends[0], near_swap), swapped(sends[1], far_swap))))
    arrived += [arrays for _, arrays in pending]
    dz_all, raw_all, near_all, far_all = carry[-1]
    bias_sum = carry[3]
    prev_in, exchanged = arrived[0], arrived[1:]
    rows = steps * streams

    def by_direction(mine, theirs):
        return jnp.stack([jnp.where(own == 0, mine, theirs), jnp.where(own == 0, theirs, mine)])

    def line_sum(chunks, axis, stride, count, first=None, gates={}):
        def chunk(*name):
            return pick(chunks, number[(stride, *name)], axis)

        def at(device):
            return (device // stride) % count

        if count == 2:
            pairs = [(i, i + stride if at(i) == 0 else i - stride) for i in range(n_batch)]
            return (chunk("here").astype(F32) + swapped(chunk("not_here"), pairs).astype(F32)).astype(BF16)
        ends = [(i, i + stride) for i in range(n_batch) if at(i) == 0]
        ends += [(i, i - stride) for i in range(n_batch) if at(i) == count - 1]
        up = down = swapped(chunk("begin") if first is None else first, ends)
        for slot in range(2, count):
            if slot in gates:
                up, down = gates[slot](up, down)
            rise = (chunk("rise", slot).astype(F32) + up.astype(F32)).astype(BF16)
            fall = (chunk("fall", slot).astype(F32) + down.astype(F32)).astype(BF16)
            up = swapped(rise, [(i, i + stride) for i in range(n_batch) if at(i) < min(slot, count - 1)])
            down = swapped(fall, [(i, i - stride) for i in range(n_batch) if at(i) > max(count - 1 - slot, 0)])
        if count in gates:
            up, down = gates[count](up, down)
        return (chunk("here").astype(F32) + up.astype(F32) + down.astype(F32)).astype(BF16)

    share_rows = depth // n_batch

    def input_grad_of(dz):
        return pl.pallas_call(
            input_grad_kernel,
            out_shape=jax.ShapeDtypeStruct((steps, streams, depth), F32),
            grid_spec=pltpu.PrefetchScalarGridSpec(
                num_scalar_prefetch=1,
                grid=(PIECES, 4),
                in_specs=[
                    pl.BlockSpec((1, steps, streams, width), lambda p, g, turn: (p, 0, 0, g)),
                    pl.BlockSpec(
                        (1, depth, width), lambda p, g, turn: (jnp.where(p < 2, g, 3), 0, jnp.where(p < 2, p, 1))
                    ),
                    pl.BlockSpec(
                        (1, depth, width), lambda p, g, turn: (jnp.where(p < 2, 0, g), 0, jnp.where(p < 2, 0, p - 2))
                    ),
                ],
                out_specs=pl.BlockSpec((steps, streams, depth), lambda p, g, turn: (0, 0, 0)),
                scratch_shapes=[pltpu.VMEM((rows, depth), F32)],
            ),
            compiler_params=params(16),
            cost_estimate=cost(0, 0),
            name="input_grad",
        )(turn, in_hbm(dz), in_hbm(win_a), in_hbm(win_b))

    grad_proj = jnp.einsum("ptnc,tnk->pkc", mixed_all, raw_all, preferred_element_type=F32).astype(BF16)
    grad_proj = grad_proj.reshape(PIECES, line, 2, share_rows, width)
    bias_rows = pl.pallas_call(
        bias_kernel,
        out_shape=jax.ShapeDtypeStruct((PIECES, 4, width), F32),
        in_specs=[VMEM],
        out_specs=VMEM,
        compiler_params=params(1),
        name="bias",
    )(pinned(bias_sum))
    bias_rows = jnp.broadcast_to(bias_rows[:, None, None].astype(BF16), (PIECES, line, 2, 4, width))
    grad_proj = jnp.concatenate([grad_proj, bias_rows], axis=3)

    def with_partner(grad):
        mine, sent = (pick(grad, number[x], grad.ndim - 3) for x in ("low", "not_low"))
        taken = swapped(sent, near_swap)
        return sent, taken, (mine.astype(F32) + taken.astype(F32)).astype(BF16)

    def across_two(grad):
        return line_sum(grad.reshape(grad.shape[:-3] + (line // 2, 2) + grad.shape[-2:]), grad.ndim - 3, 4, line // 2)

    proj_sent, proj_taken, proj_y = with_partner(grad_proj)

    lows, count = [], 0
    for x in exchanged[::-1]:
        lows.insert(0, count)
        count += x[0].shape[0]

    def gathered(kept, feat, prev, parts):
        return pl.pallas_call(
            functools.partial(gather_kernel, tuple(lows[: len(parts)])),
            out_shape=(vmem((2 * steps, streams, 2 * depth), BF16), vmem((2 * steps, streams, 4 * width), BF16)),
            in_specs=[ANY] * (5 + len(parts)),
            out_specs=[VMEM] * 2,
            scratch_shapes=[pltpu.SemaphoreType.DMA((5 + len(parts),))],
            compiler_params=params(1),
            cost_estimate=cost(0, 0),
            name="gather",
        )(*(in_hbm(x) for x in (feat_all, prev_all, feat, prev, kept, *parts)))

    def completed(begin, rows_out, left, right, parts):
        return pl.pallas_call(
            functools.partial(late_kernel, tuple(lows[len(lows) - len(parts) :])),
            out_shape=(vmem(right.shape, BF16), jax.ShapeDtypeStruct((2, max(rows_out, 8), 4 * width), BF16)),
            in_specs=[SMEM] + [VMEM] * 2 + [ANY] * len(parts),
            out_specs=[VMEM] * 2,
            scratch_shapes=[pltpu.SemaphoreType.DMA((len(parts),))],
            input_output_aliases={2: 0},
            compiler_params=params(16),
            cost_estimate=cost(0, 0),
            name="late",
        )(begin, pinned(left), pinned(right), *(in_hbm(x) for x in parts))

    def multiplied(left, right):
        return pl.pallas_call(
            product_kernel,
            out_shape=jax.ShapeDtypeStruct((2, depth, 4 * width), BF16),
            in_specs=[VMEM] * 2,
            out_specs=VMEM,
            compiler_params=params(16),
            cost_estimate=cost(0, 0),
            name="product",
        )(pinned(left), pinned(right))

    near_parts, far_parts = zip(*exchanged)
    chunk_rows = 2 * share_rows if 2 * share_rows % 128 == 0 else 0
    near_left, near_right = gathered(near_all, feat_in[0], prev_in[0], near_parts[:-LATE])
    near_late = after((near_left, proj_sent, *far_parts[-LATE:]), *near_parts[-LATE:])
    near_right, first = completed(jnp.full((1,), number["begin"], jnp.int32), chunk_rows, near_left, near_right, near_late)
    far_all, *far_parts = after((first,), far_all, *far_parts)
    far_left, far_right = gathered(far_all, feat_in[1], prev_in[1], far_parts[:-LATE])
    far_right, _ = completed(jnp.zeros((1,), jnp.int32), 0, far_left, far_right, far_parts[-LATE:])
    far = multiplied(far_left, far_right).reshape(2, line, 2, share_rows, 4 * width)
    near = multiplied(near_left, near_right).reshape(2, line, 2, share_rows, 4 * width)

    def states_of(hidden, cell):
        both_hidden = trade(hidden, hidden)

        hidden_dirs = by_direction(*both_hidden)
        outputs = (inputs.astype(F32) + jnp.transpose(hidden_dirs, (0, 2, 1, 3)).astype(F32)).astype(BF16)
        last_h = jnp.stack([hidden_dirs[0, steps - 1], hidden_dirs[1, 0]], axis=1).astype(F32)
        final_h = jnp.zeros_like(state_h).at[stream_doc].set(last_h)
        last_c = jnp.transpose(cell.reshape(QUARTERS, HALVES, streams, width), (0, 2, 1, 3)).reshape(
            QUARTERS, streams, cells
        )
        last_dirs = by_direction(*trade(last_c[0], last_c[1]))
        final_c = jnp.zeros_like(state_c).at[stream_doc].set(jnp.transpose(last_dirs, (1, 0, 2)))
        return outputs, final_h, final_c

    tokens = {}

    def second(up, down):
        up, sent, tokens["dz"], proj_sum = after((), up, far, dz_all, proj_y, free=2 * MIB)
        tokens["in"], tokens["rec"] = (with_partner(sent[i])[2] for i in range(2))
        tokens["proj"] = across_two(proj_sum)
        return up, up

    def third(up, down):
        dx = input_grad_of(tokens["dz"])
        up, down, tokens["dx"], in_sum, tokens["proj"], hidden, last_cell = after(
            (), up, down, dx, tokens["in"], tokens["proj"], hidden_all, cell, free=2 * MIB
        )
        tokens["in"] = across_two(in_sum)
        tokens["states"] = states_of(hidden, last_cell)
        return up, down

    def final(up, down):
        up, down, tokens["in"], rec_sum = after(tokens["states"], up, down, tokens["in"], tokens["rec"], free=2 * MIB)
        tokens["rec"] = across_two(rec_sum)
        return up, down

    gates = {2: second, 3: third, line: final} if line > 3 else {}
    first = first.reshape(2, 2, share_rows, 4 * width) if chunk_rows else None
    near = line_sum(near, 1, 2, line, first, gates)
    dx_all, (outputs, final_h, final_c) = tokens["dx"], tokens["states"]
    in_two, rec_two, proj_two = tokens["in"], tokens["rec"], tokens["proj"]

    def halves_of(summed, name, pairs):
        return pick(summed, number[name], 1), swapped(pick(summed, number["not_" + name], 1), pairs)

    near_pair = halves_of(near, "low", near_swap)
    far_pair = halves_of(jnp.stack([in_two, rec_two]), "high", far_swap)
    far_pair = [lax.ppermute(x, "gate", swap) for x in far_pair]
    proj_mine, proj_theirs = halves_of(proj_two, "high", far_swap)
    grad_proj = proj_mine.astype(F32) + proj_theirs.astype(F32)
    grad_shape = (2, share_rows, 4, cells)
    grad_w_in, grad_w_rec = pl.pallas_call(
        assemble_kernel,
        out_shape=(jax.ShapeDtypeStruct(grad_shape, F32),) * 2,
        in_specs=[SMEM] + [VMEM] * 4,
        out_specs=[VMEM] * 2,
        compiler_params=params(14),
        name="assemble",
    )(jnp.stack([own, low, high]), *near_pair, *far_pair)

    def home(mine, theirs):
        return by_direction(*trade(mine, theirs)).astype(F32)

    own_cells = cells // n_batch
    shaped = jnp.transpose(grad_proj[:, share_rows:].reshape(QUARTERS, HALVES, 4, width), (0, 2, 1, 3))
    shaped = pick(shaped.reshape(QUARTERS, 4, n_batch, own_cells), number["spot"], 2)
    grad_bias = home(shaped[0], shaped[1])
    grad_proj = grad_proj[:, :share_rows].reshape(QUARTERS, HALVES, share_rows, width)
    grad_proj = jnp.transpose(grad_proj, (0, 1, 3, 2)).reshape(QUARTERS, cells, share_rows).astype(BF16)
    grad_proj = home(grad_proj[0], grad_proj[1])

    def columns(array, name, size):
        return lax.dynamic_slice_in_dim(array, number[name], size, 2, allow_negative_indices=False)

    dx_half = columns(dx_all, "cols", half_cols)
    dx_sent = columns(dx_all, "other_cols", half_cols).astype(BF16)
    dx_half = dx_half + lax.ppermute(dx_sent, "gate", across).astype(F32)
    dx_half = (dx_half + columns(ups, "cols", half_cols).astype(F32)).astype(BF16)
    dx_half = dx_half.reshape(steps, streams, 2, quarter_cols)
    dx_dirs = by_direction(*trade(pick(dx_half, own, 2), pick(dx_half, number["other"], 2)))
    input_grad = jnp.transpose(dx_dirs, (0, 2, 1, 3))
    return (outputs, input_grad, grad_w_in, grad_w_rec, grad_bias, grad_proj, final_h, final_c)


def solution(mesh):
    placed = (
        P(None, "batch", None, None),
        P(None, None, None, "gate"),
        P(None, None, None, "gate"),
        P(None, None, "gate"),
        P(None, "gate", None),
        P("batch", None, None),
        P("batch", None, "gate"),
        P("batch", None),
        P("batch"),
        P(None, "batch", None, None),
    )
    return jax.shard_map(
        body,
        mesh=mesh,
        in_specs=placed,
        out_specs=(
            P(None, "batch", None, None),
            P(None, "batch", None, "gate"),
            P(None, "batch", None, "gate"),
            P(None, "batch", None, "gate"),
            P(None, None, ("gate", "batch")),
            P(None, "gate", "batch"),
            P("batch", None, None),
            P("batch", None, "gate"),
        ),
        check_vma=False,
    )
```

```python
import functools

import jax
import jax.numpy as jnp
from jax import lax
from jax.experimental import pallas as pl
from jax.experimental.pallas import tpu as pltpu
from jax.sharding import PartitionSpec as P

CLIP = 3.0
F32, BF16 = jnp.float32, jnp.bfloat16
QUARTERS, HALVES = 2, 2
PIECES = QUARTERS * HALVES
MIB = 2**20
LATE = 2
SHARES = (0.35, 0.3, 0.15, 0.1, 0.1)

VMEM = pl.BlockSpec(memory_space=pltpu.VMEM)
SMEM = pl.BlockSpec(memory_space=pltpu.SMEM)
ANY = pl.BlockSpec(memory_space=pl.ANY)


def pinned(array):
    return pltpu.with_memory_space_constraint(array, pltpu.VMEM)


def in_hbm(array):
    return pltpu.with_memory_space_constraint(array, pltpu.HBM)


def dot(left, right):
    return jnp.dot(left, right, preferred_element_type=F32)


def layout_kernel(keep, spread, which_ref, w_ref, *refs):
    buf, sems, out_sems = refs[-3:]
    out_ref = refs[0] if keep else refs[1]
    all_ref = refs[1] if keep else refs[0]
    depth, ahead, part = w_ref.shape[1], buf.shape[0], buf.shape[1]
    count = depth // part

    def fetch(i):
        return pltpu.make_async_copy(w_ref.at[which_ref[0], pl.ds(i * part, part)], buf.at[i % ahead], sems.at[i % ahead])

    def store(i):
        rows = pl.ds(i * part, part)
        return pltpu.make_async_copy(out_ref.at[:, rows], all_ref.at[:, rows], out_sems.at[i])

    for i in range(min(ahead - 1, count)):
        fetch(i).start()
    for i in range(count):
        if i + ahead - 1 < count:
            fetch(i + ahead - 1).start()
        fetch(i).wait()
        out_ref[:, i * part : (i + 1) * part, :] = jnp.swapaxes(buf[i % ahead], 0, 1)
        if spread:
            store(i).start()
    for i in range(count if spread else 0):
        store(i).wait()


def turned_kernel(wa_ref, wb_ref, pa_ref, pb_ref, wat_ref, wbt_ref, pat_ref, pbt_ref):
    for w_ref, out_ref in ((wa_ref, wat_ref), (wb_ref, wbt_ref)):
        for gate in range(4):
            for half in range(HALVES):
                width = w_ref.shape[2] // HALVES
                cols = slice(half * width, (half + 1) * width)
                out_ref[gate, cols, :] = w_ref[gate, :, cols].T
    pat_ref[...] = pa_ref[...].T
    pbt_ref[...] = pb_ref[...].T


def pass_kernel(*refs):
    pass


def after(tokens, *arrays, free=0):
    count = len(tokens)
    return pl.pallas_call(
        pass_kernel,
        out_shape=tuple(jax.ShapeDtypeStruct(x.shape, x.dtype) for x in arrays),
        in_specs=[ANY] * (count + len(arrays)),
        out_specs=[ANY] * len(arrays),
        input_output_aliases={count + i: i for i in range(len(arrays))},
        compiler_params=params(1),
        name="after",
    )(*tokens, *(in_hbm(x) if x.size * x.dtype.itemsize > free else x for x in arrays))


def gather_kernel(lows, *refs):
    (feat_ref, prev_ref, feat_too, prev_too, kept_ref), refs = refs[:5], refs[5:]
    groups, (left_ref, right_ref, sems) = refs[:-3], refs[-3:]
    steps, _, depth = feat_ref.shape
    jobs = [
        (feat_ref, left_ref.at[:steps, :, :depth]),
        (prev_ref, left_ref.at[:steps, :, depth:]),
        (feat_too, left_ref.at[steps:, :, :depth]),
        (prev_too, left_ref.at[steps:, :, depth:]),
        (kept_ref, right_ref.at[:steps]),
    ]
    jobs += [(x, right_ref.at[steps + low : steps + low + x.shape[0]]) for x, low in zip(groups, lows)]
    copies = [pltpu.make_async_copy(a, b, sems.at[i]) for i, (a, b) in enumerate(jobs)]
    for copy in copies:
        copy.start()
    for copy in copies:
        copy.wait()


def late_kernel(lows, begin_ref, left_ref, right_in, *refs):
    groups, (right_ref, first_ref, sems) = refs[:-3], refs[-3:]
    steps = left_ref.shape[0] // 2
    copies = [
        pltpu.make_async_copy(x, right_ref.at[steps + low : steps + low + x.shape[0]], sems.at[i])
        for i, (x, low) in enumerate(zip(groups, lows))
    ]
    for copy in copies:
        copy.start()
    for copy in copies:
        copy.wait()
    if first_ref.shape[1] % 128:
        return
    share, depth = first_ref.shape[1], left_ref.shape[2] // 2
    rows = left_ref.shape[0] * left_ref.shape[1]
    left = [
        left_ref[:, :, pl.ds(pl.multiple_of(i * depth + begin_ref[0] * share, 128), share)].reshape(rows, share)
        for i in range(2)
    ]
    left = jnp.concatenate([x.T for x in left], axis=0)
    width = right_ref.shape[2] // 4

    def columns(i, _):
        cols = pl.ds(pl.multiple_of(i * width, width), width)
        total = dot(left, right_ref[:, :, cols].reshape(rows, width)).astype(BF16)
        first_ref[0, :, cols] = total[:share]
        first_ref[1, :, cols] = total[share:]
        return 0

    lax.fori_loop(0, 4, columns, 0)


def product_kernel(left_ref, right_ref, out_ref):
    rows, depth = left_ref.shape[0] * left_ref.shape[1], left_ref.shape[2] // 2
    width = right_ref.shape[2] // 4
    for which in range(2):
        left = left_ref[:, :, which * depth : (which + 1) * depth].reshape(rows, depth).T

        def columns(i, _):
            cols = pl.ds(pl.multiple_of(i * width, width), width)
            out_ref[which, :, cols] = dot(left, right_ref[:, :, cols].reshape(rows, width)).astype(BF16)
            return 0

        lax.fori_loop(0, 4, columns, 0)


def assemble_kernel(place_ref, near_a, near_b, far_a, far_b, in_ref, rec_ref):
    own, low, high = place_ref[0], place_ref[1], place_ref[2]
    width = in_ref.shape[3] // HALVES
    for direction, mine_ref, theirs_ref, index in ((own, near_a, near_b, low), (1 - own, far_a, far_b, high)):
        for which, out_ref in ((0, in_ref), (1, rec_ref)):
            mine, theirs = mine_ref[which].astype(F32), theirs_ref[which].astype(F32)
            for half in range(HALVES):
                whole = jnp.where(index == half, mine, theirs)
                gates = jnp.stack([whole[:, gate * width : (gate + 1) * width] for gate in range(4)])
                out_ref[direction, :, :, half * width : (half + 1) * width] = jnp.swapaxes(gates, 0, 1)


def order_kernel(step_ref, feat_ref, out_ref, all_ref, sems):
    copies = []
    for i in range(feat_ref.shape[0]):
        source = feat_ref.at[step_ref[0] + step_ref[1] * i]
        copies.append(pltpu.make_async_copy(source, out_ref.at[i], sems.at[2 * i]))
        copies.append(pltpu.make_async_copy(source, all_ref.at[i], sems.at[2 * i + 1]))
    for copy in copies:
        copy.start()
    for copy in copies:
        copy.wait()


def numbers_kernel(in_ref, out_ref):
    for i in range(in_ref.shape[0]):
        out_ref[i] = in_ref[i]


def bias_kernel(sum_ref, out_ref):
    width = sum_ref.shape[2] // 4
    for piece in range(PIECES):
        for gate in range(4):
            out_ref[piece, gate : gate + 1, :] = jnp.sum(
                sum_ref[piece, :, gate * width : (gate + 1) * width], axis=0, keepdims=True
            )


def pieces(refs, axis):
    for piece in range(PIECES):
        quarter, half = divmod(piece, HALVES)
        width = refs[0].shape[axis] // HALVES
        yield piece, quarter, width, slice(half * width, (half + 1) * width)


def forward_kernel(
    first, step_ref, p_ref, q_ref, start_ref, keep_ref, cell_ref, inflow_ref, wa_ref, wb_ref, pa_ref, pb_ref,
    part_ref, next_ref, gates_ref, mixed_ref, prev_ref, hidden_ref, slope_ref,
):
    keep = keep_ref[step_ref[1]][:, :1]
    if first:
        hidden = start_ref[...]
    else:
        hidden = clipped(p_ref, q_ref, hidden_ref, slope_ref)
    hidden = hidden * keep.astype(BF16)
    prev_ref[...] = hidden
    part = jnp.zeros(part_ref.shape, F32)
    for piece, quarter, width, cols in pieces((wa_ref, wb_ref), 2):
        w_ref, proj_ref = ((wa_ref, pa_ref), (wb_ref, pb_ref))[quarter]
        acts = []
        for gate in range(4):
            place = slice(gate * width, (gate + 1) * width)
            pre = dot(hidden, w_ref[gate, :, cols]) + inflow_ref[piece, :, place]
            act = jnp.tanh(pre if gate == 2 else 0.5 * pre)
            gates_ref[piece, :, place] = act.astype(BF16)
            acts.append(act if gate == 2 else 0.5 + 0.5 * act)
        ingate, forget, candidate, outgate = acts
        cell = CLIP * jnp.tanh((forget * (keep * cell_ref[piece]) + ingate * candidate) * (1.0 / CLIP))
        next_ref[piece] = cell
        mixed = (outgate * jnp.tanh(cell)).astype(BF16)
        mixed_ref[piece] = mixed
        part = part + dot(mixed, proj_ref[cols, :])
    part_ref[...] = part.astype(BF16)


def clipped(p_ref, q_ref, hidden_ref, slope_ref):
    squash = jnp.tanh((p_ref[...].astype(F32) + q_ref[...].astype(F32)) * (1.0 / CLIP))
    hidden = (CLIP * squash).astype(BF16)
    hidden_ref[...] = hidden
    slope_ref[...] = 1.0 - squash * squash
    return hidden


def between_kernel(
    first, last, passed, step_ref, feat_ref, ba_ref, bb_ref, wa_ref, wb_ref, cell_ref, gates_ref, mixed_ref, prev_ref, hidden_ref,
    slope_ref, *refs,
):
    refs = refs[(0 if first else 6) + passed :]
    out_ref, gates_all, cells_all, mixed_all, prev_all, hidden_all, slope_all = refs[:7]
    sems = refs[-1]
    step, time_before = step_ref[0], step_ref[2]
    copies = [pltpu.make_async_copy(gates_ref.at[i], gates_all.at[i, step], sems.at[i]) for i in range(PIECES)]
    copies += [
        pltpu.make_async_copy(mixed_ref.at[i], mixed_all.at[i, step], sems.at[PIECES + i]) for i in range(PIECES)
    ]
    copies.append(pltpu.make_async_copy(cell_ref, cells_all.at[step], sems.at[2 * PIECES]))
    copies.append(pltpu.make_async_copy(prev_ref, prev_all.at[step], sems.at[2 * PIECES + 1]))
    if not first:
        copies.append(pltpu.make_async_copy(hidden_ref, hidden_all.at[time_before], sems.at[2 * PIECES + 2]))
        copies.append(pltpu.make_async_copy(slope_ref, slope_all.at[step - 1], sems.at[2 * PIECES + 3]))
    for copy in copies:
        copy.start()
    if not last:
        inflow_into(feat_ref[step + 1], ba_ref, bb_ref, wa_ref, wb_ref, out_ref)
    for copy in copies:
        copy.wait()


def inflow_into(feat, ba_ref, bb_ref, wa_ref, wb_ref, out_ref, quarters=(0, 1)):
    for piece, quarter, width, cols in pieces((wa_ref, wb_ref), 2):
        if quarter not in quarters:
            continue
        w_ref, bias_ref = ((wa_ref, ba_ref), (wb_ref, bb_ref))[quarter]
        for gate in range(4):
            place = slice(gate * width, (gate + 1) * width)
            out_ref[piece, :, place] = dot(feat, w_ref[gate, :, cols]) + bias_ref[gate : gate + 1, cols]


def begin_kernel(which_ref, feat_ref, wa_ref, proj_ref, *refs):
    sems = refs[-1]
    out_ref, pa_ref, *placed = refs[-11:-1]
    copies = [pltpu.make_async_copy(x, y, sems.at[i]) for i, (x, y) in enumerate(zip(refs[:-11], placed))]
    copies.append(pltpu.make_async_copy(proj_ref.at[which_ref[0]], pa_ref, sems.at[len(copies)]))
    for copy in copies:
        copy.start()
    ba_ref, bb_ref, wb_ref = placed[:3]
    copies[0].wait()
    inflow_into(feat_ref[0], ba_ref, bb_ref, wa_ref, wb_ref, out_ref, (0,))
    copies[1].wait()
    copies[2].wait()
    inflow_into(feat_ref[0], ba_ref, bb_ref, wa_ref, wb_ref, out_ref, (1,))
    for copy in copies[3:]:
        copy.wait()


def backward_kernel(
    step_ref, p_ref, q_ref, keep_ref, grad_ref, bias_ref, wa_ref, wb_ref, pa_ref, pb_ref,
    gates_ref, cell_ref, prev_ref, slope_ref, up_ref, start_ref,
    part_ref, next_ref, sum_ref, raw_ref, dz_ref,
):
    step = step_ref[0]
    keep = keep_ref[step_ref[1]][:, :1]
    raw = (up_ref[...].astype(F32) + (p_ref[...].astype(F32) + q_ref[...].astype(F32))) * slope_ref[...]
    raw = raw.astype(BF16)
    raw_ref[...] = raw
    part = jnp.zeros(part_ref.shape, F32)
    for piece, quarter, width, cols in pieces((wa_ref, wb_ref), 1):
        w_ref, proj_ref = ((wa_ref, pa_ref), (wb_ref, pb_ref))[quarter]
        mixed = dot(raw, proj_ref[:, cols])
        acts = [gates_ref[piece, :, gate * width : (gate + 1) * width].astype(F32) for gate in range(4)]
        ingate, forget, outgate = (0.5 + 0.5 * acts[gate] for gate in (0, 1, 3))
        slopes = [1.0 - act * act for act in acts]
        cell = cell_ref[piece]
        prev = keep * jnp.where(step == 0, start_ref[piece], prev_ref[piece])
        squash = jnp.tanh(cell)
        total = grad_ref[piece] + mixed * outgate * (1.0 - squash * squash)
        inner = total * (1.0 - (cell * (1.0 / CLIP)) * (cell * (1.0 / CLIP)))
        next_ref[piece] = keep * inner * forget
        quart = 0.25 * inner
        pre_grads = (
            quart * acts[2] * slopes[0],
            quart * prev * slopes[1],
            inner * ingate * slopes[2],
            0.25 * mixed * squash * slopes[3],
        )
        for gate in range(4):
            low = pre_grads[gate].astype(BF16)
            place = slice(gate * width, (gate + 1) * width)
            dz_ref[piece, :, place] = low
            rows = pre_grads[gate].reshape(-1, 8, width)
            sum_ref[piece, :, place] = bias_ref[piece, :, place] + jnp.sum(rows, axis=0)
            part = part + dot(low, w_ref[gate, cols, :])
    part_ref[...] = (part * keep).astype(BF16)


def finish_kernel(
    step_ref, p_ref, q_ref, mixed_ref, prev_ref, hidden_ref, before_ref, ups_all, mixed_in, prev_in, hidden_in, slope_in,
    slope_ref, up_ref, mixed_all, prev_all, hidden_all, slope_all, hidden_buf, sems,
):
    step, time, time_before = step_ref[0], step_ref[1], step_ref[2]
    jobs = [(mixed_ref.at[i], mixed_all.at[i, step]) for i in range(PIECES)]
    jobs += [
        (ups_all.at[time], up_ref),
        (prev_ref, prev_all.at[step]),
        (hidden_ref, hidden_all.at[time_before]),
        (before_ref, slope_all.at[step - 1]),
        (hidden_buf, hidden_all.at[time]),
    ]
    copies = [pltpu.make_async_copy(x, y, sems.at[i]) for i, (x, y) in enumerate(jobs)]
    for copy in copies[:-1]:
        copy.start()
    clipped(p_ref, q_ref, hidden_buf, slope_ref)
    copies[-1].start()
    for copy in copies:
        copy.wait()


def fetches(step, time, sources, targets, sems):
    gates_all, cells_all, ups_all = sources
    gates_ref, cell_ref, prev_ref, up_ref = targets
    before = jnp.maximum(step - 1, 0)
    return [
        pltpu.make_async_copy(gates_all.at[i, step], gates_ref.at[i], sems.at[i]) for i in range(PIECES)
    ] + [
        pltpu.make_async_copy(cells_all.at[step], cell_ref, sems.at[PIECES]),
        pltpu.make_async_copy(cells_all.at[before], prev_ref, sems.at[PIECES + 1]),
        pltpu.make_async_copy(ups_all.at[time], up_ref, sems.at[PIECES + 2]),
    ]


def aside_kernel(
    first, last, opens, passed, step_ref, dz_ref, raw_ref, gates_all, cells_all, ups_all, slope_all, *refs
):
    refs = refs[(0 if first else 4) + (0 if opens else 2) + passed :]
    gates_ref, cell_ref, prev_ref, slope_ref, up_ref = refs[:5]
    dz_all, raw_all, near_all, far_all, near_out, far_out = refs[5:11]
    sems, fetch_sems = refs[-2:]
    step, time_before = step_ref[0], step_ref[2]
    slot, low, high = step_ref[4], step_ref[5], step_ref[6]
    before = jnp.maximum(step - 1, 0)
    copies = []
    if not last:
        copies += fetches(
            before, time_before, (gates_all, cells_all, ups_all), (gates_ref, cell_ref, prev_ref, up_ref), fetch_sems
        )
        copies.append(pltpu.make_async_copy(slope_all.at[before], slope_ref, fetch_sems.at[PIECES + 3]))
    copies += [pltpu.make_async_copy(dz_ref.at[i], dz_all.at[i, step], sems.at[i]) for i in range(PIECES)]
    copies.append(pltpu.make_async_copy(raw_ref, raw_all.at[step], sems.at[PIECES]))
    copies.append(pltpu.make_async_copy(dz_ref.at[low], near_all.at[step], sems.at[PIECES + 1]))
    copies.append(pltpu.make_async_copy(dz_ref.at[HALVES + high], far_all.at[step], sems.at[PIECES + 2]))
    copies.append(pltpu.make_async_copy(dz_ref.at[1 - low], near_out.at[slot], sems.at[PIECES + 3]))
    copies.append(pltpu.make_async_copy(dz_ref.at[HALVES + 1 - high], far_out.at[slot], sems.at[PIECES + 4]))
    for copy in copies:
        copy.start()
    for copy in copies:
        copy.wait()


def input_grad_kernel(step_ref, dz_ref, wa_ref, wb_ref, out_ref, acc_ref):
    piece, gate = pl.program_id(0), pl.program_id(1)
    steps, streams, width = dz_ref.shape[1:]

    @pl.when((piece == 0) & (gate == 0))
    def _():
        acc_ref[...] = jnp.zeros(acc_ref.shape, F32)

    weights = jnp.where(piece < HALVES, wa_ref[0], wb_ref[0])
    acc_ref[...] += lax.dot_general(
        dz_ref[0].reshape(steps * streams, width), weights, (((1,), (1,)), ((), ())), preferred_element_type=F32
    )

    @pl.when((piece == PIECES - 1) & (gate == 3))
    def _():
        for step in range(steps):
            time = step_ref[0] + step_ref[1] * step
            out_ref[time] = acc_ref[step * streams : (step + 1) * streams, :]


def params(mib):
    return pltpu.CompilerParams(vmem_limit_bytes=mib * MIB)


def cost(flops, size):
    return pl.CostEstimate(flops=flops, bytes_accessed=size, transcendentals=0)


def body(inputs, w_in, w_rec, bias, proj, state_h, state_c, resets, stream_doc, cotangent):
    streams, steps, depth = inputs.shape[1:]
    cells = w_in.shape[3]
    width = cells // HALVES
    n_batch = lax.axis_size("batch")
    gates_size = lax.axis_size("gate")
    line = n_batch // 2
    swap = [(i, i ^ 1) for i in range(gates_size)]
    across = [(i, i ^ 2) for i in range(gates_size)]
    near_swap = [(i, i ^ 1) for i in range(n_batch)]
    far_swap = [(i, i ^ 2) for i in range(n_batch)]

    rank, spot = lax.axis_index("gate"), lax.axis_index("batch")
    half_cols, quarter_cols = depth // 2, depth // 4
    place_numbers = {
        "own": rank % 2,
        "other": 1 - rank % 2,
        "low": spot % 2,
        "not_low": 1 - spot % 2,
        "high": (spot // 2) % 2,
        "not_high": 1 - (spot // 2) % 2,
        "spot": spot,
        "begin": jnp.where(spot // 2 == 0, line - 1, 0),
        "cols": (rank // 2) * half_cols,
        "other_cols": (1 - rank // 2) * half_cols,
    }
    for stride, count in {(2, line), (4, line // 2)}:
        here = (spot // stride) % count
        place_numbers[stride, "here"] = here
        place_numbers[stride, "not_here"] = jnp.maximum(1 - here, 0)
        for slot in range(2, count):
            place_numbers[stride, "rise", slot] = jnp.minimum(here + count - slot, count - 1)
            place_numbers[stride, "fall", slot] = jnp.maximum(here - count + slot, 0)
        if count > 2:
            place_numbers[stride, "begin"] = jnp.where(here == 0, count - 1, 0)
    names = sorted(place_numbers, key=str)
    gathered_numbers = pl.pallas_call(
        numbers_kernel,
        out_shape=jax.ShapeDtypeStruct((len(names),), jnp.int32),
        in_specs=[SMEM],
        out_specs=SMEM,
        name="numbers",
    )(jnp.stack([place_numbers[x] for x in names]).astype(jnp.int32))
    number = {x: place_numbers[x].astype(jnp.int32) for x in names}
    own, low, high = number["own"], number["low"], number["high"]
    which = lax.slice_in_dim(gathered_numbers, names.index("own"), names.index("own") + 1)

    def pick(stacked, index, axis=0):
        return lax.dynamic_index_in_dim(stacked, index, axis, keepdims=False, allow_negative_indices=False)

    def trade(mine, theirs):
        return (mine, lax.ppermute(theirs, "gate", swap))

    def vmem(shape, dtype):
        return pltpu.VMEM(shape, dtype)

    def hbm(shape, dtype):
        return pltpu.HBM(shape, dtype)

    def by_gate(weights, index, keep, spread):
        shape = (4,) + weights.shape[1:2] + weights.shape[3:]
        count = 16
        kept, spreads = (vmem(shape, BF16),) * keep, (hbm(shape, BF16),) * spread
        return pl.pallas_call(
            functools.partial(layout_kernel, keep, spread),
            out_shape=kept + spreads,
            in_specs=[SMEM, ANY],
            out_specs=[VMEM] * keep + [ANY] * spread,
            scratch_shapes=[pltpu.VMEM(shape, BF16)] * (1 - keep)
            + [
                pltpu.VMEM((4, weights.shape[1] // count) + weights.shape[2:], BF16),
                pltpu.SemaphoreType.DMA((4,)),
                pltpu.SemaphoreType.DMA((count,)),
            ],
            compiler_params=params(8),
            name="layout",
        )(index, in_hbm(weights))

    away = jnp.full((1,), number["other"], jnp.int32)
    win_b, rec_b = (lax.ppermute(by_gate(w, away, False, True)[0], "gate", swap) for w in (w_in, w_rec))
    (win_av, win_a), (rec_av,) = by_gate(w_in, which, True, True), by_gate(w_rec, which, True, False)
    proj_b = lax.ppermute(pick(proj, number["other"]), "gate", swap)
    bias_a, bias_b = trade(pick(bias, own), pick(bias, number["other"]))

    def cells_to_pieces(pair):
        both = jnp.stack(pair).reshape(QUARTERS, streams, HALVES, width)
        return jnp.transpose(both, (0, 2, 1, 3)).reshape(PIECES, streams, width)

    def by_time(stacked):
        return jnp.transpose(pick(stacked, own), (1, 0, 2))

    feats = by_time(inputs)
    ups = by_time(cotangent)
    flags = resets.astype(F32)
    later = jnp.concatenate([flags[:, 1:], jnp.zeros_like(flags[:, :1])], axis=1)
    keep = 1.0 - jnp.where(own == 0, flags, later)
    keep = jnp.broadcast_to(jnp.transpose(keep)[:, :, None], (steps, streams, 128))

    docs_h = state_h[stream_doc]
    docs_c = state_c[stream_doc]
    start_h = pick(jnp.transpose(docs_h, (1, 0, 2)), own).astype(BF16)
    by_dir_c = jnp.transpose(docs_c, (1, 0, 2))
    start_c = cells_to_pieces(trade(pick(by_dir_c, own), pick(by_dir_c, number["other"])))

    def at_step(step):
        near = jnp.array([step, step, max(step - 1, 0), min(step + 1, steps - 1)], jnp.int32)
        turned = jnp.array([step] + [steps - 1 - x for x in (step, max(step - 1, 0), min(step + 1, steps - 1))], jnp.int32)
        return jnp.where(own == 0, near, turned)

    def swapped(array, pairs):
        return lax.ppermute(array, "batch", pairs)

    turn = jnp.where(own == 0, jnp.array([0, 1], jnp.int32), jnp.array([steps - 1, -1], jnp.int32))
    feats_v, feat_all = pl.pallas_call(
        order_kernel,
        out_shape=(vmem(feats.shape, BF16), hbm(feats.shape, BF16)),
        in_specs=[SMEM, ANY],
        out_specs=[VMEM, ANY],
        scratch_shapes=[pltpu.SemaphoreType.DMA((2 * steps,))],
        compiler_params=params(1),
        name="order",
    )(turn, feats)
    gates_shape, cell_shape = (PIECES, streams, 4 * width), (PIECES, streams, width)
    bias_shape = (PIECES, 8, 4 * width)
    sources = (bias_a.astype(F32), bias_b.astype(F32), in_hbm(win_b), in_hbm(rec_b), in_hbm(proj_b), keep, start_h, start_c)
    inflow, proj_av, bias_av, bias_bv, win_bv, rec_bv, proj_bv, keep_v, start_hv, start_cv = pl.pallas_call(
        begin_kernel,
        out_shape=(vmem(gates_shape, F32), vmem((cells, depth), BF16)) + tuple(vmem(x.shape, x.dtype) for x in sources),
        in_specs=[SMEM, VMEM, VMEM] + [ANY] * (1 + len(sources)),
        out_specs=[VMEM] * (2 + len(sources)),
        scratch_shapes=[pltpu.SemaphoreType.DMA((1 + len(sources),))],
        compiler_params=params(8),
        name="begin",
    )(which, pinned(feats_v), pinned(win_av), in_hbm(proj), *sources)

    def forward_call(first, step, part, peer, cell, inflow):
        return pl.pallas_call(
            functools.partial(forward_kernel, first),
            out_shape=(
                vmem((streams, depth), BF16),
                vmem(cell_shape, F32),
                vmem(gates_shape, BF16),
                vmem(cell_shape, BF16),
                vmem((streams, depth), BF16),
                vmem((streams, depth), BF16),
                vmem((streams, depth), F32),
            ),
            in_specs=[SMEM] + [VMEM] * 10,
            out_specs=[VMEM] * 7,
            compiler_params=params(8),
            name="forward_step",
        )(
            at_step(step), pinned(part), pinned(peer), pinned(start_hv), pinned(keep_v), pinned(cell), pinned(inflow),
            pinned(rec_av), pinned(rec_bv), pinned(proj_av), pinned(proj_bv),
        )

    def between_call(step, fresh, stacks, passing=()):
        shapes = (
            hbm((PIECES, steps, streams, 4 * width), BF16),
            hbm((steps,) + cell_shape, F32),
            hbm((PIECES, steps, streams, width), BF16),
            hbm((steps, streams, depth), BF16),
            hbm((steps, streams, depth), BF16),
            hbm((steps, streams, depth), F32),
        )
        aliases = {12 + i: 1 + i for i in range(len(stacks))}
        aliases.update({12 + len(stacks) + i: 7 + i for i in range(len(passing))})
        inflow, *out = pl.pallas_call(
            functools.partial(between_kernel, not stacks, step == steps - 1, len(passing)),
            out_shape=(vmem(gates_shape, F32),) + shapes + tuple(hbm(x.shape, x.dtype) for x in passing),
            in_specs=[SMEM] + [VMEM] * 11 + [ANY] * (len(stacks) + len(passing)),
            out_specs=[VMEM] + [ANY] * (6 + len(passing)),
            scratch_shapes=[pltpu.SemaphoreType.DMA((2 * PIECES + 4,))],
            input_output_aliases=aliases,
            compiler_params=params(8),
            cost_estimate=cost(2 * streams * depth * 8 * cells, 8 * depth * cells * 2),
            name="between",
        )(
            at_step(step), pinned(feats_v), pinned(bias_av), pinned(bias_bv), pinned(win_av), pinned(win_bv),
            *(pinned(x) for x in fresh), *(in_hbm(x) for x in (*stacks, *passing)),
        )
        return inflow, tuple(out[:6]), tuple(out[6:])

    none = jnp.zeros((streams, depth), BF16)
    part, peer, cell, stacks = none, none, start_cv, ()
    for step in range(steps):
        cell_before = cell
        part, cell, *fresh = forward_call(step == 0, step, part, peer, cell, inflow)
        peer = lax.ppermute(part, "gate", across)
        if step == steps - 1:
            break
        if step == 2:
            (early_feat,) = after((part,), feat_all)
            feat_in = (swapped(early_feat, near_swap), swapped(early_feat, far_swap))
        due = step == (3 * steps) // 4
        inflow, stacks, passed = between_call(step, (cell, *fresh), stacks, feat_in if due else ())
        feat_in = passed if due else (feat_in if step >= 2 else None)
    gates, mixed, prev, hidden, slope = fresh
    gates_all, cells_all, mixed_all, prev_all, hidden_all, slope_all = stacks

    slope_now, up_now, mixed_all, prev_all, hidden_all, slope_all = pl.pallas_call(
        finish_kernel,
        out_shape=(vmem((streams, depth), F32), vmem((streams, depth), BF16))
        + tuple(hbm(x.shape, x.dtype) for x in (mixed_all, prev_all, hidden_all, slope_all)),
        in_specs=[SMEM] + [VMEM] * 6 + [ANY] * 5,
        out_specs=[VMEM] * 2 + [ANY] * 4,
        scratch_shapes=[pltpu.VMEM((streams, depth), BF16), pltpu.SemaphoreType.DMA((PIECES + 5,))],
        input_output_aliases={8 + i: 2 + i for i in range(4)},
        compiler_params=params(8),
        name="finish",
    )(
        at_step(steps - 1), pinned(part), pinned(peer), *(pinned(x) for x in (mixed, prev, hidden, slope)), in_hbm(ups),
        *(in_hbm(x) for x in (mixed_all, prev_all, hidden_all, slope_all)),
    )
    saved = (gates, cell, cell_before, slope_now, up_now)
    saved_shapes = (
        vmem(gates_shape, BF16),
        vmem(cell_shape, F32),
        vmem(cell_shape, F32),
        vmem((streams, depth), F32),
        vmem((streams, depth), BF16),
    )

    rec_atv, rec_btv, proj_atv, proj_btv = pl.pallas_call(
        turned_kernel,
        out_shape=(vmem((4, cells, depth), BF16),) * 2 + (vmem((depth, cells), BF16),) * 2,
        in_specs=[VMEM] * 4,
        out_specs=[VMEM] * 4,
        compiler_params=params(8),
        name="turned",
    )(pinned(rec_av), pinned(rec_bv), pinned(proj_av), pinned(proj_bv))

    def backward_call(step, part, peer, grad, bias, saved):
        return pl.pallas_call(
            backward_kernel,
            out_shape=(
                vmem((streams, depth), BF16),
                vmem(cell_shape, F32),
                vmem(bias_shape, F32),
                vmem((streams, depth), BF16),
                vmem(gates_shape, BF16),
            ),
            in_specs=[SMEM] + [VMEM] * 15,
            out_specs=[VMEM] * 5,
            compiler_params=params(8),
            name="backward_step",
        )(
            at_step(step), pinned(part), pinned(peer), pinned(keep_v), pinned(grad), pinned(bias),
            pinned(rec_atv), pinned(rec_btv), pinned(proj_atv), pinned(proj_btv),
            *(pinned(x) for x in saved), pinned(start_cv),
        )

    def aside_call(step, slot, slots, dz, raw, stacks, sends, passing):
        piece_shape = (streams, 4 * width)
        shapes = (
            hbm((PIECES, steps) + piece_shape, BF16),
            hbm((steps, streams, depth), BF16),
            hbm((steps,) + piece_shape, BF16),
            hbm((steps,) + piece_shape, BF16),
            hbm((slots,) + piece_shape, BF16),
            hbm((slots,) + piece_shape, BF16),
        )
        kept = len(stacks)
        aliases = {7 + i: 5 + i for i in range(kept)}
        aliases.update({7 + kept + i: 9 + i for i in range(len(sends))})
        aliases.update({7 + kept + len(sends) + i: 11 + i for i in range(len(passing))})
        out = pl.pallas_call(
            functools.partial(aside_kernel, not stacks, step == 0, not sends, len(passing)),
            out_shape=saved_shapes + shapes + tuple(hbm(x.shape, x.dtype) for x in passing),
            in_specs=[SMEM] + [VMEM] * 2 + [ANY] * (4 + kept + len(sends) + len(passing)),
            out_specs=[VMEM] * 5 + [ANY] * (6 + len(passing)),
            scratch_shapes=[
                pltpu.SemaphoreType.DMA((PIECES + 5,)),
                pltpu.SemaphoreType.DMA((PIECES + 4,)),
            ],
            input_output_aliases=aliases,
            compiler_params=params(8),
            cost_estimate=cost(0, 8 * MIB),
            name="aside",
        )(
            jnp.concatenate([at_step(step), jnp.stack([jnp.int32(slot), low, high])]), pinned(dz), pinned(raw),
            in_hbm(gates_all), in_hbm(cells_all), in_hbm(ups), in_hbm(slope_all),
            *(in_hbm(x) for x in (*stacks, *sends, *passing)),
        )
        return out[:5], tuple(out[5:9]), tuple(out[9:11]), tuple(out[11:])

    carry = (none, none, jnp.zeros(cell_shape, F32), jnp.zeros(bias_shape, F32), saved, ())
    pending, arrived, ready, top = [], [], None, steps
    for index, share in enumerate(SHARES):
        slots = top if index == len(SHARES) - 1 else round(share * steps)
        sends = ()
        for step in range(top - 1, top - slots - 1, -1):
            part, peer, grad, bias_sum, saved, stacks = carry
            part, grad, bias_sum, raw, dz = backward_call(step, part, peer, grad, bias_sum, saved)
            peer = lax.ppermute(part, "gate", across)
            if step == steps - 1:
                (early_prev,) = after((part,), prev_all)
                pending.append((step - steps // 3, (swapped(early_prev, near_swap), swapped(early_prev, far_swap))))
            if ready is not None:
                due, sides = ready
                sides = after((part,), *sides) if step else sides
                pending.append((due, (swapped(sides[0], near_swap), swapped(sides[1], far_swap))))
                ready = None
            passing = ()
            while pending and pending[0][0] >= step:
                passing += pending.pop(0)[1]
            saved, stacks, sends, passed = aside_call(
                step, step - (top - slots), slots, dz, raw, stacks, sends, passing
            )
            arrived += [passed[i : i + 2] for i in range(0, len(passed), 2)]
            carry = (part, peer, grad, bias_sum, saved, stacks)
        top -= slots
        ready = (max(top - 1 - (3 * slots + 3) // 4, 0 if slots > 2 else -1), sends)
    pending.append((-1, (swapped(sends[0], near_swap), swapped(sends[1], far_swap))))
    arrived += [arrays for _, arrays in pending]
    dz_all, raw_all, near_all, far_all = carry[-1]
    bias_sum = carry[3]
    prev_in, exchanged = arrived[0], arrived[1:]
    rows = steps * streams

    def by_direction(mine, theirs):
        return jnp.stack([jnp.where(own == 0, mine, theirs), jnp.where(own == 0, theirs, mine)])

    def line_sum(chunks, axis, stride, count, first=None, gates={}):
        def chunk(*name):
            return pick(chunks, number[(stride, *name)], axis)

        def at(device):
            return (device // stride) % count

        if count == 2:
            pairs = [(i, i + stride if at(i) == 0 else i - stride) for i in range(n_batch)]
            return (chunk("here").astype(F32) + swapped(chunk("not_here"), pairs).astype(F32)).astype(BF16)
        ends = [(i, i + stride) for i in range(n_batch) if at(i) == 0]
        ends += [(i, i - stride) for i in range(n_batch) if at(i) == count - 1]
        up = down = swapped(chunk("begin") if first is None else first, ends)
        for slot in range(2, count):
            if slot in gates:
                up, down = gates[slot](up, down)
            rise = (chunk("rise", slot).astype(F32) + up.astype(F32)).astype(BF16)
            fall = (chunk("fall", slot).astype(F32) + down.astype(F32)).astype(BF16)
            up = swapped(rise, [(i, i + stride) for i in range(n_batch) if at(i) < min(slot, count - 1)])
            down = swapped(fall, [(i, i - stride) for i in range(n_batch) if at(i) > max(count - 1 - slot, 0)])
        if count in gates:
            up, down = gates[count](up, down)
        return (chunk("here").astype(F32) + up.astype(F32) + down.astype(F32)).astype(BF16)

    share_rows = depth // n_batch

    def input_grad_of(dz):
        return pl.pallas_call(
            input_grad_kernel,
            out_shape=jax.ShapeDtypeStruct((steps, streams, depth), F32),
            grid_spec=pltpu.PrefetchScalarGridSpec(
                num_scalar_prefetch=1,
                grid=(PIECES, 4),
                in_specs=[
                    pl.BlockSpec((1, steps, streams, width), lambda p, g, turn: (p, 0, 0, g)),
                    pl.BlockSpec(
                        (1, depth, width), lambda p, g, turn: (jnp.where(p < 2, g, 3), 0, jnp.where(p < 2, p, 1))
                    ),
                    pl.BlockSpec(
                        (1, depth, width), lambda p, g, turn: (jnp.where(p < 2, 0, g), 0, jnp.where(p < 2, 0, p - 2))
                    ),
                ],
                out_specs=pl.BlockSpec((steps, streams, depth), lambda p, g, turn: (0, 0, 0)),
                scratch_shapes=[pltpu.VMEM((rows, depth), F32)],
            ),
            compiler_params=params(16),
            cost_estimate=cost(0, 0),
            name="input_grad",
        )(turn, in_hbm(dz), in_hbm(win_a), in_hbm(win_b))

    grad_proj = jnp.einsum("ptnc,tnk->pkc", mixed_all, raw_all, preferred_element_type=F32).astype(BF16)
    grad_proj = grad_proj.reshape(PIECES, line, 2, share_rows, width)
    bias_rows = pl.pallas_call(
        bias_kernel,
        out_shape=jax.ShapeDtypeStruct((PIECES, 4, width), F32),
        in_specs=[VMEM],
        out_specs=VMEM,
        compiler_params=params(1),
        name="bias",
    )(pinned(bias_sum))
    bias_rows = jnp.broadcast_to(bias_rows[:, None, None].astype(BF16), (PIECES, line, 2, 4, width))
    grad_proj = jnp.concatenate([grad_proj, bias_rows], axis=3)

    def with_partner(grad):
        mine, sent = (pick(grad, number[x], grad.ndim - 3) for x in ("low", "not_low"))
        taken = swapped(sent, near_swap)
        return sent, taken, (mine.astype(F32) + taken.astype(F32)).astype(BF16)

    def across_two(grad):
        return line_sum(grad.reshape(grad.shape[:-3] + (line // 2, 2) + grad.shape[-2:]), grad.ndim - 3, 4, line // 2)

    proj_sent, proj_taken, proj_y = with_partner(grad_proj)

    lows, count = [], 0
    for x in exchanged[::-1]:
        lows.insert(0, count)
        count += x[0].shape[0]

    def gathered(kept, feat, prev, parts):
        return pl.pallas_call(
            functools.partial(gather_kernel, tuple(lows[: len(parts)])),
            out_shape=(vmem((2 * steps, streams, 2 * depth), BF16), vmem((2 * steps, streams, 4 * width), BF16)),
            in_specs=[ANY] * (5 + len(parts)),
            out_specs=[VMEM] * 2,
            scratch_shapes=[pltpu.SemaphoreType.DMA((5 + len(parts),))],
            compiler_params=params(1),
            cost_estimate=cost(0, 0),
            name="gather",
        )(*(in_hbm(x) for x in (feat_all, prev_all, feat, prev, kept, *parts)))

    def completed(begin, rows_out, left, right, parts):
        return pl.pallas_call(
            functools.partial(late_kernel, tuple(lows[len(lows) - len(parts) :])),
            out_shape=(vmem(right.shape, BF16), jax.ShapeDtypeStruct((2, max(rows_out, 8), 4 * width), BF16)),
            in_specs=[SMEM] + [VMEM] * 2 + [ANY] * len(parts),
            out_specs=[VMEM] * 2,
            scratch_shapes=[pltpu.SemaphoreType.DMA((len(parts),))],
            input_output_aliases={2: 0},
            compiler_params=params(16),
            cost_estimate=cost(0, 0),
            name="late",
        )(begin, pinned(left), pinned(right), *(in_hbm(x) for x in parts))

    def multiplied(left, right):
        return pl.pallas_call(
            product_kernel,
            out_shape=jax.ShapeDtypeStruct((2, depth, 4 * width), BF16),
            in_specs=[VMEM] * 2,
            out_specs=VMEM,
            compiler_params=params(16),
            cost_estimate=cost(0, 0),
            name="product",
        )(pinned(left), pinned(right))

    near_parts, far_parts = zip(*exchanged)
    chunk_rows = 2 * share_rows if 2 * share_rows % 128 == 0 else 0
    near_left, near_right = gathered(near_all, feat_in[0], prev_in[0], near_parts[:-LATE])
    near_late = after((near_left, proj_sent, *far_parts[-LATE:]), *near_parts[-LATE:])
    near_right, first = completed(jnp.full((1,), number["begin"], jnp.int32), chunk_rows, near_left, near_right, near_late)
    far_all, *far_parts = after((first,), far_all, *far_parts)
    far_left, far_right = gathered(far_all, feat_in[1], prev_in[1], far_parts[:-LATE])
    far_right, _ = completed(jnp.zeros((1,), jnp.int32), 0, far_left, far_right, far_parts[-LATE:])
    far = multiplied(far_left, far_right).reshape(2, line, 2, share_rows, 4 * width)
    near = multiplied(near_left, near_right).reshape(2, line, 2, share_rows, 4 * width)

    def states_of(hidden, cell):
        both_hidden = trade(hidden, hidden)

        hidden_dirs = by_direction(*both_hidden)
        outputs = (inputs.astype(F32) + jnp.transpose(hidden_dirs, (0, 2, 1, 3)).astype(F32)).astype(BF16)
        last_h = jnp.stack([hidden_dirs[0, steps - 1], hidden_dirs[1, 0]], axis=1).astype(F32)
        final_h = jnp.zeros_like(state_h).at[stream_doc].set(last_h)
        last_c = jnp.transpose(cell.reshape(QUARTERS, HALVES, streams, width), (0, 2, 1, 3)).reshape(
            QUARTERS, streams, cells
        )
        last_dirs = by_direction(*trade(last_c[0], last_c[1]))
        final_c = jnp.zeros_like(state_c).at[stream_doc].set(jnp.transpose(last_dirs, (1, 0, 2)))
        return outputs, final_h, final_c

    tokens = {}

    def second(up, down):
        up, sent, tokens["dz"], proj_sum = after((), up, far, dz_all, proj_y, free=2 * MIB)
        tokens["in"], tokens["rec"] = (with_partner(sent[i])[2] for i in range(2))
        tokens["proj"] = across_two(proj_sum)
        return up, up

    def third(up, down):
        dx = input_grad_of(tokens["dz"])
        up, down, tokens["dx"], in_sum, tokens["proj"], hidden, last_cell = after(
            (), up, down, dx, tokens["in"], tokens["proj"], hidden_all, cell, free=2 * MIB
        )
        tokens["in"] = across_two(in_sum)
        tokens["states"] = states_of(hidden, last_cell)
        return up, down

    def final(up, down):
        up, down, tokens["in"], rec_sum = after(tokens["states"], up, down, tokens["in"], tokens["rec"], free=2 * MIB)
        tokens["rec"] = across_two(rec_sum)
        return up, down

    gates = {2: second, 3: third, line: final} if line > 3 else {}
    first = first.reshape(2, 2, share_rows, 4 * width) if chunk_rows else None
    near = line_sum(near, 1, 2, line, first, gates)
    dx_all, (outputs, final_h, final_c) = tokens["dx"], tokens["states"]
    in_two, rec_two, proj_two = tokens["in"], tokens["rec"], tokens["proj"]

    def halves_of(summed, name, pairs):
        return pick(summed, number[name], 1), swapped(pick(summed, number["not_" + name], 1), pairs)

    near_pair = halves_of(near, "low", near_swap)
    far_pair = halves_of(jnp.stack([in_two, rec_two]), "high", far_swap)
    far_pair = [lax.ppermute(x, "gate", swap) for x in far_pair]
    proj_mine, proj_theirs = halves_of(proj_two, "high", far_swap)
    grad_proj = proj_mine.astype(F32) + proj_theirs.astype(F32)
    grad_shape = (2, share_rows, 4, cells)
    grad_w_in, grad_w_rec = pl.pallas_call(
        assemble_kernel,
        out_shape=(jax.ShapeDtypeStruct(grad_shape, F32),) * 2,
        in_specs=[SMEM] + [VMEM] * 4,
        out_specs=[VMEM] * 2,
        compiler_params=params(14),
        name="assemble",
    )(jnp.stack([own, low, high]), *near_pair, *far_pair)

    def home(mine, theirs):
        return by_direction(*trade(mine, theirs)).astype(F32)

    own_cells = cells // n_batch
    shaped = jnp.transpose(grad_proj[:, share_rows:].reshape(QUARTERS, HALVES, 4, width), (0, 2, 1, 3))
    shaped = pick(shaped.reshape(QUARTERS, 4, n_batch, own_cells), number["spot"], 2)
    grad_bias = home(shaped[0], shaped[1])
    grad_proj = grad_proj[:, :share_rows].reshape(QUARTERS, HALVES, share_rows, width)
    grad_proj = jnp.transpose(grad_proj, (0, 1, 3, 2)).reshape(QUARTERS, cells, share_rows).astype(BF16)
    grad_proj = home(grad_proj[0], grad_proj[1])

    def columns(array, name, size):
        return lax.dynamic_slice_in_dim(array, number[name], size, 2, allow_negative_indices=False)

    dx_half = columns(dx_all, "cols", half_cols)
    dx_sent = columns(dx_all, "other_cols", half_cols).astype(BF16)
    dx_half = dx_half + lax.ppermute(dx_sent, "gate", across).astype(F32)
    dx_half = (dx_half + columns(ups, "cols", half_cols).astype(F32)).astype(BF16)
    dx_half = dx_half.reshape(steps, streams, 2, quarter_cols)
    dx_dirs = by_direction(*trade(pick(dx_half, own, 2), pick(dx_half, number["other"], 2)))
    input_grad = jnp.transpose(dx_dirs, (0, 2, 1, 3))
    return (outputs, input_grad, grad_w_in, grad_w_rec, grad_bias, grad_proj, final_h, final_c)


def solution(mesh):
    placed = (
        P(None, "batch", None, None),
        P(None, None, None, "gate"),
        P(None, None, None, "gate"),
        P(None, None, "gate"),
        P(None, "gate", None),
        P("batch", None, None),
        P("batch", None, "gate"),
        P("batch", None),
        P("batch"),
        P(None, "batch", None, None),
    )
    return jax.shard_map(
        body,
        mesh=mesh,
        in_specs=placed,
        out_specs=(
            P(None, "batch", None, None),
            P(None, "batch", None, "gate"),
            P(None, "batch", None, "gate"),
            P(None, "batch", None, "gate"),
            P(None, None, ("gate", "batch")),
            P(None, "gate", "batch"),
            P("batch", None, None),
            P("batch", None, "gate"),
        ),
        check_vma=False,
    )
```

```python
import functools

import jax
import jax.numpy as jnp
from jax import lax
from jax.experimental import pallas as pl
from jax.experimental.pallas import tpu as pltpu
from jax.sharding import PartitionSpec as P

CLIP = 3.0
F32, BF16 = jnp.float32, jnp.bfloat16
QUARTERS, HALVES = 2, 2
PIECES = QUARTERS * HALVES
MIB = 2**20
LATE = 2
SHARES = (0.35, 0.3, 0.15, 0.1, 0.1)

VMEM = pl.BlockSpec(memory_space=pltpu.VMEM)
SMEM = pl.BlockSpec(memory_space=pltpu.SMEM)
ANY = pl.BlockSpec(memory_space=pl.ANY)


def pinned(array):
    return pltpu.with_memory_space_constraint(array, pltpu.VMEM)


def in_hbm(array):
    return pltpu.with_memory_space_constraint(array, pltpu.HBM)


def dot(left, right):
    return jnp.dot(left, right, preferred_element_type=F32)


def layout_kernel(keep, spread, which_ref, w_ref, *refs):
    buf, sems, out_sems = refs[-3:]
    out_ref = refs[0] if keep else refs[1]
    all_ref = refs[1] if keep else refs[0]
    depth, ahead, part = w_ref.shape[1], buf.shape[0], buf.shape[1]
    count = depth // part

    def fetch(i):
        return pltpu.make_async_copy(w_ref.at[which_ref[0], pl.ds(i * part, part)], buf.at[i % ahead], sems.at[i % ahead])

    def store(i):
        rows = pl.ds(i * part, part)
        return pltpu.make_async_copy(out_ref.at[:, rows], all_ref.at[:, rows], out_sems.at[i])

    for i in range(min(ahead - 1, count)):
        fetch(i).start()
    for i in range(count):
        if i + ahead - 1 < count:
            fetch(i + ahead - 1).start()
        fetch(i).wait()
        out_ref[:, i * part : (i + 1) * part, :] = jnp.swapaxes(buf[i % ahead], 0, 1)
        if spread:
            store(i).start()
    for i in range(count if spread else 0):
        store(i).wait()


def turned_kernel(wa_ref, wb_ref, pa_ref, pb_ref, wat_ref, wbt_ref, pat_ref, pbt_ref):
    for w_ref, out_ref in ((wa_ref, wat_ref), (wb_ref, wbt_ref)):
        for gate in range(4):
            for half in range(HALVES):
                width = w_ref.shape[2] // HALVES
                cols = slice(half * width, (half + 1) * width)
                out_ref[gate, cols, :] = w_ref[gate, :, cols].T
    pat_ref[...] = pa_ref[...].T
    pbt_ref[...] = pb_ref[...].T


def pass_kernel(*refs):
    pass


def after(tokens, *arrays, free=0):
    count = len(tokens)
    return pl.pallas_call(
        pass_kernel,
        out_shape=tuple(jax.ShapeDtypeStruct(x.shape, x.dtype) for x in arrays),
        in_specs=[ANY] * (count + len(arrays)),
        out_specs=[ANY] * len(arrays),
        input_output_aliases={count + i: i for i in range(len(arrays))},
        compiler_params=params(1),
        name="after",
    )(*tokens, *(in_hbm(x) if x.size * x.dtype.itemsize > free else x for x in arrays))


def gather_kernel(lows, *refs):
    (feat_ref, prev_ref, feat_too, prev_too, kept_ref), refs = refs[:5], refs[5:]
    groups, (left_ref, right_ref, sems) = refs[:-3], refs[-3:]
    steps, _, depth = feat_ref.shape
    jobs = [
        (feat_ref, left_ref.at[:steps, :, :depth]),
        (prev_ref, left_ref.at[:steps, :, depth:]),
        (feat_too, left_ref.at[steps:, :, :depth]),
        (prev_too, left_ref.at[steps:, :, depth:]),
        (kept_ref, right_ref.at[:steps]),
    ]
    jobs += [(x, right_ref.at[steps + low : steps + low + x.shape[0]]) for x, low in zip(groups, lows)]
    copies = [pltpu.make_async_copy(a, b, sems.at[i]) for i, (a, b) in enumerate(jobs)]
    for copy in copies:
        copy.start()
    for copy in copies:
        copy.wait()


def late_kernel(lows, begin_ref, left_ref, right_in, *refs):
    groups, (right_ref, first_ref, sems) = refs[:-3], refs[-3:]
    steps = left_ref.shape[0] // 2
    copies = [
        pltpu.make_async_copy(x, right_ref.at[steps + low : steps + low + x.shape[0]], sems.at[i])
        for i, (x, low) in enumerate(zip(groups, lows))
    ]
    for copy in copies:
        copy.start()
    for copy in copies:
        copy.wait()
    if first_ref.shape[1] % 128:
        return
    share, depth = first_ref.shape[1], left_ref.shape[2] // 2
    rows = left_ref.shape[0] * left_ref.shape[1]
    left = [
        left_ref[:, :, pl.ds(pl.multiple_of(i * depth + begin_ref[0] * share, 128), share)].reshape(rows, share)
        for i in range(2)
    ]
    left = jnp.concatenate([x.T for x in left], axis=0)
    width = right_ref.shape[2] // 4

    def columns(i, _):
        cols = pl.ds(pl.multiple_of(i * width, width), width)
        total = dot(left, right_ref[:, :, cols].reshape(rows, width)).astype(BF16)
        first_ref[0, :, cols] = total[:share]
        first_ref[1, :, cols] = total[share:]
        return 0

    lax.fori_loop(0, 4, columns, 0)


def product_kernel(left_ref, right_ref, out_ref):
    rows, depth = left_ref.shape[0] * left_ref.shape[1], left_ref.shape[2] // 2
    width = right_ref.shape[2] // 4
    for which in range(2):
        left = left_ref[:, :, which * depth : (which + 1) * depth].reshape(rows, depth).T

        def columns(i, _):
            cols = pl.ds(pl.multiple_of(i * width, width), width)
            out_ref[which, :, cols] = dot(left, right_ref[:, :, cols].reshape(rows, width)).astype(BF16)
            return 0

        lax.fori_loop(0, 4, columns, 0)


def whole_product_kernel(lows, *refs):
    (feat_ref, prev_ref, feat_too, prev_too, kept_ref), refs = refs[:5], refs[5:]
    groups, (out_ref, left_buf, turned_buf, right_buf, left_sems, sems) = refs[:-6], refs[-6:]
    steps, streams, depth = feat_ref.shape
    blocks = right_buf.shape[0]
    width = right_buf.shape[3]
    rows = 2 * steps * streams

    def fetches_of(block):
        cols = slice(block * width, (block + 1) * width)
        jobs = [(kept_ref.at[:, :, cols], right_buf.at[block, :steps])]
        jobs += [
            (x.at[:, :, cols], right_buf.at[block, steps + low : steps + low + x.shape[0]])
            for x, low in zip(groups, lows)
        ]
        return [pltpu.make_async_copy(a, b, sems.at[block, i]) for i, (a, b) in enumerate(jobs)]

    lefts = [(feat_ref, 0, 0), (feat_too, steps, 0), (prev_ref, 0, 1), (prev_too, steps, 1)]
    lefts = [
        pltpu.make_async_copy(x, left_buf.at[half, low : low + steps], left_sems.at[i])
        for i, (x, low, half) in enumerate(lefts)
    ]
    for copy in lefts:
        copy.start()
    for block in range(blocks):
        for copy in fetches_of(block):
            copy.start()
    for which in range(2):
        lefts[2 * which].wait()
        lefts[2 * which + 1].wait()
        turned_buf[which] = left_buf[which].reshape(rows, depth).T
    for block in range(blocks):
        for copy in fetches_of(block):
            copy.wait()

        def one(which, _):
            total = dot(turned_buf[which], right_buf[block].reshape(rows, width))
            out_ref[which, :, block * width : (block + 1) * width] = total.astype(BF16)
            return 0

        lax.fori_loop(0, 2, one, 0)


def assemble_kernel(place_ref, near_a, near_b, far_a, far_b, in_ref, rec_ref):
    own, low, high = place_ref[0], place_ref[1], place_ref[2]
    width = in_ref.shape[3] // HALVES
    for direction, mine_ref, theirs_ref, index in ((own, near_a, near_b, low), (1 - own, far_a, far_b, high)):
        for which, out_ref in ((0, in_ref), (1, rec_ref)):
            mine, theirs = mine_ref[which].astype(F32), theirs_ref[which].astype(F32)
            for half in range(HALVES):
                whole = jnp.where(index == half, mine, theirs)
                gates = jnp.stack([whole[:, gate * width : (gate + 1) * width] for gate in range(4)])
                out_ref[direction, :, :, half * width : (half + 1) * width] = jnp.swapaxes(gates, 0, 1)


def order_kernel(step_ref, feat_ref, out_ref, all_ref, sems):
    copies = []
    for i in range(feat_ref.shape[0]):
        source = feat_ref.at[step_ref[0] + step_ref[1] * i]
        copies.append(pltpu.make_async_copy(source, out_ref.at[i], sems.at[2 * i]))
        copies.append(pltpu.make_async_copy(source, all_ref.at[i], sems.at[2 * i + 1]))
    for copy in copies:
        copy.start()
    for copy in copies:
        copy.wait()


def numbers_kernel(in_ref, out_ref):
    for i in range(in_ref.shape[0]):
        out_ref[i] = in_ref[i]


def bias_kernel(sum_ref, out_ref):
    width = sum_ref.shape[2] // 4
    for piece in range(PIECES):
        for gate in range(4):
            out_ref[piece, gate : gate + 1, :] = jnp.sum(
                sum_ref[piece, :, gate * width : (gate + 1) * width], axis=0, keepdims=True
            )


def pieces(refs, axis):
    for piece in range(PIECES):
        quarter, half = divmod(piece, HALVES)
        width = refs[0].shape[axis] // HALVES
        yield piece, quarter, width, slice(half * width, (half + 1) * width)


def forward_kernel(
    first, step_ref, p_ref, q_ref, start_ref, keep_ref, cell_ref, inflow_ref, wa_ref, wb_ref, pa_ref, pb_ref,
    part_ref, next_ref, gates_ref, mixed_ref, prev_ref, hidden_ref, slope_ref,
):
    keep = keep_ref[step_ref[1]][:, :1]
    if first:
        hidden = start_ref[...]
    else:
        hidden = clipped(p_ref, q_ref, hidden_ref, slope_ref)
    hidden = hidden * keep.astype(BF16)
    prev_ref[...] = hidden
    part = jnp.zeros(part_ref.shape, F32)
    for piece, quarter, width, cols in pieces((wa_ref, wb_ref), 2):
        w_ref, proj_ref = ((wa_ref, pa_ref), (wb_ref, pb_ref))[quarter]
        acts = []
        for gate in range(4):
            place = slice(gate * width, (gate + 1) * width)
            pre = dot(hidden, w_ref[gate, :, cols]) + inflow_ref[piece, :, place]
            act = jnp.tanh(pre if gate == 2 else 0.5 * pre)
            gates_ref[piece, :, place] = act.astype(BF16)
            acts.append(act if gate == 2 else 0.5 + 0.5 * act)
        ingate, forget, candidate, outgate = acts
        cell = CLIP * jnp.tanh((forget * (keep * cell_ref[piece]) + ingate * candidate) * (1.0 / CLIP))
        next_ref[piece] = cell
        mixed = (outgate * jnp.tanh(cell)).astype(BF16)
        mixed_ref[piece] = mixed
        part = part + dot(mixed, proj_ref[cols, :])
    part_ref[...] = part.astype(BF16)


def clipped(p_ref, q_ref, hidden_ref, slope_ref):
    squash = jnp.tanh((p_ref[...].astype(F32) + q_ref[...].astype(F32)) * (1.0 / CLIP))
    hidden = (CLIP * squash).astype(BF16)
    hidden_ref[...] = hidden
    slope_ref[...] = 1.0 - squash * squash
    return hidden


def between_kernel(
    first, last, passed, step_ref, feat_ref, ba_ref, bb_ref, wa_ref, wb_ref, cell_ref, gates_ref, mixed_ref, prev_ref, hidden_ref,
    slope_ref, *refs,
):
    refs = refs[(0 if first else 6) + passed :]
    out_ref, gates_all, cells_all, mixed_all, prev_all, hidden_all, slope_all = refs[:7]
    sems = refs[-1]
    step, time_before = step_ref[0], step_ref[2]
    copies = [pltpu.make_async_copy(gates_ref.at[i], gates_all.at[i, step], sems.at[i]) for i in range(PIECES)]
    copies += [
        pltpu.make_async_copy(mixed_ref.at[i], mixed_all.at[i, step], sems.at[PIECES + i]) for i in range(PIECES)
    ]
    copies.append(pltpu.make_async_copy(cell_ref, cells_all.at[step], sems.at[2 * PIECES]))
    copies.append(pltpu.make_async_copy(prev_ref, prev_all.at[step], sems.at[2 * PIECES + 1]))
    if not first:
        copies.append(pltpu.make_async_copy(hidden_ref, hidden_all.at[time_before], sems.at[2 * PIECES + 2]))
        copies.append(pltpu.make_async_copy(slope_ref, slope_all.at[step - 1], sems.at[2 * PIECES + 3]))
    for copy in copies:
        copy.start()
    if not last:
        inflow_into(feat_ref[step + 1], ba_ref, bb_ref, wa_ref, wb_ref, out_ref)
    for copy in copies:
        copy.wait()


def inflow_into(feat, ba_ref, bb_ref, wa_ref, wb_ref, out_ref, quarters=(0, 1)):
    for piece, quarter, width, cols in pieces((wa_ref, wb_ref), 2):
        if quarter not in quarters:
            continue
        w_ref, bias_ref = ((wa_ref, ba_ref), (wb_ref, bb_ref))[quarter]
        for gate in range(4):
            place = slice(gate * width, (gate + 1) * width)
            out_ref[piece, :, place] = dot(feat, w_ref[gate, :, cols]) + bias_ref[gate : gate + 1, cols]


def begin_kernel(which_ref, feat_ref, wa_ref, proj_ref, *refs):
    sems = refs[-1]
    out_ref, pa_ref, *placed = refs[-11:-1]
    copies = [pltpu.make_async_copy(x, y, sems.at[i]) for i, (x, y) in enumerate(zip(refs[:-11], placed))]
    copies.append(pltpu.make_async_copy(proj_ref.at[which_ref[0]], pa_ref, sems.at[len(copies)]))
    for copy in copies:
        copy.start()
    ba_ref, bb_ref, wb_ref = placed[:3]
    copies[0].wait()
    inflow_into(feat_ref[0], ba_ref, bb_ref, wa_ref, wb_ref, out_ref, (0,))
    copies[1].wait()
    copies[2].wait()
    inflow_into(feat_ref[0], ba_ref, bb_ref, wa_ref, wb_ref, out_ref, (1,))
    for copy in copies[3:]:
        copy.wait()


def backward_kernel(
    step_ref, p_ref, q_ref, keep_ref, grad_ref, bias_ref, wa_ref, wb_ref, pa_ref, pb_ref,
    gates_ref, cell_ref, prev_ref, slope_ref, up_ref, start_ref,
    part_ref, next_ref, sum_ref, raw_ref, dz_ref,
):
    step = step_ref[0]
    keep = keep_ref[step_ref[1]][:, :1]
    raw = (up_ref[...].astype(F32) + (p_ref[...].astype(F32) + q_ref[...].astype(F32))) * slope_ref[...]
    raw = raw.astype(BF16)
    raw_ref[...] = raw
    part = jnp.zeros(part_ref.shape, F32)
    for piece, quarter, width, cols in pieces((wa_ref, wb_ref), 1):
        w_ref, proj_ref = ((wa_ref, pa_ref), (wb_ref, pb_ref))[quarter]
        mixed = dot(raw, proj_ref[:, cols])
        acts = [gates_ref[piece, :, gate * width : (gate + 1) * width].astype(F32) for gate in range(4)]
        ingate, forget, outgate = (0.5 + 0.5 * acts[gate] for gate in (0, 1, 3))
        slopes = [1.0 - act * act for act in acts]
        cell = cell_ref[piece]
        prev = keep * jnp.where(step == 0, start_ref[piece], prev_ref[piece])
        squash = jnp.tanh(cell)
        total = grad_ref[piece] + mixed * outgate * (1.0 - squash * squash)
        inner = total * (1.0 - (cell * (1.0 / CLIP)) * (cell * (1.0 / CLIP)))
        next_ref[piece] = keep * inner * forget
        quart = 0.25 * inner
        pre_grads = (
            quart * acts[2] * slopes[0],
            quart * prev * slopes[1],
            inner * ingate * slopes[2],
            0.25 * mixed * squash * slopes[3],
        )
        for gate in range(4):
            low = pre_grads[gate].astype(BF16)
            place = slice(gate * width, (gate + 1) * width)
            dz_ref[piece, :, place] = low
            rows = pre_grads[gate].reshape(-1, 8, width)
            sum_ref[piece, :, place] = bias_ref[piece, :, place] + jnp.sum(rows, axis=0)
            part = part + dot(low, w_ref[gate, cols, :])
    part_ref[...] = (part * keep).astype(BF16)


def finish_kernel(
    step_ref, p_ref, q_ref, mixed_ref, prev_ref, hidden_ref, before_ref, ups_all, mixed_in, prev_in, hidden_in, slope_in,
    slope_ref, up_ref, mixed_all, prev_all, hidden_all, slope_all, hidden_buf, sems,
):
    step, time, time_before = step_ref[0], step_ref[1], step_ref[2]
    jobs = [(mixed_ref.at[i], mixed_all.at[i, step]) for i in range(PIECES)]
    jobs += [
        (ups_all.at[time], up_ref),
        (prev_ref, prev_all.at[step]),
        (hidden_ref, hidden_all.at[time_before]),
        (before_ref, slope_all.at[step - 1]),
        (hidden_buf, hidden_all.at[time]),
    ]
    copies = [pltpu.make_async_copy(x, y, sems.at[i]) for i, (x, y) in enumerate(jobs)]
    for copy in copies[:-1]:
        copy.start()
    clipped(p_ref, q_ref, hidden_buf, slope_ref)
    copies[-1].start()
    for copy in copies:
        copy.wait()


def fetches(step, time, sources, targets, sems):
    gates_all, cells_all, ups_all = sources
    gates_ref, cell_ref, prev_ref, up_ref = targets
    before = jnp.maximum(step - 1, 0)
    return [
        pltpu.make_async_copy(gates_all.at[i, step], gates_ref.at[i], sems.at[i]) for i in range(PIECES)
    ] + [
        pltpu.make_async_copy(cells_all.at[step], cell_ref, sems.at[PIECES]),
        pltpu.make_async_copy(cells_all.at[before], prev_ref, sems.at[PIECES + 1]),
        pltpu.make_async_copy(ups_all.at[time], up_ref, sems.at[PIECES + 2]),
    ]


def aside_kernel(
    first, last, opens, passed, step_ref, dz_ref, raw_ref, gates_all, cells_all, ups_all, slope_all, *refs
):
    refs = refs[(0 if first else 4) + (0 if opens else 2) + passed :]
    gates_ref, cell_ref, prev_ref, slope_ref, up_ref = refs[:5]
    dz_all, raw_all, near_all, far_all, near_out, far_out = refs[5:11]
    sems, fetch_sems = refs[-2:]
    step, time_before = step_ref[0], step_ref[2]
    slot, low, high = step_ref[4], step_ref[5], step_ref[6]
    before = jnp.maximum(step - 1, 0)
    copies = []
    if not last:
        copies += fetches(
            before, time_before, (gates_all, cells_all, ups_all), (gates_ref, cell_ref, prev_ref, up_ref), fetch_sems
        )
        copies.append(pltpu.make_async_copy(slope_all.at[before], slope_ref, fetch_sems.at[PIECES + 3]))
    copies += [pltpu.make_async_copy(dz_ref.at[i], dz_all.at[i, step], sems.at[i]) for i in range(PIECES)]
    copies.append(pltpu.make_async_copy(raw_ref, raw_all.at[step], sems.at[PIECES]))
    copies.append(pltpu.make_async_copy(dz_ref.at[low], near_all.at[step], sems.at[PIECES + 1]))
    copies.append(pltpu.make_async_copy(dz_ref.at[HALVES + high], far_all.at[step], sems.at[PIECES + 2]))
    copies.append(pltpu.make_async_copy(dz_ref.at[1 - low], near_out.at[slot], sems.at[PIECES + 3]))
    copies.append(pltpu.make_async_copy(dz_ref.at[HALVES + 1 - high], far_out.at[slot], sems.at[PIECES + 4]))
    for copy in copies:
        copy.start()
    for copy in copies:
        copy.wait()


def input_grad_kernel(step_ref, dz_ref, wa_ref, wb_ref, out_ref, acc_ref):
    piece, gate = pl.program_id(0), pl.program_id(1)
    steps, streams, width = dz_ref.shape[1:]

    @pl.when((piece == 0) & (gate == 0))
    def _():
        acc_ref[...] = jnp.zeros(acc_ref.shape, F32)

    weights = jnp.where(piece < HALVES, wa_ref[0], wb_ref[0])
    acc_ref[...] += lax.dot_general(
        dz_ref[0].reshape(steps * streams, width), weights, (((1,), (1,)), ((), ())), preferred_element_type=F32
    )

    @pl.when((piece == PIECES - 1) & (gate == 3))
    def _():
        for step in range(steps):
            time = step_ref[0] + step_ref[1] * step
            out_ref[time] = acc_ref[step * streams : (step + 1) * streams, :]


def params(mib):
    return pltpu.CompilerParams(vmem_limit_bytes=mib * MIB)


def cost(flops, size):
    return pl.CostEstimate(flops=flops, bytes_accessed=size, transcendentals=0)


def body(inputs, w_in, w_rec, bias, proj, state_h, state_c, resets, stream_doc, cotangent):
    streams, steps, depth = inputs.shape[1:]
    cells = w_in.shape[3]
    width = cells // HALVES
    n_batch = lax.axis_size("batch")
    gates_size = lax.axis_size("gate")
    line = n_batch // 2
    swap = [(i, i ^ 1) for i in range(gates_size)]
    across = [(i, i ^ 2) for i in range(gates_size)]
    near_swap = [(i, i ^ 1) for i in range(n_batch)]
    far_swap = [(i, i ^ 2) for i in range(n_batch)]

    rank, spot = lax.axis_index("gate"), lax.axis_index("batch")
    half_cols, quarter_cols = depth // 2, depth // 4
    place_numbers = {
        "own": rank % 2,
        "other": 1 - rank % 2,
        "low": spot % 2,
        "not_low": 1 - spot % 2,
        "high": (spot // 2) % 2,
        "not_high": 1 - (spot // 2) % 2,
        "spot": spot,
        "begin": jnp.where(spot // 2 == 0, line - 1, 0),
        "cols": (rank // 2) * half_cols,
        "other_cols": (1 - rank // 2) * half_cols,
    }
    for stride, count in {(2, line), (4, line // 2)}:
        here = (spot // stride) % count
        place_numbers[stride, "here"] = here
        place_numbers[stride, "not_here"] = jnp.maximum(1 - here, 0)
        for slot in range(2, count):
            place_numbers[stride, "rise", slot] = jnp.minimum(here + count - slot, count - 1)
            place_numbers[stride, "fall", slot] = jnp.maximum(here - count + slot, 0)
        if count > 2:
            place_numbers[stride, "begin"] = jnp.where(here == 0, count - 1, 0)
    names = sorted(place_numbers, key=str)
    gathered_numbers = pl.pallas_call(
        numbers_kernel,
        out_shape=jax.ShapeDtypeStruct((len(names),), jnp.int32),
        in_specs=[SMEM],
        out_specs=SMEM,
        name="numbers",
    )(jnp.stack([place_numbers[x] for x in names]).astype(jnp.int32))
    number = {x: place_numbers[x].astype(jnp.int32) for x in names}
    own, low, high = number["own"], number["low"], number["high"]
    which = lax.slice_in_dim(gathered_numbers, names.index("own"), names.index("own") + 1)

    def pick(stacked, index, axis=0):
        return lax.dynamic_index_in_dim(stacked, index, axis, keepdims=False, allow_negative_indices=False)

    def trade(mine, theirs):
        return (mine, lax.ppermute(theirs, "gate", swap))

    def vmem(shape, dtype):
        return pltpu.VMEM(shape, dtype)

    def hbm(shape, dtype):
        return pltpu.HBM(shape, dtype)

    def by_gate(weights, index, keep, spread):
        shape = (4,) + weights.shape[1:2] + weights.shape[3:]
        count = 16
        kept, spreads = (vmem(shape, BF16),) * keep, (hbm(shape, BF16),) * spread
        return pl.pallas_call(
            functools.partial(layout_kernel, keep, spread),
            out_shape=kept + spreads,
            in_specs=[SMEM, ANY],
            out_specs=[VMEM] * keep + [ANY] * spread,
            scratch_shapes=[pltpu.VMEM(shape, BF16)] * (1 - keep)
            + [
                pltpu.VMEM((4, weights.shape[1] // count) + weights.shape[2:], BF16),
                pltpu.SemaphoreType.DMA((4,)),
                pltpu.SemaphoreType.DMA((count,)),
            ],
            compiler_params=params(8),
            name="layout",
        )(index, in_hbm(weights))

    away = jnp.full((1,), number["other"], jnp.int32)
    win_b, rec_b = (lax.ppermute(by_gate(w, away, False, True)[0], "gate", swap) for w in (w_in, w_rec))
    (win_av, win_a), (rec_av,) = by_gate(w_in, which, True, True), by_gate(w_rec, which, True, False)
    proj_b = lax.ppermute(pick(proj, number["other"]), "gate", swap)
    bias_a, bias_b = trade(pick(bias, own), pick(bias, number["other"]))

    def cells_to_pieces(pair):
        both = jnp.stack(pair).reshape(QUARTERS, streams, HALVES, width)
        return jnp.transpose(both, (0, 2, 1, 3)).reshape(PIECES, streams, width)

    def by_time(stacked):
        return jnp.transpose(pick(stacked, own), (1, 0, 2))

    feats = by_time(inputs)
    ups = by_time(cotangent)
    flags = resets.astype(F32)
    later = jnp.concatenate([flags[:, 1:], jnp.zeros_like(flags[:, :1])], axis=1)
    keep = 1.0 - jnp.where(own == 0, flags, later)
    keep = jnp.broadcast_to(jnp.transpose(keep)[:, :, None], (steps, streams, 128))

    docs_h = state_h[stream_doc]
    docs_c = state_c[stream_doc]
    start_h = pick(jnp.transpose(docs_h, (1, 0, 2)), own).astype(BF16)
    by_dir_c = jnp.transpose(docs_c, (1, 0, 2))
    start_c = cells_to_pieces(trade(pick(by_dir_c, own), pick(by_dir_c, number["other"])))

    def at_step(step):
        near = jnp.array([step, step, max(step - 1, 0), min(step + 1, steps - 1)], jnp.int32)
        turned = jnp.array([step] + [steps - 1 - x for x in (step, max(step - 1, 0), min(step + 1, steps - 1))], jnp.int32)
        return jnp.where(own == 0, near, turned)

    def swapped(array, pairs):
        return lax.ppermute(array, "batch", pairs)

    turn = jnp.where(own == 0, jnp.array([0, 1], jnp.int32), jnp.array([steps - 1, -1], jnp.int32))
    feats_v, feat_all = pl.pallas_call(
        order_kernel,
        out_shape=(vmem(feats.shape, BF16), hbm(feats.shape, BF16)),
        in_specs=[SMEM, ANY],
        out_specs=[VMEM, ANY],
        scratch_shapes=[pltpu.SemaphoreType.DMA((2 * steps,))],
        compiler_params=params(1),
        name="order",
    )(turn, feats)
    gates_shape, cell_shape = (PIECES, streams, 4 * width), (PIECES, streams, width)
    bias_shape = (PIECES, 8, 4 * width)
    sources = (bias_a.astype(F32), bias_b.astype(F32), in_hbm(win_b), in_hbm(rec_b), in_hbm(proj_b), keep, start_h, start_c)
    inflow, proj_av, bias_av, bias_bv, win_bv, rec_bv, proj_bv, keep_v, start_hv, start_cv = pl.pallas_call(
        begin_kernel,
        out_shape=(vmem(gates_shape, F32), vmem((cells, depth), BF16)) + tuple(vmem(x.shape, x.dtype) for x in sources),
        in_specs=[SMEM, VMEM, VMEM] + [ANY] * (1 + len(sources)),
        out_specs=[VMEM] * (2 + len(sources)),
        scratch_shapes=[pltpu.SemaphoreType.DMA((1 + len(sources),))],
        compiler_params=params(8),
        name="begin",
    )(which, pinned(feats_v), pinned(win_av), in_hbm(proj), *sources)

    def forward_call(first, step, part, peer, cell, inflow):
        return pl.pallas_call(
            functools.partial(forward_kernel, first),
            out_shape=(
                vmem((streams, depth), BF16),
                vmem(cell_shape, F32),
                vmem(gates_shape, BF16),
                vmem(cell_shape, BF16),
                vmem((streams, depth), BF16),
                vmem((streams, depth), BF16),
                vmem((streams, depth), F32),
            ),
            in_specs=[SMEM] + [VMEM] * 10,
            out_specs=[VMEM] * 7,
            compiler_params=params(8),
            name="forward_step",
        )(
            at_step(step), pinned(part), pinned(peer), pinned(start_hv), pinned(keep_v), pinned(cell), pinned(inflow),
            pinned(rec_av), pinned(rec_bv), pinned(proj_av), pinned(proj_bv),
        )

    def between_call(step, fresh, stacks, passing=()):
        shapes = (
            hbm((PIECES, steps, streams, 4 * width), BF16),
            hbm((steps,) + cell_shape, F32),
            hbm((PIECES, steps, streams, width), BF16),
            hbm((steps, streams, depth), BF16),
            hbm((steps, streams, depth), BF16),
            hbm((steps, streams, depth), F32),
        )
        aliases = {12 + i: 1 + i for i in range(len(stacks))}
        aliases.update({12 + len(stacks) + i: 7 + i for i in range(len(passing))})
        inflow, *out = pl.pallas_call(
            functools.partial(between_kernel, not stacks, step == steps - 1, len(passing)),
            out_shape=(vmem(gates_shape, F32),) + shapes + tuple(hbm(x.shape, x.dtype) for x in passing),
            in_specs=[SMEM] + [VMEM] * 11 + [ANY] * (len(stacks) + len(passing)),
            out_specs=[VMEM] + [ANY] * (6 + len(passing)),
            scratch_shapes=[pltpu.SemaphoreType.DMA((2 * PIECES + 4,))],
            input_output_aliases=aliases,
            compiler_params=params(8),
            cost_estimate=cost(2 * streams * depth * 8 * cells, 8 * depth * cells * 2),
            name="between",
        )(
            at_step(step), pinned(feats_v), pinned(bias_av), pinned(bias_bv), pinned(win_av), pinned(win_bv),
            *(pinned(x) for x in fresh), *(in_hbm(x) for x in (*stacks, *passing)),
        )
        return inflow, tuple(out[:6]), tuple(out[6:])

    none = jnp.zeros((streams, depth), BF16)
    part, peer, cell, stacks = none, none, start_cv, ()
    for step in range(steps):
        cell_before = cell
        part, cell, *fresh = forward_call(step == 0, step, part, peer, cell, inflow)
        peer = lax.ppermute(part, "gate", across)
        if step == steps - 1:
            break
        if step == 2:
            (early_feat,) = after((part,), feat_all)
            feat_in = (swapped(early_feat, near_swap), swapped(early_feat, far_swap))
        due = step == (3 * steps) // 4
        inflow, stacks, passed = between_call(step, (cell, *fresh), stacks, feat_in if due else ())
        feat_in = passed if due else (feat_in if step >= 2 else None)
    gates, mixed, prev, hidden, slope = fresh
    gates_all, cells_all, mixed_all, prev_all, hidden_all, slope_all = stacks

    slope_now, up_now, mixed_all, prev_all, hidden_all, slope_all = pl.pallas_call(
        finish_kernel,
        out_shape=(vmem((streams, depth), F32), vmem((streams, depth), BF16))
        + tuple(hbm(x.shape, x.dtype) for x in (mixed_all, prev_all, hidden_all, slope_all)),
        in_specs=[SMEM] + [VMEM] * 6 + [ANY] * 5,
        out_specs=[VMEM] * 2 + [ANY] * 4,
        scratch_shapes=[pltpu.VMEM((streams, depth), BF16), pltpu.SemaphoreType.DMA((PIECES + 5,))],
        input_output_aliases={8 + i: 2 + i for i in range(4)},
        compiler_params=params(8),
        name="finish",
    )(
        at_step(steps - 1), pinned(part), pinned(peer), *(pinned(x) for x in (mixed, prev, hidden, slope)), in_hbm(ups),
        *(in_hbm(x) for x in (mixed_all, prev_all, hidden_all, slope_all)),
    )
    saved = (gates, cell, cell_before, slope_now, up_now)
    saved_shapes = (
        vmem(gates_shape, BF16),
        vmem(cell_shape, F32),
        vmem(cell_shape, F32),
        vmem((streams, depth), F32),
        vmem((streams, depth), BF16),
    )

    rec_atv, rec_btv, proj_atv, proj_btv = pl.pallas_call(
        turned_kernel,
        out_shape=(vmem((4, cells, depth), BF16),) * 2 + (vmem((depth, cells), BF16),) * 2,
        in_specs=[VMEM] * 4,
        out_specs=[VMEM] * 4,
        compiler_params=params(8),
        name="turned",
    )(pinned(rec_av), pinned(rec_bv), pinned(proj_av), pinned(proj_bv))

    def backward_call(step, part, peer, grad, bias, saved):
        return pl.pallas_call(
            backward_kernel,
            out_shape=(
                vmem((streams, depth), BF16),
                vmem(cell_shape, F32),
                vmem(bias_shape, F32),
                vmem((streams, depth), BF16),
                vmem(gates_shape, BF16),
            ),
            in_specs=[SMEM] + [VMEM] * 15,
            out_specs=[VMEM] * 5,
            compiler_params=params(8),
            name="backward_step",
        )(
            at_step(step), pinned(part), pinned(peer), pinned(keep_v), pinned(grad), pinned(bias),
            pinned(rec_atv), pinned(rec_btv), pinned(proj_atv), pinned(proj_btv),
            *(pinned(x) for x in saved), pinned(start_cv),
        )

    def aside_call(step, slot, slots, dz, raw, stacks, sends, passing):
        piece_shape = (streams, 4 * width)
        shapes = (
            hbm((PIECES, steps) + piece_shape, BF16),
            hbm((steps, streams, depth), BF16),
            hbm((steps,) + piece_shape, BF16),
            hbm((steps,) + piece_shape, BF16),
            hbm((slots,) + piece_shape, BF16),
            hbm((slots,) + piece_shape, BF16),
        )
        kept = len(stacks)
        aliases = {7 + i: 5 + i for i in range(kept)}
        aliases.update({7 + kept + i: 9 + i for i in range(len(sends))})
        aliases.update({7 + kept + len(sends) + i: 11 + i for i in range(len(passing))})
        out = pl.pallas_call(
            functools.partial(aside_kernel, not stacks, step == 0, not sends, len(passing)),
            out_shape=saved_shapes + shapes + tuple(hbm(x.shape, x.dtype) for x in passing),
            in_specs=[SMEM] + [VMEM] * 2 + [ANY] * (4 + kept + len(sends) + len(passing)),
            out_specs=[VMEM] * 5 + [ANY] * (6 + len(passing)),
            scratch_shapes=[
                pltpu.SemaphoreType.DMA((PIECES + 5,)),
                pltpu.SemaphoreType.DMA((PIECES + 4,)),
            ],
            input_output_aliases=aliases,
            compiler_params=params(8),
            cost_estimate=cost(0, 8 * MIB),
            name="aside",
        )(
            jnp.concatenate([at_step(step), jnp.stack([jnp.int32(slot), low, high])]), pinned(dz), pinned(raw),
            in_hbm(gates_all), in_hbm(cells_all), in_hbm(ups), in_hbm(slope_all),
            *(in_hbm(x) for x in (*stacks, *sends, *passing)),
        )
        return out[:5], tuple(out[5:9]), tuple(out[9:11]), tuple(out[11:])

    carry = (none, none, jnp.zeros(cell_shape, F32), jnp.zeros(bias_shape, F32), saved, ())
    pending, arrived, ready, top = [], [], None, steps
    for index, share in enumerate(SHARES):
        slots = top if index == len(SHARES) - 1 else round(share * steps)
        sends = ()
        for step in range(top - 1, top - slots - 1, -1):
            part, peer, grad, bias_sum, saved, stacks = carry
            part, grad, bias_sum, raw, dz = backward_call(step, part, peer, grad, bias_sum, saved)
            peer = lax.ppermute(part, "gate", across)
            if step == steps - 1:
                (early_prev,) = after((part,), prev_all)
                pending.append((step - steps // 3, (swapped(early_prev, near_swap), swapped(early_prev, far_swap))))
            if ready is not None:
                due, sides = ready
                sides = after((part,), *sides) if step else sides
                pending.append((due, (swapped(sides[0], near_swap), swapped(sides[1], far_swap))))
                ready = None
            passing = ()
            while pending and pending[0][0] >= step:
                passing += pending.pop(0)[1]
            saved, stacks, sends, passed = aside_call(
                step, step - (top - slots), slots, dz, raw, stacks, sends, passing
            )
            arrived += [passed[i : i + 2] for i in range(0, len(passed), 2)]
            carry = (part, peer, grad, bias_sum, saved, stacks)
        top -= slots
        ready = (max(top - 1 - (3 * slots + 3) // 4, 0 if slots > 2 else -1), sends)
    pending.append((-1, (swapped(sends[0], near_swap), swapped(sends[1], far_swap))))
    arrived += [arrays for _, arrays in pending]
    dz_all, raw_all, near_all, far_all = carry[-1]
    bias_sum = carry[3]
    prev_in, exchanged = arrived[0], arrived[1:]
    rows = steps * streams

    def by_direction(mine, theirs):
        return jnp.stack([jnp.where(own == 0, mine, theirs), jnp.where(own == 0, theirs, mine)])

    def line_sum(chunks, axis, stride, count, first=None, gates={}, hooks={}):
        def chunk(*name):
            return pick(chunks, number[(stride, *name)], axis)

        def at(device):
            return (device // stride) % count

        if count == 2:
            pairs = [(i, i + stride if at(i) == 0 else i - stride) for i in range(n_batch)]
            return (chunk("here").astype(F32) + swapped(chunk("not_here"), pairs).astype(F32)).astype(BF16)
        ends = [(i, i + stride) for i in range(n_batch) if at(i) == 0]
        ends += [(i, i - stride) for i in range(n_batch) if at(i) == count - 1]
        up = down = swapped(chunk("begin") if first is None else first, ends)
        for slot in range(2, count):
            if slot in gates:
                up, down = gates[slot](up, down)
            rise = (chunk("rise", slot).astype(F32) + up.astype(F32)).astype(BF16)
            fall = (chunk("fall", slot).astype(F32) + down.astype(F32)).astype(BF16)
            if slot in hooks:
                hooks[slot](rise, fall)
            up = swapped(rise, [(i, i + stride) for i in range(n_batch) if at(i) < min(slot, count - 1)])
            down = swapped(fall, [(i, i - stride) for i in range(n_batch) if at(i) > max(count - 1 - slot, 0)])
        if count in gates:
            up, down = gates[count](up, down)
        return (chunk("here").astype(F32) + up.astype(F32) + down.astype(F32)).astype(BF16)

    share_rows = depth // n_batch

    def input_grad_of(dz):
        return pl.pallas_call(
            input_grad_kernel,
            out_shape=jax.ShapeDtypeStruct((steps, streams, depth), F32),
            grid_spec=pltpu.PrefetchScalarGridSpec(
                num_scalar_prefetch=1,
                grid=(PIECES, 4),
                in_specs=[
                    pl.BlockSpec((1, steps, streams, width), lambda p, g, turn: (p, 0, 0, g)),
                    pl.BlockSpec(
                        (1, depth, width), lambda p, g, turn: (jnp.where(p < 2, g, 3), 0, jnp.where(p < 2, p, 1))
                    ),
                    pl.BlockSpec(
                        (1, depth, width), lambda p, g, turn: (jnp.where(p < 2, 0, g), 0, jnp.where(p < 2, 0, p - 2))
                    ),
                ],
                out_specs=pl.BlockSpec((steps, streams, depth), lambda p, g, turn: (0, 0, 0)),
                scratch_shapes=[pltpu.VMEM((rows, depth), F32)],
            ),
            compiler_params=params(16),
            cost_estimate=cost(0, 0),
            name="input_grad",
        )(turn, in_hbm(dz), in_hbm(win_a), in_hbm(win_b))

    grad_proj = jnp.einsum("ptnc,tnk->pkc", mixed_all, raw_all, preferred_element_type=F32).astype(BF16)
    grad_proj = grad_proj.reshape(PIECES, line, 2, share_rows, width)
    bias_rows = pl.pallas_call(
        bias_kernel,
        out_shape=jax.ShapeDtypeStruct((PIECES, 4, width), F32),
        in_specs=[VMEM],
        out_specs=VMEM,
        compiler_params=params(1),
        name="bias",
    )(pinned(bias_sum))
    bias_rows = jnp.broadcast_to(bias_rows[:, None, None].astype(BF16), (PIECES, line, 2, 4, width))
    grad_proj = jnp.concatenate([grad_proj, bias_rows], axis=3)

    def with_partner(grad):
        mine, sent = (pick(grad, number[x], grad.ndim - 3) for x in ("low", "not_low"))
        taken = swapped(sent, near_swap)
        return sent, taken, (mine.astype(F32) + taken.astype(F32)).astype(BF16)

    def across_two(grad):
        return line_sum(grad.reshape(grad.shape[:-3] + (line // 2, 2) + grad.shape[-2:]), grad.ndim - 3, 4, line // 2)

    proj_sent, proj_taken, proj_y = with_partner(grad_proj)

    lows, count = [], 0
    for x in exchanged[::-1]:
        lows.insert(0, count)
        count += x[0].shape[0]

    def gathered(kept, feat, prev, parts):
        return pl.pallas_call(
            functools.partial(gather_kernel, tuple(lows[: len(parts)])),
            out_shape=(vmem((2 * steps, streams, 2 * depth), BF16), vmem((2 * steps, streams, 4 * width), BF16)),
            in_specs=[ANY] * (5 + len(parts)),
            out_specs=[VMEM] * 2,
            scratch_shapes=[pltpu.SemaphoreType.DMA((5 + len(parts),))],
            compiler_params=params(1),
            cost_estimate=cost(0, 0),
            name="gather",
        )(*(in_hbm(x) for x in (feat_all, prev_all, feat, prev, kept, *parts)))

    def completed(begin, rows_out, left, right, parts):
        return pl.pallas_call(
            functools.partial(late_kernel, tuple(lows[len(lows) - len(parts) :])),
            out_shape=(vmem(right.shape, BF16), jax.ShapeDtypeStruct((2, max(rows_out, 8), 4 * width), BF16)),
            in_specs=[SMEM] + [VMEM] * 2 + [ANY] * len(parts),
            out_specs=[VMEM] * 2,
            scratch_shapes=[pltpu.SemaphoreType.DMA((len(parts),))],
            input_output_aliases={2: 0},
            compiler_params=params(16),
            cost_estimate=cost(0, 0),
            name="late",
        )(begin, pinned(left), pinned(right), *(in_hbm(x) for x in parts))

    def multiplied(left, right):
        return pl.pallas_call(
            product_kernel,
            out_shape=jax.ShapeDtypeStruct((2, depth, 4 * width), BF16),
            in_specs=[VMEM] * 2,
            out_specs=VMEM,
            compiler_params=params(16),
            cost_estimate=cost(0, 0),
            name="product",
        )(pinned(left), pinned(right))

    near_parts, far_parts = zip(*exchanged)
    chunk_rows = 2 * share_rows if 2 * share_rows % 128 == 0 else 0
    near_left, near_right = gathered(near_all, feat_in[0], prev_in[0], near_parts[:-LATE])
    near_late = after((near_left, proj_sent, *far_parts[-LATE:]), *near_parts[-LATE:])
    near_right, first = completed(jnp.full((1,), number["begin"], jnp.int32), chunk_rows, near_left, near_right, near_late)
    far_all, *far_parts = after((first,), far_all, *far_parts)
    blocks = 4
    far = pl.pallas_call(
        functools.partial(whole_product_kernel, tuple(lows)),
        out_shape=jax.ShapeDtypeStruct((2, depth, 4 * width), BF16),
        in_specs=[ANY] * (5 + len(far_parts)),
        out_specs=VMEM,
        scratch_shapes=[
            pltpu.VMEM((2, 2 * steps, streams, depth), BF16),
            pltpu.VMEM((2, depth, 2 * steps * streams), BF16),
            pltpu.VMEM((blocks, 2 * steps, streams, 4 * width // blocks), BF16),
            pltpu.SemaphoreType.DMA((4,)),
            pltpu.SemaphoreType.DMA((blocks, 1 + len(far_parts))),
        ],
        compiler_params=params(28),
        cost_estimate=cost(0, 0),
        name="whole_product",
    )(*(in_hbm(x) for x in (feat_all, prev_all, feat_in[1], prev_in[1], far_all, *far_parts)))
    far = far.reshape(2, line, 2, share_rows, 4 * width)
    near = multiplied(near_left, near_right).reshape(2, line, 2, share_rows, 4 * width)

    def states_of(hidden, cell):
        both_hidden = trade(hidden, hidden)

        hidden_dirs = by_direction(*both_hidden)
        outputs = (inputs.astype(F32) + jnp.transpose(hidden_dirs, (0, 2, 1, 3)).astype(F32)).astype(BF16)
        last_h = jnp.stack([hidden_dirs[0, steps - 1], hidden_dirs[1, 0]], axis=1).astype(F32)
        final_h = jnp.zeros_like(state_h).at[stream_doc].set(last_h)
        last_c = jnp.transpose(cell.reshape(QUARTERS, HALVES, streams, width), (0, 2, 1, 3)).reshape(
            QUARTERS, streams, cells
        )
        last_dirs = by_direction(*trade(last_c[0], last_c[1]))
        final_c = jnp.zeros_like(state_c).at[stream_doc].set(jnp.transpose(last_dirs, (1, 0, 2)))
        return outputs, final_h, final_c

    tokens = {}

    def second(up, down):
        up, tokens["far"], tokens["dz"], tokens["proj"] = after((), up, far, dz_all, proj_y, free=5 * MIB)
        return up, up

    def beside_second(rise, fall):
        (sent,) = after((rise, fall), tokens["far"], free=5 * MIB)
        tokens["in"], tokens["rec"] = (with_partner(sent[i])[2] for i in range(2))
        tokens["proj"] = across_two(tokens["proj"])

    def third(up, down):
        dx = input_grad_of(tokens["dz"])
        up, down, tokens["dx"], tokens["in"], tokens["proj"] = after(
            (), up, down, dx, tokens["in"], tokens["proj"], free=2 * MIB
        )
        return up, down

    def beside_third(rise, fall):
        in_sum, hidden, last_cell = after((rise, fall), tokens["in"], hidden_all, cell, free=2 * MIB)
        tokens["in"], tokens["rec"] = across_two(in_sum), across_two(tokens["rec"])
        tokens["states"] = states_of(hidden, last_cell)

    def final(up, down):
        up, down, tokens["in"], tokens["rec"], tokens["proj"] = after(
            tokens["states"], up, down, tokens["in"], tokens["rec"], tokens["proj"], free=2 * MIB
        )
        return up, down

    gates = {2: second, 3: third, line: final} if line > 3 else {}
    hooks = {2: beside_second, 3: beside_third} if line > 3 else {}
    first = first.reshape(2, 2, share_rows, 4 * width) if chunk_rows else None
    near = line_sum(near, 1, 2, line, first, gates, hooks)
    dx_all, (outputs, final_h, final_c) = tokens["dx"], tokens["states"]
    in_two, rec_two, proj_two = tokens["in"], tokens["rec"], tokens["proj"]

    def halves_of(summed, name, pairs):
        return pick(summed, number[name], 1), swapped(pick(summed, number["not_" + name], 1), pairs)

    near_pair = halves_of(near, "low", near_swap)
    far_pair = halves_of(jnp.stack([in_two, rec_two]), "high", far_swap)
    far_pair = [lax.ppermute(x, "gate", swap) for x in far_pair]
    proj_mine, proj_theirs = halves_of(proj_two, "high", far_swap)
    grad_proj = proj_mine.astype(F32) + proj_theirs.astype(F32)
    grad_shape = (2, share_rows, 4, cells)
    grad_w_in, grad_w_rec = pl.pallas_call(
        assemble_kernel,
        out_shape=(jax.ShapeDtypeStruct(grad_shape, F32),) * 2,
        in_specs=[SMEM] + [VMEM] * 4,
        out_specs=[VMEM] * 2,
        compiler_params=params(14),
        name="assemble",
    )(jnp.stack([own, low, high]), *near_pair, *far_pair)

    def home(mine, theirs):
        return by_direction(*trade(mine, theirs)).astype(F32)

    own_cells = cells // n_batch
    shaped = jnp.transpose(grad_proj[:, share_rows:].reshape(QUARTERS, HALVES, 4, width), (0, 2, 1, 3))
    shaped = pick(shaped.reshape(QUARTERS, 4, n_batch, own_cells), number["spot"], 2)
    grad_bias = home(shaped[0], shaped[1])
    grad_proj = grad_proj[:, :share_rows].reshape(QUARTERS, HALVES, share_rows, width)
    grad_proj = jnp.transpose(grad_proj, (0, 1, 3, 2)).reshape(QUARTERS, cells, share_rows).astype(BF16)
    grad_proj = home(grad_proj[0], grad_proj[1])

    def columns(array, name, size):
        return lax.dynamic_slice_in_dim(array, number[name], size, 2, allow_negative_indices=False)

    dx_half = columns(dx_all, "cols", half_cols)
    dx_sent = columns(dx_all, "other_cols", half_cols).astype(BF16)
    dx_half = dx_half + lax.ppermute(dx_sent, "gate", across).astype(F32)
    dx_half = (dx_half + columns(ups, "cols", half_cols).astype(F32)).astype(BF16)
    dx_half = dx_half.reshape(steps, streams, 2, quarter_cols)
    dx_dirs = by_direction(*trade(pick(dx_half, own, 2), pick(dx_half, number["other"], 2)))
    input_grad = jnp.transpose(dx_dirs, (0, 2, 1, 3))
    return (outputs, input_grad, grad_w_in, grad_w_rec, grad_bias, grad_proj, final_h, final_c)


def solution(mesh):
    placed = (
        P(None, "batch", None, None),
        P(None, None, None, "gate"),
        P(None, None, None, "gate"),
        P(None, None, "gate"),
        P(None, "gate", None),
        P("batch", None, None),
        P("batch", None, "gate"),
        P("batch", None),
        P("batch"),
        P(None, "batch", None, None),
    )
    return jax.shard_map(
        body,
        mesh=mesh,
        in_specs=placed,
        out_specs=(
            P(None, "batch", None, None),
            P(None, "batch", None, "gate"),
            P(None, "batch", None, "gate"),
            P(None, "batch", None, "gate"),
            P(None, None, ("gate", "batch")),
            P(None, "gate", "batch"),
            P("batch", None, None),
            P("batch", None, "gate"),
        ),
        check_vma=False,
    )
```

```python
import functools

import jax
import jax.numpy as jnp
from jax import lax
from jax.experimental import pallas as pl
from jax.experimental.pallas import tpu as pltpu
from jax.sharding import PartitionSpec as P

CLIP = 3.0
F32, BF16 = jnp.float32, jnp.bfloat16
QUARTERS, HALVES = 2, 2
PIECES = QUARTERS * HALVES
MIB = 2**20
LATE = 2
SHARES = (0.35, 0.3, 0.15, 0.1, 0.1)

VMEM = pl.BlockSpec(memory_space=pltpu.VMEM)
SMEM = pl.BlockSpec(memory_space=pltpu.SMEM)
ANY = pl.BlockSpec(memory_space=pl.ANY)


def pinned(array):
    return pltpu.with_memory_space_constraint(array, pltpu.VMEM)


def in_hbm(array):
    return pltpu.with_memory_space_constraint(array, pltpu.HBM)


def dot(left, right):
    return jnp.dot(left, right, preferred_element_type=F32)


def layout_kernel(keep, spread, which_ref, w_ref, *refs):
    buf, sems, out_sems = refs[-3:]
    out_ref = refs[0] if keep else refs[1]
    all_ref = refs[1] if keep else refs[0]
    depth, ahead, part = w_ref.shape[1], buf.shape[0], buf.shape[1]
    count = depth // part

    def fetch(i):
        return pltpu.make_async_copy(w_ref.at[which_ref[0], pl.ds(i * part, part)], buf.at[i % ahead], sems.at[i % ahead])

    def store(i):
        rows = pl.ds(i * part, part)
        return pltpu.make_async_copy(out_ref.at[:, rows], all_ref.at[:, rows], out_sems.at[i])

    for i in range(min(ahead - 1, count)):
        fetch(i).start()
    for i in range(count):
        if i + ahead - 1 < count:
            fetch(i + ahead - 1).start()
        fetch(i).wait()
        out_ref[:, i * part : (i + 1) * part, :] = jnp.swapaxes(buf[i % ahead], 0, 1)
        if spread:
            store(i).start()
    for i in range(count if spread else 0):
        store(i).wait()


def turned_kernel(wa_ref, wb_ref, pa_ref, pb_ref, wat_ref, wbt_ref, pat_ref, pbt_ref):
    for w_ref, out_ref in ((wa_ref, wat_ref), (wb_ref, wbt_ref)):
        for gate in range(4):
            for half in range(HALVES):
                width = w_ref.shape[2] // HALVES
                cols = slice(half * width, (half + 1) * width)
                out_ref[gate, cols, :] = w_ref[gate, :, cols].T
    pat_ref[...] = pa_ref[...].T
    pbt_ref[...] = pb_ref[...].T


def pass_kernel(*refs):
    pass


def after(tokens, *arrays, free=0):
    count = len(tokens)
    return pl.pallas_call(
        pass_kernel,
        out_shape=tuple(jax.ShapeDtypeStruct(x.shape, x.dtype) for x in arrays),
        in_specs=[ANY] * (count + len(arrays)),
        out_specs=[ANY] * len(arrays),
        input_output_aliases={count + i: i for i in range(len(arrays))},
        compiler_params=params(1),
        name="after",
    )(*tokens, *(in_hbm(x) if x.size * x.dtype.itemsize > free else x for x in arrays))


def gather_kernel(lows, *refs):
    (feat_ref, prev_ref, feat_too, prev_too, kept_ref), refs = refs[:5], refs[5:]
    groups, (left_ref, right_ref, sems) = refs[:-3], refs[-3:]
    steps, _, depth = feat_ref.shape
    jobs = [
        (feat_ref, left_ref.at[:steps, :, :depth]),
        (prev_ref, left_ref.at[:steps, :, depth:]),
        (feat_too, left_ref.at[steps:, :, :depth]),
        (prev_too, left_ref.at[steps:, :, depth:]),
        (kept_ref, right_ref.at[:steps]),
    ]
    jobs += [(x, right_ref.at[steps + low : steps + low + x.shape[0]]) for x, low in zip(groups, lows)]
    copies = [pltpu.make_async_copy(a, b, sems.at[i]) for i, (a, b) in enumerate(jobs)]
    for copy in copies:
        copy.start()
    for copy in copies:
        copy.wait()


def late_kernel(lows, begin_ref, left_ref, right_in, *refs):
    groups, (right_ref, first_ref, sems) = refs[:-3], refs[-3:]
    steps = left_ref.shape[0] // 2
    copies = [
        pltpu.make_async_copy(x, right_ref.at[steps + low : steps + low + x.shape[0]], sems.at[i])
        for i, (x, low) in enumerate(zip(groups, lows))
    ]
    for copy in copies:
        copy.start()
    for copy in copies:
        copy.wait()
    if first_ref.shape[1] % 128:
        return
    share, depth = first_ref.shape[1], left_ref.shape[2] // 2
    rows = left_ref.shape[0] * left_ref.shape[1]
    left = [
        left_ref[:, :, pl.ds(pl.multiple_of(i * depth + begin_ref[0] * share, 128), share)].reshape(rows, share)
        for i in range(2)
    ]
    left = jnp.concatenate([x.T for x in left], axis=0)
    width = right_ref.shape[2] // 4

    def columns(i, _):
        cols = pl.ds(pl.multiple_of(i * width, width), width)
        total = dot(left, right_ref[:, :, cols].reshape(rows, width)).astype(BF16)
        first_ref[0, :, cols] = total[:share]
        first_ref[1, :, cols] = total[share:]
        return 0

    lax.fori_loop(0, 4, columns, 0)


def product_kernel(left_ref, right_ref, out_ref):
    rows, depth = left_ref.shape[0] * left_ref.shape[1], left_ref.shape[2] // 2
    width = right_ref.shape[2] // 4
    for which in range(2):
        left = left_ref[:, :, which * depth : (which + 1) * depth].reshape(rows, depth).T

        def columns(i, _):
            cols = pl.ds(pl.multiple_of(i * width, width), width)
            out_ref[which, :, cols] = dot(left, right_ref[:, :, cols].reshape(rows, width)).astype(BF16)
            return 0

        lax.fori_loop(0, 4, columns, 0)


def whole_product_kernel(lows, *refs):
    (feat_ref, prev_ref, feat_too, prev_too, kept_ref), refs = refs[:5], refs[5:]
    groups, (out_ref, left_buf, turned_buf, right_buf, left_sems, sems) = refs[:-6], refs[-6:]
    steps, streams, depth = feat_ref.shape
    blocks = right_buf.shape[0]
    width = right_buf.shape[3]
    rows = 2 * steps * streams

    def fetches_of(block):
        cols = slice(block * width, (block + 1) * width)
        jobs = [(kept_ref.at[:, :, cols], right_buf.at[block, :steps])]
        jobs += [
            (x.at[:, :, cols], right_buf.at[block, steps + low : steps + low + x.shape[0]])
            for x, low in zip(groups, lows)
        ]
        return [pltpu.make_async_copy(a, b, sems.at[block, i]) for i, (a, b) in enumerate(jobs)]

    lefts = [(feat_ref, 0, 0), (feat_too, steps, 0), (prev_ref, 0, 1), (prev_too, steps, 1)]
    lefts = [
        pltpu.make_async_copy(x, left_buf.at[half, low : low + steps], left_sems.at[i])
        for i, (x, low, half) in enumerate(lefts)
    ]
    for copy in lefts:
        copy.start()
    for block in range(blocks):
        for copy in fetches_of(block):
            copy.start()
    for which in range(2):
        lefts[2 * which].wait()
        lefts[2 * which + 1].wait()
        turned_buf[which] = left_buf[which].reshape(rows, depth).T
    for block in range(blocks):
        for copy in fetches_of(block):
            copy.wait()

        def one(which, _):
            total = dot(turned_buf[which], right_buf[block].reshape(rows, width))
            out_ref[which, :, block * width : (block + 1) * width] = total.astype(BF16)
            return 0

        lax.fori_loop(0, 2, one, 0)


def assemble_kernel(place_ref, near_a, near_b, far_a, far_b, in_ref, rec_ref):
    own, low, high = place_ref[0], place_ref[1], place_ref[2]
    width = in_ref.shape[3] // HALVES
    for direction, mine_ref, theirs_ref, index in ((own, near_a, near_b, low), (1 - own, far_a, far_b, high)):
        for which, out_ref in ((0, in_ref), (1, rec_ref)):
            mine, theirs = mine_ref[which].astype(F32), theirs_ref[which].astype(F32)
            for half in range(HALVES):
                whole = jnp.where(index == half, mine, theirs)
                gates = jnp.stack([whole[:, gate * width : (gate + 1) * width] for gate in range(4)])
                out_ref[direction, :, :, half * width : (half + 1) * width] = jnp.swapaxes(gates, 0, 1)


def order_kernel(step_ref, feat_ref, out_ref, all_ref, sems):
    copies = []
    for i in range(feat_ref.shape[0]):
        source = feat_ref.at[step_ref[0] + step_ref[1] * i]
        copies.append(pltpu.make_async_copy(source, out_ref.at[i], sems.at[2 * i]))
        copies.append(pltpu.make_async_copy(source, all_ref.at[i], sems.at[2 * i + 1]))
    for copy in copies:
        copy.start()
    for copy in copies:
        copy.wait()


def numbers_kernel(in_ref, out_ref):
    for i in range(in_ref.shape[0]):
        out_ref[i] = in_ref[i]


def bias_kernel(sum_ref, out_ref):
    width = sum_ref.shape[2] // 4
    for piece in range(PIECES):
        for gate in range(4):
            out_ref[piece, gate : gate + 1, :] = jnp.sum(
                sum_ref[piece, :, gate * width : (gate + 1) * width], axis=0, keepdims=True
            )


def pieces(refs, axis):
    for piece in range(PIECES):
        quarter, half = divmod(piece, HALVES)
        width = refs[0].shape[axis] // HALVES
        yield piece, quarter, width, slice(half * width, (half + 1) * width)


def forward_kernel(
    first, step_ref, p_ref, q_ref, start_ref, keep_ref, cell_ref, inflow_ref, wa_ref, wb_ref, pa_ref, pb_ref,
    part_ref, next_ref, gates_ref, mixed_ref, prev_ref, hidden_ref, slope_ref,
):
    keep = keep_ref[step_ref[1]][:, :1]
    if first:
        hidden = start_ref[...]
    else:
        hidden = clipped(p_ref, q_ref, hidden_ref, slope_ref)
    hidden = hidden * keep.astype(BF16)
    prev_ref[...] = hidden
    part = jnp.zeros(part_ref.shape, F32)
    for piece, quarter, width, cols in pieces((wa_ref, wb_ref), 2):
        w_ref, proj_ref = ((wa_ref, pa_ref), (wb_ref, pb_ref))[quarter]
        acts = []
        for gate in range(4):
            place = slice(gate * width, (gate + 1) * width)
            pre = dot(hidden, w_ref[gate, :, cols]) + inflow_ref[piece, :, place]
            act = jnp.tanh(pre if gate == 2 else 0.5 * pre)
            gates_ref[piece, :, place] = act.astype(BF16)
            acts.append(act if gate == 2 else 0.5 + 0.5 * act)
        ingate, forget, candidate, outgate = acts
        cell = CLIP * jnp.tanh((forget * (keep * cell_ref[piece]) + ingate * candidate) * (1.0 / CLIP))
        next_ref[piece] = cell
        mixed = (outgate * jnp.tanh(cell)).astype(BF16)
        mixed_ref[piece] = mixed
        part = part + dot(mixed, proj_ref[cols, :])
    part_ref[...] = part.astype(BF16)


def clipped(p_ref, q_ref, hidden_ref, slope_ref):
    squash = jnp.tanh((p_ref[...].astype(F32) + q_ref[...].astype(F32)) * (1.0 / CLIP))
    hidden = (CLIP * squash).astype(BF16)
    hidden_ref[...] = hidden
    slope_ref[...] = 1.0 - squash * squash
    return hidden


def between_kernel(
    first, last, passed, step_ref, feat_ref, ba_ref, bb_ref, wa_ref, wb_ref, cell_ref, gates_ref, mixed_ref, prev_ref, hidden_ref,
    slope_ref, *refs,
):
    refs = refs[(0 if first else 6) + passed :]
    out_ref, gates_all, cells_all, mixed_all, prev_all, hidden_all, slope_all = refs[:7]
    sems = refs[-1]
    step, time_before = step_ref[0], step_ref[2]
    copies = [pltpu.make_async_copy(gates_ref.at[i], gates_all.at[i, step], sems.at[i]) for i in range(PIECES)]
    copies += [
        pltpu.make_async_copy(mixed_ref.at[i], mixed_all.at[i, step], sems.at[PIECES + i]) for i in range(PIECES)
    ]
    copies.append(pltpu.make_async_copy(cell_ref, cells_all.at[step], sems.at[2 * PIECES]))
    copies.append(pltpu.make_async_copy(prev_ref, prev_all.at[step], sems.at[2 * PIECES + 1]))
    if not first:
        copies.append(pltpu.make_async_copy(hidden_ref, hidden_all.at[time_before], sems.at[2 * PIECES + 2]))
        copies.append(pltpu.make_async_copy(slope_ref, slope_all.at[step - 1], sems.at[2 * PIECES + 3]))
    for copy in copies:
        copy.start()
    if not last:
        inflow_into(feat_ref[step + 1], ba_ref, bb_ref, wa_ref, wb_ref, out_ref)
    for copy in copies:
        copy.wait()


def inflow_into(feat, ba_ref, bb_ref, wa_ref, wb_ref, out_ref, quarters=(0, 1)):
    for piece, quarter, width, cols in pieces((wa_ref, wb_ref), 2):
        if quarter not in quarters:
            continue
        w_ref, bias_ref = ((wa_ref, ba_ref), (wb_ref, bb_ref))[quarter]
        for gate in range(4):
            place = slice(gate * width, (gate + 1) * width)
            out_ref[piece, :, place] = dot(feat, w_ref[gate, :, cols]) + bias_ref[gate : gate + 1, cols]


def begin_kernel(which_ref, feat_ref, wa_ref, proj_ref, *refs):
    sems = refs[-1]
    out_ref, pa_ref, *placed = refs[-11:-1]
    copies = [pltpu.make_async_copy(x, y, sems.at[i]) for i, (x, y) in enumerate(zip(refs[:-11], placed))]
    copies.append(pltpu.make_async_copy(proj_ref.at[which_ref[0]], pa_ref, sems.at[len(copies)]))
    for copy in copies:
        copy.start()
    ba_ref, bb_ref, wb_ref = placed[:3]
    copies[0].wait()
    inflow_into(feat_ref[0], ba_ref, bb_ref, wa_ref, wb_ref, out_ref, (0,))
    copies[1].wait()
    copies[2].wait()
    inflow_into(feat_ref[0], ba_ref, bb_ref, wa_ref, wb_ref, out_ref, (1,))
    for copy in copies[3:]:
        copy.wait()


def backward_kernel(
    step_ref, p_ref, q_ref, keep_ref, grad_ref, bias_ref, wa_ref, wb_ref, pa_ref, pb_ref,
    gates_ref, cell_ref, prev_ref, slope_ref, up_ref, start_ref,
    part_ref, next_ref, sum_ref, raw_ref, dz_ref,
):
    step = step_ref[0]
    keep = keep_ref[step_ref[1]][:, :1]
    raw = (up_ref[...].astype(F32) + (p_ref[...].astype(F32) + q_ref[...].astype(F32))) * slope_ref[...]
    raw = raw.astype(BF16)
    raw_ref[...] = raw
    part = jnp.zeros(part_ref.shape, F32)
    for piece, quarter, width, cols in pieces((wa_ref, wb_ref), 1):
        w_ref, proj_ref = ((wa_ref, pa_ref), (wb_ref, pb_ref))[quarter]
        mixed = dot(raw, proj_ref[:, cols])
        acts = [gates_ref[piece, :, gate * width : (gate + 1) * width].astype(F32) for gate in range(4)]
        ingate, forget, outgate = (0.5 + 0.5 * acts[gate] for gate in (0, 1, 3))
        slopes = [1.0 - act * act for act in acts]
        cell = cell_ref[piece]
        prev = keep * jnp.where(step == 0, start_ref[piece], prev_ref[piece])
        squash = jnp.tanh(cell)
        total = grad_ref[piece] + mixed * outgate * (1.0 - squash * squash)
        inner = total * (1.0 - (cell * (1.0 / CLIP)) * (cell * (1.0 / CLIP)))
        next_ref[piece] = keep * inner * forget
        quart = 0.25 * inner
        pre_grads = (
            quart * acts[2] * slopes[0],
            quart * prev * slopes[1],
            inner * ingate * slopes[2],
            0.25 * mixed * squash * slopes[3],
        )
        for gate in range(4):
            low = pre_grads[gate].astype(BF16)
            place = slice(gate * width, (gate + 1) * width)
            dz_ref[piece, :, place] = low
            rows = pre_grads[gate].reshape(-1, 8, width)
            sum_ref[piece, :, place] = bias_ref[piece, :, place] + jnp.sum(rows, axis=0)
            part = part + dot(low, w_ref[gate, cols, :])
    part_ref[...] = (part * keep).astype(BF16)


def finish_kernel(
    step_ref, p_ref, q_ref, mixed_ref, prev_ref, hidden_ref, before_ref, ups_all, mixed_in, prev_in, hidden_in, slope_in,
    slope_ref, up_ref, mixed_all, prev_all, hidden_all, slope_all, hidden_buf, sems,
):
    step, time, time_before = step_ref[0], step_ref[1], step_ref[2]
    jobs = [(mixed_ref.at[i], mixed_all.at[i, step]) for i in range(PIECES)]
    jobs += [
        (ups_all.at[time], up_ref),
        (prev_ref, prev_all.at[step]),
        (hidden_ref, hidden_all.at[time_before]),
        (before_ref, slope_all.at[step - 1]),
        (hidden_buf, hidden_all.at[time]),
    ]
    copies = [pltpu.make_async_copy(x, y, sems.at[i]) for i, (x, y) in enumerate(jobs)]
    for copy in copies[:-1]:
        copy.start()
    clipped(p_ref, q_ref, hidden_buf, slope_ref)
    copies[-1].start()
    for copy in copies:
        copy.wait()


def fetches(step, time, sources, targets, sems):
    gates_all, cells_all, ups_all = sources
    gates_ref, cell_ref, prev_ref, up_ref = targets
    before = jnp.maximum(step - 1, 0)
    return [
        pltpu.make_async_copy(gates_all.at[i, step], gates_ref.at[i], sems.at[i]) for i in range(PIECES)
    ] + [
        pltpu.make_async_copy(cells_all.at[step], cell_ref, sems.at[PIECES]),
        pltpu.make_async_copy(cells_all.at[before], prev_ref, sems.at[PIECES + 1]),
        pltpu.make_async_copy(ups_all.at[time], up_ref, sems.at[PIECES + 2]),
    ]


def aside_kernel(
    first, last, opens, passed, step_ref, dz_ref, raw_ref, gates_all, cells_all, ups_all, slope_all, *refs
):
    refs = refs[(0 if first else 4) + (0 if opens else 2) + passed :]
    gates_ref, cell_ref, prev_ref, slope_ref, up_ref = refs[:5]
    dz_all, raw_all, near_all, far_all, near_out, far_out = refs[5:11]
    sems, fetch_sems = refs[-2:]
    step, time_before = step_ref[0], step_ref[2]
    slot, low, high = step_ref[4], step_ref[5], step_ref[6]
    before = jnp.maximum(step - 1, 0)
    copies = []
    if not last:
        copies += fetches(
            before, time_before, (gates_all, cells_all, ups_all), (gates_ref, cell_ref, prev_ref, up_ref), fetch_sems
        )
        copies.append(pltpu.make_async_copy(slope_all.at[before], slope_ref, fetch_sems.at[PIECES + 3]))
    copies += [pltpu.make_async_copy(dz_ref.at[i], dz_all.at[i, step], sems.at[i]) for i in range(PIECES)]
    copies.append(pltpu.make_async_copy(raw_ref, raw_all.at[step], sems.at[PIECES]))
    copies.append(pltpu.make_async_copy(dz_ref.at[low], near_all.at[step], sems.at[PIECES + 1]))
    copies.append(pltpu.make_async_copy(dz_ref.at[HALVES + high], far_all.at[step], sems.at[PIECES + 2]))
    copies.append(pltpu.make_async_copy(dz_ref.at[1 - low], near_out.at[slot], sems.at[PIECES + 3]))
    copies.append(pltpu.make_async_copy(dz_ref.at[HALVES + 1 - high], far_out.at[slot], sems.at[PIECES + 4]))
    for copy in copies:
        copy.start()
    for copy in copies:
        copy.wait()


def input_grad_kernel(step_ref, dz_ref, wa_ref, wb_ref, out_ref, acc_ref):
    piece, gate = pl.program_id(0), pl.program_id(1)
    steps, streams, width = dz_ref.shape[1:]

    @pl.when((piece == 0) & (gate == 0))
    def _():
        acc_ref[...] = jnp.zeros(acc_ref.shape, F32)

    weights = jnp.where(piece < HALVES, wa_ref[0], wb_ref[0])
    acc_ref[...] += lax.dot_general(
        dz_ref[0].reshape(steps * streams, width), weights, (((1,), (1,)), ((), ())), preferred_element_type=F32
    )

    @pl.when((piece == PIECES - 1) & (gate == 3))
    def _():
        for step in range(steps):
            time = step_ref[0] + step_ref[1] * step
            out_ref[time] = acc_ref[step * streams : (step + 1) * streams, :]


def params(mib):
    return pltpu.CompilerParams(vmem_limit_bytes=mib * MIB)


def cost(flops, size):
    return pl.CostEstimate(flops=flops, bytes_accessed=size, transcendentals=0)


def body(inputs, w_in, w_rec, bias, proj, state_h, state_c, resets, stream_doc, cotangent):
    streams, steps, depth = inputs.shape[1:]
    cells = w_in.shape[3]
    width = cells // HALVES
    n_batch = lax.axis_size("batch")
    gates_size = lax.axis_size("gate")
    line = n_batch // 2
    swap = [(i, i ^ 1) for i in range(gates_size)]
    across = [(i, i ^ 2) for i in range(gates_size)]
    near_swap = [(i, i ^ 1) for i in range(n_batch)]
    far_swap = [(i, i ^ 2) for i in range(n_batch)]

    rank, spot = lax.axis_index("gate"), lax.axis_index("batch")
    half_cols, quarter_cols = depth // 2, depth // 4
    place_numbers = {
        "own": rank % 2,
        "other": 1 - rank % 2,
        "low": spot % 2,
        "not_low": 1 - spot % 2,
        "high": (spot // 2) % 2,
        "not_high": 1 - (spot // 2) % 2,
        "spot": spot,
        "begin": jnp.where(spot // 2 == 0, line - 1, 0),
        "cols": (rank // 2) * half_cols,
        "other_cols": (1 - rank // 2) * half_cols,
    }
    for stride, count in {(2, line), (4, line // 2)}:
        here = (spot // stride) % count
        place_numbers[stride, "here"] = here
        place_numbers[stride, "not_here"] = jnp.maximum(1 - here, 0)
        for slot in range(2, count):
            place_numbers[stride, "rise", slot] = jnp.minimum(here + count - slot, count - 1)
            place_numbers[stride, "fall", slot] = jnp.maximum(here - count + slot, 0)
        if count > 2:
            place_numbers[stride, "begin"] = jnp.where(here == 0, count - 1, 0)
    names = sorted(place_numbers, key=str)
    gathered_numbers = pl.pallas_call(
        numbers_kernel,
        out_shape=jax.ShapeDtypeStruct((len(names),), jnp.int32),
        in_specs=[SMEM],
        out_specs=SMEM,
        name="numbers",
    )(jnp.stack([place_numbers[x] for x in names]).astype(jnp.int32))
    number = {x: place_numbers[x].astype(jnp.int32) for x in names}
    own, low, high = number["own"], number["low"], number["high"]
    which = lax.slice_in_dim(gathered_numbers, names.index("own"), names.index("own") + 1)

    def pick(stacked, index, axis=0):
        return lax.dynamic_index_in_dim(stacked, index, axis, keepdims=False, allow_negative_indices=False)

    def trade(mine, theirs):
        return (mine, lax.ppermute(theirs, "gate", swap))

    def vmem(shape, dtype):
        return pltpu.VMEM(shape, dtype)

    def hbm(shape, dtype):
        return pltpu.HBM(shape, dtype)

    def by_gate(weights, index, keep, spread):
        shape = (4,) + weights.shape[1:2] + weights.shape[3:]
        count = 16
        kept, spreads = (vmem(shape, BF16),) * keep, (hbm(shape, BF16),) * spread
        return pl.pallas_call(
            functools.partial(layout_kernel, keep, spread),
            out_shape=kept + spreads,
            in_specs=[SMEM, ANY],
            out_specs=[VMEM] * keep + [ANY] * spread,
            scratch_shapes=[pltpu.VMEM(shape, BF16)] * (1 - keep)
            + [
                pltpu.VMEM((4, weights.shape[1] // count) + weights.shape[2:], BF16),
                pltpu.SemaphoreType.DMA((4,)),
                pltpu.SemaphoreType.DMA((count,)),
            ],
            compiler_params=params(8),
            name="layout",
        )(index, in_hbm(weights))

    away = jnp.full((1,), number["other"], jnp.int32)
    win_b, rec_b = (lax.ppermute(by_gate(w, away, False, True)[0], "gate", swap) for w in (w_in, w_rec))
    (win_av, win_a), (rec_av,) = by_gate(w_in, which, True, True), by_gate(w_rec, which, True, False)
    proj_b = lax.ppermute(pick(proj, number["other"]), "gate", swap)
    bias_a, bias_b = trade(pick(bias, own), pick(bias, number["other"]))

    def cells_to_pieces(pair):
        both = jnp.stack(pair).reshape(QUARTERS, streams, HALVES, width)
        return jnp.transpose(both, (0, 2, 1, 3)).reshape(PIECES, streams, width)

    def by_time(stacked):
        return jnp.transpose(pick(stacked, own), (1, 0, 2))

    feats = by_time(inputs)
    ups = by_time(cotangent)
    flags = resets.astype(F32)
    later = jnp.concatenate([flags[:, 1:], jnp.zeros_like(flags[:, :1])], axis=1)
    keep = 1.0 - jnp.where(own == 0, flags, later)
    keep = jnp.broadcast_to(jnp.transpose(keep)[:, :, None], (steps, streams, 128))

    docs_h = state_h[stream_doc]
    docs_c = state_c[stream_doc]
    start_h = pick(jnp.transpose(docs_h, (1, 0, 2)), own).astype(BF16)
    by_dir_c = jnp.transpose(docs_c, (1, 0, 2))
    start_c = cells_to_pieces(trade(pick(by_dir_c, own), pick(by_dir_c, number["other"])))

    def at_step(step):
        near = jnp.array([step, step, max(step - 1, 0), min(step + 1, steps - 1)], jnp.int32)
        turned = jnp.array([step] + [steps - 1 - x for x in (step, max(step - 1, 0), min(step + 1, steps - 1))], jnp.int32)
        return jnp.where(own == 0, near, turned)

    def swapped(array, pairs):
        return lax.ppermute(array, "batch", pairs)

    turn = jnp.where(own == 0, jnp.array([0, 1], jnp.int32), jnp.array([steps - 1, -1], jnp.int32))
    feats_v, feat_all = pl.pallas_call(
        order_kernel,
        out_shape=(vmem(feats.shape, BF16), hbm(feats.shape, BF16)),
        in_specs=[SMEM, ANY],
        out_specs=[VMEM, ANY],
        scratch_shapes=[pltpu.SemaphoreType.DMA((2 * steps,))],
        compiler_params=params(1),
        name="order",
    )(turn, feats)
    gates_shape, cell_shape = (PIECES, streams, 4 * width), (PIECES, streams, width)
    bias_shape = (PIECES, 8, 4 * width)
    sources = (bias_a.astype(F32), bias_b.astype(F32), in_hbm(win_b), in_hbm(rec_b), in_hbm(proj_b), keep, start_h, start_c)
    inflow, proj_av, bias_av, bias_bv, win_bv, rec_bv, proj_bv, keep_v, start_hv, start_cv = pl.pallas_call(
        begin_kernel,
        out_shape=(vmem(gates_shape, F32), vmem((cells, depth), BF16)) + tuple(vmem(x.shape, x.dtype) for x in sources),
        in_specs=[SMEM, VMEM, VMEM] + [ANY] * (1 + len(sources)),
        out_specs=[VMEM] * (2 + len(sources)),
        scratch_shapes=[pltpu.SemaphoreType.DMA((1 + len(sources),))],
        compiler_params=params(8),
        name="begin",
    )(which, pinned(feats_v), pinned(win_av), in_hbm(proj), *sources)

    def forward_call(first, step, part, peer, cell, inflow):
        return pl.pallas_call(
            functools.partial(forward_kernel, first),
            out_shape=(
                vmem((streams, depth), BF16),
                vmem(cell_shape, F32),
                vmem(gates_shape, BF16),
                vmem(cell_shape, BF16),
                vmem((streams, depth), BF16),
                vmem((streams, depth), BF16),
                vmem((streams, depth), F32),
            ),
            in_specs=[SMEM] + [VMEM] * 10,
            out_specs=[VMEM] * 7,
            compiler_params=params(8),
            name="forward_step",
        )(
            at_step(step), pinned(part), pinned(peer), pinned(start_hv), pinned(keep_v), pinned(cell), pinned(inflow),
            pinned(rec_av), pinned(rec_bv), pinned(proj_av), pinned(proj_bv),
        )

    def between_call(step, fresh, stacks, passing=()):
        shapes = (
            hbm((PIECES, steps, streams, 4 * width), BF16),
            hbm((steps,) + cell_shape, F32),
            hbm((PIECES, steps, streams, width), BF16),
            hbm((steps, streams, depth), BF16),
            hbm((steps, streams, depth), BF16),
            hbm((steps, streams, depth), F32),
        )
        aliases = {12 + i: 1 + i for i in range(len(stacks))}
        aliases.update({12 + len(stacks) + i: 7 + i for i in range(len(passing))})
        inflow, *out = pl.pallas_call(
            functools.partial(between_kernel, not stacks, step == steps - 1, len(passing)),
            out_shape=(vmem(gates_shape, F32),) + shapes + tuple(hbm(x.shape, x.dtype) for x in passing),
            in_specs=[SMEM] + [VMEM] * 11 + [ANY] * (len(stacks) + len(passing)),
            out_specs=[VMEM] + [ANY] * (6 + len(passing)),
            scratch_shapes=[pltpu.SemaphoreType.DMA((2 * PIECES + 4,))],
            input_output_aliases=aliases,
            compiler_params=params(8),
            cost_estimate=cost(2 * streams * depth * 8 * cells, 8 * depth * cells * 2),
            name="between",
        )(
            at_step(step), pinned(feats_v), pinned(bias_av), pinned(bias_bv), pinned(win_av), pinned(win_bv),
            *(pinned(x) for x in fresh), *(in_hbm(x) for x in (*stacks, *passing)),
        )
        return inflow, tuple(out[:6]), tuple(out[6:])

    none = jnp.zeros((streams, depth), BF16)
    part, peer, cell, stacks = none, none, start_cv, ()
    for step in range(steps):
        cell_before = cell
        part, cell, *fresh = forward_call(step == 0, step, part, peer, cell, inflow)
        peer = lax.ppermute(part, "gate", across)
        if step == steps - 1:
            break
        if step == 2:
            (early_feat,) = after((part,), feat_all)
            feat_in = (swapped(early_feat, near_swap), swapped(early_feat, far_swap))
        due = step == (3 * steps) // 4
        inflow, stacks, passed = between_call(step, (cell, *fresh), stacks, feat_in if due else ())
        feat_in = passed if due else (feat_in if step >= 2 else None)
    gates, mixed, prev, hidden, slope = fresh
    gates_all, cells_all, mixed_all, prev_all, hidden_all, slope_all = stacks

    slope_now, up_now, mixed_all, prev_all, hidden_all, slope_all = pl.pallas_call(
        finish_kernel,
        out_shape=(vmem((streams, depth), F32), vmem((streams, depth), BF16))
        + tuple(hbm(x.shape, x.dtype) for x in (mixed_all, prev_all, hidden_all, slope_all)),
        in_specs=[SMEM] + [VMEM] * 6 + [ANY] * 5,
        out_specs=[VMEM] * 2 + [ANY] * 4,
        scratch_shapes=[pltpu.VMEM((streams, depth), BF16), pltpu.SemaphoreType.DMA((PIECES + 5,))],
        input_output_aliases={8 + i: 2 + i for i in range(4)},
        compiler_params=params(8),
        name="finish",
    )(
        at_step(steps - 1), pinned(part), pinned(peer), *(pinned(x) for x in (mixed, prev, hidden, slope)), in_hbm(ups),
        *(in_hbm(x) for x in (mixed_all, prev_all, hidden_all, slope_all)),
    )
    saved = (gates, cell, cell_before, slope_now, up_now)
    saved_shapes = (
        vmem(gates_shape, BF16),
        vmem(cell_shape, F32),
        vmem(cell_shape, F32),
        vmem((streams, depth), F32),
        vmem((streams, depth), BF16),
    )

    rec_atv, rec_btv, proj_atv, proj_btv = pl.pallas_call(
        turned_kernel,
        out_shape=(vmem((4, cells, depth), BF16),) * 2 + (vmem((depth, cells), BF16),) * 2,
        in_specs=[VMEM] * 4,
        out_specs=[VMEM] * 4,
        compiler_params=params(8),
        name="turned",
    )(pinned(rec_av), pinned(rec_bv), pinned(proj_av), pinned(proj_bv))

    def backward_call(step, part, peer, grad, bias, saved):
        return pl.pallas_call(
            backward_kernel,
            out_shape=(
                vmem((streams, depth), BF16),
                vmem(cell_shape, F32),
                vmem(bias_shape, F32),
                vmem((streams, depth), BF16),
                vmem(gates_shape, BF16),
            ),
            in_specs=[SMEM] + [VMEM] * 15,
            out_specs=[VMEM] * 5,
            compiler_params=params(8),
            name="backward_step",
        )(
            at_step(step), pinned(part), pinned(peer), pinned(keep_v), pinned(grad), pinned(bias),
            pinned(rec_atv), pinned(rec_btv), pinned(proj_atv), pinned(proj_btv),
            *(pinned(x) for x in saved), pinned(start_cv),
        )

    def aside_call(step, slot, slots, dz, raw, stacks, sends, passing):
        piece_shape = (streams, 4 * width)
        shapes = (
            hbm((PIECES, steps) + piece_shape, BF16),
            hbm((steps, streams, depth), BF16),
            hbm((steps,) + piece_shape, BF16),
            hbm((steps,) + piece_shape, BF16),
            hbm((slots,) + piece_shape, BF16),
            hbm((slots,) + piece_shape, BF16),
        )
        kept = len(stacks)
        aliases = {7 + i: 5 + i for i in range(kept)}
        aliases.update({7 + kept + i: 9 + i for i in range(len(sends))})
        aliases.update({7 + kept + len(sends) + i: 11 + i for i in range(len(passing))})
        out = pl.pallas_call(
            functools.partial(aside_kernel, not stacks, step == 0, not sends, len(passing)),
            out_shape=saved_shapes + shapes + tuple(hbm(x.shape, x.dtype) for x in passing),
            in_specs=[SMEM] + [VMEM] * 2 + [ANY] * (4 + kept + len(sends) + len(passing)),
            out_specs=[VMEM] * 5 + [ANY] * (6 + len(passing)),
            scratch_shapes=[
                pltpu.SemaphoreType.DMA((PIECES + 5,)),
                pltpu.SemaphoreType.DMA((PIECES + 4,)),
            ],
            input_output_aliases=aliases,
            compiler_params=params(8),
            cost_estimate=cost(0, 8 * MIB),
            name="aside",
        )(
            jnp.concatenate([at_step(step), jnp.stack([jnp.int32(slot), low, high])]), pinned(dz), pinned(raw),
            in_hbm(gates_all), in_hbm(cells_all), in_hbm(ups), in_hbm(slope_all),
            *(in_hbm(x) for x in (*stacks, *sends, *passing)),
        )
        return out[:5], tuple(out[5:9]), tuple(out[9:11]), tuple(out[11:])

    carry = (none, none, jnp.zeros(cell_shape, F32), jnp.zeros(bias_shape, F32), saved, ())
    pending, arrived, ready, top = [], [], None, steps
    for index, share in enumerate(SHARES):
        slots = top if index == len(SHARES) - 1 else round(share * steps)
        sends = ()
        for step in range(top - 1, top - slots - 1, -1):
            part, peer, grad, bias_sum, saved, stacks = carry
            part, grad, bias_sum, raw, dz = backward_call(step, part, peer, grad, bias_sum, saved)
            peer = lax.ppermute(part, "gate", across)
            if step == steps - 1:
                (early_prev,) = after((part,), prev_all)
                pending.append((step - steps // 3, (swapped(early_prev, near_swap), swapped(early_prev, far_swap))))
            if ready is not None:
                due, sides = ready
                sides = after((part,), *sides) if step else sides
                pending.append((due, (swapped(sides[0], near_swap), swapped(sides[1], far_swap))))
                ready = None
            passing = ()
            while pending and pending[0][0] >= step:
                passing += pending.pop(0)[1]
            saved, stacks, sends, passed = aside_call(
                step, step - (top - slots), slots, dz, raw, stacks, sends, passing
            )
            arrived += [passed[i : i + 2] for i in range(0, len(passed), 2)]
            carry = (part, peer, grad, bias_sum, saved, stacks)
        top -= slots
        ready = (max(top - 1 - (3 * slots + 3) // 4, 0 if slots > 2 else -1), sends)
    pending.append((-1, (swapped(sends[0], near_swap), swapped(sends[1], far_swap))))
    arrived += [arrays for _, arrays in pending]
    dz_all, raw_all, near_all, far_all = carry[-1]
    bias_sum = carry[3]
    prev_in, exchanged = arrived[0], arrived[1:]
    rows = steps * streams

    def by_direction(mine, theirs):
        return jnp.stack([jnp.where(own == 0, mine, theirs), jnp.where(own == 0, theirs, mine)])

    def line_sum(chunks, axis, stride, count, first=None, gates={}, hooks={}):
        def chunk(*name):
            return pick(chunks, number[(stride, *name)], axis)

        def at(device):
            return (device // stride) % count

        if count == 2:
            pairs = [(i, i + stride if at(i) == 0 else i - stride) for i in range(n_batch)]
            return (chunk("here").astype(F32) + swapped(chunk("not_here"), pairs).astype(F32)).astype(BF16)
        ends = [(i, i + stride) for i in range(n_batch) if at(i) == 0]
        ends += [(i, i - stride) for i in range(n_batch) if at(i) == count - 1]
        up = down = swapped(chunk("begin") if first is None else first, ends)
        for slot in range(2, count):
            if slot in gates:
                up, down = gates[slot](up, down)
            rise = (chunk("rise", slot).astype(F32) + up.astype(F32)).astype(BF16)
            fall = (chunk("fall", slot).astype(F32) + down.astype(F32)).astype(BF16)
            if slot in hooks:
                hooks[slot](rise, fall)
            up = swapped(rise, [(i, i + stride) for i in range(n_batch) if at(i) < min(slot, count - 1)])
            down = swapped(fall, [(i, i - stride) for i in range(n_batch) if at(i) > max(count - 1 - slot, 0)])
        if count in gates:
            up, down = gates[count](up, down)
        return (chunk("here").astype(F32) + up.astype(F32) + down.astype(F32)).astype(BF16)

    share_rows = depth // n_batch

    def input_grad_of(dz):
        return pl.pallas_call(
            input_grad_kernel,
            out_shape=jax.ShapeDtypeStruct((steps, streams, depth), F32),
            grid_spec=pltpu.PrefetchScalarGridSpec(
                num_scalar_prefetch=1,
                grid=(PIECES, 4),
                in_specs=[
                    pl.BlockSpec((1, steps, streams, width), lambda p, g, turn: (p, 0, 0, g)),
                    pl.BlockSpec(
                        (1, depth, width), lambda p, g, turn: (jnp.where(p < 2, g, 3), 0, jnp.where(p < 2, p, 1))
                    ),
                    pl.BlockSpec(
                        (1, depth, width), lambda p, g, turn: (jnp.where(p < 2, 0, g), 0, jnp.where(p < 2, 0, p - 2))
                    ),
                ],
                out_specs=pl.BlockSpec((steps, streams, depth), lambda p, g, turn: (0, 0, 0)),
                scratch_shapes=[pltpu.VMEM((rows, depth), F32)],
            ),
            compiler_params=params(16),
            cost_estimate=cost(0, 0),
            name="input_grad",
        )(turn, in_hbm(dz), in_hbm(win_a), in_hbm(win_b))

    grad_proj = jnp.einsum("ptnc,tnk->pkc", mixed_all, raw_all, preferred_element_type=F32).astype(BF16)
    grad_proj = grad_proj.reshape(PIECES, line, 2, share_rows, width)
    bias_rows = pl.pallas_call(
        bias_kernel,
        out_shape=jax.ShapeDtypeStruct((PIECES, 4, width), F32),
        in_specs=[VMEM],
        out_specs=VMEM,
        compiler_params=params(1),
        name="bias",
    )(pinned(bias_sum))
    bias_rows = jnp.broadcast_to(bias_rows[:, None, None].astype(BF16), (PIECES, line, 2, 4, width))
    grad_proj = jnp.concatenate([grad_proj, bias_rows], axis=3)

    def with_partner(grad):
        mine, sent = (pick(grad, number[x], grad.ndim - 3) for x in ("low", "not_low"))
        taken = swapped(sent, near_swap)
        return sent, taken, (mine.astype(F32) + taken.astype(F32)).astype(BF16)

    def across_two(grad):
        return line_sum(grad.reshape(grad.shape[:-3] + (line // 2, 2) + grad.shape[-2:]), grad.ndim - 3, 4, line // 2)

    proj_sent, proj_taken, proj_y = with_partner(grad_proj)

    lows, count = [], 0
    for x in exchanged[::-1]:
        lows.insert(0, count)
        count += x[0].shape[0]

    def gathered(kept, feat, prev, parts):
        return pl.pallas_call(
            functools.partial(gather_kernel, tuple(lows[: len(parts)])),
            out_shape=(vmem((2 * steps, streams, 2 * depth), BF16), vmem((2 * steps, streams, 4 * width), BF16)),
            in_specs=[ANY] * (5 + len(parts)),
            out_specs=[VMEM] * 2,
            scratch_shapes=[pltpu.SemaphoreType.DMA((5 + len(parts),))],
            compiler_params=params(1),
            cost_estimate=cost(0, 0),
            name="gather",
        )(*(in_hbm(x) for x in (feat_all, prev_all, feat, prev, kept, *parts)))

    def completed(begin, rows_out, left, right, parts):
        return pl.pallas_call(
            functools.partial(late_kernel, tuple(lows[len(lows) - len(parts) :])),
            out_shape=(vmem(right.shape, BF16), jax.ShapeDtypeStruct((2, max(rows_out, 8), 4 * width), BF16)),
            in_specs=[SMEM] + [VMEM] * 2 + [ANY] * len(parts),
            out_specs=[VMEM] * 2,
            scratch_shapes=[pltpu.SemaphoreType.DMA((len(parts),))],
            input_output_aliases={2: 0},
            compiler_params=params(16),
            cost_estimate=cost(0, 0),
            name="late",
        )(begin, pinned(left), pinned(right), *(in_hbm(x) for x in parts))

    def multiplied(left, right):
        return pl.pallas_call(
            product_kernel,
            out_shape=jax.ShapeDtypeStruct((2, depth, 4 * width), BF16),
            in_specs=[VMEM] * 2,
            out_specs=VMEM,
            compiler_params=params(16),
            cost_estimate=cost(0, 0),
            name="product",
        )(pinned(left), pinned(right))

    near_parts, far_parts = zip(*exchanged)
    chunk_rows = 2 * share_rows if 2 * share_rows % 128 == 0 else 0
    near_left, near_right = gathered(near_all, feat_in[0], prev_in[0], near_parts[:-LATE])
    near_late = after((near_left, proj_sent, *far_parts[-LATE:]), *near_parts[-LATE:])
    near_right, first = completed(jnp.full((1,), number["begin"], jnp.int32), chunk_rows, near_left, near_right, near_late)
    far_all, *far_parts = after((first,), far_all, *far_parts)
    blocks = 4
    far = pl.pallas_call(
        functools.partial(whole_product_kernel, tuple(lows)),
        out_shape=jax.ShapeDtypeStruct((2, depth, 4 * width), BF16),
        in_specs=[ANY] * (5 + len(far_parts)),
        out_specs=VMEM,
        scratch_shapes=[
            pltpu.VMEM((2, 2 * steps, streams, depth), BF16),
            pltpu.VMEM((2, depth, 2 * steps * streams), BF16),
            pltpu.VMEM((blocks, 2 * steps, streams, 4 * width // blocks), BF16),
            pltpu.SemaphoreType.DMA((4,)),
            pltpu.SemaphoreType.DMA((blocks, 1 + len(far_parts))),
        ],
        compiler_params=params(28),
        cost_estimate=cost(0, 0),
        name="whole_product",
    )(*(in_hbm(x) for x in (feat_all, prev_all, feat_in[1], prev_in[1], far_all, *far_parts)))
    far = far.reshape(2, line, 2, share_rows, 4 * width)
    near = multiplied(near_left, near_right).reshape(2, line, 2, share_rows, 4 * width)

    def states_of(hidden, cell):
        both_hidden = trade(hidden, hidden)

        hidden_dirs = by_direction(*both_hidden)
        outputs = (inputs.astype(F32) + jnp.transpose(hidden_dirs, (0, 2, 1, 3)).astype(F32)).astype(BF16)
        last_h = jnp.stack([hidden_dirs[0, steps - 1], hidden_dirs[1, 0]], axis=1).astype(F32)
        final_h = jnp.zeros_like(state_h).at[stream_doc].set(last_h)
        last_c = jnp.transpose(cell.reshape(QUARTERS, HALVES, streams, width), (0, 2, 1, 3)).reshape(
            QUARTERS, streams, cells
        )
        last_dirs = by_direction(*trade(last_c[0], last_c[1]))
        final_c = jnp.zeros_like(state_c).at[stream_doc].set(jnp.transpose(last_dirs, (1, 0, 2)))
        return outputs, final_h, final_c

    tokens = {}

    def second(up, down):
        up, tokens["far"], tokens["dz"], tokens["proj"] = after((), up, far, dz_all, proj_y, free=5 * MIB)
        return up, up

    def beside_second(rise, fall):
        (sent,) = after((rise, fall), tokens["far"], free=5 * MIB)
        tokens["in"], tokens["rec"] = (with_partner(sent[i])[2] for i in range(2))
        tokens["proj"] = across_two(tokens["proj"])

    def third(up, down):
        dx = input_grad_of(tokens["dz"])
        up, down, tokens["dx"], tokens["in"], tokens["proj"] = after(
            (), up, down, dx, tokens["in"], tokens["proj"], free=2 * MIB
        )
        return up, down

    def beside_third(rise, fall):
        (in_sum,) = after((rise, fall), tokens["in"], free=2 * MIB)
        tokens["in"] = across_two(in_sum)

    def final(up, down):
        up, down, tokens["in"], rec_sum, tokens["proj"], hidden, last_cell = after(
            (), up, down, tokens["in"], tokens["rec"], tokens["proj"], hidden_all, cell, free=2 * MIB
        )
        tokens["states"] = states_of(hidden, last_cell)
        (tokens["rec"],) = after(tokens["states"], across_two(rec_sum), free=2 * MIB)
        return up, down

    gates = {2: second, 3: third, line: final} if line > 3 else {}
    hooks = {2: beside_second, 3: beside_third} if line > 3 else {}
    first = first.reshape(2, 2, share_rows, 4 * width) if chunk_rows else None
    near = line_sum(near, 1, 2, line, first, gates, hooks)
    dx_all, (outputs, final_h, final_c) = tokens["dx"], tokens["states"]
    in_two, rec_two, proj_two = tokens["in"], tokens["rec"], tokens["proj"]

    def halves_of(summed, name, pairs):
        return pick(summed, number[name], 1), swapped(pick(summed, number["not_" + name], 1), pairs)

    near_pair = halves_of(near, "low", near_swap)
    far_pair = halves_of(jnp.stack([in_two, rec_two]), "high", far_swap)
    far_pair = [lax.ppermute(x, "gate", swap) for x in far_pair]
    proj_mine, proj_theirs = halves_of(proj_two, "high", far_swap)
    grad_proj = proj_mine.astype(F32) + proj_theirs.astype(F32)
    grad_shape = (2, share_rows, 4, cells)
    grad_w_in, grad_w_rec = pl.pallas_call(
        assemble_kernel,
        out_shape=(jax.ShapeDtypeStruct(grad_shape, F32),) * 2,
        in_specs=[SMEM] + [VMEM] * 4,
        out_specs=[VMEM] * 2,
        compiler_params=params(14),
        name="assemble",
    )(jnp.stack([own, low, high]), *near_pair, *far_pair)

    def home(mine, theirs):
        return by_direction(*trade(mine, theirs)).astype(F32)

    own_cells = cells // n_batch
    shaped = jnp.transpose(grad_proj[:, share_rows:].reshape(QUARTERS, HALVES, 4, width), (0, 2, 1, 3))
    shaped = pick(shaped.reshape(QUARTERS, 4, n_batch, own_cells), number["spot"], 2)
    grad_bias = home(shaped[0], shaped[1])
    grad_proj = grad_proj[:, :share_rows].reshape(QUARTERS, HALVES, share_rows, width)
    grad_proj = jnp.transpose(grad_proj, (0, 1, 3, 2)).reshape(QUARTERS, cells, share_rows).astype(BF16)
    grad_proj = home(grad_proj[0], grad_proj[1])

    def columns(array, name, size):
        return lax.dynamic_slice_in_dim(array, number[name], size, 2, allow_negative_indices=False)

    dx_half = columns(dx_all, "cols", half_cols)
    dx_sent = columns(dx_all, "other_cols", half_cols).astype(BF16)
    dx_half = dx_half + lax.ppermute(dx_sent, "gate", across).astype(F32)
    dx_half = (dx_half + columns(ups, "cols", half_cols).astype(F32)).astype(BF16)
    dx_half = dx_half.reshape(steps, streams, 2, quarter_cols)
    dx_dirs = by_direction(*trade(pick(dx_half, own, 2), pick(dx_half, number["other"], 2)))
    input_grad = jnp.transpose(dx_dirs, (0, 2, 1, 3))
    return (outputs, input_grad, grad_w_in, grad_w_rec, grad_bias, grad_proj, final_h, final_c)


def solution(mesh):
    placed = (
        P(None, "batch", None, None),
        P(None, None, None, "gate"),
        P(None, None, None, "gate"),
        P(None, None, "gate"),
        P(None, "gate", None),
        P("batch", None, None),
        P("batch", None, "gate"),
        P("batch", None),
        P("batch"),
        P(None, "batch", None, None),
    )
    return jax.shard_map(
        body,
        mesh=mesh,
        in_specs=placed,
        out_specs=(
            P(None, "batch", None, None),
            P(None, "batch", None, "gate"),
            P(None, "batch", None, "gate"),
            P(None, "batch", None, "gate"),
            P(None, None, ("gate", "batch")),
            P(None, "gate", "batch"),
            P("batch", None, None),
            P("batch", None, "gate"),
        ),
        check_vma=False,
    )
```

```python
import functools

import jax
import jax.numpy as jnp
from jax import lax
from jax.experimental import pallas as pl
from jax.experimental.pallas import tpu as pltpu
from jax.sharding import PartitionSpec as P

CLIP = 3.0
F32, BF16 = jnp.float32, jnp.bfloat16
QUARTERS, HALVES = 2, 2
PIECES = QUARTERS * HALVES
MIB = 2**20
LATE = 2
SHARES = (0.35, 0.3, 0.15, 0.1, 0.1)

VMEM = pl.BlockSpec(memory_space=pltpu.VMEM)
SMEM = pl.BlockSpec(memory_space=pltpu.SMEM)
ANY = pl.BlockSpec(memory_space=pl.ANY)


def pinned(array):
    return pltpu.with_memory_space_constraint(array, pltpu.VMEM)


def in_hbm(array):
    return pltpu.with_memory_space_constraint(array, pltpu.HBM)


def dot(left, right):
    return jnp.dot(left, right, preferred_element_type=F32)


def layout_kernel(keep, spread, which_ref, w_ref, *refs):
    buf, sems, out_sems = refs[-3:]
    out_ref = refs[0] if keep else refs[1]
    all_ref = refs[1] if keep else refs[0]
    depth, ahead, part = w_ref.shape[1], buf.shape[0], buf.shape[1]
    count = depth // part

    def fetch(i):
        return pltpu.make_async_copy(w_ref.at[which_ref[0], pl.ds(i * part, part)], buf.at[i % ahead], sems.at[i % ahead])

    def store(i):
        rows = pl.ds(i * part, part)
        return pltpu.make_async_copy(out_ref.at[:, rows], all_ref.at[:, rows], out_sems.at[i])

    for i in range(min(ahead - 1, count)):
        fetch(i).start()
    for i in range(count):
        if i + ahead - 1 < count:
            fetch(i + ahead - 1).start()
        fetch(i).wait()
        out_ref[:, i * part : (i + 1) * part, :] = jnp.swapaxes(buf[i % ahead], 0, 1)
        if spread:
            store(i).start()
    for i in range(count if spread else 0):
        store(i).wait()


def turned_kernel(wa_ref, wb_ref, pa_ref, pb_ref, wat_ref, wbt_ref, pat_ref, pbt_ref):
    for w_ref, out_ref in ((wa_ref, wat_ref), (wb_ref, wbt_ref)):
        for gate in range(4):
            for half in range(HALVES):
                width = w_ref.shape[2] // HALVES
                cols = slice(half * width, (half + 1) * width)
                out_ref[gate, cols, :] = w_ref[gate, :, cols].T
    pat_ref[...] = pa_ref[...].T
    pbt_ref[...] = pb_ref[...].T


def pass_kernel(*refs):
    pass


def after(tokens, *arrays, free=0):
    count = len(tokens)
    return pl.pallas_call(
        pass_kernel,
        out_shape=tuple(jax.ShapeDtypeStruct(x.shape, x.dtype) for x in arrays),
        in_specs=[ANY] * (count + len(arrays)),
        out_specs=[ANY] * len(arrays),
        input_output_aliases={count + i: i for i in range(len(arrays))},
        compiler_params=params(1),
        name="after",
    )(*tokens, *(in_hbm(x) if x.size * x.dtype.itemsize > free else x for x in arrays))


def gather_kernel(lows, *refs):
    (feat_ref, prev_ref, feat_too, prev_too, kept_ref), refs = refs[:5], refs[5:]
    groups, (left_ref, right_ref, sems) = refs[:-3], refs[-3:]
    steps, _, depth = feat_ref.shape
    jobs = [
        (feat_ref, left_ref.at[:steps, :, :depth]),
        (prev_ref, left_ref.at[:steps, :, depth:]),
        (feat_too, left_ref.at[steps:, :, :depth]),
        (prev_too, left_ref.at[steps:, :, depth:]),
        (kept_ref, right_ref.at[:steps]),
    ]
    jobs += [(x, right_ref.at[steps + low : steps + low + x.shape[0]]) for x, low in zip(groups, lows)]
    copies = [pltpu.make_async_copy(a, b, sems.at[i]) for i, (a, b) in enumerate(jobs)]
    for copy in copies:
        copy.start()
    for copy in copies:
        copy.wait()


def late_kernel(lows, begin_ref, left_ref, right_in, *refs):
    groups, (right_ref, first_ref, sems) = refs[:-3], refs[-3:]
    steps = left_ref.shape[0] // 2
    copies = [
        pltpu.make_async_copy(x, right_ref.at[steps + low : steps + low + x.shape[0]], sems.at[i])
        for i, (x, low) in enumerate(zip(groups, lows))
    ]
    for copy in copies:
        copy.start()
    for copy in copies:
        copy.wait()
    if first_ref.shape[1] % 128:
        return
    share, depth = first_ref.shape[1], left_ref.shape[2] // 2
    rows = left_ref.shape[0] * left_ref.shape[1]
    left = [
        left_ref[:, :, pl.ds(pl.multiple_of(i * depth + begin_ref[0] * share, 128), share)].reshape(rows, share)
        for i in range(2)
    ]
    left = jnp.concatenate([x.T for x in left], axis=0)
    width = right_ref.shape[2] // 4

    def columns(i, _):
        cols = pl.ds(pl.multiple_of(i * width, width), width)
        total = dot(left, right_ref[:, :, cols].reshape(rows, width)).astype(BF16)
        first_ref[0, :, cols] = total[:share]
        first_ref[1, :, cols] = total[share:]
        return 0

    lax.fori_loop(0, 4, columns, 0)


def product_kernel(left_ref, right_ref, out_ref):
    rows, depth = left_ref.shape[0] * left_ref.shape[1], left_ref.shape[2] // 2
    width = right_ref.shape[2] // 4
    for which in range(2):
        left = left_ref[:, :, which * depth : (which + 1) * depth].reshape(rows, depth).T

        def columns(i, _):
            cols = pl.ds(pl.multiple_of(i * width, width), width)
            out_ref[which, :, cols] = dot(left, right_ref[:, :, cols].reshape(rows, width)).astype(BF16)
            return 0

        lax.fori_loop(0, 4, columns, 0)


def whole_product_kernel(lows, *refs):
    (feat_ref, prev_ref, feat_too, prev_too, kept_ref), refs = refs[:5], refs[5:]
    groups, (out_ref, left_buf, turned_buf, right_buf, left_sems, sems) = refs[:-6], refs[-6:]
    steps, streams, depth = feat_ref.shape
    blocks = right_buf.shape[0]
    width = right_buf.shape[3]
    rows = 2 * steps * streams

    def fetches_of(block):
        cols = slice(block * width, (block + 1) * width)
        jobs = [(kept_ref.at[:, :, cols], right_buf.at[block, :steps])]
        jobs += [
            (x.at[:, :, cols], right_buf.at[block, steps + low : steps + low + x.shape[0]])
            for x, low in zip(groups, lows)
        ]
        return [pltpu.make_async_copy(a, b, sems.at[block, i]) for i, (a, b) in enumerate(jobs)]

    lefts = [(feat_ref, 0, 0), (feat_too, steps, 0), (prev_ref, 0, 1), (prev_too, steps, 1)]
    lefts = [
        pltpu.make_async_copy(x, left_buf.at[half, low : low + steps], left_sems.at[i])
        for i, (x, low, half) in enumerate(lefts)
    ]
    for copy in lefts:
        copy.start()
    for block in range(blocks):
        for copy in fetches_of(block):
            copy.start()
    for which in range(2):
        lefts[2 * which].wait()
        lefts[2 * which + 1].wait()
        turned_buf[which] = left_buf[which].reshape(rows, depth).T
    for block in range(blocks):
        for copy in fetches_of(block):
            copy.wait()

        def one(which, _):
            total = dot(turned_buf[which], right_buf[block].reshape(rows, width))
            out_ref[which, :, block * width : (block + 1) * width] = total.astype(BF16)
            return 0

        lax.fori_loop(0, 2, one, 0)


def assemble_kernel(place_ref, near_a, near_b, far_a, far_b, in_ref, rec_ref):
    own, low, high = place_ref[0], place_ref[1], place_ref[2]
    width = in_ref.shape[3] // HALVES
    for direction, mine_ref, theirs_ref, index in ((own, near_a, near_b, low), (1 - own, far_a, far_b, high)):
        for which, out_ref in ((0, in_ref), (1, rec_ref)):
            mine, theirs = mine_ref[which].astype(F32), theirs_ref[which].astype(F32)
            for half in range(HALVES):
                whole = jnp.where(index == half, mine, theirs)
                gates = jnp.stack([whole[:, gate * width : (gate + 1) * width] for gate in range(4)])
                out_ref[direction, :, :, half * width : (half + 1) * width] = jnp.swapaxes(gates, 0, 1)


def order_kernel(step_ref, feat_ref, out_ref, all_ref, sems):
    copies = []
    for i in range(feat_ref.shape[0]):
        source = feat_ref.at[step_ref[0] + step_ref[1] * i]
        copies.append(pltpu.make_async_copy(source, out_ref.at[i], sems.at[2 * i]))
        copies.append(pltpu.make_async_copy(source, all_ref.at[i], sems.at[2 * i + 1]))
    for copy in copies:
        copy.start()
    for copy in copies:
        copy.wait()


def numbers_kernel(index, in_ref, out_ref):
    out_ref[0] = in_ref[index]


def bias_kernel(sum_ref, out_ref):
    width = sum_ref.shape[2] // 4
    for piece in range(PIECES):
        for gate in range(4):
            out_ref[piece, gate : gate + 1, :] = jnp.sum(
                sum_ref[piece, :, gate * width : (gate + 1) * width], axis=0, keepdims=True
            )


def pieces(refs, axis):
    for piece in range(PIECES):
        quarter, half = divmod(piece, HALVES)
        width = refs[0].shape[axis] // HALVES
        yield piece, quarter, width, slice(half * width, (half + 1) * width)


def forward_kernel(
    first, step_ref, p_ref, q_ref, start_ref, keep_ref, cell_ref, inflow_ref, wa_ref, wb_ref, pa_ref, pb_ref,
    part_ref, next_ref, gates_ref, mixed_ref, prev_ref, hidden_ref, slope_ref,
):
    keep = keep_ref[step_ref[1]][:, :1]
    if first:
        hidden = start_ref[...]
    else:
        hidden = clipped(p_ref, q_ref, hidden_ref, slope_ref)
    hidden = hidden * keep.astype(BF16)
    prev_ref[...] = hidden
    part = jnp.zeros(part_ref.shape, F32)
    for piece, quarter, width, cols in pieces((wa_ref, wb_ref), 2):
        w_ref, proj_ref = ((wa_ref, pa_ref), (wb_ref, pb_ref))[quarter]
        acts = []
        for gate in range(4):
            place = slice(gate * width, (gate + 1) * width)
            pre = dot(hidden, w_ref[gate, :, cols]) + inflow_ref[piece, :, place]
            act = jnp.tanh(pre if gate == 2 else 0.5 * pre)
            gates_ref[piece, :, place] = act.astype(BF16)
            acts.append(act if gate == 2 else 0.5 + 0.5 * act)
        ingate, forget, candidate, outgate = acts
        cell = CLIP * jnp.tanh((forget * (keep * cell_ref[piece]) + ingate * candidate) * (1.0 / CLIP))
        next_ref[piece] = cell
        mixed = (outgate * jnp.tanh(cell)).astype(BF16)
        mixed_ref[piece] = mixed
        part = part + dot(mixed, proj_ref[cols, :])
    part_ref[...] = part.astype(BF16)


def clipped(p_ref, q_ref, hidden_ref, slope_ref):
    squash = jnp.tanh((p_ref[...].astype(F32) + q_ref[...].astype(F32)) * (1.0 / CLIP))
    hidden = (CLIP * squash).astype(BF16)
    hidden_ref[...] = hidden
    slope_ref[...] = 1.0 - squash * squash
    return hidden


def between_kernel(
    first, last, passed, step_ref, feat_ref, ba_ref, bb_ref, wa_ref, wb_ref, cell_ref, gates_ref, mixed_ref, prev_ref, hidden_ref,
    slope_ref, *refs,
):
    refs = refs[(0 if first else 6) + passed :]
    out_ref, gates_all, cells_all, mixed_all, prev_all, hidden_all, slope_all = refs[:7]
    sems = refs[-1]
    step, time_before = step_ref[0], step_ref[2]
    copies = [pltpu.make_async_copy(gates_ref.at[i], gates_all.at[i, step], sems.at[i]) for i in range(PIECES)]
    copies += [
        pltpu.make_async_copy(mixed_ref.at[i], mixed_all.at[i, step], sems.at[PIECES + i]) for i in range(PIECES)
    ]
    copies.append(pltpu.make_async_copy(cell_ref, cells_all.at[step], sems.at[2 * PIECES]))
    copies.append(pltpu.make_async_copy(prev_ref, prev_all.at[step], sems.at[2 * PIECES + 1]))
    if not first:
        copies.append(pltpu.make_async_copy(hidden_ref, hidden_all.at[time_before], sems.at[2 * PIECES + 2]))
        copies.append(pltpu.make_async_copy(slope_ref, slope_all.at[step - 1], sems.at[2 * PIECES + 3]))
    for copy in copies:
        copy.start()
    if not last:
        inflow_into(feat_ref[step + 1], ba_ref, bb_ref, wa_ref, wb_ref, out_ref)
    for copy in copies:
        copy.wait()


def inflow_into(feat, ba_ref, bb_ref, wa_ref, wb_ref, out_ref, quarters=(0, 1)):
    for piece, quarter, width, cols in pieces((wa_ref, wb_ref), 2):
        if quarter not in quarters:
            continue
        w_ref, bias_ref = ((wa_ref, ba_ref), (wb_ref, bb_ref))[quarter]
        for gate in range(4):
            place = slice(gate * width, (gate + 1) * width)
            out_ref[piece, :, place] = dot(feat, w_ref[gate, :, cols]) + bias_ref[gate : gate + 1, cols]


def begin_kernel(which_ref, feat_ref, wa_ref, proj_ref, *refs):
    sems = refs[-1]
    out_ref, pa_ref, *placed = refs[-11:-1]
    copies = [pltpu.make_async_copy(x, y, sems.at[i]) for i, (x, y) in enumerate(zip(refs[:-11], placed))]
    copies.append(pltpu.make_async_copy(proj_ref.at[which_ref[0]], pa_ref, sems.at[len(copies)]))
    for copy in copies:
        copy.start()
    ba_ref, bb_ref, wb_ref = placed[:3]
    copies[0].wait()
    inflow_into(feat_ref[0], ba_ref, bb_ref, wa_ref, wb_ref, out_ref, (0,))
    copies[1].wait()
    copies[2].wait()
    inflow_into(feat_ref[0], ba_ref, bb_ref, wa_ref, wb_ref, out_ref, (1,))
    for copy in copies[3:]:
        copy.wait()


def backward_kernel(
    step_ref, p_ref, q_ref, keep_ref, grad_ref, bias_ref, wa_ref, wb_ref, pa_ref, pb_ref,
    gates_ref, cell_ref, prev_ref, slope_ref, up_ref, start_ref,
    part_ref, next_ref, sum_ref, raw_ref, dz_ref,
):
    step = step_ref[0]
    keep = keep_ref[step_ref[1]][:, :1]
    raw = (up_ref[...].astype(F32) + (p_ref[...].astype(F32) + q_ref[...].astype(F32))) * slope_ref[...]
    raw = raw.astype(BF16)
    raw_ref[...] = raw
    part = jnp.zeros(part_ref.shape, F32)
    for piece, quarter, width, cols in pieces((wa_ref, wb_ref), 1):
        w_ref, proj_ref = ((wa_ref, pa_ref), (wb_ref, pb_ref))[quarter]
        mixed = dot(raw, proj_ref[:, cols])
        acts = [gates_ref[piece, :, gate * width : (gate + 1) * width].astype(F32) for gate in range(4)]
        ingate, forget, outgate = (0.5 + 0.5 * acts[gate] for gate in (0, 1, 3))
        slopes = [1.0 - act * act for act in acts]
        cell = cell_ref[piece]
        prev = keep * jnp.where(step == 0, start_ref[piece], prev_ref[piece])
        squash = jnp.tanh(cell)
        total = grad_ref[piece] + mixed * outgate * (1.0 - squash * squash)
        inner = total * (1.0 - (cell * (1.0 / CLIP)) * (cell * (1.0 / CLIP)))
        next_ref[piece] = keep * inner * forget
        quart = 0.25 * inner
        pre_grads = (
            quart * acts[2] * slopes[0],
            quart * prev * slopes[1],
            inner * ingate * slopes[2],
            0.25 * mixed * squash * slopes[3],
        )
        for gate in range(4):
            low = pre_grads[gate].astype(BF16)
            place = slice(gate * width, (gate + 1) * width)
            dz_ref[piece, :, place] = low
            rows = pre_grads[gate].reshape(-1, 8, width)
            sum_ref[piece, :, place] = bias_ref[piece, :, place] + jnp.sum(rows, axis=0)
            part = part + dot(low, w_ref[gate, cols, :])
    part_ref[...] = (part * keep).astype(BF16)


def finish_kernel(
    step_ref, p_ref, q_ref, mixed_ref, prev_ref, hidden_ref, before_ref, ups_all, mixed_in, prev_in, hidden_in, slope_in,
    slope_ref, up_ref, mixed_all, prev_all, hidden_all, slope_all, hidden_buf, sems,
):
    step, time, time_before = step_ref[0], step_ref[1], step_ref[2]
    jobs = [(mixed_ref.at[i], mixed_all.at[i, step]) for i in range(PIECES)]
    jobs += [
        (ups_all.at[time], up_ref),
        (prev_ref, prev_all.at[step]),
        (hidden_ref, hidden_all.at[time_before]),
        (before_ref, slope_all.at[step - 1]),
        (hidden_buf, hidden_all.at[time]),
    ]
    copies = [pltpu.make_async_copy(x, y, sems.at[i]) for i, (x, y) in enumerate(jobs)]
    for copy in copies[:-1]:
        copy.start()
    clipped(p_ref, q_ref, hidden_buf, slope_ref)
    copies[-1].start()
    for copy in copies:
        copy.wait()


def fetches(step, time, sources, targets, sems):
    gates_all, cells_all, ups_all = sources
    gates_ref, cell_ref, prev_ref, up_ref = targets
    before = jnp.maximum(step - 1, 0)
    return [
        pltpu.make_async_copy(gates_all.at[i, step], gates_ref.at[i], sems.at[i]) for i in range(PIECES)
    ] + [
        pltpu.make_async_copy(cells_all.at[step], cell_ref, sems.at[PIECES]),
        pltpu.make_async_copy(cells_all.at[before], prev_ref, sems.at[PIECES + 1]),
        pltpu.make_async_copy(ups_all.at[time], up_ref, sems.at[PIECES + 2]),
    ]


def aside_kernel(
    first, last, opens, passed, step_ref, dz_ref, raw_ref, gates_all, cells_all, ups_all, slope_all, *refs
):
    refs = refs[(0 if first else 4) + (0 if opens else 2) + passed :]
    gates_ref, cell_ref, prev_ref, slope_ref, up_ref = refs[:5]
    dz_all, raw_all, near_all, far_all, near_out, far_out = refs[5:11]
    sems, fetch_sems = refs[-2:]
    step, time_before = step_ref[0], step_ref[2]
    slot, low, high = step_ref[4], step_ref[5], step_ref[6]
    before = jnp.maximum(step - 1, 0)
    copies = []
    if not last:
        copies += fetches(
            before, time_before, (gates_all, cells_all, ups_all), (gates_ref, cell_ref, prev_ref, up_ref), fetch_sems
        )
        copies.append(pltpu.make_async_copy(slope_all.at[before], slope_ref, fetch_sems.at[PIECES + 3]))
    copies += [pltpu.make_async_copy(dz_ref.at[i], dz_all.at[i, step], sems.at[i]) for i in range(PIECES)]
    copies.append(pltpu.make_async_copy(raw_ref, raw_all.at[step], sems.at[PIECES]))
    copies.append(pltpu.make_async_copy(dz_ref.at[low], near_all.at[step], sems.at[PIECES + 1]))
    copies.append(pltpu.make_async_copy(dz_ref.at[HALVES + high], far_all.at[step], sems.at[PIECES + 2]))
    copies.append(pltpu.make_async_copy(dz_ref.at[1 - low], near_out.at[slot], sems.at[PIECES + 3]))
    copies.append(pltpu.make_async_copy(dz_ref.at[HALVES + 1 - high], far_out.at[slot], sems.at[PIECES + 4]))
    for copy in copies:
        copy.start()
    for copy in copies:
        copy.wait()


def input_grad_kernel(step_ref, dz_ref, wa_ref, wb_ref, out_ref, acc_ref):
    piece, gate = pl.program_id(0), pl.program_id(1)
    steps, streams, width = dz_ref.shape[1:]

    @pl.when((piece == 0) & (gate == 0))
    def _():
        acc_ref[...] = jnp.zeros(acc_ref.shape, F32)

    weights = jnp.where(piece < HALVES, wa_ref[0], wb_ref[0])
    acc_ref[...] += lax.dot_general(
        dz_ref[0].reshape(steps * streams, width), weights, (((1,), (1,)), ((), ())), preferred_element_type=F32
    )

    @pl.when((piece == PIECES - 1) & (gate == 3))
    def _():
        for step in range(steps):
            time = step_ref[0] + step_ref[1] * step
            out_ref[time] = acc_ref[step * streams : (step + 1) * streams, :]


def params(mib):
    return pltpu.CompilerParams(vmem_limit_bytes=mib * MIB)


def cost(flops, size):
    return pl.CostEstimate(flops=flops, bytes_accessed=size, transcendentals=0)


def body(inputs, w_in, w_rec, bias, proj, state_h, state_c, resets, stream_doc, cotangent):
    streams, steps, depth = inputs.shape[1:]
    cells = w_in.shape[3]
    width = cells // HALVES
    n_batch = lax.axis_size("batch")
    gates_size = lax.axis_size("gate")
    line = n_batch // 2
    swap = [(i, i ^ 1) for i in range(gates_size)]
    across = [(i, i ^ 2) for i in range(gates_size)]
    near_swap = [(i, i ^ 1) for i in range(n_batch)]
    far_swap = [(i, i ^ 2) for i in range(n_batch)]

    rank, spot = lax.axis_index("gate"), lax.axis_index("batch")
    half_cols, quarter_cols = depth // 2, depth // 4
    place_numbers = {
        "own": rank % 2,
        "other": 1 - rank % 2,
        "low": spot % 2,
        "not_low": 1 - spot % 2,
        "high": (spot // 2) % 2,
        "not_high": 1 - (spot // 2) % 2,
        "spot": spot,
        "begin": jnp.where(spot // 2 == 0, line - 1, 0),
        "cols": (rank // 2) * half_cols,
        "other_cols": (1 - rank // 2) * half_cols,
    }
    for stride, count in {(2, line), (4, line // 2)}:
        here = (spot // stride) % count
        place_numbers[stride, "here"] = here
        place_numbers[stride, "not_here"] = jnp.maximum(1 - here, 0)
        for slot in range(2, count):
            place_numbers[stride, "rise", slot] = jnp.minimum(here + count - slot, count - 1)
            place_numbers[stride, "fall", slot] = jnp.maximum(here - count + slot, 0)
        if count > 2:
            place_numbers[stride, "begin"] = jnp.where(here == 0, count - 1, 0)
    names = sorted(place_numbers, key=str)
    which = pl.pallas_call(
        functools.partial(numbers_kernel, names.index("own")),
        out_shape=jax.ShapeDtypeStruct((1,), jnp.int32),
        in_specs=[SMEM],
        out_specs=SMEM,
        name="numbers",
    )(jnp.stack([place_numbers[x] for x in names]).astype(jnp.int32))
    number = {x: place_numbers[x].astype(jnp.int32) for x in names}
    own, low, high = number["own"], number["low"], number["high"]

    def pick(stacked, index, axis=0):
        return lax.dynamic_index_in_dim(stacked, index, axis, keepdims=False, allow_negative_indices=False)

    def trade(mine, theirs):
        return (mine, lax.ppermute(theirs, "gate", swap))

    def vmem(shape, dtype):
        return pltpu.VMEM(shape, dtype)

    def hbm(shape, dtype):
        return pltpu.HBM(shape, dtype)

    def by_gate(weights, index, keep, spread):
        shape = (4,) + weights.shape[1:2] + weights.shape[3:]
        count = 16
        kept, spreads = (vmem(shape, BF16),) * keep, (hbm(shape, BF16),) * spread
        return pl.pallas_call(
            functools.partial(layout_kernel, keep, spread),
            out_shape=kept + spreads,
            in_specs=[SMEM, ANY],
            out_specs=[VMEM] * keep + [ANY] * spread,
            scratch_shapes=[pltpu.VMEM(shape, BF16)] * (1 - keep)
            + [
                pltpu.VMEM((4, weights.shape[1] // count) + weights.shape[2:], BF16),
                pltpu.SemaphoreType.DMA((4,)),
                pltpu.SemaphoreType.DMA((count,)),
            ],
            compiler_params=params(8),
            name="layout",
        )(index, in_hbm(weights))

    away = jnp.full((1,), number["other"], jnp.int32)
    win_b, rec_b = (lax.ppermute(by_gate(w, away, False, True)[0], "gate", swap) for w in (w_in, w_rec))
    (win_av, win_a), (rec_av,) = by_gate(w_in, which, True, True), by_gate(w_rec, which, True, False)
    proj_b = lax.ppermute(pick(proj, number["other"]), "gate", swap)
    bias_a, bias_b = trade(pick(bias, own), pick(bias, number["other"]))

    def cells_to_pieces(pair):
        both = jnp.stack(pair).reshape(QUARTERS, streams, HALVES, width)
        return jnp.transpose(both, (0, 2, 1, 3)).reshape(PIECES, streams, width)

    def by_time(stacked):
        return jnp.transpose(pick(stacked, own), (1, 0, 2))

    feats = by_time(inputs)
    ups = by_time(cotangent)
    flags = resets.astype(F32)
    later = jnp.concatenate([flags[:, 1:], jnp.zeros_like(flags[:, :1])], axis=1)
    keep = 1.0 - jnp.where(own == 0, flags, later)
    keep = jnp.broadcast_to(jnp.transpose(keep)[:, :, None], (steps, streams, 128))

    docs_h = state_h[stream_doc]
    docs_c = state_c[stream_doc]
    start_h = pick(jnp.transpose(docs_h, (1, 0, 2)), own).astype(BF16)
    by_dir_c = jnp.transpose(docs_c, (1, 0, 2))
    start_c = cells_to_pieces(trade(pick(by_dir_c, own), pick(by_dir_c, number["other"])))

    def at_step(step):
        near = jnp.array([step, step, max(step - 1, 0), min(step + 1, steps - 1)], jnp.int32)
        turned = jnp.array([step] + [steps - 1 - x for x in (step, max(step - 1, 0), min(step + 1, steps - 1))], jnp.int32)
        return jnp.where(own == 0, near, turned)

    def swapped(array, pairs):
        return lax.ppermute(array, "batch", pairs)

    turn = jnp.where(own == 0, jnp.array([0, 1], jnp.int32), jnp.array([steps - 1, -1], jnp.int32))
    feats_v, feat_all = pl.pallas_call(
        order_kernel,
        out_shape=(vmem(feats.shape, BF16), hbm(feats.shape, BF16)),
        in_specs=[SMEM, ANY],
        out_specs=[VMEM, ANY],
        scratch_shapes=[pltpu.SemaphoreType.DMA((2 * steps,))],
        compiler_params=params(1),
        name="order",
    )(turn, feats)
    gates_shape, cell_shape = (PIECES, streams, 4 * width), (PIECES, streams, width)
    bias_shape = (PIECES, 8, 4 * width)
    sources = (bias_a.astype(F32), bias_b.astype(F32), in_hbm(win_b), in_hbm(rec_b), in_hbm(proj_b), keep, start_h, start_c)
    inflow, proj_av, bias_av, bias_bv, win_bv, rec_bv, proj_bv, keep_v, start_hv, start_cv = pl.pallas_call(
        begin_kernel,
        out_shape=(vmem(gates_shape, F32), vmem((cells, depth), BF16)) + tuple(vmem(x.shape, x.dtype) for x in sources),
        in_specs=[SMEM, VMEM, VMEM] + [ANY] * (1 + len(sources)),
        out_specs=[VMEM] * (2 + len(sources)),
        scratch_shapes=[pltpu.SemaphoreType.DMA((1 + len(sources),))],
        compiler_params=params(8),
        name="begin",
    )(which, pinned(feats_v), pinned(win_av), in_hbm(proj), *sources)

    def forward_call(first, step, part, peer, cell, inflow):
        return pl.pallas_call(
            functools.partial(forward_kernel, first),
            out_shape=(
                vmem((streams, depth), BF16),
                vmem(cell_shape, F32),
                vmem(gates_shape, BF16),
                vmem(cell_shape, BF16),
                vmem((streams, depth), BF16),
                vmem((streams, depth), BF16),
                vmem((streams, depth), F32),
            ),
            in_specs=[SMEM] + [VMEM] * 10,
            out_specs=[VMEM] * 7,
            compiler_params=params(8),
            name="forward_step",
        )(
            at_step(step), pinned(part), pinned(peer), pinned(start_hv), pinned(keep_v), pinned(cell), pinned(inflow),
            pinned(rec_av), pinned(rec_bv), pinned(proj_av), pinned(proj_bv),
        )

    def between_call(step, fresh, stacks, passing=()):
        shapes = (
            hbm((PIECES, steps, streams, 4 * width), BF16),
            hbm((steps,) + cell_shape, F32),
            hbm((PIECES, steps, streams, width), BF16),
            hbm((steps, streams, depth), BF16),
            hbm((steps, streams, depth), BF16),
            hbm((steps, streams, depth), F32),
        )
        aliases = {12 + i: 1 + i for i in range(len(stacks))}
        aliases.update({12 + len(stacks) + i: 7 + i for i in range(len(passing))})
        inflow, *out = pl.pallas_call(
            functools.partial(between_kernel, not stacks, step == steps - 1, len(passing)),
            out_shape=(vmem(gates_shape, F32),) + shapes + tuple(hbm(x.shape, x.dtype) for x in passing),
            in_specs=[SMEM] + [VMEM] * 11 + [ANY] * (len(stacks) + len(passing)),
            out_specs=[VMEM] + [ANY] * (6 + len(passing)),
            scratch_shapes=[pltpu.SemaphoreType.DMA((2 * PIECES + 4,))],
            input_output_aliases=aliases,
            compiler_params=params(8),
            cost_estimate=cost(2 * streams * depth * 8 * cells, 8 * depth * cells * 2),
            name="between",
        )(
            at_step(step), pinned(feats_v), pinned(bias_av), pinned(bias_bv), pinned(win_av), pinned(win_bv),
            *(pinned(x) for x in fresh), *(in_hbm(x) for x in (*stacks, *passing)),
        )
        return inflow, tuple(out[:6]), tuple(out[6:])

    none = jnp.zeros((streams, depth), BF16)
    part, peer, cell, stacks = none, none, start_cv, ()
    for step in range(steps):
        cell_before = cell
        part, cell, *fresh = forward_call(step == 0, step, part, peer, cell, inflow)
        peer = lax.ppermute(part, "gate", across)
        if step == steps - 1:
            break
        if step == 2:
            (feat_all,) = after((part,), feat_all)
            feat_in = (swapped(feat_all, near_swap), swapped(feat_all, far_swap))
        due = step == (3 * steps) // 4
        inflow, stacks, passed = between_call(step, (cell, *fresh), stacks, feat_in if due else ())
        feat_in = passed if due else (feat_in if step >= 2 else None)
    gates, mixed, prev, hidden, slope = fresh
    gates_all, cells_all, mixed_all, prev_all, hidden_all, slope_all = stacks

    slope_now, up_now, mixed_all, prev_all, hidden_all, slope_all = pl.pallas_call(
        finish_kernel,
        out_shape=(vmem((streams, depth), F32), vmem((streams, depth), BF16))
        + tuple(hbm(x.shape, x.dtype) for x in (mixed_all, prev_all, hidden_all, slope_all)),
        in_specs=[SMEM] + [VMEM] * 6 + [ANY] * 5,
        out_specs=[VMEM] * 2 + [ANY] * 4,
        scratch_shapes=[pltpu.VMEM((streams, depth), BF16), pltpu.SemaphoreType.DMA((PIECES + 5,))],
        input_output_aliases={8 + i: 2 + i for i in range(4)},
        compiler_params=params(8),
        name="finish",
    )(
        at_step(steps - 1), pinned(part), pinned(peer), *(pinned(x) for x in (mixed, prev, hidden, slope)), in_hbm(ups),
        *(in_hbm(x) for x in (mixed_all, prev_all, hidden_all, slope_all)),
    )
    saved = (gates, cell, cell_before, slope_now, up_now)
    saved_shapes = (
        vmem(gates_shape, BF16),
        vmem(cell_shape, F32),
        vmem(cell_shape, F32),
        vmem((streams, depth), F32),
        vmem((streams, depth), BF16),
    )

    rec_atv, rec_btv, proj_atv, proj_btv = pl.pallas_call(
        turned_kernel,
        out_shape=(vmem((4, cells, depth), BF16),) * 2 + (vmem((depth, cells), BF16),) * 2,
        in_specs=[VMEM] * 4,
        out_specs=[VMEM] * 4,
        compiler_params=params(8),
        name="turned",
    )(pinned(rec_av), pinned(rec_bv), pinned(proj_av), pinned(proj_bv))

    def backward_call(step, part, peer, grad, bias, saved):
        return pl.pallas_call(
            backward_kernel,
            out_shape=(
                vmem((streams, depth), BF16),
                vmem(cell_shape, F32),
                vmem(bias_shape, F32),
                vmem((streams, depth), BF16),
                vmem(gates_shape, BF16),
            ),
            in_specs=[SMEM] + [VMEM] * 15,
            out_specs=[VMEM] * 5,
            compiler_params=params(8),
            name="backward_step",
        )(
            at_step(step), pinned(part), pinned(peer), pinned(keep_v), pinned(grad), pinned(bias),
            pinned(rec_atv), pinned(rec_btv), pinned(proj_atv), pinned(proj_btv),
            *(pinned(x) for x in saved), pinned(start_cv),
        )

    def aside_call(step, slot, slots, dz, raw, stacks, sends, passing):
        piece_shape = (streams, 4 * width)
        shapes = (
            hbm((PIECES, steps) + piece_shape, BF16),
            hbm((steps, streams, depth), BF16),
            hbm((steps,) + piece_shape, BF16),
            hbm((steps,) + piece_shape, BF16),
            hbm((slots,) + piece_shape, BF16),
            hbm((slots,) + piece_shape, BF16),
        )
        kept = len(stacks)
        aliases = {7 + i: 5 + i for i in range(kept)}
        aliases.update({7 + kept + i: 9 + i for i in range(len(sends))})
        aliases.update({7 + kept + len(sends) + i: 11 + i for i in range(len(passing))})
        out = pl.pallas_call(
            functools.partial(aside_kernel, not stacks, step == 0, not sends, len(passing)),
            out_shape=saved_shapes + shapes + tuple(hbm(x.shape, x.dtype) for x in passing),
            in_specs=[SMEM] + [VMEM] * 2 + [ANY] * (4 + kept + len(sends) + len(passing)),
            out_specs=[VMEM] * 5 + [ANY] * (6 + len(passing)),
            scratch_shapes=[
                pltpu.SemaphoreType.DMA((PIECES + 5,)),
                pltpu.SemaphoreType.DMA((PIECES + 4,)),
            ],
            input_output_aliases=aliases,
            compiler_params=params(8),
            cost_estimate=cost(0, 8 * MIB),
            name="aside",
        )(
            jnp.concatenate([at_step(step), jnp.stack([jnp.int32(slot), low, high])]), pinned(dz), pinned(raw),
            in_hbm(gates_all), in_hbm(cells_all), in_hbm(ups), in_hbm(slope_all),
            *(in_hbm(x) for x in (*stacks, *sends, *passing)),
        )
        return out[:5], tuple(out[5:9]), tuple(out[9:11]), tuple(out[11:])

    carry = (none, none, jnp.zeros(cell_shape, F32), jnp.zeros(bias_shape, F32), saved, ())
    pending, arrived, ready, top = [], [], None, steps
    for index, share in enumerate(SHARES):
        slots = top if index == len(SHARES) - 1 else round(share * steps)
        sends = ()
        for step in range(top - 1, top - slots - 1, -1):
            part, peer, grad, bias_sum, saved, stacks = carry
            part, grad, bias_sum, raw, dz = backward_call(step, part, peer, grad, bias_sum, saved)
            peer = lax.ppermute(part, "gate", across)
            if step == steps - 1:
                (prev_all,) = after((part,), prev_all)
                pending.append((step - steps // 3, (swapped(prev_all, near_swap), swapped(prev_all, far_swap))))
            if ready is not None:
                due, sides = ready
                sides = after((part,), *sides) if step else sides
                pending.append((due, (swapped(sides[0], near_swap), swapped(sides[1], far_swap))))
                ready = None
            passing = ()
            while pending and pending[0][0] >= step:
                passing += pending.pop(0)[1]
            saved, stacks, sends, passed = aside_call(
                step, step - (top - slots), slots, dz, raw, stacks, sends, passing
            )
            arrived += [passed[i : i + 2] for i in range(0, len(passed), 2)]
            carry = (part, peer, grad, bias_sum, saved, stacks)
        top -= slots
        ready = (max(top - 1 - (3 * slots + 3) // 4, 0 if slots > 2 else -1), sends)
    pending.append((-1, (swapped(sends[0], near_swap), swapped(sends[1], far_swap))))
    arrived += [arrays for _, arrays in pending]
    dz_all, raw_all, near_all, far_all = carry[-1]
    bias_sum = carry[3]
    prev_in, exchanged = arrived[0], arrived[1:]
    rows = steps * streams

    def by_direction(mine, theirs):
        return jnp.stack([jnp.where(own == 0, mine, theirs), jnp.where(own == 0, theirs, mine)])

    def line_sum(chunks, axis, stride, count, first=None, gates={}, hooks={}):
        def chunk(*name):
            return pick(chunks, number[(stride, *name)], axis)

        def at(device):
            return (device // stride) % count

        if count == 2:
            pairs = [(i, i + stride if at(i) == 0 else i - stride) for i in range(n_batch)]
            return (chunk("here").astype(F32) + swapped(chunk("not_here"), pairs).astype(F32)).astype(BF16)
        ends = [(i, i + stride) for i in range(n_batch) if at(i) == 0]
        ends += [(i, i - stride) for i in range(n_batch) if at(i) == count - 1]
        up = down = swapped(chunk("begin") if first is None else first, ends)
        for slot in range(2, count):
            if slot in gates:
                up, down = gates[slot](up, down)
            rise = (chunk("rise", slot).astype(F32) + up.astype(F32)).astype(BF16)
            fall = (chunk("fall", slot).astype(F32) + down.astype(F32)).astype(BF16)
            if slot in hooks:
                hooks[slot](rise, fall)
            up = swapped(rise, [(i, i + stride) for i in range(n_batch) if at(i) < min(slot, count - 1)])
            down = swapped(fall, [(i, i - stride) for i in range(n_batch) if at(i) > max(count - 1 - slot, 0)])
        if count in gates:
            up, down = gates[count](up, down)
        return (chunk("here").astype(F32) + up.astype(F32) + down.astype(F32)).astype(BF16)

    share_rows = depth // n_batch

    def input_grad_of(dz):
        return pl.pallas_call(
            input_grad_kernel,
            out_shape=jax.ShapeDtypeStruct((steps, streams, depth), F32),
            grid_spec=pltpu.PrefetchScalarGridSpec(
                num_scalar_prefetch=1,
                grid=(PIECES, 4),
                in_specs=[
                    pl.BlockSpec((1, steps, streams, width), lambda p, g, turn: (p, 0, 0, g)),
                    pl.BlockSpec(
                        (1, depth, width), lambda p, g, turn: (jnp.where(p < 2, g, 3), 0, jnp.where(p < 2, p, 1))
                    ),
                    pl.BlockSpec(
                        (1, depth, width), lambda p, g, turn: (jnp.where(p < 2, 0, g), 0, jnp.where(p < 2, 0, p - 2))
                    ),
                ],
                out_specs=pl.BlockSpec((steps, streams, depth), lambda p, g, turn: (0, 0, 0)),
                scratch_shapes=[pltpu.VMEM((rows, depth), F32)],
            ),
            compiler_params=params(16),
            cost_estimate=cost(0, 0),
            name="input_grad",
        )(turn, in_hbm(dz), in_hbm(win_a), in_hbm(win_b))

    grad_proj = jnp.einsum("ptnc,tnk->pkc", mixed_all, raw_all, preferred_element_type=F32).astype(BF16)
    grad_proj = grad_proj.reshape(PIECES, line, 2, share_rows, width)
    bias_rows = pl.pallas_call(
        bias_kernel,
        out_shape=jax.ShapeDtypeStruct((PIECES, 4, width), F32),
        in_specs=[VMEM],
        out_specs=VMEM,
        compiler_params=params(1),
        name="bias",
    )(pinned(bias_sum))
    bias_rows = jnp.broadcast_to(bias_rows[:, None, None].astype(BF16), (PIECES, line, 2, 4, width))
    grad_proj = jnp.concatenate([grad_proj, bias_rows], axis=3)

    def with_partner(grad):
        mine, sent = (pick(grad, number[x], grad.ndim - 3) for x in ("low", "not_low"))
        taken = swapped(sent, near_swap)
        return sent, taken, (mine.astype(F32) + taken.astype(F32)).astype(BF16)

    def across_two(grad):
        return line_sum(grad.reshape(grad.shape[:-3] + (line // 2, 2) + grad.shape[-2:]), grad.ndim - 3, 4, line // 2)

    proj_sent, proj_taken, proj_y = with_partner(grad_proj)

    lows, count = [], 0
    for x in exchanged[::-1]:
        lows.insert(0, count)
        count += x[0].shape[0]

    def gathered(kept, feat, prev, parts):
        return pl.pallas_call(
            functools.partial(gather_kernel, tuple(lows[: len(parts)])),
            out_shape=(vmem((2 * steps, streams, 2 * depth), BF16), vmem((2 * steps, streams, 4 * width), BF16)),
            in_specs=[ANY] * (5 + len(parts)),
            out_specs=[VMEM] * 2,
            scratch_shapes=[pltpu.SemaphoreType.DMA((5 + len(parts),))],
            compiler_params=params(1),
            cost_estimate=cost(0, 0),
            name="gather",
        )(*(in_hbm(x) for x in (feat_all, prev_all, feat, prev, kept, *parts)))

    def completed(begin, rows_out, left, right, parts):
        return pl.pallas_call(
            functools.partial(late_kernel, tuple(lows[len(lows) - len(parts) :])),
            out_shape=(vmem(right.shape, BF16), jax.ShapeDtypeStruct((2, max(rows_out, 8), 4 * width), BF16)),
            in_specs=[SMEM] + [VMEM] * 2 + [ANY] * len(parts),
            out_specs=[VMEM] * 2,
            scratch_shapes=[pltpu.SemaphoreType.DMA((len(parts),))],
            input_output_aliases={2: 0},
            compiler_params=params(16),
            cost_estimate=cost(0, 0),
            name="late",
        )(begin, pinned(left), pinned(right), *(in_hbm(x) for x in parts))

    def multiplied(left, right):
        return pl.pallas_call(
            product_kernel,
            out_shape=jax.ShapeDtypeStruct((2, depth, 4 * width), BF16),
            in_specs=[VMEM] * 2,
            out_specs=VMEM,
            compiler_params=params(16),
            cost_estimate=cost(0, 0),
            name="product",
        )(pinned(left), pinned(right))

    near_parts, far_parts = zip(*exchanged)
    chunk_rows = 2 * share_rows if 2 * share_rows % 128 == 0 else 0
    near_left, near_right = gathered(near_all, feat_in[0], prev_in[0], near_parts[:-LATE])
    near_late = after((near_left, proj_sent, *far_parts[-LATE:]), *near_parts[-LATE:])
    near_right, first = completed(jnp.full((1,), number["begin"], jnp.int32), chunk_rows, near_left, near_right, near_late)
    far_all, *far_parts = after((first,), far_all, *far_parts)
    blocks = 4
    far = pl.pallas_call(
        functools.partial(whole_product_kernel, tuple(lows)),
        out_shape=jax.ShapeDtypeStruct((2, depth, 4 * width), BF16),
        in_specs=[ANY] * (5 + len(far_parts)),
        out_specs=VMEM,
        scratch_shapes=[
            pltpu.VMEM((2, 2 * steps, streams, depth), BF16),
            pltpu.VMEM((2, depth, 2 * steps * streams), BF16),
            pltpu.VMEM((blocks, 2 * steps, streams, 4 * width // blocks), BF16),
            pltpu.SemaphoreType.DMA((4,)),
            pltpu.SemaphoreType.DMA((blocks, 1 + len(far_parts))),
        ],
        compiler_params=params(28),
        cost_estimate=cost(0, 0),
        name="whole_product",
    )(*(in_hbm(x) for x in (feat_all, prev_all, feat_in[1], prev_in[1], far_all, *far_parts)))
    far = far.reshape(2, line, 2, share_rows, 4 * width)
    near = multiplied(near_left, near_right).reshape(2, line, 2, share_rows, 4 * width)

    def states_of(hidden, cell):
        both_hidden = trade(hidden, hidden)

        hidden_dirs = by_direction(*both_hidden)
        outputs = (inputs.astype(F32) + jnp.transpose(hidden_dirs, (0, 2, 1, 3)).astype(F32)).astype(BF16)
        last_h = jnp.stack([hidden_dirs[0, steps - 1], hidden_dirs[1, 0]], axis=1).astype(F32)
        final_h = jnp.zeros_like(state_h).at[stream_doc].set(last_h)
        last_c = jnp.transpose(cell.reshape(QUARTERS, HALVES, streams, width), (0, 2, 1, 3)).reshape(
            QUARTERS, streams, cells
        )
        last_dirs = by_direction(*trade(last_c[0], last_c[1]))
        final_c = jnp.zeros_like(state_c).at[stream_doc].set(jnp.transpose(last_dirs, (1, 0, 2)))
        return outputs, final_h, final_c

    tokens = {}

    def second(up, down):
        up, tokens["far"], tokens["dz"], tokens["proj"] = after((), up, far, dz_all, proj_y, free=5 * MIB)
        return up, up

    def beside_second(rise, fall):
        (sent,) = after((rise, fall), tokens["far"], free=5 * MIB)
        tokens["in"], tokens["rec"] = (with_partner(sent[i])[2] for i in range(2))
        tokens["proj"] = across_two(tokens["proj"])

    def third(up, down):
        dx = input_grad_of(tokens["dz"])
        up, down, tokens["dx"], in_sum, tokens["proj"], hidden, last_cell = after(
            (), up, down, dx, tokens["in"], tokens["proj"], hidden_all, cell, free=2 * MIB
        )
        tokens["in"] = across_two(in_sum)
        tokens["states"] = states_of(hidden, last_cell)
        return up, down

    def final(up, down):
        up, down, tokens["in"], rec_sum = after(
            tokens["states"], up, down, tokens["in"], tokens["rec"], free=2 * MIB
        )
        tokens["rec"] = across_two(rec_sum)
        return up, down

    gates = {2: second, 3: third, line: final} if line > 3 else {}
    hooks = {2: beside_second} if line > 3 else {}
    first = first.reshape(2, 2, share_rows, 4 * width) if chunk_rows else None
    near = line_sum(near, 1, 2, line, first, gates, hooks)
    dx_all, (outputs, final_h, final_c) = tokens["dx"], tokens["states"]
    in_two, rec_two, proj_two = tokens["in"], tokens["rec"], tokens["proj"]

    def halves_of(summed, name, pairs):
        return pick(summed, number[name], 1), swapped(pick(summed, number["not_" + name], 1), pairs)

    near_pair = halves_of(near, "low", near_swap)
    far_pair = halves_of(jnp.stack([in_two, rec_two]), "high", far_swap)
    far_pair = [lax.ppermute(x, "gate", swap) for x in far_pair]
    proj_mine, proj_theirs = halves_of(proj_two, "high", far_swap)
    grad_proj = proj_mine.astype(F32) + proj_theirs.astype(F32)
    grad_shape = (2, share_rows, 4, cells)
    grad_w_in, grad_w_rec = pl.pallas_call(
        assemble_kernel,
        out_shape=(jax.ShapeDtypeStruct(grad_shape, F32),) * 2,
        in_specs=[SMEM] + [VMEM] * 4,
        out_specs=[VMEM] * 2,
        compiler_params=params(14),
        name="assemble",
    )(jnp.stack([own, low, high]), *near_pair, *far_pair)

    def home(mine, theirs):
        return by_direction(*trade(mine, theirs)).astype(F32)

    own_cells = cells // n_batch
    shaped = jnp.transpose(grad_proj[:, share_rows:].reshape(QUARTERS, HALVES, 4, width), (0, 2, 1, 3))
    shaped = pick(shaped.reshape(QUARTERS, 4, n_batch, own_cells), number["spot"], 2)
    grad_bias = home(shaped[0], shaped[1])
    grad_proj = grad_proj[:, :share_rows].reshape(QUARTERS, HALVES, share_rows, width)
    grad_proj = jnp.transpose(grad_proj, (0, 1, 3, 2)).reshape(QUARTERS, cells, share_rows).astype(BF16)
    grad_proj = home(grad_proj[0], grad_proj[1])

    def columns(array, name, size):
        return lax.dynamic_slice_in_dim(array, number[name], size, 2, allow_negative_indices=False)

    dx_half = columns(dx_all, "cols", half_cols)
    dx_sent = columns(dx_all, "other_cols", half_cols).astype(BF16)
    dx_half = dx_half + lax.ppermute(dx_sent, "gate", across).astype(F32)
    dx_half = (dx_half + columns(ups, "cols", half_cols).astype(F32)).astype(BF16)
    dx_half = dx_half.reshape(steps, streams, 2, quarter_cols)
    dx_dirs = by_direction(*trade(pick(dx_half, own, 2), pick(dx_half, number["other"], 2)))
    input_grad = jnp.transpose(dx_dirs, (0, 2, 1, 3))
    return (outputs, input_grad, grad_w_in, grad_w_rec, grad_bias, grad_proj, final_h, final_c)


def solution(mesh):
    placed = (
        P(None, "batch", None, None),
        P(None, None, None, "gate"),
        P(None, None, None, "gate"),
        P(None, None, "gate"),
        P(None, "gate", None),
        P("batch", None, None),
        P("batch", None, "gate"),
        P("batch", None),
        P("batch"),
        P(None, "batch", None, None),
    )
    return jax.shard_map(
        body,
        mesh=mesh,
        in_specs=placed,
        out_specs=(
            P(None, "batch", None, None),
            P(None, "batch", None, "gate"),
            P(None, "batch", None, "gate"),
            P(None, "batch", None, "gate"),
            P(None, None, ("gate", "batch")),
            P(None, "gate", "batch"),
            P("batch", None, None),
            P("batch", None, "gate"),
        ),
        check_vma=False,
    )
```

```python
import functools

import jax
import jax.numpy as jnp
from jax import lax
from jax.experimental import pallas as pl
from jax.experimental.pallas import tpu as pltpu
from jax.sharding import PartitionSpec as P

CLIP = 3.0
F32, BF16 = jnp.float32, jnp.bfloat16
QUARTERS, HALVES = 2, 2
PIECES = QUARTERS * HALVES
MIB = 2**20
LATE = 2
SHARES = (0.35, 0.3, 0.15, 0.1, 0.1)

VMEM = pl.BlockSpec(memory_space=pltpu.VMEM)
SMEM = pl.BlockSpec(memory_space=pltpu.SMEM)
ANY = pl.BlockSpec(memory_space=pl.ANY)


def pinned(array):
    return pltpu.with_memory_space_constraint(array, pltpu.VMEM)


def in_hbm(array):
    return pltpu.with_memory_space_constraint(array, pltpu.HBM)


def dot(left, right):
    return jnp.dot(left, right, preferred_element_type=F32)


def layout_kernel(keep, spread, which_ref, w_ref, *refs):
    buf, sems, out_sems = refs[-3:]
    out_ref = refs[0] if keep else refs[1]
    all_ref = refs[1] if keep else refs[0]
    depth, ahead, part = w_ref.shape[1], buf.shape[0], buf.shape[1]
    count = depth // part

    def fetch(i):
        return pltpu.make_async_copy(w_ref.at[which_ref[0], pl.ds(i * part, part)], buf.at[i % ahead], sems.at[i % ahead])

    def store(i):
        rows = pl.ds(i * part, part)
        return pltpu.make_async_copy(out_ref.at[:, rows], all_ref.at[:, rows], out_sems.at[i])

    for i in range(min(ahead - 1, count)):
        fetch(i).start()
    for i in range(count):
        if i + ahead - 1 < count:
            fetch(i + ahead - 1).start()
        fetch(i).wait()
        out_ref[:, i * part : (i + 1) * part, :] = jnp.swapaxes(buf[i % ahead], 0, 1)
        if spread:
            store(i).start()
    for i in range(count if spread else 0):
        store(i).wait()


def turned_kernel(wa_ref, wb_ref, pa_ref, pb_ref, wat_ref, wbt_ref, pat_ref, pbt_ref):
    for w_ref, out_ref in ((wa_ref, wat_ref), (wb_ref, wbt_ref)):
        for gate in range(4):
            for half in range(HALVES):
                width = w_ref.shape[2] // HALVES
                cols = slice(half * width, (half + 1) * width)
                out_ref[gate, cols, :] = w_ref[gate, :, cols].T
    pat_ref[...] = pa_ref[...].T
    pbt_ref[...] = pb_ref[...].T


def pass_kernel(*refs):
    pass


def after(tokens, *arrays, free=0):
    count = len(tokens)
    return pl.pallas_call(
        pass_kernel,
        out_shape=tuple(jax.ShapeDtypeStruct(x.shape, x.dtype) for x in arrays),
        in_specs=[ANY] * (count + len(arrays)),
        out_specs=[ANY] * len(arrays),
        input_output_aliases={count + i: i for i in range(len(arrays))},
        compiler_params=params(1),
        name="after",
    )(*tokens, *(in_hbm(x) if x.size * x.dtype.itemsize > free else x for x in arrays))


def gather_kernel(lows, *refs):
    (feat_ref, prev_ref, feat_too, prev_too, kept_ref), refs = refs[:5], refs[5:]
    groups, (left_ref, right_ref, sems) = refs[:-3], refs[-3:]
    steps, _, depth = feat_ref.shape
    jobs = [
        (feat_ref, left_ref.at[:steps, :, :depth]),
        (prev_ref, left_ref.at[:steps, :, depth:]),
        (feat_too, left_ref.at[steps:, :, :depth]),
        (prev_too, left_ref.at[steps:, :, depth:]),
        (kept_ref, right_ref.at[:steps]),
    ]
    jobs += [(x, right_ref.at[steps + low : steps + low + x.shape[0]]) for x, low in zip(groups, lows)]
    copies = [pltpu.make_async_copy(a, b, sems.at[i]) for i, (a, b) in enumerate(jobs)]
    for copy in copies:
        copy.start()
    for copy in copies:
        copy.wait()


def late_kernel(lows, begin_ref, left_ref, right_in, *refs):
    groups, (right_ref, first_ref, sems) = refs[:-3], refs[-3:]
    steps = left_ref.shape[0] // 2
    copies = [
        pltpu.make_async_copy(x, right_ref.at[steps + low : steps + low + x.shape[0]], sems.at[i])
        for i, (x, low) in enumerate(zip(groups, lows))
    ]
    for copy in copies:
        copy.start()
    for copy in copies:
        copy.wait()
    if first_ref.shape[1] % 128:
        return
    share, depth = first_ref.shape[1], left_ref.shape[2] // 2
    rows = left_ref.shape[0] * left_ref.shape[1]
    left = [
        left_ref[:, :, pl.ds(pl.multiple_of(i * depth + begin_ref[0] * share, 128), share)].reshape(rows, share)
        for i in range(2)
    ]
    left = jnp.concatenate([x.T for x in left], axis=0)
    width = right_ref.shape[2] // 4

    def columns(i, _):
        cols = pl.ds(pl.multiple_of(i * width, width), width)
        total = dot(left, right_ref[:, :, cols].reshape(rows, width)).astype(BF16)
        first_ref[0, :, cols] = total[:share]
        first_ref[1, :, cols] = total[share:]
        return 0

    lax.fori_loop(0, 4, columns, 0)


def product_kernel(left_ref, right_ref, out_ref):
    rows, depth = left_ref.shape[0] * left_ref.shape[1], left_ref.shape[2] // 2
    width = right_ref.shape[2] // 4
    for which in range(2):
        left = left_ref[:, :, which * depth : (which + 1) * depth].reshape(rows, depth).T

        def columns(i, _):
            cols = pl.ds(pl.multiple_of(i * width, width), width)
            out_ref[which, :, cols] = dot(left, right_ref[:, :, cols].reshape(rows, width)).astype(BF16)
            return 0

        lax.fori_loop(0, 4, columns, 0)


def whole_product_kernel(lows, mine_ref, theirs_ref, kept_ref, *refs):
    groups, (out_ref, left_buf, turned_buf, right_buf, left_sems, sems) = refs[:-6], refs[-6:]
    steps, streams, depth = mine_ref.shape
    blocks = right_buf.shape[0]
    width = right_buf.shape[3]
    rows = 2 * steps * streams

    def fetches_of(block):
        cols = slice(block * width, (block + 1) * width)
        jobs = [(kept_ref.at[:, :, cols], right_buf.at[block, :steps])]
        jobs += [
            (x.at[:, :, cols], right_buf.at[block, steps + low : steps + low + x.shape[0]])
            for x, low in zip(groups, lows)
        ]
        return [pltpu.make_async_copy(a, b, sems.at[block, i]) for i, (a, b) in enumerate(jobs)]

    lefts = [
        pltpu.make_async_copy(mine_ref, left_buf.at[:steps], left_sems.at[0]),
        pltpu.make_async_copy(theirs_ref, left_buf.at[steps:], left_sems.at[1]),
    ]
    for copy in lefts:
        copy.start()
    for block in range(blocks):
        for copy in fetches_of(block):
            copy.start()
    for copy in lefts:
        copy.wait()
    turned_buf[...] = left_buf[...].reshape(rows, depth).T
    for block in range(blocks):
        for copy in fetches_of(block):
            copy.wait()
        total = dot(turned_buf[...], right_buf[block].reshape(rows, width))
        out_ref[:, block * width : (block + 1) * width] = total.astype(BF16)


def assemble_kernel(place_ref, near_a, near_b, in_a, in_b, rec_a, rec_b, in_ref, rec_ref):
    own, low, high = place_ref[0], place_ref[1], place_ref[2]
    width = in_ref.shape[3] // HALVES
    jobs = [
        (own, near_a, near_b, 0, low, in_ref),
        (own, near_a, near_b, 1, low, rec_ref),
        (1 - own, in_a, in_b, 0, high, in_ref),
        (1 - own, rec_a, rec_b, 0, high, rec_ref),
    ]
    for direction, mine_ref, theirs_ref, which, index, out_ref in jobs:
        mine, theirs = mine_ref[which].astype(F32), theirs_ref[which].astype(F32)
        for half in range(HALVES):
            whole = jnp.where(index == half, mine, theirs)
            gates = jnp.stack([whole[:, gate * width : (gate + 1) * width] for gate in range(4)])
            out_ref[direction, :, :, half * width : (half + 1) * width] = jnp.swapaxes(gates, 0, 1)


def order_kernel(step_ref, feat_ref, out_ref, all_ref, sems):
    copies = []
    for i in range(feat_ref.shape[0]):
        source = feat_ref.at[step_ref[0] + step_ref[1] * i]
        copies.append(pltpu.make_async_copy(source, out_ref.at[i], sems.at[2 * i]))
        copies.append(pltpu.make_async_copy(source, all_ref.at[i], sems.at[2 * i + 1]))
    for copy in copies:
        copy.start()
    for copy in copies:
        copy.wait()


def numbers_kernel(index, in_ref, out_ref):
    out_ref[0] = in_ref[index]


def bias_kernel(sum_ref, out_ref):
    width = sum_ref.shape[2] // 4
    for piece in range(PIECES):
        for gate in range(4):
            out_ref[piece, gate : gate + 1, :] = jnp.sum(
                sum_ref[piece, :, gate * width : (gate + 1) * width], axis=0, keepdims=True
            )


def pieces(refs, axis):
    for piece in range(PIECES):
        quarter, half = divmod(piece, HALVES)
        width = refs[0].shape[axis] // HALVES
        yield piece, quarter, width, slice(half * width, (half + 1) * width)


def forward_kernel(
    first, step_ref, p_ref, q_ref, start_ref, keep_ref, cell_ref, inflow_ref, wa_ref, wb_ref, pa_ref, pb_ref,
    part_ref, next_ref, gates_ref, mixed_ref, prev_ref, hidden_ref, slope_ref,
):
    keep = keep_ref[step_ref[1]][:, :1]
    if first:
        hidden = start_ref[...]
    else:
        hidden = clipped(p_ref, q_ref, hidden_ref, slope_ref)
    hidden = hidden * keep.astype(BF16)
    prev_ref[...] = hidden
    part = jnp.zeros(part_ref.shape, F32)
    for piece, quarter, width, cols in pieces((wa_ref, wb_ref), 2):
        w_ref, proj_ref = ((wa_ref, pa_ref), (wb_ref, pb_ref))[quarter]
        acts = []
        for gate in range(4):
            place = slice(gate * width, (gate + 1) * width)
            pre = dot(hidden, w_ref[gate, :, cols]) + inflow_ref[piece, :, place]
            act = jnp.tanh(pre if gate == 2 else 0.5 * pre)
            gates_ref[piece, :, place] = act.astype(BF16)
            acts.append(act if gate == 2 else 0.5 + 0.5 * act)
        ingate, forget, candidate, outgate = acts
        cell = CLIP * jnp.tanh((forget * (keep * cell_ref[piece]) + ingate * candidate) * (1.0 / CLIP))
        next_ref[piece] = cell
        mixed = (outgate * jnp.tanh(cell)).astype(BF16)
        mixed_ref[piece] = mixed
        part = part + dot(mixed, proj_ref[cols, :])
    part_ref[...] = part.astype(BF16)


def clipped(p_ref, q_ref, hidden_ref, slope_ref):
    squash = jnp.tanh((p_ref[...].astype(F32) + q_ref[...].astype(F32)) * (1.0 / CLIP))
    hidden = (CLIP * squash).astype(BF16)
    hidden_ref[...] = hidden
    slope_ref[...] = 1.0 - squash * squash
    return hidden


def between_kernel(
    first, last, passed, step_ref, feat_ref, ba_ref, bb_ref, wa_ref, wb_ref, cell_ref, gates_ref, mixed_ref, prev_ref, hidden_ref,
    slope_ref, *refs,
):
    refs = refs[(0 if first else 6) + passed :]
    out_ref, gates_all, cells_all, mixed_all, prev_all, hidden_all, slope_all = refs[:7]
    sems = refs[-1]
    step, time_before = step_ref[0], step_ref[2]
    copies = [pltpu.make_async_copy(gates_ref.at[i], gates_all.at[i, step], sems.at[i]) for i in range(PIECES)]
    copies += [
        pltpu.make_async_copy(mixed_ref.at[i], mixed_all.at[i, step], sems.at[PIECES + i]) for i in range(PIECES)
    ]
    copies.append(pltpu.make_async_copy(cell_ref, cells_all.at[step], sems.at[2 * PIECES]))
    copies.append(pltpu.make_async_copy(prev_ref, prev_all.at[step], sems.at[2 * PIECES + 1]))
    if not first:
        copies.append(pltpu.make_async_copy(hidden_ref, hidden_all.at[time_before], sems.at[2 * PIECES + 2]))
        copies.append(pltpu.make_async_copy(slope_ref, slope_all.at[step - 1], sems.at[2 * PIECES + 3]))
    for copy in copies:
        copy.start()
    if not last:
        inflow_into(feat_ref[step + 1], ba_ref, bb_ref, wa_ref, wb_ref, out_ref)
    for copy in copies:
        copy.wait()


def inflow_into(feat, ba_ref, bb_ref, wa_ref, wb_ref, out_ref, quarters=(0, 1)):
    for piece, quarter, width, cols in pieces((wa_ref, wb_ref), 2):
        if quarter not in quarters:
            continue
        w_ref, bias_ref = ((wa_ref, ba_ref), (wb_ref, bb_ref))[quarter]
        for gate in range(4):
            place = slice(gate * width, (gate + 1) * width)
            out_ref[piece, :, place] = dot(feat, w_ref[gate, :, cols]) + bias_ref[gate : gate + 1, cols]


def begin_kernel(which_ref, feat_ref, wa_ref, proj_ref, *refs):
    sems = refs[-1]
    out_ref, pa_ref, *placed = refs[-11:-1]
    copies = [pltpu.make_async_copy(x, y, sems.at[i]) for i, (x, y) in enumerate(zip(refs[:-11], placed))]
    copies.append(pltpu.make_async_copy(proj_ref.at[which_ref[0]], pa_ref, sems.at[len(copies)]))
    for copy in copies:
        copy.start()
    ba_ref, bb_ref, wb_ref = placed[:3]
    copies[0].wait()
    inflow_into(feat_ref[0], ba_ref, bb_ref, wa_ref, wb_ref, out_ref, (0,))
    copies[1].wait()
    copies[2].wait()
    inflow_into(feat_ref[0], ba_ref, bb_ref, wa_ref, wb_ref, out_ref, (1,))
    for copy in copies[3:]:
        copy.wait()


def backward_kernel(
    step_ref, p_ref, q_ref, keep_ref, grad_ref, bias_ref, wa_ref, wb_ref, pa_ref, pb_ref,
    gates_ref, cell_ref, prev_ref, slope_ref, up_ref, start_ref,
    part_ref, next_ref, sum_ref, raw_ref, dz_ref,
):
    step = step_ref[0]
    keep = keep_ref[step_ref[1]][:, :1]
    raw = (up_ref[...].astype(F32) + (p_ref[...].astype(F32) + q_ref[...].astype(F32))) * slope_ref[...]
    raw = raw.astype(BF16)
    raw_ref[...] = raw
    part = jnp.zeros(part_ref.shape, F32)
    for piece, quarter, width, cols in pieces((wa_ref, wb_ref), 1):
        w_ref, proj_ref = ((wa_ref, pa_ref), (wb_ref, pb_ref))[quarter]
        mixed = dot(raw, proj_ref[:, cols])
        acts = [gates_ref[piece, :, gate * width : (gate + 1) * width].astype(F32) for gate in range(4)]
        ingate, forget, outgate = (0.5 + 0.5 * acts[gate] for gate in (0, 1, 3))
        slopes = [1.0 - act * act for act in acts]
        cell = cell_ref[piece]
        prev = keep * jnp.where(step == 0, start_ref[piece], prev_ref[piece])
        squash = jnp.tanh(cell)
        total = grad_ref[piece] + mixed * outgate * (1.0 - squash * squash)
        inner = total * (1.0 - (cell * (1.0 / CLIP)) * (cell * (1.0 / CLIP)))
        next_ref[piece] = keep * inner * forget
        quart = 0.25 * inner
        pre_grads = (
            quart * acts[2] * slopes[0],
            quart * prev * slopes[1],
            inner * ingate * slopes[2],
            0.25 * mixed * squash * slopes[3],
        )
        for gate in range(4):
            low = pre_grads[gate].astype(BF16)
            place = slice(gate * width, (gate + 1) * width)
            dz_ref[piece, :, place] = low
            rows = pre_grads[gate].reshape(-1, 8, width)
            sum_ref[piece, :, place] = bias_ref[piece, :, place] + jnp.sum(rows, axis=0)
            part = part + dot(low, w_ref[gate, cols, :])
    part_ref[...] = (part * keep).astype(BF16)


def finish_kernel(
    step_ref, p_ref, q_ref, mixed_ref, prev_ref, hidden_ref, before_ref, ups_all, mixed_in, prev_in, hidden_in, slope_in,
    slope_ref, up_ref, mixed_all, prev_all, hidden_all, slope_all, hidden_buf, sems,
):
    step, time, time_before = step_ref[0], step_ref[1], step_ref[2]
    jobs = [(mixed_ref.at[i], mixed_all.at[i, step]) for i in range(PIECES)]
    jobs += [
        (ups_all.at[time], up_ref),
        (prev_ref, prev_all.at[step]),
        (hidden_ref, hidden_all.at[time_before]),
        (before_ref, slope_all.at[step - 1]),
        (hidden_buf, hidden_all.at[time]),
    ]
    copies = [pltpu.make_async_copy(x, y, sems.at[i]) for i, (x, y) in enumerate(jobs)]
    for copy in copies[:-1]:
        copy.start()
    clipped(p_ref, q_ref, hidden_buf, slope_ref)
    copies[-1].start()
    for copy in copies:
        copy.wait()


def fetches(step, time, sources, targets, sems):
    gates_all, cells_all, ups_all = sources
    gates_ref, cell_ref, prev_ref, up_ref = targets
    before = jnp.maximum(step - 1, 0)
    return [
        pltpu.make_async_copy(gates_all.at[i, step], gates_ref.at[i], sems.at[i]) for i in range(PIECES)
    ] + [
        pltpu.make_async_copy(cells_all.at[step], cell_ref, sems.at[PIECES]),
        pltpu.make_async_copy(cells_all.at[before], prev_ref, sems.at[PIECES + 1]),
        pltpu.make_async_copy(ups_all.at[time], up_ref, sems.at[PIECES + 2]),
    ]


def aside_kernel(
    first, last, opens, passed, step_ref, dz_ref, raw_ref, gates_all, cells_all, ups_all, slope_all, *refs
):
    refs = refs[(0 if first else 4) + (0 if opens else 2) + passed :]
    gates_ref, cell_ref, prev_ref, slope_ref, up_ref = refs[:5]
    dz_all, raw_all, near_all, far_all, near_out, far_out = refs[5:11]
    sems, fetch_sems = refs[-2:]
    step, time_before = step_ref[0], step_ref[2]
    slot, low, high = step_ref[4], step_ref[5], step_ref[6]
    before = jnp.maximum(step - 1, 0)
    copies = []
    if not last:
        copies += fetches(
            before, time_before, (gates_all, cells_all, ups_all), (gates_ref, cell_ref, prev_ref, up_ref), fetch_sems
        )
        copies.append(pltpu.make_async_copy(slope_all.at[before], slope_ref, fetch_sems.at[PIECES + 3]))
    copies += [pltpu.make_async_copy(dz_ref.at[i], dz_all.at[i, step], sems.at[i]) for i in range(PIECES)]
    copies.append(pltpu.make_async_copy(raw_ref, raw_all.at[step], sems.at[PIECES]))
    copies.append(pltpu.make_async_copy(dz_ref.at[low], near_all.at[step], sems.at[PIECES + 1]))
    copies.append(pltpu.make_async_copy(dz_ref.at[HALVES + high], far_all.at[step], sems.at[PIECES + 2]))
    copies.append(pltpu.make_async_copy(dz_ref.at[1 - low], near_out.at[slot], sems.at[PIECES + 3]))
    copies.append(pltpu.make_async_copy(dz_ref.at[HALVES + 1 - high], far_out.at[slot], sems.at[PIECES + 4]))
    for copy in copies:
        copy.start()
    for copy in copies:
        copy.wait()


def input_grad_kernel(step_ref, dz_ref, wa_ref, wb_ref, out_ref, acc_ref):
    piece, gate = pl.program_id(0), pl.program_id(1)
    steps, streams, width = dz_ref.shape[1:]

    @pl.when((piece == 0) & (gate == 0))
    def _():
        acc_ref[...] = jnp.zeros(acc_ref.shape, F32)

    weights = jnp.where(piece < HALVES, wa_ref[0], wb_ref[0])
    acc_ref[...] += lax.dot_general(
        dz_ref[0].reshape(steps * streams, width), weights, (((1,), (1,)), ((), ())), preferred_element_type=F32
    )

    @pl.when((piece == PIECES - 1) & (gate == 3))
    def _():
        for step in range(steps):
            time = step_ref[0] + step_ref[1] * step
            out_ref[time] = acc_ref[step * streams : (step + 1) * streams, :]


def params(mib):
    return pltpu.CompilerParams(vmem_limit_bytes=mib * MIB)


def cost(flops, size):
    return pl.CostEstimate(flops=flops, bytes_accessed=size, transcendentals=0)


def body(inputs, w_in, w_rec, bias, proj, state_h, state_c, resets, stream_doc, cotangent):
    streams, steps, depth = inputs.shape[1:]
    cells = w_in.shape[3]
    width = cells // HALVES
    n_batch = lax.axis_size("batch")
    gates_size = lax.axis_size("gate")
    line = n_batch // 2
    swap = [(i, i ^ 1) for i in range(gates_size)]
    across = [(i, i ^ 2) for i in range(gates_size)]
    near_swap = [(i, i ^ 1) for i in range(n_batch)]
    far_swap = [(i, i ^ 2) for i in range(n_batch)]

    rank, spot = lax.axis_index("gate"), lax.axis_index("batch")
    half_cols, quarter_cols = depth // 2, depth // 4
    place_numbers = {
        "own": rank % 2,
        "other": 1 - rank % 2,
        "low": spot % 2,
        "not_low": 1 - spot % 2,
        "high": (spot // 2) % 2,
        "not_high": 1 - (spot // 2) % 2,
        "spot": spot,
        "begin": jnp.where(spot // 2 == 0, line - 1, 0),
        "cols": (rank // 2) * half_cols,
        "other_cols": (1 - rank // 2) * half_cols,
    }
    for stride, count in {(2, line), (4, line // 2)}:
        here = (spot // stride) % count
        place_numbers[stride, "here"] = here
        place_numbers[stride, "not_here"] = jnp.maximum(1 - here, 0)
        for slot in range(2, count):
            place_numbers[stride, "rise", slot] = jnp.minimum(here + count - slot, count - 1)
            place_numbers[stride, "fall", slot] = jnp.maximum(here - count + slot, 0)
        if count > 2:
            place_numbers[stride, "begin"] = jnp.where(here == 0, count - 1, 0)
    names = sorted(place_numbers, key=str)
    which = pl.pallas_call(
        functools.partial(numbers_kernel, names.index("own")),
        out_shape=jax.ShapeDtypeStruct((1,), jnp.int32),
        in_specs=[SMEM],
        out_specs=SMEM,
        name="numbers",
    )(jnp.stack([place_numbers[x] for x in names]).astype(jnp.int32))
    number = {x: place_numbers[x].astype(jnp.int32) for x in names}
    own, low, high = number["own"], number["low"], number["high"]

    def pick(stacked, index, axis=0):
        return lax.dynamic_index_in_dim(stacked, index, axis, keepdims=False, allow_negative_indices=False)

    def trade(mine, theirs):
        return (mine, lax.ppermute(theirs, "gate", swap))

    def vmem(shape, dtype):
        return pltpu.VMEM(shape, dtype)

    def hbm(shape, dtype):
        return pltpu.HBM(shape, dtype)

    def by_gate(weights, index, keep, spread):
        shape = (4,) + weights.shape[1:2] + weights.shape[3:]
        count = 16
        kept, spreads = (vmem(shape, BF16),) * keep, (hbm(shape, BF16),) * spread
        return pl.pallas_call(
            functools.partial(layout_kernel, keep, spread),
            out_shape=kept + spreads,
            in_specs=[SMEM, ANY],
            out_specs=[VMEM] * keep + [ANY] * spread,
            scratch_shapes=[pltpu.VMEM(shape, BF16)] * (1 - keep)
            + [
                pltpu.VMEM((4, weights.shape[1] // count) + weights.shape[2:], BF16),
                pltpu.SemaphoreType.DMA((4,)),
                pltpu.SemaphoreType.DMA((count,)),
            ],
            compiler_params=params(8),
            name="layout",
        )(index, in_hbm(weights))

    away = jnp.full((1,), number["other"], jnp.int32)
    win_b, rec_b = (lax.ppermute(by_gate(w, away, False, True)[0], "gate", swap) for w in (w_in, w_rec))
    (win_av, win_a), (rec_av,) = by_gate(w_in, which, True, True), by_gate(w_rec, which, True, False)
    proj_b = lax.ppermute(pick(proj, number["other"]), "gate", swap)
    bias_a, bias_b = trade(pick(bias, own), pick(bias, number["other"]))

    def cells_to_pieces(pair):
        both = jnp.stack(pair).reshape(QUARTERS, streams, HALVES, width)
        return jnp.transpose(both, (0, 2, 1, 3)).reshape(PIECES, streams, width)

    def by_time(stacked):
        return jnp.transpose(pick(stacked, own), (1, 0, 2))

    feats = by_time(inputs)
    ups = by_time(cotangent)
    flags = resets.astype(F32)
    later = jnp.concatenate([flags[:, 1:], jnp.zeros_like(flags[:, :1])], axis=1)
    keep = 1.0 - jnp.where(own == 0, flags, later)
    keep = jnp.broadcast_to(jnp.transpose(keep)[:, :, None], (steps, streams, 128))

    docs_h = state_h[stream_doc]
    docs_c = state_c[stream_doc]
    start_h = pick(jnp.transpose(docs_h, (1, 0, 2)), own).astype(BF16)
    by_dir_c = jnp.transpose(docs_c, (1, 0, 2))
    start_c = cells_to_pieces(trade(pick(by_dir_c, own), pick(by_dir_c, number["other"])))

    def at_step(step):
        near = jnp.array([step, step, max(step - 1, 0), min(step + 1, steps - 1)], jnp.int32)
        turned = jnp.array([step] + [steps - 1 - x for x in (step, max(step - 1, 0), min(step + 1, steps - 1))], jnp.int32)
        return jnp.where(own == 0, near, turned)

    def swapped(array, pairs):
        return lax.ppermute(array, "batch", pairs)

    turn = jnp.where(own == 0, jnp.array([0, 1], jnp.int32), jnp.array([steps - 1, -1], jnp.int32))
    feats_v, feat_all = pl.pallas_call(
        order_kernel,
        out_shape=(vmem(feats.shape, BF16), hbm(feats.shape, BF16)),
        in_specs=[SMEM, ANY],
        out_specs=[VMEM, ANY],
        scratch_shapes=[pltpu.SemaphoreType.DMA((2 * steps,))],
        compiler_params=params(1),
        name="order",
    )(turn, feats)
    gates_shape, cell_shape = (PIECES, streams, 4 * width), (PIECES, streams, width)
    bias_shape = (PIECES, 8, 4 * width)
    sources = (bias_a.astype(F32), bias_b.astype(F32), in_hbm(win_b), in_hbm(rec_b), in_hbm(proj_b), keep, start_h, start_c)
    inflow, proj_av, bias_av, bias_bv, win_bv, rec_bv, proj_bv, keep_v, start_hv, start_cv = pl.pallas_call(
        begin_kernel,
        out_shape=(vmem(gates_shape, F32), vmem((cells, depth), BF16)) + tuple(vmem(x.shape, x.dtype) for x in sources),
        in_specs=[SMEM, VMEM, VMEM] + [ANY] * (1 + len(sources)),
        out_specs=[VMEM] * (2 + len(sources)),
        scratch_shapes=[pltpu.SemaphoreType.DMA((1 + len(sources),))],
        compiler_params=params(8),
        name="begin",
    )(which, pinned(feats_v), pinned(win_av), in_hbm(proj), *sources)

    def forward_call(first, step, part, peer, cell, inflow):
        return pl.pallas_call(
            functools.partial(forward_kernel, first),
            out_shape=(
                vmem((streams, depth), BF16),
                vmem(cell_shape, F32),
                vmem(gates_shape, BF16),
                vmem(cell_shape, BF16),
                vmem((streams, depth), BF16),
                vmem((streams, depth), BF16),
                vmem((streams, depth), F32),
            ),
            in_specs=[SMEM] + [VMEM] * 10,
            out_specs=[VMEM] * 7,
            compiler_params=params(8),
            name="forward_step",
        )(
            at_step(step), pinned(part), pinned(peer), pinned(start_hv), pinned(keep_v), pinned(cell), pinned(inflow),
            pinned(rec_av), pinned(rec_bv), pinned(proj_av), pinned(proj_bv),
        )

    def between_call(step, fresh, stacks, passing=()):
        shapes = (
            hbm((PIECES, steps, streams, 4 * width), BF16),
            hbm((steps,) + cell_shape, F32),
            hbm((PIECES, steps, streams, width), BF16),
            hbm((steps, streams, depth), BF16),
            hbm((steps, streams, depth), BF16),
            hbm((steps, streams, depth), F32),
        )
        aliases = {12 + i: 1 + i for i in range(len(stacks))}
        aliases.update({12 + len(stacks) + i: 7 + i for i in range(len(passing))})
        inflow, *out = pl.pallas_call(
            functools.partial(between_kernel, not stacks, step == steps - 1, len(passing)),
            out_shape=(vmem(gates_shape, F32),) + shapes + tuple(hbm(x.shape, x.dtype) for x in passing),
            in_specs=[SMEM] + [VMEM] * 11 + [ANY] * (len(stacks) + len(passing)),
            out_specs=[VMEM] + [ANY] * (6 + len(passing)),
            scratch_shapes=[pltpu.SemaphoreType.DMA((2 * PIECES + 4,))],
            input_output_aliases=aliases,
            compiler_params=params(8),
            cost_estimate=cost(2 * streams * depth * 8 * cells, 8 * depth * cells * 2),
            name="between",
        )(
            at_step(step), pinned(feats_v), pinned(bias_av), pinned(bias_bv), pinned(win_av), pinned(win_bv),
            *(pinned(x) for x in fresh), *(in_hbm(x) for x in (*stacks, *passing)),
        )
        return inflow, tuple(out[:6]), tuple(out[6:])

    none = jnp.zeros((streams, depth), BF16)
    part, peer, cell, stacks = none, none, start_cv, ()
    for step in range(steps):
        cell_before = cell
        part, cell, *fresh = forward_call(step == 0, step, part, peer, cell, inflow)
        peer = lax.ppermute(part, "gate", across)
        if step == steps - 1:
            break
        if step == 2:
            (feat_all,) = after((part,), feat_all)
            feat_in = (swapped(feat_all, near_swap), swapped(feat_all, far_swap))
        due = step == (3 * steps) // 4
        inflow, stacks, passed = between_call(step, (cell, *fresh), stacks, feat_in if due else ())
        feat_in = passed if due else (feat_in if step >= 2 else None)
    gates, mixed, prev, hidden, slope = fresh
    gates_all, cells_all, mixed_all, prev_all, hidden_all, slope_all = stacks

    slope_now, up_now, mixed_all, prev_all, hidden_all, slope_all = pl.pallas_call(
        finish_kernel,
        out_shape=(vmem((streams, depth), F32), vmem((streams, depth), BF16))
        + tuple(hbm(x.shape, x.dtype) for x in (mixed_all, prev_all, hidden_all, slope_all)),
        in_specs=[SMEM] + [VMEM] * 6 + [ANY] * 5,
        out_specs=[VMEM] * 2 + [ANY] * 4,
        scratch_shapes=[pltpu.VMEM((streams, depth), BF16), pltpu.SemaphoreType.DMA((PIECES + 5,))],
        input_output_aliases={8 + i: 2 + i for i in range(4)},
        compiler_params=params(8),
        name="finish",
    )(
        at_step(steps - 1), pinned(part), pinned(peer), *(pinned(x) for x in (mixed, prev, hidden, slope)), in_hbm(ups),
        *(in_hbm(x) for x in (mixed_all, prev_all, hidden_all, slope_all)),
    )
    saved = (gates, cell, cell_before, slope_now, up_now)
    saved_shapes = (
        vmem(gates_shape, BF16),
        vmem(cell_shape, F32),
        vmem(cell_shape, F32),
        vmem((streams, depth), F32),
        vmem((streams, depth), BF16),
    )

    rec_atv, rec_btv, proj_atv, proj_btv = pl.pallas_call(
        turned_kernel,
        out_shape=(vmem((4, cells, depth), BF16),) * 2 + (vmem((depth, cells), BF16),) * 2,
        in_specs=[VMEM] * 4,
        out_specs=[VMEM] * 4,
        compiler_params=params(8),
        name="turned",
    )(pinned(rec_av), pinned(rec_bv), pinned(proj_av), pinned(proj_bv))

    def backward_call(step, part, peer, grad, bias, saved):
        return pl.pallas_call(
            backward_kernel,
            out_shape=(
                vmem((streams, depth), BF16),
                vmem(cell_shape, F32),
                vmem(bias_shape, F32),
                vmem((streams, depth), BF16),
                vmem(gates_shape, BF16),
            ),
            in_specs=[SMEM] + [VMEM] * 15,
            out_specs=[VMEM] * 5,
            compiler_params=params(8),
            name="backward_step",
        )(
            at_step(step), pinned(part), pinned(peer), pinned(keep_v), pinned(grad), pinned(bias),
            pinned(rec_atv), pinned(rec_btv), pinned(proj_atv), pinned(proj_btv),
            *(pinned(x) for x in saved), pinned(start_cv),
        )

    def aside_call(step, slot, slots, dz, raw, stacks, sends, passing):
        piece_shape = (streams, 4 * width)
        shapes = (
            hbm((PIECES, steps) + piece_shape, BF16),
            hbm((steps, streams, depth), BF16),
            hbm((steps,) + piece_shape, BF16),
            hbm((steps,) + piece_shape, BF16),
            hbm((slots,) + piece_shape, BF16),
            hbm((slots,) + piece_shape, BF16),
        )
        kept = len(stacks)
        aliases = {7 + i: 5 + i for i in range(kept)}
        aliases.update({7 + kept + i: 9 + i for i in range(len(sends))})
        aliases.update({7 + kept + len(sends) + i: 11 + i for i in range(len(passing))})
        out = pl.pallas_call(
            functools.partial(aside_kernel, not stacks, step == 0, not sends, len(passing)),
            out_shape=saved_shapes + shapes + tuple(hbm(x.shape, x.dtype) for x in passing),
            in_specs=[SMEM] + [VMEM] * 2 + [ANY] * (4 + kept + len(sends) + len(passing)),
            out_specs=[VMEM] * 5 + [ANY] * (6 + len(passing)),
            scratch_shapes=[
                pltpu.SemaphoreType.DMA((PIECES + 5,)),
                pltpu.SemaphoreType.DMA((PIECES + 4,)),
            ],
            input_output_aliases=aliases,
            compiler_params=params(8),
            cost_estimate=cost(0, 8 * MIB),
            name="aside",
        )(
            jnp.concatenate([at_step(step), jnp.stack([jnp.int32(slot), low, high])]), pinned(dz), pinned(raw),
            in_hbm(gates_all), in_hbm(cells_all), in_hbm(ups), in_hbm(slope_all),
            *(in_hbm(x) for x in (*stacks, *sends, *passing)),
        )
        return out[:5], tuple(out[5:9]), tuple(out[9:11]), tuple(out[11:])

    carry = (none, none, jnp.zeros(cell_shape, F32), jnp.zeros(bias_shape, F32), saved, ())
    pending, arrived, ready, top = [], [], None, steps
    for index, share in enumerate(SHARES):
        slots = top if index == len(SHARES) - 1 else round(share * steps)
        sends = ()
        for step in range(top - 1, top - slots - 1, -1):
            part, peer, grad, bias_sum, saved, stacks = carry
            part, grad, bias_sum, raw, dz = backward_call(step, part, peer, grad, bias_sum, saved)
            peer = lax.ppermute(part, "gate", across)
            if step == steps - 1:
                (prev_all,) = after((part,), prev_all)
                pending.append((step - steps // 3, (swapped(prev_all, near_swap), swapped(prev_all, far_swap))))
            if ready is not None:
                due, sides = ready
                sides = after((part,), *sides) if step else sides
                pending.append((due, (swapped(sides[0], near_swap), swapped(sides[1], far_swap))))
                ready = None
            passing = ()
            while pending and pending[0][0] >= step:
                passing += pending.pop(0)[1]
            saved, stacks, sends, passed = aside_call(
                step, step - (top - slots), slots, dz, raw, stacks, sends, passing
            )
            arrived += [passed[i : i + 2] for i in range(0, len(passed), 2)]
            carry = (part, peer, grad, bias_sum, saved, stacks)
        top -= slots
        ready = (max(top - 1 - (3 * slots + 3) // 4, 0 if slots > 2 else -1), sends)
    pending.append((-1, (swapped(sends[0], near_swap), swapped(sends[1], far_swap))))
    arrived += [arrays for _, arrays in pending]
    dz_all, raw_all, near_all, far_all = carry[-1]
    bias_sum = carry[3]
    prev_in, exchanged = arrived[0], arrived[1:]
    rows = steps * streams

    def by_direction(mine, theirs):
        return jnp.stack([jnp.where(own == 0, mine, theirs), jnp.where(own == 0, theirs, mine)])

    def line_sum(chunks, axis, stride, count, first=None, gates={}, hooks={}):
        def chunk(*name):
            return pick(chunks, number[(stride, *name)], axis)

        def at(device):
            return (device // stride) % count

        if count == 2:
            pairs = [(i, i + stride if at(i) == 0 else i - stride) for i in range(n_batch)]
            return (chunk("here").astype(F32) + swapped(chunk("not_here"), pairs).astype(F32)).astype(BF16)
        ends = [(i, i + stride) for i in range(n_batch) if at(i) == 0]
        ends += [(i, i - stride) for i in range(n_batch) if at(i) == count - 1]
        up = down = swapped(chunk("begin") if first is None else first, ends)
        for slot in range(2, count):
            if slot in gates:
                up, down = gates[slot](up, down)
            rise = (chunk("rise", slot).astype(F32) + up.astype(F32)).astype(BF16)
            fall = (chunk("fall", slot).astype(F32) + down.astype(F32)).astype(BF16)
            if slot in hooks:
                hooks[slot](rise, fall)
            up = swapped(rise, [(i, i + stride) for i in range(n_batch) if at(i) < min(slot, count - 1)])
            down = swapped(fall, [(i, i - stride) for i in range(n_batch) if at(i) > max(count - 1 - slot, 0)])
        if count in gates:
            up, down = gates[count](up, down)
        return (chunk("here").astype(F32) + up.astype(F32) + down.astype(F32)).astype(BF16)

    share_rows = depth // n_batch

    def input_grad_of(dz):
        return pl.pallas_call(
            input_grad_kernel,
            out_shape=jax.ShapeDtypeStruct((steps, streams, depth), F32),
            grid_spec=pltpu.PrefetchScalarGridSpec(
                num_scalar_prefetch=1,
                grid=(PIECES, 4),
                in_specs=[
                    pl.BlockSpec((1, steps, streams, width), lambda p, g, turn: (p, 0, 0, g)),
                    pl.BlockSpec(
                        (1, depth, width), lambda p, g, turn: (jnp.where(p < 2, g, 3), 0, jnp.where(p < 2, p, 1))
                    ),
                    pl.BlockSpec(
                        (1, depth, width), lambda p, g, turn: (jnp.where(p < 2, 0, g), 0, jnp.where(p < 2, 0, p - 2))
                    ),
                ],
                out_specs=pl.BlockSpec((steps, streams, depth), lambda p, g, turn: (0, 0, 0)),
                scratch_shapes=[pltpu.VMEM((rows, depth), F32)],
            ),
            compiler_params=params(16),
            cost_estimate=cost(0, 0),
            name="input_grad",
        )(turn, in_hbm(dz), in_hbm(win_a), in_hbm(win_b))

    grad_proj = jnp.einsum("ptnc,tnk->pkc", mixed_all, raw_all, preferred_element_type=F32).astype(BF16)
    grad_proj = grad_proj.reshape(PIECES, line, 2, share_rows, width)
    bias_rows = pl.pallas_call(
        bias_kernel,
        out_shape=jax.ShapeDtypeStruct((PIECES, 4, width), F32),
        in_specs=[VMEM],
        out_specs=VMEM,
        compiler_params=params(1),
        name="bias",
    )(pinned(bias_sum))
    bias_rows = jnp.broadcast_to(bias_rows[:, None, None].astype(BF16), (PIECES, line, 2, 4, width))
    grad_proj = jnp.concatenate([grad_proj, bias_rows], axis=3)

    def with_partner(grad):
        mine, sent = (pick(grad, number[x], grad.ndim - 3) for x in ("low", "not_low"))
        taken = swapped(sent, near_swap)
        return sent, taken, (mine.astype(F32) + taken.astype(F32)).astype(BF16)

    def across_two(grad):
        return line_sum(grad.reshape(grad.shape[:-3] + (line // 2, 2) + grad.shape[-2:]), grad.ndim - 3, 4, line // 2)

    proj_sent, proj_taken, proj_y = with_partner(grad_proj)

    lows, count = [], 0
    for x in exchanged[::-1]:
        lows.insert(0, count)
        count += x[0].shape[0]

    def gathered(kept, feat, prev, parts):
        return pl.pallas_call(
            functools.partial(gather_kernel, tuple(lows[: len(parts)])),
            out_shape=(vmem((2 * steps, streams, 2 * depth), BF16), vmem((2 * steps, streams, 4 * width), BF16)),
            in_specs=[ANY] * (5 + len(parts)),
            out_specs=[VMEM] * 2,
            scratch_shapes=[pltpu.SemaphoreType.DMA((5 + len(parts),))],
            compiler_params=params(1),
            cost_estimate=cost(0, 0),
            name="gather",
        )(*(in_hbm(x) for x in (feat_all, prev_all, feat, prev, kept, *parts)))

    def completed(begin, rows_out, left, right, parts):
        return pl.pallas_call(
            functools.partial(late_kernel, tuple(lows[len(lows) - len(parts) :])),
            out_shape=(vmem(right.shape, BF16), jax.ShapeDtypeStruct((2, max(rows_out, 8), 4 * width), BF16)),
            in_specs=[SMEM] + [VMEM] * 2 + [ANY] * len(parts),
            out_specs=[VMEM] * 2,
            scratch_shapes=[pltpu.SemaphoreType.DMA((len(parts),))],
            input_output_aliases={2: 0},
            compiler_params=params(16),
            cost_estimate=cost(0, 0),
            name="late",
        )(begin, pinned(left), pinned(right), *(in_hbm(x) for x in parts))

    def multiplied(left, right):
        return pl.pallas_call(
            product_kernel,
            out_shape=jax.ShapeDtypeStruct((2, depth, 4 * width), BF16),
            in_specs=[VMEM] * 2,
            out_specs=VMEM,
            compiler_params=params(16),
            cost_estimate=cost(0, 0),
            name="product",
        )(pinned(left), pinned(right))

    near_parts, far_parts = zip(*exchanged)
    chunk_rows = 2 * share_rows if 2 * share_rows % 128 == 0 else 0
    near_left, near_right = gathered(near_all, feat_in[0], prev_in[0], near_parts[:-LATE])
    near_late = after((near_left, proj_sent, *far_parts[-LATE:]), *near_parts[-LATE:])
    near_right, first = completed(jnp.full((1,), number["begin"], jnp.int32), chunk_rows, near_left, near_right, near_late)
    far_all, *far_parts = after((first,), far_all, *far_parts)
    blocks = 4

    def far_product(mine, theirs):
        grad = pl.pallas_call(
            functools.partial(whole_product_kernel, tuple(lows)),
            out_shape=jax.ShapeDtypeStruct((depth, 4 * width), BF16),
            in_specs=[ANY] * (3 + len(far_parts)),
            out_specs=VMEM,
            scratch_shapes=[
                pltpu.VMEM((2 * steps, streams, depth), BF16),
                pltpu.VMEM((depth, 2 * steps * streams), BF16),
                pltpu.VMEM((blocks, 2 * steps, streams, 4 * width // blocks), BF16),
                pltpu.SemaphoreType.DMA((2,)),
                pltpu.SemaphoreType.DMA((blocks, 1 + len(far_parts))),
            ],
            compiler_params=params(24),
            cost_estimate=cost(0, 0),
            name="whole_product",
        )(*(in_hbm(x) for x in (mine, theirs, far_all, *far_parts)))
        return grad.reshape(line, 2, share_rows, 4 * width)

    far_in = far_product(feat_all, feat_in[1])
    near = multiplied(near_left, near_right).reshape(2, line, 2, share_rows, 4 * width)

    def states_of(hidden, cell):
        both_hidden = trade(hidden, hidden)

        hidden_dirs = by_direction(*both_hidden)
        outputs = (inputs.astype(F32) + jnp.transpose(hidden_dirs, (0, 2, 1, 3)).astype(F32)).astype(BF16)
        last_h = jnp.stack([hidden_dirs[0, steps - 1], hidden_dirs[1, 0]], axis=1).astype(F32)
        final_h = jnp.zeros_like(state_h).at[stream_doc].set(last_h)
        last_c = jnp.transpose(cell.reshape(QUARTERS, HALVES, streams, width), (0, 2, 1, 3)).reshape(
            QUARTERS, streams, cells
        )
        last_dirs = by_direction(*trade(last_c[0], last_c[1]))
        final_c = jnp.zeros_like(state_c).at[stream_doc].set(jnp.transpose(last_dirs, (1, 0, 2)))
        return outputs, final_h, final_c

    tokens = {}

    def second(up, down):
        up, tokens["far"], tokens["dz"], tokens["proj"], tokens["prev"] = after(
            (), up, far_in, dz_all, proj_y, prev_in[1], free=5 * MIB
        )
        return up, up

    def beside_second(rise, fall):
        (sent,) = after((rise, fall), tokens["far"], free=5 * MIB)
        tokens["in"] = with_partner(sent)[2]
        tokens["rec"] = with_partner(far_product(prev_all, tokens["prev"]))[2]
        tokens["proj"] = across_two(tokens["proj"])

    def third(up, down):
        dx = input_grad_of(tokens["dz"])
        up, down, tokens["dx"], in_sum, tokens["proj"], hidden, last_cell = after(
            (), up, down, dx, tokens["in"], tokens["proj"], hidden_all, cell, free=2 * MIB
        )
        tokens["in"] = across_two(in_sum)
        tokens["states"] = states_of(hidden, last_cell)
        return up, down

    def final(up, down):
        up, down, tokens["in"], rec_sum = after(
            tokens["states"], up, down, tokens["in"], tokens["rec"], free=2 * MIB
        )
        tokens["rec"] = across_two(rec_sum)
        return up, down

    gates = {2: second, 3: third, line: final} if line > 3 else {}
    hooks = {2: beside_second} if line > 3 else {}
    first = first.reshape(2, 2, share_rows, 4 * width) if chunk_rows else None
    near = line_sum(near, 1, 2, line, first, gates, hooks)
    dx_all, (outputs, final_h, final_c) = tokens["dx"], tokens["states"]
    in_two, rec_two, proj_two = tokens["in"], tokens["rec"], tokens["proj"]

    def halves_of(summed, name, pairs):
        return pick(summed, number[name], 1), swapped(pick(summed, number["not_" + name], 1), pairs)

    near_pair = halves_of(near, "low", near_swap)
    in_pair, rec_pair = (
        [lax.ppermute(y, "gate", swap) for y in halves_of(x[None], "high", far_swap)] for x in (in_two, rec_two)
    )
    proj_mine, proj_theirs = halves_of(proj_two, "high", far_swap)
    grad_proj = proj_mine.astype(F32) + proj_theirs.astype(F32)
    grad_shape = (2, share_rows, 4, cells)
    grad_w_in, grad_w_rec = pl.pallas_call(
        assemble_kernel,
        out_shape=(jax.ShapeDtypeStruct(grad_shape, F32),) * 2,
        in_specs=[SMEM] + [VMEM] * 6,
        out_specs=[VMEM] * 2,
        compiler_params=params(14),
        name="assemble",
    )(jnp.stack([own, low, high]), *near_pair, *in_pair, *rec_pair)

    def home(mine, theirs):
        return by_direction(*trade(mine, theirs)).astype(F32)

    own_cells = cells // n_batch
    shaped = jnp.transpose(grad_proj[:, share_rows:].reshape(QUARTERS, HALVES, 4, width), (0, 2, 1, 3))
    shaped = pick(shaped.reshape(QUARTERS, 4, n_batch, own_cells), number["spot"], 2)
    grad_bias = home(shaped[0], shaped[1])
    grad_proj = grad_proj[:, :share_rows].reshape(QUARTERS, HALVES, share_rows, width)
    grad_proj = jnp.transpose(grad_proj, (0, 1, 3, 2)).reshape(QUARTERS, cells, share_rows).astype(BF16)
    grad_proj = home(grad_proj[0], grad_proj[1])

    def columns(array, name, size):
        return lax.dynamic_slice_in_dim(array, number[name], size, 2, allow_negative_indices=False)

    dx_half = columns(dx_all, "cols", half_cols)
    dx_sent = columns(dx_all, "other_cols", half_cols).astype(BF16)
    dx_half = dx_half + lax.ppermute(dx_sent, "gate", across).astype(F32)
    dx_half = (dx_half + columns(ups, "cols", half_cols).astype(F32)).astype(BF16)
    dx_half = dx_half.reshape(steps, streams, 2, quarter_cols)
    dx_dirs = by_direction(*trade(pick(dx_half, own, 2), pick(dx_half, number["other"], 2)))
    input_grad = jnp.transpose(dx_dirs, (0, 2, 1, 3))
    return (outputs, input_grad, grad_w_in, grad_w_rec, grad_bias, grad_proj, final_h, final_c)


def solution(mesh):
    placed = (
        P(None, "batch", None, None),
        P(None, None, None, "gate"),
        P(None, None, None, "gate"),
        P(None, None, "gate"),
        P(None, "gate", None),
        P("batch", None, None),
        P("batch", None, "gate"),
        P("batch", None),
        P("batch"),
        P(None, "batch", None, None),
    )
    return jax.shard_map(
        body,
        mesh=mesh,
        in_specs=placed,
        out_specs=(
            P(None, "batch", None, None),
            P(None, "batch", None, "gate"),
            P(None, "batch", None, "gate"),
            P(None, "batch", None, "gate"),
            P(None, None, ("gate", "batch")),
            P(None, "gate", "batch"),
            P("batch", None, None),
            P("batch", None, "gate"),
        ),
        check_vma=False,
    )
```

```python
import functools

import jax
import jax.numpy as jnp
from jax import lax
from jax.experimental import pallas as pl
from jax.experimental.pallas import tpu as pltpu
from jax.sharding import PartitionSpec as P

CLIP = 3.0
F32, BF16 = jnp.float32, jnp.bfloat16
QUARTERS, HALVES = 2, 2
PIECES = QUARTERS * HALVES
MIB = 2**20
LATE = 2
SHARES = (0.35, 0.3, 0.15, 0.1, 0.1)

VMEM = pl.BlockSpec(memory_space=pltpu.VMEM)
SMEM = pl.BlockSpec(memory_space=pltpu.SMEM)
ANY = pl.BlockSpec(memory_space=pl.ANY)


def pinned(array):
    return pltpu.with_memory_space_constraint(array, pltpu.VMEM)


def in_hbm(array):
    return pltpu.with_memory_space_constraint(array, pltpu.HBM)


def dot(left, right):
    return jnp.dot(left, right, preferred_element_type=F32)


def layout_kernel(keep, spread, which_ref, w_ref, *refs):
    buf, sems, out_sems = refs[-3:]
    out_ref = refs[0] if keep else refs[1]
    all_ref = refs[1] if keep else refs[0]
    depth, ahead, part = w_ref.shape[1], buf.shape[0], buf.shape[1]
    count = depth // part

    def fetch(i):
        return pltpu.make_async_copy(w_ref.at[which_ref[0], pl.ds(i * part, part)], buf.at[i % ahead], sems.at[i % ahead])

    def store(i):
        rows = pl.ds(i * part, part)
        return pltpu.make_async_copy(out_ref.at[:, rows], all_ref.at[:, rows], out_sems.at[i])

    for i in range(min(ahead - 1, count)):
        fetch(i).start()
    for i in range(count):
        if i + ahead - 1 < count:
            fetch(i + ahead - 1).start()
        fetch(i).wait()
        out_ref[:, i * part : (i + 1) * part, :] = jnp.swapaxes(buf[i % ahead], 0, 1)
        if spread:
            store(i).start()
    for i in range(count if spread else 0):
        store(i).wait()


def turned_kernel(wa_ref, wb_ref, pa_ref, pb_ref, wat_ref, wbt_ref, pat_ref, pbt_ref):
    for w_ref, out_ref in ((wa_ref, wat_ref), (wb_ref, wbt_ref)):
        for gate in range(4):
            for half in range(HALVES):
                width = w_ref.shape[2] // HALVES
                cols = slice(half * width, (half + 1) * width)
                out_ref[gate, cols, :] = w_ref[gate, :, cols].T
    pat_ref[...] = pa_ref[...].T
    pbt_ref[...] = pb_ref[...].T


def pass_kernel(*refs):
    pass


def after(tokens, *arrays, free=0):
    count = len(tokens)
    return pl.pallas_call(
        pass_kernel,
        out_shape=tuple(jax.ShapeDtypeStruct(x.shape, x.dtype) for x in arrays),
        in_specs=[ANY] * (count + len(arrays)),
        out_specs=[ANY] * len(arrays),
        input_output_aliases={count + i: i for i in range(len(arrays))},
        compiler_params=params(1),
        name="after",
    )(*tokens, *(in_hbm(x) if x.size * x.dtype.itemsize > free else x for x in arrays))


def gather_kernel(lows, *refs):
    (feat_ref, prev_ref, feat_too, prev_too, kept_ref), refs = refs[:5], refs[5:]
    groups, (left_ref, right_ref, sems) = refs[:-3], refs[-3:]
    steps, _, depth = feat_ref.shape
    jobs = [
        (feat_ref, left_ref.at[:steps, :, :depth]),
        (prev_ref, left_ref.at[:steps, :, depth:]),
        (feat_too, left_ref.at[steps:, :, :depth]),
        (prev_too, left_ref.at[steps:, :, depth:]),
        (kept_ref, right_ref.at[:steps]),
    ]
    jobs += [(x, right_ref.at[steps + low : steps + low + x.shape[0]]) for x, low in zip(groups, lows)]
    copies = [pltpu.make_async_copy(a, b, sems.at[i]) for i, (a, b) in enumerate(jobs)]
    for copy in copies:
        copy.start()
    for copy in copies:
        copy.wait()


def late_kernel(lows, begin_ref, left_ref, right_in, *refs):
    groups, (right_ref, first_ref, sems) = refs[:-3], refs[-3:]
    steps = left_ref.shape[0] // 2
    copies = [
        pltpu.make_async_copy(x, right_ref.at[steps + low : steps + low + x.shape[0]], sems.at[i])
        for i, (x, low) in enumerate(zip(groups, lows))
    ]
    for copy in copies:
        copy.start()
    for copy in copies:
        copy.wait()
    if first_ref.shape[1] % 128:
        return
    share, depth = first_ref.shape[1], left_ref.shape[2] // 2
    rows = left_ref.shape[0] * left_ref.shape[1]
    left = [
        left_ref[:, :, pl.ds(pl.multiple_of(i * depth + begin_ref[0] * share, 128), share)].reshape(rows, share)
        for i in range(2)
    ]
    left = jnp.concatenate([x.T for x in left], axis=0)
    width = right_ref.shape[2] // 4

    def columns(i, _):
        cols = pl.ds(pl.multiple_of(i * width, width), width)
        total = dot(left, right_ref[:, :, cols].reshape(rows, width)).astype(BF16)
        first_ref[0, :, cols] = total[:share]
        first_ref[1, :, cols] = total[share:]
        return 0

    lax.fori_loop(0, 4, columns, 0)


def product_kernel(left_ref, right_ref, out_ref):
    rows, depth = left_ref.shape[0] * left_ref.shape[1], left_ref.shape[2] // 2
    width = right_ref.shape[2] // 4
    for which in range(2):
        left = left_ref[:, :, which * depth : (which + 1) * depth].reshape(rows, depth).T

        def columns(i, _):
            cols = pl.ds(pl.multiple_of(i * width, width), width)
            out_ref[which, :, cols] = dot(left, right_ref[:, :, cols].reshape(rows, width)).astype(BF16)
            return 0

        lax.fori_loop(0, 4, columns, 0)


def whole_product_kernel(lows, mine_ref, theirs_ref, kept_ref, *refs):
    groups, (out_ref, left_buf, turned_buf, right_buf, left_sems, sems) = refs[:-6], refs[-6:]
    steps, streams, depth = mine_ref.shape
    blocks = right_buf.shape[0]
    width = right_buf.shape[3]
    rows = 2 * steps * streams

    def fetches_of(block):
        cols = slice(block * width, (block + 1) * width)
        jobs = [(kept_ref.at[:, :, cols], right_buf.at[block, :steps])]
        jobs += [
            (x.at[:, :, cols], right_buf.at[block, steps + low : steps + low + x.shape[0]])
            for x, low in zip(groups, lows)
        ]
        return [pltpu.make_async_copy(a, b, sems.at[block, i]) for i, (a, b) in enumerate(jobs)]

    lefts = [
        pltpu.make_async_copy(mine_ref, left_buf.at[:steps], left_sems.at[0]),
        pltpu.make_async_copy(theirs_ref, left_buf.at[steps:], left_sems.at[1]),
    ]
    for copy in lefts:
        copy.start()
    for block in range(blocks):
        for copy in fetches_of(block):
            copy.start()
    for copy in lefts:
        copy.wait()
    turned_buf[...] = left_buf[...].reshape(rows, depth).T
    for block in range(blocks):
        for copy in fetches_of(block):
            copy.wait()
        total = dot(turned_buf[...], right_buf[block].reshape(rows, width))
        out_ref[:, block * width : (block + 1) * width] = total.astype(BF16)


def assemble_kernel(place_ref, near_a, near_b, in_a, in_b, rec_a, rec_b, in_ref, rec_ref):
    own, low, high = place_ref[0], place_ref[1], place_ref[2]
    width = in_ref.shape[3] // HALVES
    jobs = [
        (own, near_a, near_b, 0, low, in_ref),
        (own, near_a, near_b, 1, low, rec_ref),
        (1 - own, in_a, in_b, 0, high, in_ref),
        (1 - own, rec_a, rec_b, 0, high, rec_ref),
    ]
    for direction, mine_ref, theirs_ref, which, index, out_ref in jobs:
        mine, theirs = mine_ref[which].astype(F32), theirs_ref[which].astype(F32)
        for half in range(HALVES):
            whole = jnp.where(index == half, mine, theirs)
            gates = jnp.stack([whole[:, gate * width : (gate + 1) * width] for gate in range(4)])
            out_ref[direction, :, :, half * width : (half + 1) * width] = jnp.swapaxes(gates, 0, 1)


def order_kernel(step_ref, feat_ref, out_ref, all_ref, sems):
    copies = []
    for i in range(feat_ref.shape[0]):
        source = feat_ref.at[step_ref[0] + step_ref[1] * i]
        copies.append(pltpu.make_async_copy(source, out_ref.at[i], sems.at[2 * i]))
        copies.append(pltpu.make_async_copy(source, all_ref.at[i], sems.at[2 * i + 1]))
    for copy in copies:
        copy.start()
    for copy in copies:
        copy.wait()


def numbers_kernel(index, in_ref, out_ref):
    out_ref[0] = in_ref[index]


def bias_kernel(sum_ref, out_ref):
    width = sum_ref.shape[2] // 4
    for piece in range(PIECES):
        for gate in range(4):
            out_ref[piece, gate : gate + 1, :] = jnp.sum(
                sum_ref[piece, :, gate * width : (gate + 1) * width], axis=0, keepdims=True
            )


def pieces(refs, axis):
    for piece in range(PIECES):
        quarter, half = divmod(piece, HALVES)
        width = refs[0].shape[axis] // HALVES
        yield piece, quarter, width, slice(half * width, (half + 1) * width)


def forward_kernel(
    first, step_ref, p_ref, q_ref, start_ref, keep_ref, cell_ref, inflow_ref, wa_ref, wb_ref, pa_ref, pb_ref,
    part_ref, next_ref, gates_ref, mixed_ref, prev_ref, hidden_ref, slope_ref,
):
    keep = keep_ref[step_ref[1]][:, :1]
    if first:
        hidden = start_ref[...]
    else:
        hidden = clipped(p_ref, q_ref, hidden_ref, slope_ref)
    hidden = hidden * keep.astype(BF16)
    prev_ref[...] = hidden
    part = jnp.zeros(part_ref.shape, F32)
    for piece, quarter, width, cols in pieces((wa_ref, wb_ref), 2):
        w_ref, proj_ref = ((wa_ref, pa_ref), (wb_ref, pb_ref))[quarter]
        acts = []
        for gate in range(4):
            place = slice(gate * width, (gate + 1) * width)
            pre = dot(hidden, w_ref[gate, :, cols]) + inflow_ref[piece, :, place]
            act = jnp.tanh(pre if gate == 2 else 0.5 * pre)
            gates_ref[piece, :, place] = act.astype(BF16)
            acts.append(act if gate == 2 else 0.5 + 0.5 * act)
        ingate, forget, candidate, outgate = acts
        cell = CLIP * jnp.tanh((forget * (keep * cell_ref[piece]) + ingate * candidate) * (1.0 / CLIP))
        next_ref[piece] = cell
        mixed = (outgate * jnp.tanh(cell)).astype(BF16)
        mixed_ref[piece] = mixed
        part = part + dot(mixed, proj_ref[cols, :])
    part_ref[...] = part.astype(BF16)


def clipped(p_ref, q_ref, hidden_ref, slope_ref):
    squash = jnp.tanh((p_ref[...].astype(F32) + q_ref[...].astype(F32)) * (1.0 / CLIP))
    hidden = (CLIP * squash).astype(BF16)
    hidden_ref[...] = hidden
    slope_ref[...] = 1.0 - squash * squash
    return hidden


def between_kernel(
    first, last, passed, step_ref, feat_ref, ba_ref, bb_ref, wa_ref, wb_ref, cell_ref, gates_ref, mixed_ref, prev_ref, hidden_ref,
    slope_ref, *refs,
):
    refs = refs[(0 if first else 6) + passed :]
    out_ref, gates_all, cells_all, mixed_all, prev_all, hidden_all, slope_all = refs[:7]
    sems = refs[-1]
    step, time_before = step_ref[0], step_ref[2]
    copies = [pltpu.make_async_copy(gates_ref.at[i], gates_all.at[i, step], sems.at[i]) for i in range(PIECES)]
    copies += [
        pltpu.make_async_copy(mixed_ref.at[i], mixed_all.at[i, step], sems.at[PIECES + i]) for i in range(PIECES)
    ]
    copies.append(pltpu.make_async_copy(cell_ref, cells_all.at[step], sems.at[2 * PIECES]))
    copies.append(pltpu.make_async_copy(prev_ref, prev_all.at[step], sems.at[2 * PIECES + 1]))
    if not first:
        copies.append(pltpu.make_async_copy(hidden_ref, hidden_all.at[time_before], sems.at[2 * PIECES + 2]))
        copies.append(pltpu.make_async_copy(slope_ref, slope_all.at[step - 1], sems.at[2 * PIECES + 3]))
    for copy in copies:
        copy.start()
    if not last:
        inflow_into(feat_ref[step + 1], ba_ref, bb_ref, wa_ref, wb_ref, out_ref)
    for copy in copies:
        copy.wait()


def inflow_into(feat, ba_ref, bb_ref, wa_ref, wb_ref, out_ref, quarters=(0, 1)):
    for piece, quarter, width, cols in pieces((wa_ref, wb_ref), 2):
        if quarter not in quarters:
            continue
        w_ref, bias_ref = ((wa_ref, ba_ref), (wb_ref, bb_ref))[quarter]
        for gate in range(4):
            place = slice(gate * width, (gate + 1) * width)
            out_ref[piece, :, place] = dot(feat, w_ref[gate, :, cols]) + bias_ref[gate : gate + 1, cols]


def begin_kernel(which_ref, feat_ref, wa_ref, proj_ref, *refs):
    sems = refs[-1]
    out_ref, pa_ref, *placed = refs[-11:-1]
    copies = [pltpu.make_async_copy(x, y, sems.at[i]) for i, (x, y) in enumerate(zip(refs[:-11], placed))]
    copies.append(pltpu.make_async_copy(proj_ref.at[which_ref[0]], pa_ref, sems.at[len(copies)]))
    for copy in copies:
        copy.start()
    ba_ref, bb_ref, wb_ref = placed[:3]
    copies[0].wait()
    inflow_into(feat_ref[0], ba_ref, bb_ref, wa_ref, wb_ref, out_ref, (0,))
    copies[1].wait()
    copies[2].wait()
    inflow_into(feat_ref[0], ba_ref, bb_ref, wa_ref, wb_ref, out_ref, (1,))
    for copy in copies[3:]:
        copy.wait()


def backward_kernel(
    step_ref, p_ref, q_ref, keep_ref, grad_ref, bias_ref, wa_ref, wb_ref, pa_ref, pb_ref,
    gates_ref, cell_ref, prev_ref, slope_ref, up_ref, start_ref,
    part_ref, next_ref, sum_ref, raw_ref, dz_ref,
):
    step = step_ref[0]
    keep = keep_ref[step_ref[1]][:, :1]
    raw = (up_ref[...].astype(F32) + (p_ref[...].astype(F32) + q_ref[...].astype(F32))) * slope_ref[...]
    raw = raw.astype(BF16)
    raw_ref[...] = raw
    part = jnp.zeros(part_ref.shape, F32)
    for piece, quarter, width, cols in pieces((wa_ref, wb_ref), 1):
        w_ref, proj_ref = ((wa_ref, pa_ref), (wb_ref, pb_ref))[quarter]
        mixed = dot(raw, proj_ref[:, cols])
        acts = [gates_ref[piece, :, gate * width : (gate + 1) * width].astype(F32) for gate in range(4)]
        ingate, forget, outgate = (0.5 + 0.5 * acts[gate] for gate in (0, 1, 3))
        slopes = [1.0 - act * act for act in acts]
        cell = cell_ref[piece]
        prev = keep * jnp.where(step == 0, start_ref[piece], prev_ref[piece])
        squash = jnp.tanh(cell)
        total = grad_ref[piece] + mixed * outgate * (1.0 - squash * squash)
        inner = total * (1.0 - (cell * (1.0 / CLIP)) * (cell * (1.0 / CLIP)))
        next_ref[piece] = keep * inner * forget
        quart = 0.25 * inner
        pre_grads = (
            quart * acts[2] * slopes[0],
            quart * prev * slopes[1],
            inner * ingate * slopes[2],
            0.25 * mixed * squash * slopes[3],
        )
        for gate in range(4):
            low = pre_grads[gate].astype(BF16)
            place = slice(gate * width, (gate + 1) * width)
            dz_ref[piece, :, place] = low
            rows = pre_grads[gate].reshape(-1, 8, width)
            sum_ref[piece, :, place] = bias_ref[piece, :, place] + jnp.sum(rows, axis=0)
            part = part + dot(low, w_ref[gate, cols, :])
    part_ref[...] = (part * keep).astype(BF16)


def finish_kernel(
    step_ref, p_ref, q_ref, mixed_ref, prev_ref, hidden_ref, before_ref, ups_all, mixed_in, prev_in, hidden_in, slope_in,
    slope_ref, up_ref, mixed_all, prev_all, hidden_all, slope_all, hidden_buf, sems,
):
    step, time, time_before = step_ref[0], step_ref[1], step_ref[2]
    jobs = [(mixed_ref.at[i], mixed_all.at[i, step]) for i in range(PIECES)]
    jobs += [
        (ups_all.at[time], up_ref),
        (prev_ref, prev_all.at[step]),
        (hidden_ref, hidden_all.at[time_before]),
        (before_ref, slope_all.at[step - 1]),
        (hidden_buf, hidden_all.at[time]),
    ]
    copies = [pltpu.make_async_copy(x, y, sems.at[i]) for i, (x, y) in enumerate(jobs)]
    for copy in copies[:-1]:
        copy.start()
    clipped(p_ref, q_ref, hidden_buf, slope_ref)
    copies[-1].start()
    for copy in copies:
        copy.wait()


def fetches(step, time, sources, targets, sems):
    gates_all, cells_all, ups_all = sources
    gates_ref, cell_ref, prev_ref, up_ref = targets
    before = jnp.maximum(step - 1, 0)
    return [
        pltpu.make_async_copy(gates_all.at[i, step], gates_ref.at[i], sems.at[i]) for i in range(PIECES)
    ] + [
        pltpu.make_async_copy(cells_all.at[step], cell_ref, sems.at[PIECES]),
        pltpu.make_async_copy(cells_all.at[before], prev_ref, sems.at[PIECES + 1]),
        pltpu.make_async_copy(ups_all.at[time], up_ref, sems.at[PIECES + 2]),
    ]


def aside_kernel(
    first, last, opens, passed, step_ref, dz_ref, raw_ref, gates_all, cells_all, ups_all, slope_all, *refs
):
    refs = refs[(0 if first else 4) + (0 if opens else 2) + passed :]
    gates_ref, cell_ref, prev_ref, slope_ref, up_ref = refs[:5]
    dz_all, raw_all, near_all, far_all, near_out, far_out = refs[5:11]
    sems, fetch_sems = refs[-2:]
    step, time_before = step_ref[0], step_ref[2]
    slot, low, high = step_ref[4], step_ref[5], step_ref[6]
    before = jnp.maximum(step - 1, 0)
    copies = []
    if not last:
        copies += fetches(
            before, time_before, (gates_all, cells_all, ups_all), (gates_ref, cell_ref, prev_ref, up_ref), fetch_sems
        )
        copies.append(pltpu.make_async_copy(slope_all.at[before], slope_ref, fetch_sems.at[PIECES + 3]))
    copies += [pltpu.make_async_copy(dz_ref.at[i], dz_all.at[i, step], sems.at[i]) for i in range(PIECES)]
    copies.append(pltpu.make_async_copy(raw_ref, raw_all.at[step], sems.at[PIECES]))
    copies.append(pltpu.make_async_copy(dz_ref.at[low], near_all.at[step], sems.at[PIECES + 1]))
    copies.append(pltpu.make_async_copy(dz_ref.at[HALVES + high], far_all.at[step], sems.at[PIECES + 2]))
    copies.append(pltpu.make_async_copy(dz_ref.at[1 - low], near_out.at[slot], sems.at[PIECES + 3]))
    copies.append(pltpu.make_async_copy(dz_ref.at[HALVES + 1 - high], far_out.at[slot], sems.at[PIECES + 4]))
    for copy in copies:
        copy.start()
    for copy in copies:
        copy.wait()


def input_grad_kernel(step_ref, dz_ref, wa_ref, wb_ref, out_ref, acc_ref):
    piece, gate = pl.program_id(0), pl.program_id(1)
    steps, streams, width = dz_ref.shape[1:]

    @pl.when((piece == 0) & (gate == 0))
    def _():
        acc_ref[...] = jnp.zeros(acc_ref.shape, F32)

    weights = jnp.where(piece < HALVES, wa_ref[0], wb_ref[0])
    acc_ref[...] += lax.dot_general(
        dz_ref[0].reshape(steps * streams, width), weights, (((1,), (1,)), ((), ())), preferred_element_type=F32
    )

    @pl.when((piece == PIECES - 1) & (gate == 3))
    def _():
        for step in range(steps):
            time = step_ref[0] + step_ref[1] * step
            out_ref[time] = acc_ref[step * streams : (step + 1) * streams, :]


def params(mib):
    return pltpu.CompilerParams(vmem_limit_bytes=mib * MIB)


def cost(flops, size):
    return pl.CostEstimate(flops=flops, bytes_accessed=size, transcendentals=0)


def body(inputs, w_in, w_rec, bias, proj, state_h, state_c, resets, stream_doc, cotangent):
    streams, steps, depth = inputs.shape[1:]
    cells = w_in.shape[3]
    width = cells // HALVES
    n_batch = lax.axis_size("batch")
    gates_size = lax.axis_size("gate")
    line = n_batch // 2
    swap = [(i, i ^ 1) for i in range(gates_size)]
    across = [(i, i ^ 2) for i in range(gates_size)]
    near_swap = [(i, i ^ 1) for i in range(n_batch)]
    far_swap = [(i, i ^ 2) for i in range(n_batch)]

    rank, spot = lax.axis_index("gate"), lax.axis_index("batch")
    half_cols, quarter_cols = depth // 2, depth // 4
    place_numbers = {
        "own": rank % 2,
        "other": 1 - rank % 2,
        "low": spot % 2,
        "not_low": 1 - spot % 2,
        "high": (spot // 2) % 2,
        "not_high": 1 - (spot // 2) % 2,
        "spot": spot,
        "begin": jnp.where(spot // 2 == 0, line - 1, 0),
        "cols": (rank // 2) * half_cols,
        "other_cols": (1 - rank // 2) * half_cols,
    }
    for stride, count in {(2, line), (4, line // 2)}:
        here = (spot // stride) % count
        place_numbers[stride, "here"] = here
        place_numbers[stride, "not_here"] = jnp.maximum(1 - here, 0)
        for slot in range(2, count):
            place_numbers[stride, "rise", slot] = jnp.minimum(here + count - slot, count - 1)
            place_numbers[stride, "fall", slot] = jnp.maximum(here - count + slot, 0)
        if count > 2:
            place_numbers[stride, "begin"] = jnp.where(here == 0, count - 1, 0)
    names = sorted(place_numbers, key=str)
    which = pl.pallas_call(
        functools.partial(numbers_kernel, names.index("own")),
        out_shape=jax.ShapeDtypeStruct((1,), jnp.int32),
        in_specs=[SMEM],
        out_specs=SMEM,
        name="numbers",
    )(jnp.stack([place_numbers[x] for x in names]).astype(jnp.int32))
    number = {x: place_numbers[x].astype(jnp.int32) for x in names}
    own, low, high = number["own"], number["low"], number["high"]

    def pick(stacked, index, axis=0):
        return lax.dynamic_index_in_dim(stacked, index, axis, keepdims=False, allow_negative_indices=False)

    def trade(mine, theirs):
        return (mine, lax.ppermute(theirs, "gate", swap))

    def vmem(shape, dtype):
        return pltpu.VMEM(shape, dtype)

    def hbm(shape, dtype):
        return pltpu.HBM(shape, dtype)

    def by_gate(weights, index, keep, spread):
        shape = (4,) + weights.shape[1:2] + weights.shape[3:]
        count = 16
        kept, spreads = (vmem(shape, BF16),) * keep, (hbm(shape, BF16),) * spread
        return pl.pallas_call(
            functools.partial(layout_kernel, keep, spread),
            out_shape=kept + spreads,
            in_specs=[SMEM, ANY],
            out_specs=[VMEM] * keep + [ANY] * spread,
            scratch_shapes=[pltpu.VMEM(shape, BF16)] * (1 - keep)
            + [
                pltpu.VMEM((4, weights.shape[1] // count) + weights.shape[2:], BF16),
                pltpu.SemaphoreType.DMA((4,)),
                pltpu.SemaphoreType.DMA((count,)),
            ],
            compiler_params=params(8),
            name="layout",
        )(index, in_hbm(weights))

    away = jnp.full((1,), number["other"], jnp.int32)
    win_b, rec_b = (lax.ppermute(by_gate(w, away, False, True)[0], "gate", swap) for w in (w_in, w_rec))
    (win_av, win_a), (rec_av,) = by_gate(w_in, which, True, True), by_gate(w_rec, which, True, False)
    proj_b = lax.ppermute(pick(proj, number["other"]), "gate", swap)
    bias_a, bias_b = trade(pick(bias, own), pick(bias, number["other"]))

    def cells_to_pieces(pair):
        both = jnp.stack(pair).reshape(QUARTERS, streams, HALVES, width)
        return jnp.transpose(both, (0, 2, 1, 3)).reshape(PIECES, streams, width)

    def by_time(stacked):
        return jnp.transpose(pick(stacked, own), (1, 0, 2))

    feats = by_time(inputs)
    ups = by_time(cotangent)
    flags = resets.astype(F32)
    later = jnp.concatenate([flags[:, 1:], jnp.zeros_like(flags[:, :1])], axis=1)
    keep = 1.0 - jnp.where(own == 0, flags, later)
    keep = jnp.broadcast_to(jnp.transpose(keep)[:, :, None], (steps, streams, 128))

    docs_h = state_h[stream_doc]
    docs_c = state_c[stream_doc]
    start_h = pick(jnp.transpose(docs_h, (1, 0, 2)), own).astype(BF16)
    by_dir_c = jnp.transpose(docs_c, (1, 0, 2))
    start_c = cells_to_pieces(trade(pick(by_dir_c, own), pick(by_dir_c, number["other"])))

    def at_step(step):
        near = jnp.array([step, step, max(step - 1, 0), min(step + 1, steps - 1)], jnp.int32)
        turned = jnp.array([step] + [steps - 1 - x for x in (step, max(step - 1, 0), min(step + 1, steps - 1))], jnp.int32)
        return jnp.where(own == 0, near, turned)

    def swapped(array, pairs):
        return lax.ppermute(array, "batch", pairs)

    turn = jnp.where(own == 0, jnp.array([0, 1], jnp.int32), jnp.array([steps - 1, -1], jnp.int32))
    feats_v, feat_all = pl.pallas_call(
        order_kernel,
        out_shape=(vmem(feats.shape, BF16), hbm(feats.shape, BF16)),
        in_specs=[SMEM, ANY],
        out_specs=[VMEM, ANY],
        scratch_shapes=[pltpu.SemaphoreType.DMA((2 * steps,))],
        compiler_params=params(1),
        name="order",
    )(turn, feats)
    gates_shape, cell_shape = (PIECES, streams, 4 * width), (PIECES, streams, width)
    bias_shape = (PIECES, 8, 4 * width)
    sources = (bias_a.astype(F32), bias_b.astype(F32), in_hbm(win_b), in_hbm(rec_b), in_hbm(proj_b), keep, start_h, start_c)
    inflow, proj_av, bias_av, bias_bv, win_bv, rec_bv, proj_bv, keep_v, start_hv, start_cv = pl.pallas_call(
        begin_kernel,
        out_shape=(vmem(gates_shape, F32), vmem((cells, depth), BF16)) + tuple(vmem(x.shape, x.dtype) for x in sources),
        in_specs=[SMEM, VMEM, VMEM] + [ANY] * (1 + len(sources)),
        out_specs=[VMEM] * (2 + len(sources)),
        scratch_shapes=[pltpu.SemaphoreType.DMA((1 + len(sources),))],
        compiler_params=params(8),
        name="begin",
    )(which, pinned(feats_v), pinned(win_av), in_hbm(proj), *sources)

    def forward_call(first, step, part, peer, cell, inflow):
        return pl.pallas_call(
            functools.partial(forward_kernel, first),
            out_shape=(
                vmem((streams, depth), BF16),
                vmem(cell_shape, F32),
                vmem(gates_shape, BF16),
                vmem(cell_shape, BF16),
                vmem((streams, depth), BF16),
                vmem((streams, depth), BF16),
                vmem((streams, depth), F32),
            ),
            in_specs=[SMEM] + [VMEM] * 10,
            out_specs=[VMEM] * 7,
            compiler_params=params(8),
            name="forward_step",
        )(
            at_step(step), pinned(part), pinned(peer), pinned(start_hv), pinned(keep_v), pinned(cell), pinned(inflow),
            pinned(rec_av), pinned(rec_bv), pinned(proj_av), pinned(proj_bv),
        )

    def between_call(step, fresh, stacks, passing=()):
        shapes = (
            hbm((PIECES, steps, streams, 4 * width), BF16),
            hbm((steps,) + cell_shape, F32),
            hbm((PIECES, steps, streams, width), BF16),
            hbm((steps, streams, depth), BF16),
            hbm((steps, streams, depth), BF16),
            hbm((steps, streams, depth), F32),
        )
        aliases = {12 + i: 1 + i for i in range(len(stacks))}
        aliases.update({12 + len(stacks) + i: 7 + i for i in range(len(passing))})
        inflow, *out = pl.pallas_call(
            functools.partial(between_kernel, not stacks, step == steps - 1, len(passing)),
            out_shape=(vmem(gates_shape, F32),) + shapes + tuple(hbm(x.shape, x.dtype) for x in passing),
            in_specs=[SMEM] + [VMEM] * 11 + [ANY] * (len(stacks) + len(passing)),
            out_specs=[VMEM] + [ANY] * (6 + len(passing)),
            scratch_shapes=[pltpu.SemaphoreType.DMA((2 * PIECES + 4,))],
            input_output_aliases=aliases,
            compiler_params=params(8),
            cost_estimate=cost(2 * streams * depth * 8 * cells, 8 * depth * cells * 2),
            name="between",
        )(
            at_step(step), pinned(feats_v), pinned(bias_av), pinned(bias_bv), pinned(win_av), pinned(win_bv),
            *(pinned(x) for x in fresh), *(in_hbm(x) for x in (*stacks, *passing)),
        )
        return inflow, tuple(out[:6]), tuple(out[6:])

    none = jnp.zeros((streams, depth), BF16)
    part, peer, cell, stacks = none, none, start_cv, ()
    for step in range(steps):
        cell_before = cell
        part, cell, *fresh = forward_call(step == 0, step, part, peer, cell, inflow)
        peer = lax.ppermute(part, "gate", across)
        if step == steps - 1:
            break
        if step == 2:
            (feat_all,) = after((part,), feat_all)
            feat_in = (swapped(feat_all, near_swap), swapped(feat_all, far_swap))
        due = step == (3 * steps) // 4
        inflow, stacks, passed = between_call(step, (cell, *fresh), stacks, feat_in if due else ())
        feat_in = passed if due else (feat_in if step >= 2 else None)
    gates, mixed, prev, hidden, slope = fresh
    gates_all, cells_all, mixed_all, prev_all, hidden_all, slope_all = stacks

    slope_now, up_now, mixed_all, prev_all, hidden_all, slope_all = pl.pallas_call(
        finish_kernel,
        out_shape=(vmem((streams, depth), F32), vmem((streams, depth), BF16))
        + tuple(hbm(x.shape, x.dtype) for x in (mixed_all, prev_all, hidden_all, slope_all)),
        in_specs=[SMEM] + [VMEM] * 6 + [ANY] * 5,
        out_specs=[VMEM] * 2 + [ANY] * 4,
        scratch_shapes=[pltpu.VMEM((streams, depth), BF16), pltpu.SemaphoreType.DMA((PIECES + 5,))],
        input_output_aliases={8 + i: 2 + i for i in range(4)},
        compiler_params=params(8),
        name="finish",
    )(
        at_step(steps - 1), pinned(part), pinned(peer), *(pinned(x) for x in (mixed, prev, hidden, slope)), in_hbm(ups),
        *(in_hbm(x) for x in (mixed_all, prev_all, hidden_all, slope_all)),
    )
    saved = (gates, cell, cell_before, slope_now, up_now)
    saved_shapes = (
        vmem(gates_shape, BF16),
        vmem(cell_shape, F32),
        vmem(cell_shape, F32),
        vmem((streams, depth), F32),
        vmem((streams, depth), BF16),
    )

    rec_atv, rec_btv, proj_atv, proj_btv = pl.pallas_call(
        turned_kernel,
        out_shape=(vmem((4, cells, depth), BF16),) * 2 + (vmem((depth, cells), BF16),) * 2,
        in_specs=[VMEM] * 4,
        out_specs=[VMEM] * 4,
        compiler_params=params(8),
        name="turned",
    )(pinned(rec_av), pinned(rec_bv), pinned(proj_av), pinned(proj_bv))

    def backward_call(step, part, peer, grad, bias, saved):
        return pl.pallas_call(
            backward_kernel,
            out_shape=(
                vmem((streams, depth), BF16),
                vmem(cell_shape, F32),
                vmem(bias_shape, F32),
                vmem((streams, depth), BF16),
                vmem(gates_shape, BF16),
            ),
            in_specs=[SMEM] + [VMEM] * 15,
            out_specs=[VMEM] * 5,
            compiler_params=params(8),
            name="backward_step",
        )(
            at_step(step), pinned(part), pinned(peer), pinned(keep_v), pinned(grad), pinned(bias),
            pinned(rec_atv), pinned(rec_btv), pinned(proj_atv), pinned(proj_btv),
            *(pinned(x) for x in saved), pinned(start_cv),
        )

    def aside_call(step, slot, slots, dz, raw, stacks, sends, passing):
        piece_shape = (streams, 4 * width)
        shapes = (
            hbm((PIECES, steps) + piece_shape, BF16),
            hbm((steps, streams, depth), BF16),
            hbm((steps,) + piece_shape, BF16),
            hbm((steps,) + piece_shape, BF16),
            hbm((slots,) + piece_shape, BF16),
            hbm((slots,) + piece_shape, BF16),
        )
        kept = len(stacks)
        aliases = {7 + i: 5 + i for i in range(kept)}
        aliases.update({7 + kept + i: 9 + i for i in range(len(sends))})
        aliases.update({7 + kept + len(sends) + i: 11 + i for i in range(len(passing))})
        out = pl.pallas_call(
            functools.partial(aside_kernel, not stacks, step == 0, not sends, len(passing)),
            out_shape=saved_shapes + shapes + tuple(hbm(x.shape, x.dtype) for x in passing),
            in_specs=[SMEM] + [VMEM] * 2 + [ANY] * (4 + kept + len(sends) + len(passing)),
            out_specs=[VMEM] * 5 + [ANY] * (6 + len(passing)),
            scratch_shapes=[
                pltpu.SemaphoreType.DMA((PIECES + 5,)),
                pltpu.SemaphoreType.DMA((PIECES + 4,)),
            ],
            input_output_aliases=aliases,
            compiler_params=params(8),
            cost_estimate=cost(0, 8 * MIB),
            name="aside",
        )(
            jnp.concatenate([at_step(step), jnp.stack([jnp.int32(slot), low, high])]), pinned(dz), pinned(raw),
            in_hbm(gates_all), in_hbm(cells_all), in_hbm(ups), in_hbm(slope_all),
            *(in_hbm(x) for x in (*stacks, *sends, *passing)),
        )
        return out[:5], tuple(out[5:9]), tuple(out[9:11]), tuple(out[11:])

    carry = (none, none, jnp.zeros(cell_shape, F32), jnp.zeros(bias_shape, F32), saved, ())
    pending, arrived, ready, top = [], [], None, steps
    for index, share in enumerate(SHARES):
        slots = top if index == len(SHARES) - 1 else round(share * steps)
        sends = ()
        for step in range(top - 1, top - slots - 1, -1):
            part, peer, grad, bias_sum, saved, stacks = carry
            part, grad, bias_sum, raw, dz = backward_call(step, part, peer, grad, bias_sum, saved)
            peer = lax.ppermute(part, "gate", across)
            if step == steps - 1:
                (prev_all,) = after((part,), prev_all)
                pending.append((step - steps // 3, (swapped(prev_all, near_swap), swapped(prev_all, far_swap))))
            if ready is not None:
                due, sides = ready
                sides = after((part,), *sides) if step else sides
                pending.append((due, (swapped(sides[0], near_swap), swapped(sides[1], far_swap))))
                ready = None
            passing = ()
            while pending and pending[0][0] >= step:
                passing += pending.pop(0)[1]
            saved, stacks, sends, passed = aside_call(
                step, step - (top - slots), slots, dz, raw, stacks, sends, passing
            )
            arrived += [passed[i : i + 2] for i in range(0, len(passed), 2)]
            carry = (part, peer, grad, bias_sum, saved, stacks)
        top -= slots
        ready = (max(top - 1 - (3 * slots + 3) // 4, 0 if slots > 2 else -1), sends)
    pending.append((-1, (swapped(sends[0], near_swap), swapped(sends[1], far_swap))))
    arrived += [arrays for _, arrays in pending]
    dz_all, raw_all, near_all, far_all = carry[-1]
    bias_sum = carry[3]
    prev_in, exchanged = arrived[0], arrived[1:]
    rows = steps * streams

    def by_direction(mine, theirs):
        return jnp.stack([jnp.where(own == 0, mine, theirs), jnp.where(own == 0, theirs, mine)])

    def line_sum(chunks, axis, stride, count, first=None, gates={}, hooks={}):
        def chunk(*name):
            return pick(chunks, number[(stride, *name)], axis)

        def at(device):
            return (device // stride) % count

        if count == 2:
            pairs = [(i, i + stride if at(i) == 0 else i - stride) for i in range(n_batch)]
            return (chunk("here").astype(F32) + swapped(chunk("not_here"), pairs).astype(F32)).astype(BF16)
        ends = [(i, i + stride) for i in range(n_batch) if at(i) == 0]
        ends += [(i, i - stride) for i in range(n_batch) if at(i) == count - 1]
        up = down = swapped(chunk("begin") if first is None else first, ends)
        for slot in range(2, count):
            if slot in gates:
                up, down = gates[slot](up, down)
            rise = (chunk("rise", slot).astype(F32) + up.astype(F32)).astype(BF16)
            fall = (chunk("fall", slot).astype(F32) + down.astype(F32)).astype(BF16)
            if slot in hooks:
                hooks[slot](rise, fall)
            up = swapped(rise, [(i, i + stride) for i in range(n_batch) if at(i) < min(slot, count - 1)])
            down = swapped(fall, [(i, i - stride) for i in range(n_batch) if at(i) > max(count - 1 - slot, 0)])
        if count in gates:
            up, down = gates[count](up, down)
        return (chunk("here").astype(F32) + up.astype(F32) + down.astype(F32)).astype(BF16)

    share_rows = depth // n_batch

    def input_grad_of(dz):
        return pl.pallas_call(
            input_grad_kernel,
            out_shape=jax.ShapeDtypeStruct((steps, streams, depth), F32),
            grid_spec=pltpu.PrefetchScalarGridSpec(
                num_scalar_prefetch=1,
                grid=(PIECES, 4),
                in_specs=[
                    pl.BlockSpec((1, steps, streams, width), lambda p, g, turn: (p, 0, 0, g)),
                    pl.BlockSpec(
                        (1, depth, width), lambda p, g, turn: (jnp.where(p < 2, g, 3), 0, jnp.where(p < 2, p, 1))
                    ),
                    pl.BlockSpec(
                        (1, depth, width), lambda p, g, turn: (jnp.where(p < 2, 0, g), 0, jnp.where(p < 2, 0, p - 2))
                    ),
                ],
                out_specs=pl.BlockSpec((steps, streams, depth), lambda p, g, turn: (0, 0, 0)),
                scratch_shapes=[pltpu.VMEM((rows, depth), F32)],
            ),
            compiler_params=params(16),
            cost_estimate=cost(0, 0),
            name="input_grad",
        )(turn, in_hbm(dz), in_hbm(win_a), in_hbm(win_b))

    grad_proj = jnp.einsum("ptnc,tnk->pkc", mixed_all, raw_all, preferred_element_type=F32).astype(BF16)
    grad_proj = grad_proj.reshape(PIECES, line, 2, share_rows, width)
    bias_rows = pl.pallas_call(
        bias_kernel,
        out_shape=jax.ShapeDtypeStruct((PIECES, 4, width), F32),
        in_specs=[VMEM],
        out_specs=VMEM,
        compiler_params=params(1),
        name="bias",
    )(pinned(bias_sum))
    bias_rows = jnp.broadcast_to(bias_rows[:, None, None].astype(BF16), (PIECES, line, 2, 4, width))
    grad_proj = jnp.concatenate([grad_proj, bias_rows], axis=3)

    def with_partner(grad):
        mine, sent = (pick(grad, number[x], grad.ndim - 3) for x in ("low", "not_low"))
        taken = swapped(sent, near_swap)
        return sent, taken, (mine.astype(F32) + taken.astype(F32)).astype(BF16)

    def across_two(grad):
        return line_sum(grad.reshape(grad.shape[:-3] + (line // 2, 2) + grad.shape[-2:]), grad.ndim - 3, 4, line // 2)

    proj_sent, proj_taken, proj_y = with_partner(grad_proj)

    lows, count = [], 0
    for x in exchanged[::-1]:
        lows.insert(0, count)
        count += x[0].shape[0]

    def gathered(kept, feat, prev, parts):
        return pl.pallas_call(
            functools.partial(gather_kernel, tuple(lows[: len(parts)])),
            out_shape=(vmem((2 * steps, streams, 2 * depth), BF16), vmem((2 * steps, streams, 4 * width), BF16)),
            in_specs=[ANY] * (5 + len(parts)),
            out_specs=[VMEM] * 2,
            scratch_shapes=[pltpu.SemaphoreType.DMA((5 + len(parts),))],
            compiler_params=params(1),
            cost_estimate=cost(0, 0),
            name="gather",
        )(*(in_hbm(x) for x in (feat_all, prev_all, feat, prev, kept, *parts)))

    def completed(begin, rows_out, left, right, parts):
        return pl.pallas_call(
            functools.partial(late_kernel, tuple(lows[len(lows) - len(parts) :])),
            out_shape=(vmem(right.shape, BF16), jax.ShapeDtypeStruct((2, max(rows_out, 8), 4 * width), BF16)),
            in_specs=[SMEM] + [VMEM] * 2 + [ANY] * len(parts),
            out_specs=[VMEM] * 2,
            scratch_shapes=[pltpu.SemaphoreType.DMA((len(parts),))],
            input_output_aliases={2: 0},
            compiler_params=params(16),
            cost_estimate=cost(0, 0),
            name="late",
        )(begin, pinned(left), pinned(right), *(in_hbm(x) for x in parts))

    def multiplied(left, right):
        return pl.pallas_call(
            product_kernel,
            out_shape=jax.ShapeDtypeStruct((2, depth, 4 * width), BF16),
            in_specs=[VMEM] * 2,
            out_specs=VMEM,
            compiler_params=params(16),
            cost_estimate=cost(0, 0),
            name="product",
        )(pinned(left), pinned(right))

    near_parts, far_parts = zip(*exchanged)
    chunk_rows = 2 * share_rows if 2 * share_rows % 128 == 0 else 0
    near_left, near_right = gathered(near_all, feat_in[0], prev_in[0], near_parts[:-LATE])
    near_late = after((near_left, proj_sent, *far_parts[-LATE:]), *near_parts[-LATE:])
    near_right, first = completed(jnp.full((1,), number["begin"], jnp.int32), chunk_rows, near_left, near_right, near_late)
    far_all, *far_parts = after((first,), far_all, *far_parts)
    blocks = 4

    def far_product(mine, theirs):
        grad = pl.pallas_call(
            functools.partial(whole_product_kernel, tuple(lows)),
            out_shape=jax.ShapeDtypeStruct((depth, 4 * width), BF16),
            in_specs=[ANY] * (3 + len(far_parts)),
            out_specs=VMEM,
            scratch_shapes=[
                pltpu.VMEM((2 * steps, streams, depth), BF16),
                pltpu.VMEM((depth, 2 * steps * streams), BF16),
                pltpu.VMEM((blocks, 2 * steps, streams, 4 * width // blocks), BF16),
                pltpu.SemaphoreType.DMA((2,)),
                pltpu.SemaphoreType.DMA((blocks, 1 + len(far_parts))),
            ],
            compiler_params=params(24),
            cost_estimate=cost(0, 0),
            name="whole_product",
        )(*(in_hbm(x) for x in (mine, theirs, far_all, *far_parts)))
        return grad.reshape(line, 2, share_rows, 4 * width)

    far_in = far_product(feat_all, feat_in[1])
    near = multiplied(near_left, near_right).reshape(2, line, 2, share_rows, 4 * width)

    def states_of(hidden, cell):
        both_hidden = trade(hidden, hidden)

        hidden_dirs = by_direction(*both_hidden)
        outputs = (inputs.astype(F32) + jnp.transpose(hidden_dirs, (0, 2, 1, 3)).astype(F32)).astype(BF16)
        last_h = jnp.stack([hidden_dirs[0, steps - 1], hidden_dirs[1, 0]], axis=1).astype(F32)
        final_h = jnp.zeros_like(state_h).at[stream_doc].set(last_h)
        last_c = jnp.transpose(cell.reshape(QUARTERS, HALVES, streams, width), (0, 2, 1, 3)).reshape(
            QUARTERS, streams, cells
        )
        last_dirs = by_direction(*trade(last_c[0], last_c[1]))
        final_c = jnp.zeros_like(state_c).at[stream_doc].set(jnp.transpose(last_dirs, (1, 0, 2)))
        return outputs, final_h, final_c

    tokens = {}

    def second(up, down):
        up, tokens["far"], tokens["dz"], tokens["proj"], tokens["prev"] = after(
            (), up, far_in, dz_all, proj_y, prev_in[1], free=5 * MIB
        )
        return up, up

    def beside_second(rise, fall):
        (sent,) = after((rise, fall), tokens["far"], free=5 * MIB)
        tokens["in"] = with_partner(sent)[2]
        tokens["rec"] = with_partner(far_product(prev_all, tokens["prev"]))[2]
        tokens["proj"] = across_two(tokens["proj"])

    def third(up, down):
        dx = input_grad_of(tokens["dz"])
        up, down, tokens["dx"], in_sum, tokens["proj"], hidden, last_cell = after(
            (), up, down, dx, tokens["in"], tokens["proj"], hidden_all, cell, free=2 * MIB
        )
        tokens["in"] = across_two(in_sum)
        tokens["states"] = states_of(hidden, last_cell)
        return up, down

    def final(up, down):
        up, down, tokens["in"], rec_sum = after(
            tokens["states"][1:], up, down, tokens["in"], tokens["rec"], free=2 * MIB
        )
        tokens["rec"] = across_two(rec_sum)
        return up, down

    gates = {2: second, 3: third, line: final} if line > 3 else {}
    hooks = {2: beside_second} if line > 3 else {}
    first = first.reshape(2, 2, share_rows, 4 * width) if chunk_rows else None
    near = line_sum(near, 1, 2, line, first, gates, hooks)
    dx_all, (outputs, final_h, final_c) = tokens["dx"], tokens["states"]
    in_two, rec_two, proj_two = tokens["in"], tokens["rec"], tokens["proj"]

    def halves_of(summed, name, pairs):
        return pick(summed, number[name], 1), swapped(pick(summed, number["not_" + name], 1), pairs)

    near_pair = halves_of(near, "low", near_swap)
    in_pair, rec_pair = (
        [lax.ppermute(y, "gate", swap) for y in halves_of(x[None], "high", far_swap)] for x in (in_two, rec_two)
    )
    proj_mine, proj_theirs = halves_of(proj_two, "high", far_swap)
    grad_proj = proj_mine.astype(F32) + proj_theirs.astype(F32)
    grad_shape = (2, share_rows, 4, cells)
    grad_w_in, grad_w_rec = pl.pallas_call(
        assemble_kernel,
        out_shape=(jax.ShapeDtypeStruct(grad_shape, F32),) * 2,
        in_specs=[SMEM] + [VMEM] * 6,
        out_specs=[VMEM] * 2,
        compiler_params=params(14),
        name="assemble",
    )(jnp.stack([own, low, high]), *near_pair, *in_pair, *rec_pair)

    def home(mine, theirs):
        return by_direction(*trade(mine, theirs)).astype(F32)

    own_cells = cells // n_batch
    shaped = jnp.transpose(grad_proj[:, share_rows:].reshape(QUARTERS, HALVES, 4, width), (0, 2, 1, 3))
    shaped = pick(shaped.reshape(QUARTERS, 4, n_batch, own_cells), number["spot"], 2)
    grad_bias = home(shaped[0], shaped[1])
    grad_proj = grad_proj[:, :share_rows].reshape(QUARTERS, HALVES, share_rows, width)
    grad_proj = jnp.transpose(grad_proj, (0, 1, 3, 2)).reshape(QUARTERS, cells, share_rows).astype(BF16)
    grad_proj = home(grad_proj[0], grad_proj[1])

    def columns(array, name, size):
        return lax.dynamic_slice_in_dim(array, number[name], size, 2, allow_negative_indices=False)

    dx_half = columns(dx_all, "cols", half_cols)
    dx_sent = columns(dx_all, "other_cols", half_cols).astype(BF16)
    dx_half = dx_half + lax.ppermute(dx_sent, "gate", across).astype(F32)
    dx_half = (dx_half + columns(ups, "cols", half_cols).astype(F32)).astype(BF16)
    dx_half = dx_half.reshape(steps, streams, 2, quarter_cols)
    dx_dirs = by_direction(*trade(pick(dx_half, own, 2), pick(dx_half, number["other"], 2)))
    input_grad = jnp.transpose(dx_dirs, (0, 2, 1, 3))
    return (outputs, input_grad, grad_w_in, grad_w_rec, grad_bias, grad_proj, final_h, final_c)


def solution(mesh):
    placed = (
        P(None, "batch", None, None),
        P(None, None, None, "gate"),
        P(None, None, None, "gate"),
        P(None, None, "gate"),
        P(None, "gate", None),
        P("batch", None, None),
        P("batch", None, "gate"),
        P("batch", None),
        P("batch"),
        P(None, "batch", None, None),
    )
    return jax.shard_map(
        body,
        mesh=mesh,
        in_specs=placed,
        out_specs=(
            P(None, "batch", None, None),
            P(None, "batch", None, "gate"),
            P(None, "batch", None, "gate"),
            P(None, "batch", None, "gate"),
            P(None, None, ("gate", "batch")),
            P(None, "gate", "batch"),
            P("batch", None, None),
            P("batch", None, "gate"),
        ),
        check_vma=False,
    )
```
